128 devices in a mesh: ctx: 16 (over z, x_lo, core), tp: 8 (over x_hi, y).
Axes of the slice: x: 4 (x_hi: 2, x_lo: 2; x = x_hi * 2 + x_lo), y: 4, z: 4, core: 2. Of those that a mesh axis runs over, the one named last changes fastest.
Arguments:
- tokens: bfloat16 [2, 2048, 2048], P(None, 'ctx', 'tp'), may hold values from -6 to 6
- norm1_gain: float32 [2048], replicated, may hold values from 0.5 to 1.5
- router_attn: bfloat16 [2048, 4], replicated, may hold values from -0.125 to 0.125
- w_query: bfloat16 [4, 2048, 2048], P(None, 'ctx', 'tp'), may hold values from -0.125 to 0.125
- w_key_value: bfloat16 [2048, 2, 2048], P('ctx', None, 'tp'), may hold values from -0.125 to 0.125
- w_out: bfloat16 [4, 2048, 2048], P(None, 'tp', 'ctx'), may hold values from -1 to 1
- norm2_gain: float32 [2048], replicated, may hold values from 0.5 to 1.5
- router_ffn: bfloat16 [2048, 4], replicated, may hold values from -0.125 to 0.125
- w_gate_up: bfloat16 [4, 2048, 2, 5632], P(None, 'ctx', None, 'tp'), may hold values from -0.125 to 0.125
- w_down: bfloat16 [4, 5632, 2048], P(None, 'tp', 'ctx'), may hold values from -0.078125 to 0.078125
- adapt_wide: float32 [2, 22, 16, 2048], P(None, None, None, ('ctx', 'tp'))
- adapt_heads: float32 [2, 10, 16, 2048], P(None, None, None, 'tp')
- adapt_ffn: float32 [2, 12, 16, 5632], P(None, None, None, 'tp')
- attention_routes: int32 [2, 2048, 2], P(None, 'ctx'), may hold values from 0 to 3, all different within a row
- feedforward_routes: int32 [2, 2048, 2], P(None, 'ctx'), may hold values from 0 to 3, all different within a row
- doc_lengths: int32 [2, 8], replicated, may hold values from 0 to 2048, as said below
- adapter_index: int32 [2], replicated, may hold values from 0 to 1, each once
- cotangent: bfloat16 [2, 2048, 2048], P(None, 'ctx', 'tp'), may hold values from -6 to 6
Outputs:
- mixed: bfloat16 [2, 2048, 2048], P(None, 'ctx', 'tp')
- grad_tokens: bfloat16 [2, 2048, 2048], P(None, 'ctx', 'tp')
- grad_wide: float32 [2, 22, 16, 2048], P(None, None, None, ('ctx', 'tp'))
- grad_heads: float32 [2, 10, 16, 2048], P(None, None, None, 'tp')
- grad_ffn: float32 [2, 12, 16, 5632], P(None, None, None, 'tp')
The draws below stay inside these ranges and needn't reach their ends.
Inputs may be any that keep to these rules, and one draw needn't show every extreme that they name: `doc_lengths`: each row sums to at most 2048; positions past the sum are padding; in every draw one sequence, drawn from the seed, is a single document of 2048 positions. `attention_routes`: each token names 2 different attention experts. `feedforward_routes`: each token names 2 different feed-forward experts. `adapter_index`: each adapter set serves exactly one sequence.
All inputs are finite; a program needn't handle non-finite values.
Results may differ from the reference program's by a relative error of at most 0.03.
Values may be sent and summed in bfloat16 or wider, within the bound.
A program may use at most 384 MiB of HBM per device.

```python
import jax
import jax.numpy as jnp
from jax import lax

D = 2048
HEADS = 16
HEAD_DIM = 128
FF = 5632
TOPK = 2
ATTENTION_EXPERTS = 4
FEEDFWD_EXPERTS = 4
RANK = 16
WINDOW = 1024
SEQ_LEN = 2048
DOCS = 8
SEQS = 2
ADAPTERS = 2
INNER = 2048
WIDE_SLOTS = 22
HEAD_SLOTS = 10
FFN_SLOTS = 12


def slot_values(key, shape):
    return jax.random.normal(key, shape, jnp.float32)


def draw_adapt_wide(key, part):
    key = jax.random.fold_in(key, 11)
    slots = jnp.arange(WIDE_SLOTS)
    first_out = ATTENTION_EXPERTS + 2 + 2 * FEEDFWD_EXPERTS
    scales = jnp.where(slots < first_out, D ** (-0.5), jnp.where(slots < first_out + ATTENTION_EXPERTS, 2.0, 0.25))
    return slot_values(key, (ADAPTERS, WIDE_SLOTS, RANK, D)) * scales[None, :, None, None]


def draw_adapt_heads(key, part):
    key = jax.random.fold_in(key, 12)
    slots = jnp.arange(HEAD_SLOTS)
    scales = jnp.where(slots < ATTENTION_EXPERTS + 2, 0.25, INNER ** (-0.5))
    return slot_values(key, (ADAPTERS, HEAD_SLOTS, RANK, INNER)) * scales[None, :, None, None]


def draw_adapt_ffn(key, part):
    key = jax.random.fold_in(key, 13)
    slots = jnp.arange(FFN_SLOTS)
    scales = jnp.where(slots < 2 * FEEDFWD_EXPERTS, 0.25, FF ** (-0.5))
    return slot_values(key, (ADAPTERS, FFN_SLOTS, RANK, FF)) * scales[None, :, None, None]


def draw_doc_lengths(key, part):
    key = jax.random.fold_in(key, 5)
    keys_three = jax.random.split(key, 3)
    padding = jax.random.randint(keys_three[0], (SEQS, 1), 0, SEQ_LEN // 8 + 1)
    usable = SEQ_LEN - padding
    cuts = jnp.sort(jax.random.randint(keys_three[1], (SEQS, DOCS - 1), 0, SEQ_LEN + 1), axis=1)
    cuts = jnp.minimum(cuts, usable)
    bounds = jnp.concatenate([jnp.zeros((SEQS, 1), jnp.int32), cuts, usable], axis=1)
    lengths = bounds[:, 1:] - bounds[:, :-1]
    whole_seq = jax.random.randint(keys_three[2], (), 0, SEQS)
    single = jnp.zeros((DOCS,), jnp.int32).at[0].set(SEQ_LEN)
    chosen = (jnp.arange(SEQS) == whole_seq)[:, None]
    return jnp.where(chosen, single[None, :], lengths).astype(jnp.int32)


def level_of(rng, shape, cuts, low, top_value):
    def one(dim, shards_of):
        steps = jax.random.uniform(jax.random.fold_in(jax.random.fold_in(rng, 6), dim), (shards_of,), jnp.float32, low / len(cuts), top_value / len(cuts))
        return jnp.repeat(jnp.exp(steps), shape[dim] // shards_of).reshape((-1,) + (1,) * (len(shape) - dim - 1))

    loudness = one(*cuts[0])
    for cut in cuts[1:]:
        loudness = loudness * one(*cut)
    return loudness


def different_ones(key, rows, number_of, top, lift):
    ranking = jax.random.permutation(jax.random.fold_in(key, 1), number_of)
    pull = ranking
    for power in range(3):
        pull = pull * pull // number_of
    pull = pull * lift // number_of
    tickets = jax.random.randint(jax.random.fold_in(key, 2), (rows, number_of), 0, 4096) + pull
    holders = jax.random.permutation(jax.random.fold_in(key, 3), rows)[jnp.arange(number_of) % rows]
    tickets = jnp.where(jnp.arange(rows)[:, None] == holders[None, :], 1 << 14, tickets)
    priority = tickets * number_of + jnp.arange(number_of)
    return lax.top_k(priority.astype(jnp.int32), top)[1].astype(jnp.int32)


def scatter_about(key, shape, scale, reach, cuts=(), kind=jnp.bfloat16):
    factor_of = level_of(key, shape, cuts, -0.22, 0.18) if cuts else 1.0
    array = jax.random.normal(key, shape, jnp.float32) * scale * factor_of
    return jnp.minimum(jnp.maximum(array, -reach), reach).astype(kind)


def setup_inputs(seed: int = 0) -> dict:
    key_of = jax.random.split(jax.random.key(seed), 19)
    tokens = scatter_about(key_of[0], (SEQS, SEQ_LEN, D), 1.0, 6.0, ((1, 16), (2, 8)))
    norm1_gain = jnp.clip(1.0 + 0.1 * jax.random.normal(key_of[1], (D,), jnp.float32), 0.5, 1.5)
    router_attn = scatter_about(key_of[2], (D, ATTENTION_EXPERTS), D ** -0.5, 0.125)
    w_query = scatter_about(key_of[3], (ATTENTION_EXPERTS, D, INNER), D ** -0.5, 0.125, ((1, 16), (2, 8)))
    w_key_value = scatter_about(key_of[4], (D, 2, INNER), D ** -0.5, 0.125, ((0, 16), (2, 8)))
    w_out = scatter_about(key_of[5], (ATTENTION_EXPERTS, INNER, D), (INNER // 64) ** -0.5, 1.0, ((1, 8), (2, 16)))
    norm2_gain = jnp.clip(1.0 + 0.1 * jax.random.normal(key_of[6], (D,), jnp.float32), 0.5, 1.5)
    router_ffn = scatter_about(key_of[7], (D, FEEDFWD_EXPERTS), D ** -0.5, 0.125)
    w_gate_up = scatter_about(key_of[8], (FEEDFWD_EXPERTS, D, 2, FF), D ** -0.5, 0.125, ((1, 16), (3, 8)))
    w_down = scatter_about(key_of[9], (FEEDFWD_EXPERTS, FF, D), FF ** -0.5, 0.078125, ((1, 8), (2, 16)))
    adapt_wide = draw_adapt_wide(jax.random.fold_in(key_of[18], 71), 0)
    adapt_heads = draw_adapt_heads(jax.random.fold_in(key_of[18], 71), 0)
    adapt_ffn = draw_adapt_ffn(jax.random.fold_in(key_of[18], 71), 0)
    attention_routes = different_ones(key_of[13], SEQS * SEQ_LEN, ATTENTION_EXPERTS, TOPK, 4096).reshape((SEQS, SEQ_LEN, TOPK))
    feedforward_routes = different_ones(key_of[14], SEQS * SEQ_LEN, FEEDFWD_EXPERTS, TOPK, 4096).reshape((SEQS, SEQ_LEN, TOPK))
    doc_lengths = draw_doc_lengths(jax.random.fold_in(key_of[18], 71), 0)
    adapter_index = jax.random.permutation(key_of[16], ADAPTERS).astype(jnp.int32)
    cotangent = scatter_about(key_of[17], (SEQS, SEQ_LEN, D), 1.0, 6.0, ((1, 16), (2, 8)))
    return {"tokens": tokens, "norm1_gain": norm1_gain, "router_attn": router_attn, "w_query": w_query, "w_key_value": w_key_value, "w_out": w_out, "norm2_gain": norm2_gain, "router_ffn": router_ffn, "w_gate_up": w_gate_up, "w_down": w_down, "adapt_wide": adapt_wide, "adapt_heads": adapt_heads, "adapt_ffn": adapt_ffn, "attention_routes": attention_routes, "feedforward_routes": feedforward_routes, "doc_lengths": doc_lengths, "adapter_index": adapter_index, "cotangent": cotangent}


@jax.custom_vjp
def low(v):
    return lax.optimization_barrier(v.astype(jnp.bfloat16)).astype(jnp.float32)

@jax.custom_vjp
def low_back(v):
    return v

def low_keep(v):
    return (low(v), None)

def low_pass(kept, grad):
    return (grad,)

def back_keep(v):
    return (v, None)

def back_low(kept, grad):
    return (low(grad),)
low.defvjp(low_keep, low_pass)
low_back.defvjp(back_keep, back_low)
highest = lax.Precision.HIGHEST
eps = 1e-06

def multiplier(form, left, right):
    return jnp.einsum(form, left, right, precision=highest)

def rms_scale(values, gain):
    return values * lax.rsqrt(lax.optimization_barrier(jnp.mean(values * values, axis=-1, keepdims=True)) + eps) * gain

def doc_layout(doc_lengths, positions):
    ends = jnp.cumsum(doc_lengths, axis=1)
    passed = positions[None, :, None] >= ends[:, None, :]
    doc_ids = lax.optimization_barrier(jnp.sum(passed.astype(jnp.int32), axis=2))
    starting = lax.optimization_barrier(jnp.sum(jnp.where(passed, doc_lengths[:, None, :], 0), axis=2))
    inside = positions[None, :] < ends[:, -1:]
    doc_ids = jnp.where(inside, doc_ids, -1 - positions[None, :])
    return (doc_ids, positions[None, :] - starting)

def rotate(values, offsets):
    half_dim = values.shape[-1] // 2
    frequency = 10000.0 ** (-2.0 * jnp.arange(half_dim, dtype=jnp.float32) / values.shape[-1])
    angles = offsets.astype(jnp.float32)[..., None] * frequency
    angles = angles.reshape(angles.shape[:2] + (1,) * (values.ndim - 3) + (half_dim,))
    cosine = jnp.cos(angles)
    sine_part = jnp.sin(angles)
    first_half = values[..., :half_dim]
    second_half = values[..., half_dim:]
    return jnp.concatenate([first_half * cosine - second_half * sine_part, second_half * cosine + first_half * sine_part], axis=-1)

def mixture_weights(logits, routes, expert_count):
    chosen = jnp.take_along_axis(logits, routes, axis=-1)
    gates = jax.nn.softmax(chosen, axis=-1)
    return multiplier('slk,slke->sle', gates, jax.nn.one_hot(routes, expert_count, dtype=jnp.float32))

def reference(tokens, norm1_gain, router_attn, w_query, w_key_value, w_out, norm2_gain, router_ffn, w_gate_up, w_down, adapt_wide, adapt_heads, adapt_ffn, attention_routes, feedforward_routes, doc_lengths, adapter_index, cotangent):
    attention_router_weight = router_attn.astype(jnp.float32)
    query_matrix = w_query.astype(jnp.float32)
    key_value_weight = w_key_value.astype(jnp.float32)
    out_weight = w_out.astype(jnp.float32)
    feedforward_router_weight = router_ffn.astype(jnp.float32)
    gate_up_matrix = w_gate_up.astype(jnp.float32)
    down_weight = w_down.astype(jnp.float32)
    positions = jnp.arange(SEQ_LEN, dtype=jnp.int32)
    doc_ids, offsets = doc_layout(doc_lengths, positions)
    score_scale = HEAD_DIM ** (-0.5)
    query_block = min(256, SEQ_LEN)
    block_starts = jnp.arange(SEQ_LEN // query_block, dtype=jnp.int32) * query_block
    adapter_slot_key_value = ATTENTION_EXPERTS
    adapter_slot_gate = ATTENTION_EXPERTS + 2
    slot_up = adapter_slot_gate + FEEDFWD_EXPERTS
    adapter_slot_output = slot_up + FEEDFWD_EXPERTS
    slot_down = adapter_slot_output + ATTENTION_EXPERTS

    def forward(resid_in, wide_adapter, head_adapter, feedforward_adapter):
        wide_adapter = low(wide_adapter)[adapter_index]
        head_adapter = low(head_adapter)[adapter_index]
        feedforward_adapter = low(feedforward_adapter)[adapter_index]
        first_normalized = low(rms_scale(resid_in, norm1_gain))
        attention_mixture = mixture_weights(multiplier('nkh,hg->nkg', first_normalized, attention_router_weight), attention_routes, ATTENTION_EXPERTS)
        lowrank_query = multiplier('nig,nvhg->nivh', first_normalized, wide_adapter[:, :ATTENTION_EXPERTS])
        query_every_expert = multiplier('cfn,mnw->cfmw', first_normalized, query_matrix) + multiplier('wgyj,wyja->wgya', lowrank_query, head_adapter[:, :ATTENTION_EXPERTS])
        query_every_expert = low_back(query_every_expert)
        query_pick = jnp.take_along_axis(query_every_expert, attention_routes[..., None], axis=2)
        queries = low(rotate(query_pick.reshape(SEQS, SEQ_LEN, TOPK, HEADS, HEAD_DIM), offsets))
        lowrank_key_value = multiplier('xha,xfba->xhfb', first_normalized, wide_adapter[:, adapter_slot_key_value:adapter_slot_key_value + 2])
        key_value_rows = multiplier('nbq,qjg->nbjg', first_normalized, key_value_weight) + multiplier('njik,niku->njiu', lowrank_key_value, head_adapter[:, adapter_slot_key_value:adapter_slot_key_value + 2])
        key_value_rows = low_back(key_value_rows)
        keys = low(rotate(key_value_rows[:, :, 0].reshape(SEQS, SEQ_LEN, HEADS, HEAD_DIM), offsets))
        values = low(key_value_rows[:, :, 1]).reshape(SEQS, SEQ_LEN, HEADS, HEAD_DIM)

        def attend(first_row):
            query_rows = lax.dynamic_slice_in_dim(queries, first_row, query_block, 1)
            query_pos = first_row + jnp.arange(query_block, dtype=jnp.int32)
            query_doc = lax.dynamic_slice_in_dim(doc_ids, first_row, query_block, 1)
            allowed = (query_doc[:, :, None] == doc_ids[:, None, :]) & (positions[None, None, :] <= query_pos[None, :, None]) & (query_pos[None, :, None] - positions[None, None, :] < WINDOW)
            scores = low_back(multiplier('sqthd,skhd->sthqk', query_rows, keys) * score_scale)
            scores = jnp.where(allowed[:, None, None], scores, -1e+30)
            largest = lax.optimization_barrier(jnp.max(scores, axis=-1, keepdims=True))
            weights = jnp.exp(scores - largest)
            probs = weights / lax.optimization_barrier(jnp.sum(weights, axis=-1, keepdims=True))
            return multiplier('sthqk,skhd->sqthd', low(probs), values)
        attended = lax.map(jax.checkpoint(attend), block_starts)
        attended = jnp.moveaxis(attended, 0, 1).reshape(SEQS, SEQ_LEN, TOPK, HEADS * HEAD_DIM)
        attended = low(low_back(attended))
        out_dense = multiplier('slke,slkh->sleh', jax.nn.one_hot(attention_routes, ATTENTION_EXPERTS, dtype=jnp.float32), attended)
        low_out = multiplier('sleh,serh->sler', out_dense, head_adapter[:, adapter_slot_key_value + 2:])
        projected = multiplier('sleh,ehm->slem', out_dense, out_weight) + multiplier('sler,serm->slem', low_out, wide_adapter[:, adapter_slot_output:slot_down])
        resid_mid = resid_in + lax.optimization_barrier(jnp.sum(attention_mixture[..., None] * low_back(projected), axis=2))
        second_normalized = low(rms_scale(resid_mid, norm2_gain))
        feedforward_mixture = mixture_weights(multiplier('nkh,hg->nkg', second_normalized, feedforward_router_weight), feedforward_routes, FEEDFWD_EXPERTS)
        lowrank_gate_up = multiplier('nig,nvhg->nivh', second_normalized, wide_adapter[:, adapter_slot_gate:adapter_slot_output])
        ffn_total = jnp.zeros_like(resid_mid)
        for expert_number in range(FEEDFWD_EXPERTS):
            gate_before_act = multiplier('jwk,kp->jwp', second_normalized, gate_up_matrix[expert_number, :, 0]) + multiplier('vwo,voh->vwh', lowrank_gate_up[:, :, expert_number], feedforward_adapter[:, expert_number])
            up_before_act = multiplier('jwk,kp->jwp', second_normalized, gate_up_matrix[expert_number, :, 1]) + multiplier('vwo,voh->vwh', lowrank_gate_up[:, :, FEEDFWD_EXPERTS + expert_number], feedforward_adapter[:, FEEDFWD_EXPERTS + expert_number])
            hidden = low(jax.nn.silu(low_back(gate_before_act)) * low_back(up_before_act))
            low_down = multiplier('slf,srf->slr', hidden, feedforward_adapter[:, 2 * FEEDFWD_EXPERTS + expert_number])
            expert_out = multiplier('slf,fm->slm', hidden, down_weight[expert_number]) + multiplier('slr,srm->slm', low_down, wide_adapter[:, slot_down + expert_number])
            ffn_total = ffn_total + feedforward_mixture[..., expert_number:expert_number + 1] * low_back(expert_out)
        return resid_mid + ffn_total
    resid_in = tokens.astype(jnp.float32)
    mixed, pullback = jax.vjp(forward, resid_in, adapt_wide, adapt_heads, adapt_ffn)
    grad_tokens, grad_wide, grad_heads, grad_ffn = pullback(cotangent.astype(jnp.float32))
    return (mixed.astype(jnp.bfloat16), grad_tokens.astype(jnp.bfloat16), grad_wide, grad_heads, grad_ffn)
```

```python
import functools

import jax
import jax.numpy as jnp
from jax import lax
from jax.experimental import pallas as pl
from jax.experimental.pallas import tpu as pltpu
from jax.sharding import PartitionSpec as P

HEAD_DIM = 128
WINDOW = 1024
eps = 1e-06
big_negative = -1e30
bf16 = jnp.bfloat16
f32 = jnp.float32

MESH = pl.DeviceIdType.MESH
ANY = pl.BlockSpec(memory_space=pl.ANY)
VMEM = pl.BlockSpec(memory_space=pltpu.VMEM)
N_CTX, N_TP = 16, 8
PAST = 8


def region(kind, ref, owner, low, high):
    if kind == "rows":
        return ref.at[pl.ds(low, high - low), pl.ds(pl.multiple_of(owner * 128, 128), 128), :]
    if kind == "flat":
        return ref.at[pl.ds(pl.multiple_of(owner * 128 + 32 * low, 32), 32 * (high - low)), :]
    return ref.at[pl.ds(low, high - low), :, pl.ds(pl.multiple_of(owner * 128, 128), 128)]


def own_part(kind, ref, low, high):
    if kind == "flat":
        return ref.at[pl.ds(32 * low, 32 * (high - low)), :]
    return ref.at[pl.ds(low, high - low)]


def tp_part(kind, ref, rank, size):
    if kind == "cols":
        return ref.at[:, pl.ds(pl.multiple_of(rank * size, size), size)]
    return ref.at[pl.ds(pl.multiple_of(rank * size, size), size), :]


def gather_kernel(kinds, tp_kinds, *refs):
    n, m = len(kinds), len(tp_kinds)
    src, refs = list(refs[:n]), refs[n:]
    tp_src, refs = refs[:m], refs[m:]
    dst, refs = refs[:n], refs[n:]
    tp_dst, refs = refs[:m], refs[m:]
    send, recv, local, tp_send, tp_recv, tp_local = refs
    src = [tp_dst[m - 1] if r is None else r for r in src]
    me, tp = lax.axis_index("ctx"), lax.axis_index("tp")
    core, side = me ^ 1, me ^ 2
    up, down, far = lax.rem(me + 4, 16), lax.rem(me + 12, 16), lax.rem(me + 8, 16)
    barrier = pltpu.get_barrier_semaphore()
    for d in (core, side, up, down):
        pl.semaphore_signal(barrier, inc=1, device_id=(d, tp), device_id_type=MESH)
    for d in range(1, N_TP):
        pl.semaphore_signal(barrier, inc=1, device_id=(me, tp ^ d), device_id_type=MESH)
    pl.semaphore_wait(barrier, 4 + N_TP - 1)
    started, staying = [], []
    counter = [0] * n

    def tp_copy(i, d, rank):
        size = tp_src[i].shape[1 if tp_kinds[i] == "cols" else 0]
        return pltpu.make_async_remote_copy(
            src_ref=tp_src[i],
            dst_ref=tp_part(tp_kinds[i], tp_dst[i], rank, size),
            send_sem=tp_send.at[i, d],
            recv_sem=tp_recv.at[i, d],
            device_id=(me, tp ^ d),
            device_id_type=MESH,
        )

    for i in range(m):
        for d in range(1, N_TP):
            c = tp_copy(i, d, tp)
            c.start()
            started.append(c)
        size = tp_src[i].shape[1 if tp_kinds[i] == "cols" else 0]
        c = pltpu.make_async_copy(
            tp_src[i], tp_part(tp_kinds[i], tp_dst[i], tp, size), tp_local.at[i]
        )
        c.start()
        staying.append(c)

    def copy(t, item, owner, low, high, to, slot, own):
        there = region(kinds[t], dst[t], owner, low, high)
        return pltpu.make_async_remote_copy(
            src_ref=own_part(kinds[t], src[t], low, high) if own else there,
            dst_ref=there,
            send_sem=send.at[t, slot],
            recv_sem=recv.at[t, item],
            device_id=(to, tp),
            device_id_type=MESH,
        )

    def go(t, item, owner, low, high, to, own=False):
        c = copy(t, item, owner, low, high, to, counter[t], own)
        counter[t] += 1
        c.start()
        started.append(c)

    arrive = {
        0: (side, 0, 4),
        1: (down, 0, 4),
        2: (up, 0, 4),
        3: (down ^ 2, 0, 2),
        4: (up ^ 2, 0, 2),
        5: (far, 1, 3),
        6: (far, 0, 1),
        7: (far, 3, 4),
        8: (far ^ 2, 1, 2),
        9: (far ^ 2, 0, 1),
        10: (down ^ 2, 2, 4),
        11: (up ^ 2, 2, 4),
        12: (far ^ 2, 2, 4),
    }

    def got(t, item):
        owner, low, high = arrive[item]
        copy(t, item, owner, low, high, core, 0, False).wait_recv()
        go(t, 13 + item, owner, low, high, core)

    def first(t):
        go(t, 0, me, 0, 4, side, True)
        go(t, 2, me, 0, 4, down, True)
        go(t, 1, me, 0, 4, up, True)
        go(t, 26, me, 0, 4, core, True)
        c = pltpu.make_async_copy(src[t], region(kinds[t], dst[t], me, 0, 4), local.at[t])
        c.start()
        staying.append(c)

    for t in range(n - 1):
        first(t)
    for i in range(m):
        for d in range(1, N_TP):
            tp_copy(i, d, tp ^ d).wait_recv()
    staying[m - 1].wait()
    first(n - 1)
    for t in range(n):
        got(t, 0)
        go(t, 3, side, 0, 2, up)
        go(t, 4, side, 0, 2, down)
        got(t, 1)
        go(t, 5, down, 1, 3, up)
        go(t, 10, down, 2, 4, side)
        got(t, 2)
        go(t, 6, up, 0, 1, down)
        go(t, 7, up, 3, 4, down)
        go(t, 11, up, 2, 4, side)
    for t in range(n):
        got(t, 3)
        go(t, 8, down ^ 2, 1, 2, up)
        got(t, 4)
        go(t, 9, up ^ 2, 0, 1, down)
        got(t, 5)
        got(t, 6)
        got(t, 7)
        go(t, 12, far, 2, 4, side)
    for t in range(n):
        for item in range(8, 13):
            got(t, item)
    for t in range(n):
        for item in range(13):
            owner, low, high = arrive[item]
            copy(t, 13 + item, owner ^ 1, low, high, core, 0, False).wait_recv()
        copy(t, 26, core, 0, 4, core, 0, False).wait_recv()
    for c in started:
        c.wait_send()
    for i, c in enumerate(staying):
        if i != m - 1:
            c.wait()


def gather_all(shards, kinds, tp_shards, tp_kinds):
    n, m = len(kinds), len(tp_kinds)
    shapes, tp_shapes = [], []
    for s, k in zip(tp_shards, tp_kinds):
        shape = list(s.shape)
        shape[1 if k == "cols" else 0] *= N_TP
        tp_shapes.append(jax.ShapeDtypeStruct(tuple(shape), s.dtype))
    for s, k in zip(list(shards) + [tp_shapes[-1]], kinds):
        shape = list(s.shape)
        shape[{"rows": 1, "flat": 0, "cols": 2}[k]] *= N_CTX
        shapes.append(jax.ShapeDtypeStruct(tuple(shape), s.dtype))

    def body(*refs):
        gather_kernel(kinds, tp_kinds, *refs[: n - 1], None, *refs[n - 1 :])

    out = pl.pallas_call(
        body,
        out_shape=tuple(shapes + tp_shapes),
        in_specs=[ANY] * (n - 1 + m),
        out_specs=tuple([ANY] * (n + m)),
        scratch_shapes=[
            pltpu.SemaphoreType.DMA((n, 32)),
            pltpu.SemaphoreType.DMA((n, 27)),
            pltpu.SemaphoreType.DMA((n,)),
            pltpu.SemaphoreType.DMA((m, N_TP)),
            pltpu.SemaphoreType.DMA((m, N_TP)),
            pltpu.SemaphoreType.DMA((m,)),
        ],
        compiler_params=pltpu.CompilerParams(collective_id=0, has_side_effects=True),
        name="gather_all",
    )(*shards, *tp_shards)
    return out[:n], out[n : n + m - 1]


def exchange_kernel(kinds, *refs):
    n = len(kinds)
    src, refs = refs[:n], refs[n:]
    dst, refs = refs[:n], refs[n:]
    held, refs = refs[:n], refs[n:]
    send, recv = refs
    me, tp = lax.axis_index("ctx"), lax.axis_index("tp")
    barrier = pltpu.get_barrier_semaphore()
    for d in range(1, N_TP):
        pl.semaphore_signal(barrier, inc=1, device_id=(me, tp ^ d), device_id_type=MESH)
    pl.semaphore_wait(barrier, N_TP - 1)

    def part(i, ref, rank):
        if kinds[i].endswith("rows"):
            size = src[i].shape[0] // N_TP
            return ref.at[pl.ds(pl.multiple_of(rank * size, size), size), :]
        size = src[i].shape[1] // N_TP
        return ref.at[:, pl.ds(pl.multiple_of(rank * size, size), size)]

    def scatter(i, d):
        return pltpu.make_async_remote_copy(
            src_ref=part(i, src[i], tp ^ d),
            dst_ref=held[i].at[d],
            send_sem=send.at[i, d],
            recv_sem=recv.at[i, d],
            device_id=(me, tp ^ d),
            device_id_type=MESH,
        )

    def spread(i, d, rank):
        return pltpu.make_async_remote_copy(
            src_ref=part(i, dst[i], rank),
            dst_ref=part(i, dst[i], rank),
            send_sem=send.at[i, N_TP + d],
            recv_sem=recv.at[i, N_TP + d],
            device_id=(me, tp ^ d),
            device_id_type=MESH,
        )

    for i in range(n):
        for d in range(1, N_TP):
            scatter(i, d).start()
    for i in range(n):
        for d in range(1, N_TP):
            scatter(i, d).wait_recv()
        total = part(i, src[i], tp)[...].astype(f32)
        for d in range(1, N_TP):
            total = total + held[i][d].astype(f32)
        if kinds[i].startswith("ar"):
            part(i, dst[i], tp)[...] = total.astype(dst[i].dtype)
            for d in range(1, N_TP):
                spread(i, d, tp).start()
        else:
            dst[i][...] = total
    for i in range(n):
        for d in range(1, N_TP):
            scatter(i, d).wait_send()
            if kinds[i].startswith("ar"):
                spread(i, d, tp ^ d).wait_recv()
                spread(i, d, tp).wait_send()


def exchange(arrays, kinds, cid):
    outs, held = [], []
    for a, k in zip(arrays, kinds):
        if k == "rs_cols":
            outs.append(jax.ShapeDtypeStruct((a.shape[0], a.shape[1] // N_TP), f32))
        else:
            outs.append(jax.ShapeDtypeStruct(a.shape, a.dtype))
        r, c = a.shape
        held.append(
            pltpu.VMEM((N_TP, r // N_TP, c) if k == "ar_rows" else (N_TP, r, c // N_TP), a.dtype)
        )
    n = len(kinds)
    return pl.pallas_call(
        functools.partial(exchange_kernel, kinds),
        out_shape=tuple(outs),
        in_specs=[VMEM] * n,
        out_specs=tuple([VMEM] * n),
        scratch_shapes=held
        + [pltpu.SemaphoreType.DMA((n, 2 * N_TP)), pltpu.SemaphoreType.DMA((n, 2 * N_TP))],
        compiler_params=pltpu.CompilerParams(
            collective_id=cid, has_side_effects=True, vmem_limit_bytes=48 << 20
        ),
        name=f"exchange_{cid}",
    )(*arrays)


def halo_kernel(src, dst, send, recv, local):
    me, tp = lax.axis_index("ctx"), lax.axis_index("tp")
    block = src.shape[1]
    barrier = pltpu.get_barrier_semaphore()
    for d in range(1, N_CTX):
        pl.semaphore_signal(
            barrier, inc=1, device_id=(lax.rem(me + d, N_CTX), tp), device_id_type=MESH
        )
    pl.semaphore_wait(barrier, N_CTX - 1)

    def copy(d):
        return pltpu.make_async_remote_copy(
            src_ref=src,
            dst_ref=dst.at[:, pl.ds((PAST - d) * block, block), :],
            send_sem=send.at[d],
            recv_sem=recv.at[d],
            device_id=(lax.rem(me + d, N_CTX), tp),
            device_id_type=MESH,
        )

    own = pltpu.make_async_copy(src, dst.at[:, pl.ds(PAST * block, block), :], local)
    own.start()
    for d in range(1, PAST + 1):
        copy(d).start()
    own.wait()
    for d in range(1, PAST + 1):
        copy(d).wait()


def halo(kv_own):
    seqs, block, cols = kv_own.shape
    return pl.pallas_call(
        halo_kernel,
        out_shape=jax.ShapeDtypeStruct((seqs, (PAST + 1) * block, cols), kv_own.dtype),
        in_specs=[ANY],
        out_specs=ANY,
        scratch_shapes=[
            pltpu.SemaphoreType.DMA((PAST + 1,)),
            pltpu.SemaphoreType.DMA((PAST + 1,)),
            pltpu.SemaphoreType.DMA,
        ],
        compiler_params=pltpu.CompilerParams(collective_id=8, has_side_effects=True),
        name="halo",
    )(kv_own)


def halo_back_kernel(src, dst, held, send, recv):
    me, tp = lax.axis_index("ctx"), lax.axis_index("tp")
    block = dst.shape[1]
    barrier = pltpu.get_barrier_semaphore()
    for d in range(1, N_CTX):
        pl.semaphore_signal(
            barrier, inc=1, device_id=(lax.rem(me + d, N_CTX), tp), device_id_type=MESH
        )
    pl.semaphore_wait(barrier, N_CTX - 1)

    def copy(d):
        return pltpu.make_async_remote_copy(
            src_ref=src.at[:, pl.ds((PAST - d) * block, block), :],
            dst_ref=held.at[d],
            send_sem=send.at[d],
            recv_sem=recv.at[d],
            device_id=(lax.rem(me + N_CTX - d, N_CTX), tp),
            device_id_type=MESH,
        )

    for d in range(1, PAST + 1):
        copy(d).start()
    total = src[:, pl.ds(PAST * block, block), :].astype(f32)
    for d in range(1, PAST + 1):
        copy(d).wait_recv()
        total = total + held[d].astype(f32)
    dst[...] = total
    for d in range(1, PAST + 1):
        copy(d).wait_send()


def halo_back(partial):
    seqs, length, cols = partial.shape
    block = length // (PAST + 1)
    return pl.pallas_call(
        halo_back_kernel,
        out_shape=jax.ShapeDtypeStruct((seqs, block, cols), f32),
        in_specs=[VMEM],
        out_specs=VMEM,
        scratch_shapes=[
            pltpu.VMEM((PAST + 1, seqs, block, cols), partial.dtype),
            pltpu.SemaphoreType.DMA((PAST + 1,)),
            pltpu.SemaphoreType.DMA((PAST + 1,)),
        ],
        compiler_params=pltpu.CompilerParams(
            collective_id=9, has_side_effects=True, vmem_limit_bytes=48 << 20
        ),
        name="halo_back",
    )(partial)


def reduce_kernel(spread_too, *refs):
    n = len(spread_too)
    src, refs = refs[:n], refs[n:]
    dst, refs = refs[:n], refs[n:]
    held, refs = refs[:n], refs[n:]
    send, recv = refs
    me, tp = lax.axis_index("ctx"), lax.axis_index("tp")
    barrier = pltpu.get_barrier_semaphore()
    for d in range(1, N_CTX):
        pl.semaphore_signal(barrier, inc=1, device_id=(me ^ d, tp), device_id_type=MESH)
    pl.semaphore_wait(barrier, N_CTX - 1)

    def scatter(i, d):
        return pltpu.make_async_remote_copy(
            src_ref=src[i].at[me ^ d],
            dst_ref=held[i].at[d],
            send_sem=send.at[i, d],
            recv_sem=recv.at[i, d],
            device_id=(me ^ d, tp),
            device_id_type=MESH,
        )

    def spread(i, d, rank):
        return pltpu.make_async_remote_copy(
            src_ref=dst[i].at[rank],
            dst_ref=dst[i].at[rank],
            send_sem=send.at[i, N_CTX + d],
            recv_sem=recv.at[i, N_CTX + d],
            device_id=(me ^ d, tp),
            device_id_type=MESH,
        )

    for i in range(n):
        for d in range(1, N_CTX):
            scatter(i, d).start()
    for i in range(n):
        for d in range(1, N_CTX):
            scatter(i, d).wait_recv()
        total = src[i][me].astype(f32)
        for d in range(1, N_CTX):
            total = total + held[i][d].astype(f32)
        if spread_too[i]:
            dst[i][me] = total.astype(dst[i].dtype)
            for d in range(1, N_CTX):
                spread(i, d, me).start()
        else:
            dst[i][...] = total
    for i in range(n):
        for d in range(1, N_CTX):
            scatter(i, d).wait_send()
            if spread_too[i]:
                spread(i, d, me ^ d).wait_recv()
                spread(i, d, me).wait_send()


def reduce_ctx(arrays, spread_too):
    outs = [
        jax.ShapeDtypeStruct(a.shape if s else a.shape[1:], a.dtype if s else f32)
        for a, s in zip(arrays, spread_too)
    ]
    n = len(arrays)
    return pl.pallas_call(
        functools.partial(reduce_kernel, spread_too),
        out_shape=tuple(outs),
        in_specs=[VMEM] * n,
        out_specs=tuple([VMEM] * n),
        scratch_shapes=[pltpu.VMEM(a.shape, a.dtype) for a in arrays]
        + [pltpu.SemaphoreType.DMA((n, 2 * N_CTX)), pltpu.SemaphoreType.DMA((n, 2 * N_CTX))],
        compiler_params=pltpu.CompilerParams(
            collective_id=10, has_side_effects=True, vmem_limit_bytes=48 << 20
        ),
        name="reduce_ctx",
    )(*arrays)


def rms_scale(values, gain):
    return values * lax.rsqrt(jnp.mean(values * values, axis=-1, keepdims=True) + eps) * gain


def norm_back(values, gain, grad_normed):
    inverse = lax.rsqrt(jnp.mean(values * values, axis=-1, keepdims=True) + eps)
    scaled = grad_normed * gain
    return inverse * scaled - values * inverse**3 * jnp.mean(
        scaled * values, axis=-1, keepdims=True
    )


def doc_layout(doc_lengths, positions):
    ends = jnp.cumsum(doc_lengths, axis=1)
    passed = positions[None, :, None] >= ends[:, None, :]
    doc_ids = jnp.sum(passed.astype(jnp.int32), axis=2)
    starting = jnp.sum(jnp.where(passed, doc_lengths[:, None, :], 0), axis=2)
    inside = positions[None, :] < ends[:, -1:]
    doc_ids = jnp.where(inside, doc_ids, -1 - positions[None, :])
    return (doc_ids, positions[None, :] - starting)


def dot(a, b, ca=1, cb=0):
    return lax.dot_general(a, b, (((ca,), (cb,)), ((), ())), preferred_element_type=f32)


def rope(x, cosine, sine, sign):
    half = HEAD_DIM // 2
    x1, x2 = x[..., :half], x[..., half:]
    s = sine * sign
    return jnp.concatenate([x1 * cosine - x2 * s, x2 * cosine + x1 * s], axis=-1)


def gates_of(logits, onehot):
    chosen = jnp.sum(logits[:, None, :] * onehot, axis=-1)
    return jax.nn.softmax(chosen, axis=-1)


def gates_back(gates, grad_gates, onehot):
    inner = gates * (grad_gates - jnp.sum(gates * grad_gates, axis=-1, keepdims=True))
    return jnp.sum(inner[..., None] * onehot, axis=1)


def shards(
    tokens,
    norm1_gain,
    router_attn,
    w_query,
    w_key_value,
    w_out,
    norm2_gain,
    router_ffn,
    w_gate_up,
    w_down,
    adapt_wide,
    adapt_heads,
    adapt_ffn,
    attention_routes,
    feedforward_routes,
    doc_lengths,
    adapter_index,
    cotangent,
):
    seqs, block, part = tokens.shape
    rows = seqs * block
    n_ctx = lax.axis_size("ctx")
    n_tp = lax.axis_size("tp")
    model = part * n_tp
    experts = w_query.shape[0]
    width = w_query.shape[2]
    heads = width // HEAD_DIM
    hidden = w_down.shape[1]
    rank = adapt_heads.shape[2]
    wide_slots = adapt_wide.shape[1]
    ctx_rank = lax.axis_index("ctx")
    tp_rank = lax.axis_index("tp")

    def split(a):
        return a.reshape((seqs, block) + a.shape[1:])

    def merge(a):
        return a.reshape((rows,) + a.shape[2:])

    wide_own = adapt_wide.astype(bf16)[adapter_index]
    wide_cols = wide_own.reshape(seqs * wide_slots * rank, -1).T
    heads_low = adapt_heads.astype(bf16)[adapter_index]
    ffn_low = adapt_ffn.astype(bf16)[adapter_index]
    (w_query, w_key_value, w_out, w_gate_up, w_down, wide), (x0, dy) = gather_all(
        [
            w_query,
            w_key_value.reshape(-1, 2 * width),
            w_out,
            w_gate_up.reshape(experts, -1, 2 * hidden),
            w_down,
        ],
        ["rows", "flat", "cols", "rows", "cols", "flat"],
        [tokens.reshape(rows, part), cotangent.reshape(rows, part), wide_cols],
        ["cols", "cols", "rows"],
    )
    w_gate_up = w_gate_up.reshape(experts, model, 2, hidden)
    wide = wide.reshape(model, seqs, wide_slots, rank)
    xf = x0.astype(f32)
    n1 = rms_scale(xf, norm1_gain).astype(bf16)
    route_a = attention_routes.reshape(rows, -1)
    route_f = feedforward_routes.reshape(rows, -1)
    hot_a = jax.nn.one_hot(route_a, experts, dtype=f32)
    hot_f = jax.nn.one_hot(route_f, experts, dtype=f32)
    ga = gates_of(dot(n1, router_attn), hot_a)
    ga_e = jnp.sum(ga[..., None] * hot_a, axis=1)

    positions = ctx_rank * block + jnp.arange(block, dtype=jnp.int32)
    doc_ids, offsets = doc_layout(doc_lengths, positions)
    half = HEAD_DIM // 2
    frequency = 10000.0 ** (-2.0 * jnp.arange(half, dtype=f32) / HEAD_DIM)
    angles = offsets.astype(f32).reshape(rows)[:, None] * frequency
    cosine, sine = jnp.cos(angles), jnp.sin(angles)

    def low_in(v, first, count):
        return merge(
            jnp.einsum(
                "sbd,dscr->sbcr", split(v), wide[:, :, first : first + count],
                preferred_element_type=f32,
            )
        )

    def low_out(z, factor):
        return merge(
            jnp.einsum("sbcr,scrh->sbch", split(z).astype(bf16), factor, preferred_element_type=f32)
        )

    def low_sum(z, factor):
        return merge(
            jnp.einsum("sbcr,scrh->sbh", split(z).astype(bf16), factor, preferred_element_type=f32)
        )

    def low_back(dp, factor):
        return merge(
            jnp.einsum("sbch,scrh->sbcr", split(dp), factor, preferred_element_type=f32)
        )

    def low_grad(z, dp):
        return jnp.einsum(
            "sbcr,sbch->scrh", split(z).astype(bf16), split(dp), preferred_element_type=f32
        )

    z_q = low_in(n1, 0, experts)
    z_kv = low_in(n1, experts, 2)
    b_q, b_kv, a_o = heads_low[:, :experts], heads_low[:, experts : experts + 2], heads_low[:, experts + 2 :]
    q_all = jnp.stack([dot(n1, w_query[e]) for e in range(experts)], axis=1) + low_out(z_q, b_q)
    q_pre = jnp.einsum("rke,reh->rkh", hot_a, q_all, precision=lax.Precision.HIGHEST)
    q = rope(
        q_pre.reshape(rows, -1, heads, HEAD_DIM), cosine[:, None, None], sine[:, None, None], 1.0
    ).astype(bf16)
    kv = dot(n1, w_key_value.reshape(model, 2 * width)).reshape(rows, 2, width) + low_out(z_kv, b_kv)
    k_own = rope(
        kv[:, 0].reshape(rows, heads, HEAD_DIM), cosine[:, None], sine[:, None], 1.0
    ).astype(bf16)
    v_own = kv[:, 1].reshape(rows, heads, HEAD_DIM).astype(bf16)
    kv_own = jnp.concatenate([k_own, v_own], axis=1).reshape(seqs, block, 2 * width)
    kv_all = halo(kv_own)
    length = kv_all.shape[1]
    kv_all = kv_all.reshape(seqs, length, 2, heads, HEAD_DIM)
    key_pos = (ctx_rank - PAST) * block + jnp.arange(length, dtype=jnp.int32)
    key_doc = doc_layout(doc_lengths, jnp.maximum(key_pos, 0))[0]
    allowed = (
        (key_pos >= 0)[None, None, :] &
        (doc_ids[:, :, None] == key_doc[:, None, :])
        & (key_pos[None, None, :] <= positions[None, :, None])
        & (positions[None, :, None] - key_pos[None, None, :] < WINDOW)
    )[:, None, None]
    scale = HEAD_DIM ** (-0.5)
    q_s = q.reshape(seqs, block, -1, heads, HEAD_DIM)
    scores = jnp.einsum("sqthd,skhd->sthqk", q_s, kv_all[:, :, 0], preferred_element_type=f32) * scale
    scores = jnp.where(allowed, scores, big_negative)
    peak = jnp.max(scores, axis=-1, keepdims=True)
    weights = jnp.where(allowed, jnp.exp(scores - peak), 0.0)
    total = jnp.sum(weights, axis=-1, keepdims=True)
    probs = weights / total
    o = jnp.einsum(
        "sthqk,skhd->sqthd", probs.astype(bf16), kv_all[:, :, 1], preferred_element_type=f32
    )
    ob = o.astype(bf16).reshape(rows, -1, width)
    ob_e = jnp.einsum("rke,rkh->reh", hot_a.astype(bf16), ob, preferred_element_type=f32).astype(bf16)
    z_o = low_back(ob_e, a_o)
    b_o = jnp.transpose(wide[:, :, 14:18], (1, 2, 3, 0))
    part_out = sum(ga_e[:, e, None] * dot(ob_e[:, e], w_out[e]) for e in range(experts))
    part_out = part_out + low_sum(z_o * ga_e[..., None], b_o)
    (sum_out,) = exchange([part_out.astype(bf16)], ["ar_cols"], 1)
    sum_out = sum_out.astype(f32)
    x1 = xf + sum_out
    n2 = rms_scale(x1, norm2_gain).astype(bf16)
    gf = gates_of(dot(n2, router_ffn), hot_f)
    gf_e = jnp.sum(gf[..., None] * hot_f, axis=1)
    z_gu = low_in(n2, experts + 2, 2 * experts)
    b_gu, a_d = ffn_low[:, : 2 * experts], ffn_low[:, 2 * experts :]
    b_d = jnp.transpose(wide[:, :, 18:22], (1, 2, 3, 0))
    dz_d = low_in(dy, 18, experts)
    low_gu = low_out(z_gu, b_gu)
    low_dh = low_out(dz_d, a_d)
    h_all, dh_gate, dgp_all, dup_all = [], [], [], []
    for e in range(experts):
        gp = dot(n2, w_gate_up[e, :, 0]) + low_gu[:, e]
        up = dot(n2, w_gate_up[e, :, 1]) + low_gu[:, experts + e]
        sg = jax.nn.sigmoid(gp)
        silu = gp * sg
        h = (silu * up).astype(bf16)
        dh0 = dot(dy, w_down[e], 1, 1) + low_dh[:, e]
        dh_gate.append(jnp.sum(dh0 * h.astype(f32), axis=1))
        dh = dh0 * gf_e[:, e, None]
        dgp_all.append((dh * up * sg * (1.0 + gp * (1.0 - sg))).astype(bf16))
        dup_all.append((dh * silu).astype(bf16))
        h_all.append(h)
    h_all = jnp.stack(h_all, axis=1)
    d_gu = jnp.stack(dgp_all + dup_all, axis=1)
    z_d = low_back(h_all, a_d)
    part_ffn = sum(gf_e[:, e, None] * dot(h_all[:, e], w_down[e]) for e in range(experts))
    part_ffn = part_ffn + low_sum(z_d * gf_e[..., None], b_d)

    def own(a):
        return lax.dynamic_slice_in_dim(a, tp_rank * part, part, 1)

    dgf = jnp.sum(jnp.stack(dh_gate, axis=1)[:, None, :] * hot_f, axis=-1)
    dlf = gates_back(gf, dgf, hot_f)
    dz_gu = low_back(d_gu, b_gu)
    a_gu = jnp.transpose(wide[:, :, 6:14], (1, 2, 3, 0))
    dn2 = sum(
        dot(d_gu[:, e], w_gate_up[e, :, 0], 1, 1) + dot(d_gu[:, experts + e], w_gate_up[e, :, 1], 1, 1)
        for e in range(experts)
    )
    dn2 = dn2 + low_sum(dz_gu, a_gu) + dot(dlf.astype(bf16), router_ffn, 1, 1)
    back2 = norm_back(x1, norm2_gain, dn2)
    z_part = jnp.concatenate([z_o * ga_e[..., None], dz_gu, z_d * gf_e[..., None]], axis=1)
    z_part = jnp.pad(z_part.reshape(rows, -1).astype(bf16), ((0, 0), (0, 128)))
    sum_back, mixed_own, z_sum = exchange(
        [back2.astype(bf16), part_ffn.astype(bf16), z_part], ["ar_cols", "rs_cols", "ar_rows"], 2
    )
    z_sum = z_sum[:, :256].reshape(rows, 16, rank)
    dx1 = dy.astype(f32) + sum_back.astype(f32)
    mixed = (mixed_own + own(x1)).astype(bf16)
    dx1b = dx1.astype(bf16)
    dz_o = low_in(dx1b, 14, experts)
    g_e = jnp.stack([dot(dx1b, w_out[e], 1, 1) for e in range(experts)], axis=1) + low_out(dz_o, a_o)
    g_k = jnp.einsum("rke,reh->rkh", hot_a, g_e, precision=lax.Precision.HIGHEST)
    dga = jnp.sum(g_k * ob.astype(f32), axis=-1)
    dob = (g_k * ga[..., None]).astype(bf16)
    dob_s = dob.reshape(seqs, block, -1, heads, HEAD_DIM)
    delta = jnp.sum(dob_s.astype(f32) * o, axis=-1)
    delta = jnp.transpose(delta, (0, 2, 3, 1))[..., None]
    d_p = jnp.einsum("sqthd,skhd->sthqk", dob_s, kv_all[:, :, 1], preferred_element_type=f32)
    d_s = (probs * (d_p - delta)).astype(bf16)
    dqr = jnp.einsum("sthqk,skhd->sqthd", d_s, kv_all[:, :, 0], preferred_element_type=f32) * scale
    dkr = jnp.einsum("sthqk,sqthd->skhd", d_s, q_s, preferred_element_type=f32) * scale
    dvv = jnp.einsum("sthqk,sqthd->skhd", probs.astype(bf16), dob_s, preferred_element_type=f32)
    dkv = jnp.concatenate([dkr, dvv], axis=2).reshape(seqs, length, 2 * width).astype(bf16)
    dkv = halo_back(dkv)
    dkv = dkv.reshape(rows, 2, heads, HEAD_DIM)
    dkp = rope(dkv[:, 0], cosine[:, None], sine[:, None], -1.0).astype(bf16).reshape(rows, width)
    dvp = dkv[:, 1].astype(bf16).reshape(rows, width)
    dqp = rope(
        dqr.reshape(rows, -1, heads, HEAD_DIM), cosine[:, None, None], sine[:, None, None], -1.0
    ).astype(bf16).reshape(rows, -1, width)
    dq_e = jnp.einsum("rke,rkh->reh", hot_a.astype(bf16), dqp, preferred_element_type=f32).astype(bf16)
    dkv_p = jnp.stack([dkp, dvp], axis=1)
    dz_q = low_back(dq_e, b_q)
    dz_kv = low_back(dkv_p, b_kv)
    a_qkv = jnp.transpose(wide[:, :, :6], (1, 2, 3, 0))
    dz_qkv = jnp.concatenate([dz_q, dz_kv], axis=1)
    dla = gates_back(ga, dga, hot_a)
    dn1 = sum(dot(dq_e[:, e], w_query[e], 1, 1) for e in range(experts))
    dn1 = dn1 + dot(dkv_p.reshape(rows, 2 * width), w_key_value.reshape(model, 2 * width), 1, 1)
    dn1 = dn1 + low_sum(dz_qkv, a_qkv) + dot(dla.astype(bf16), router_attn, 1, 1)
    back1 = norm_back(xf, norm1_gain, dn1)
    dz_part = jnp.pad(dz_qkv.reshape(rows, -1).astype(bf16), ((0, 0), (0, 32)))
    back_own, dz_sum = exchange([back1.astype(bf16), dz_part], ["rs_cols", "ar_rows"], 3)
    dz_sum = dz_sum[:, :96].reshape(rows, 6, rank)
    grad_tokens = (back_own + own(dx1)).astype(bf16)
    grad_heads = jnp.concatenate(
        [low_grad(z_q, dq_e), low_grad(z_kv, dkv_p), low_grad(dz_o * ga_e[..., None], ob_e)], axis=1
    )
    grad_ffn = jnp.concatenate(
        [low_grad(z_gu, d_gu), low_grad(dz_d * gf_e[..., None], h_all)], axis=1
    )
    def strided(a):
        return lax.dynamic_slice_in_dim(
            a.reshape(rows, n_ctx, n_tp, model // (n_ctx * n_tp)), tp_rank, 1, 2
        ).reshape(seqs, block, -1)

    def wide_grad(z, v):
        return jnp.einsum("sbcr,sbm->mscr", split(z).astype(bf16), strided(v), preferred_element_type=f32)

    wide_terms = jnp.concatenate(
        [
            wide_grad(dz_sum, n1),
            wide_grad(z_sum[:, 4:12], n2),
            wide_grad(z_sum[:, :4], dx1b),
            wide_grad(z_sum[:, 12:], dy),
        ],
        axis=2,
    ).reshape(-1, seqs * wide_slots * rank)
    head_rows = seqs * grad_heads.shape[1] * rank // N_CTX
    head_terms = jnp.pad(
        grad_heads.reshape(N_CTX, head_rows, width).astype(bf16), ((0, 0), (0, 32 - head_rows), (0, 0))
    )
    grad_wide, head_sum = reduce_ctx(
        [wide_terms.reshape(N_CTX, -1, seqs * wide_slots * rank).astype(bf16), head_terms],
        [False, True],
    )
    grad_wide = grad_wide.T.reshape(seqs, wide_slots, rank, -1)[adapter_index]
    grad_heads = head_sum[:, :head_rows].astype(f32).reshape(grad_heads.shape)[adapter_index]
    grad_ffn = lax.psum(grad_ffn.astype(bf16), "ctx").astype(f32)[adapter_index]
    mixed = mixed.reshape(seqs, block, part)
    grad_tokens = grad_tokens.reshape(seqs, block, part)
    return (mixed, grad_tokens, grad_wide, grad_heads, grad_ffn)


def solution(mesh):
    placed = (
        P(None, "ctx", "tp"),
        P(),
        P(),
        P(None, "ctx", "tp"),
        P("ctx", None, "tp"),
        P(None, "tp", "ctx"),
        P(),
        P(),
        P(None, "ctx", None, "tp"),
        P(None, "tp", "ctx"),
        P(None, None, None, ("ctx", "tp")),
        P(None, None, None, "tp"),
        P(None, None, None, "tp"),
        P(None, "ctx", None),
        P(None, "ctx", None),
        P(),
        P(),
        P(None, "ctx", "tp"),
    )
    return jax.shard_map(
        shards,
        mesh=mesh,
        in_specs=placed,
        out_specs=(
            P(None, "ctx", "tp"),
            P(None, "ctx", "tp"),
            P(None, None, None, ("ctx", "tp")),
            P(None, None, None, "tp"),
            P(None, None, None, "tp"),
        ),
        check_vma=False,
    )
```

```python
import functools

import jax
import numpy as np
import jax.numpy as jnp
from jax import lax
from jax.experimental import pallas as pl
from jax.experimental.pallas import tpu as pltpu
from jax.sharding import PartitionSpec as P

HEAD_DIM = 128
WINDOW = 1024
eps = 1e-06
big_negative = -1e30
bf16 = jnp.bfloat16
f32 = jnp.float32

MESH = pl.DeviceIdType.MESH
ANY = pl.BlockSpec(memory_space=pl.ANY)
VMEM = pl.BlockSpec(memory_space=pltpu.VMEM)
N_CTX, N_TP = 16, 8
PAST = 8


def region(kind, ref, owner, low, high):
    if kind == "rows":
        return ref.at[pl.ds(low, high - low), pl.ds(pl.multiple_of(owner * 128, 128), 128), :]
    if kind == "flat":
        return ref.at[pl.ds(pl.multiple_of(owner * 128 + 32 * low, 32), 32 * (high - low)), :]
    return ref.at[pl.ds(low, high - low), :, pl.ds(pl.multiple_of(owner * 128, 128), 128)]


def own_part(kind, ref, low, high):
    if kind == "flat":
        return ref.at[pl.ds(32 * low, 32 * (high - low)), :]
    return ref.at[pl.ds(low, high - low)]


def tp_part(kind, ref, rank, size):
    if kind == "cols":
        return ref.at[:, pl.ds(pl.multiple_of(rank * size, size), size)]
    return ref.at[pl.ds(pl.multiple_of(rank * size, size), size), :]


def gather_kernel(kinds, tp_kinds, *refs):
    n, m = len(kinds), len(tp_kinds)
    src, refs = list(refs[:n]), refs[n:]
    tp_src, refs = refs[:m], refs[m:]
    dst, refs = refs[:n], refs[n:]
    tp_dst, refs = refs[:m], refs[m:]
    send, recv, local, tp_send, tp_recv, tp_local = refs
    src = [tp_dst[m - 1] if r is None else r for r in src]
    me, tp = lax.axis_index("ctx"), lax.axis_index("tp")
    core, side = me ^ 1, me ^ 2
    up, down, far = lax.rem(me + 4, 16), lax.rem(me + 12, 16), lax.rem(me + 8, 16)
    barrier = pltpu.get_barrier_semaphore()
    for d in (core, side, up, down):
        pl.semaphore_signal(barrier, inc=1, device_id=(d, tp), device_id_type=MESH)
    for d in range(1, N_TP):
        pl.semaphore_signal(barrier, inc=1, device_id=(me, tp ^ d), device_id_type=MESH)
    pl.semaphore_wait(barrier, 4 + N_TP - 1)
    started, staying = [], []
    counter = [0] * n

    def tp_copy(i, d, rank):
        size = tp_src[i].shape[1 if tp_kinds[i] == "cols" else 0]
        return pltpu.make_async_remote_copy(
            src_ref=tp_src[i],
            dst_ref=tp_part(tp_kinds[i], tp_dst[i], rank, size),
            send_sem=tp_send.at[i, d],
            recv_sem=tp_recv.at[i, d],
            device_id=(me, tp ^ d),
            device_id_type=MESH,
        )

    for i in range(m):
        for d in range(1, N_TP):
            c = tp_copy(i, d, tp)
            c.start()
            started.append(c)
        size = tp_src[i].shape[1 if tp_kinds[i] == "cols" else 0]
        c = pltpu.make_async_copy(
            tp_src[i], tp_part(tp_kinds[i], tp_dst[i], tp, size), tp_local.at[i]
        )
        c.start()
        staying.append(c)

    def copy(t, item, owner, low, high, to, slot, own):
        there = region(kinds[t], dst[t], owner, low, high)
        return pltpu.make_async_remote_copy(
            src_ref=own_part(kinds[t], src[t], low, high) if own else there,
            dst_ref=there,
            send_sem=send.at[t, slot],
            recv_sem=recv.at[t, item],
            device_id=(to, tp),
            device_id_type=MESH,
        )

    def go(t, item, owner, low, high, to, own=False):
        c = copy(t, item, owner, low, high, to, counter[t], own)
        counter[t] += 1
        c.start()
        started.append(c)

    arrive = {
        0: (side, 0, 4),
        1: (down, 0, 4),
        2: (up, 0, 4),
        3: (down ^ 2, 0, 2),
        4: (up ^ 2, 0, 2),
        5: (far, 1, 3),
        6: (far, 0, 1),
        7: (far, 3, 4),
        8: (far ^ 2, 1, 2),
        9: (far ^ 2, 0, 1),
        10: (down ^ 2, 2, 4),
        11: (up ^ 2, 2, 4),
        12: (far ^ 2, 2, 4),
    }

    def got(t, item):
        owner, low, high = arrive[item]
        copy(t, item, owner, low, high, core, 0, False).wait_recv()
        go(t, 13 + item, owner, low, high, core)

    def first(t):
        go(t, 0, me, 0, 4, side, True)
        go(t, 2, me, 0, 4, down, True)
        go(t, 1, me, 0, 4, up, True)
        go(t, 26, me, 0, 4, core, True)
        c = pltpu.make_async_copy(src[t], region(kinds[t], dst[t], me, 0, 4), local.at[t])
        c.start()
        staying.append(c)

    for t in range(n - 1):
        first(t)
    for i in range(m):
        for d in range(1, N_TP):
            tp_copy(i, d, tp ^ d).wait_recv()
    staying[m - 1].wait()
    first(n - 1)
    for t in range(n):
        got(t, 0)
        go(t, 3, side, 0, 2, up)
        go(t, 4, side, 0, 2, down)
        got(t, 1)
        go(t, 5, down, 1, 3, up)
        go(t, 10, down, 2, 4, side)
        got(t, 2)
        go(t, 6, up, 0, 1, down)
        go(t, 7, up, 3, 4, down)
        go(t, 11, up, 2, 4, side)
    for t in range(n):
        got(t, 3)
        go(t, 8, down ^ 2, 1, 2, up)
        got(t, 4)
        go(t, 9, up ^ 2, 0, 1, down)
        got(t, 5)
        got(t, 6)
        got(t, 7)
        go(t, 12, far, 2, 4, side)
    for t in range(n):
        for item in range(8, 13):
            got(t, item)
    for t in range(n):
        for item in range(13):
            owner, low, high = arrive[item]
            copy(t, 13 + item, owner ^ 1, low, high, core, 0, False).wait_recv()
        copy(t, 26, core, 0, 4, core, 0, False).wait_recv()
    for c in started:
        c.wait_send()
    for i, c in enumerate(staying):
        if i != m - 1:
            c.wait()


def gather_all(shards, kinds, tp_shards, tp_kinds):
    n, m = len(kinds), len(tp_kinds)
    shapes, tp_shapes = [], []
    for s, k in zip(tp_shards, tp_kinds):
        shape = list(s.shape)
        shape[1 if k == "cols" else 0] *= N_TP
        tp_shapes.append(jax.ShapeDtypeStruct(tuple(shape), s.dtype))
    for s, k in zip(list(shards) + [tp_shapes[-1]], kinds):
        shape = list(s.shape)
        shape[{"rows": 1, "flat": 0, "cols": 2}[k]] *= N_CTX
        shapes.append(jax.ShapeDtypeStruct(tuple(shape), s.dtype))

    def body(*refs):
        gather_kernel(kinds, tp_kinds, *refs[: n - 1], None, *refs[n - 1 :])

    out = pl.pallas_call(
        body,
        out_shape=tuple(shapes + tp_shapes),
        in_specs=[ANY] * (n - 1 + m),
        out_specs=tuple([ANY] * (n + m)),
        scratch_shapes=[
            pltpu.SemaphoreType.DMA((n, 32)),
            pltpu.SemaphoreType.DMA((n, 27)),
            pltpu.SemaphoreType.DMA((n,)),
            pltpu.SemaphoreType.DMA((m, N_TP)),
            pltpu.SemaphoreType.DMA((m, N_TP)),
            pltpu.SemaphoreType.DMA((m,)),
        ],
        compiler_params=pltpu.CompilerParams(collective_id=0, has_side_effects=True),
        name="gather_all",
    )(*shards, *tp_shards)
    return out[:n], out[n : n + m - 1]


def exchange_kernel(kinds, *refs):
    n = len(kinds)
    src, refs = refs[:n], refs[n:]
    dst, refs = refs[:n], refs[n:]
    held, refs = refs[:n], refs[n:]
    send, recv = refs
    me, tp = lax.axis_index("ctx"), lax.axis_index("tp")
    barrier = pltpu.get_barrier_semaphore()
    for d in range(1, N_TP):
        pl.semaphore_signal(barrier, inc=1, device_id=(me, tp ^ d), device_id_type=MESH)
    pl.semaphore_wait(barrier, N_TP - 1)

    def part(i, ref, rank):
        if kinds[i].endswith("rows"):
            size = src[i].shape[0] // N_TP
            return ref.at[pl.ds(pl.multiple_of(rank * size, size), size), :]
        size = src[i].shape[1] // N_TP
        return ref.at[:, pl.ds(pl.multiple_of(rank * size, size), size)]

    def scatter(i, d):
        return pltpu.make_async_remote_copy(
            src_ref=part(i, src[i], tp ^ d),
            dst_ref=held[i].at[d],
            send_sem=send.at[i, d],
            recv_sem=recv.at[i, d],
            device_id=(me, tp ^ d),
            device_id_type=MESH,
        )

    def spread(i, d, rank):
        return pltpu.make_async_remote_copy(
            src_ref=part(i, dst[i], rank),
            dst_ref=part(i, dst[i], rank),
            send_sem=send.at[i, N_TP + d],
            recv_sem=recv.at[i, N_TP + d],
            device_id=(me, tp ^ d),
            device_id_type=MESH,
        )

    for i in range(n):
        for d in range(1, N_TP):
            scatter(i, d).start()
    for i in range(n):
        for d in range(1, N_TP):
            scatter(i, d).wait_recv()
        total = part(i, src[i], tp)[...].astype(f32)
        for d in range(1, N_TP):
            total = total + held[i][d].astype(f32)
        if kinds[i].startswith("ar"):
            part(i, dst[i], tp)[...] = total.astype(dst[i].dtype)
            for d in range(1, N_TP):
                spread(i, d, tp).start()
        else:
            dst[i][...] = total
    for i in range(n):
        for d in range(1, N_TP):
            scatter(i, d).wait_send()
            if kinds[i].startswith("ar"):
                spread(i, d, tp ^ d).wait_recv()
                spread(i, d, tp).wait_send()


def exchange(arrays, kinds, cid):
    outs, held = [], []
    for a, k in zip(arrays, kinds):
        if k == "rs_cols":
            outs.append(jax.ShapeDtypeStruct((a.shape[0], a.shape[1] // N_TP), f32))
        else:
            outs.append(jax.ShapeDtypeStruct(a.shape, a.dtype))
        r, c = a.shape
        held.append(
            pltpu.VMEM((N_TP, r // N_TP, c) if k == "ar_rows" else (N_TP, r, c // N_TP), a.dtype)
        )
    n = len(kinds)
    return pl.pallas_call(
        functools.partial(exchange_kernel, kinds),
        out_shape=tuple(outs),
        in_specs=[VMEM] * n,
        out_specs=tuple([VMEM] * n),
        scratch_shapes=held
        + [pltpu.SemaphoreType.DMA((n, 2 * N_TP)), pltpu.SemaphoreType.DMA((n, 2 * N_TP))],
        compiler_params=pltpu.CompilerParams(
            collective_id=cid, has_side_effects=True, vmem_limit_bytes=48 << 20
        ),
        name=f"exchange_{cid}",
    )(*arrays)


def halo_kernel(src, dst, send, recv, local):
    me, tp = lax.axis_index("ctx"), lax.axis_index("tp")
    block = src.shape[1]
    barrier = pltpu.get_barrier_semaphore()
    for d in range(1, N_CTX):
        pl.semaphore_signal(
            barrier, inc=1, device_id=(lax.rem(me + d, N_CTX), tp), device_id_type=MESH
        )
    pl.semaphore_wait(barrier, N_CTX - 1)

    def copy(d):
        return pltpu.make_async_remote_copy(
            src_ref=src,
            dst_ref=dst.at[:, pl.ds((PAST - d) * block, block), :],
            send_sem=send.at[d],
            recv_sem=recv.at[d],
            device_id=(lax.rem(me + d, N_CTX), tp),
            device_id_type=MESH,
        )

    own = pltpu.make_async_copy(src, dst.at[:, pl.ds(PAST * block, block), :], local)
    own.start()
    for d in range(1, PAST + 1):
        copy(d).start()
    own.wait()
    for d in range(1, PAST + 1):
        copy(d).wait()


def halo(kv_own):
    seqs, block, cols = kv_own.shape
    return pl.pallas_call(
        halo_kernel,
        out_shape=jax.ShapeDtypeStruct((seqs, (PAST + 1) * block, cols), kv_own.dtype),
        in_specs=[ANY],
        out_specs=ANY,
        scratch_shapes=[
            pltpu.SemaphoreType.DMA((PAST + 1,)),
            pltpu.SemaphoreType.DMA((PAST + 1,)),
            pltpu.SemaphoreType.DMA,
        ],
        compiler_params=pltpu.CompilerParams(collective_id=8, has_side_effects=True),
        name="halo",
    )(kv_own)


def halo_back_kernel(src, dst, held, send, recv):
    me, tp = lax.axis_index("ctx"), lax.axis_index("tp")
    block = dst.shape[1]
    barrier = pltpu.get_barrier_semaphore()
    for d in range(1, N_CTX):
        pl.semaphore_signal(
            barrier, inc=1, device_id=(lax.rem(me + d, N_CTX), tp), device_id_type=MESH
        )
    pl.semaphore_wait(barrier, N_CTX - 1)

    def copy(d):
        return pltpu.make_async_remote_copy(
            src_ref=src.at[:, pl.ds((PAST - d) * block, block), :],
            dst_ref=held.at[d],
            send_sem=send.at[d],
            recv_sem=recv.at[d],
            device_id=(lax.rem(me + N_CTX - d, N_CTX), tp),
            device_id_type=MESH,
        )

    for d in range(1, PAST + 1):
        copy(d).start()
    total = src[:, pl.ds(PAST * block, block), :].astype(f32)
    for d in range(1, PAST + 1):
        copy(d).wait_recv()
        total = total + held[d].astype(f32)
    dst[...] = total
    for d in range(1, PAST + 1):
        copy(d).wait_send()


def halo_back(partial):
    seqs, length, cols = partial.shape
    block = length // (PAST + 1)
    return pl.pallas_call(
        halo_back_kernel,
        out_shape=jax.ShapeDtypeStruct((seqs, block, cols), f32),
        in_specs=[VMEM],
        out_specs=VMEM,
        scratch_shapes=[
            pltpu.VMEM((PAST + 1, seqs, block, cols), partial.dtype),
            pltpu.SemaphoreType.DMA((PAST + 1,)),
            pltpu.SemaphoreType.DMA((PAST + 1,)),
        ],
        compiler_params=pltpu.CompilerParams(
            collective_id=9, has_side_effects=True, vmem_limit_bytes=48 << 20
        ),
        name="halo_back",
    )(partial)


def reduce_kernel(spread_too, *refs):
    n = len(spread_too)
    src, refs = refs[:n], refs[n:]
    dst, refs = refs[:n], refs[n:]
    held, refs = refs[:n], refs[n:]
    send, recv = refs
    me, tp = lax.axis_index("ctx"), lax.axis_index("tp")
    barrier = pltpu.get_barrier_semaphore()
    for d in range(1, N_CTX):
        pl.semaphore_signal(barrier, inc=1, device_id=(me ^ d, tp), device_id_type=MESH)
    pl.semaphore_wait(barrier, N_CTX - 1)

    def scatter(i, d):
        return pltpu.make_async_remote_copy(
            src_ref=src[i].at[me ^ d],
            dst_ref=held[i].at[d],
            send_sem=send.at[i, d],
            recv_sem=recv.at[i, d],
            device_id=(me ^ d, tp),
            device_id_type=MESH,
        )

    def spread(i, d, rank):
        return pltpu.make_async_remote_copy(
            src_ref=dst[i].at[rank],
            dst_ref=dst[i].at[rank],
            send_sem=send.at[i, N_CTX + d],
            recv_sem=recv.at[i, N_CTX + d],
            device_id=(me ^ d, tp),
            device_id_type=MESH,
        )

    for i in range(n):
        for d in range(1, N_CTX):
            scatter(i, d).start()
    for i in range(n):
        for d in range(1, N_CTX):
            scatter(i, d).wait_recv()
        total = src[i][me].astype(f32)
        for d in range(1, N_CTX):
            total = total + held[i][d].astype(f32)
        if spread_too[i]:
            dst[i][me] = total.astype(dst[i].dtype)
            for d in range(1, N_CTX):
                spread(i, d, me).start()
        else:
            dst[i][...] = total
    for i in range(n):
        for d in range(1, N_CTX):
            scatter(i, d).wait_send()
            if spread_too[i]:
                spread(i, d, me ^ d).wait_recv()
                spread(i, d, me).wait_send()


def reduce_ctx(arrays, spread_too):
    outs = [
        jax.ShapeDtypeStruct(a.shape if s else a.shape[1:], a.dtype if s else f32)
        for a, s in zip(arrays, spread_too)
    ]
    n = len(arrays)
    return pl.pallas_call(
        functools.partial(reduce_kernel, spread_too),
        out_shape=tuple(outs),
        in_specs=[VMEM] * n,
        out_specs=tuple([VMEM] * n),
        scratch_shapes=[pltpu.VMEM(a.shape, a.dtype) for a in arrays]
        + [pltpu.SemaphoreType.DMA((n, 2 * N_CTX)), pltpu.SemaphoreType.DMA((n, 2 * N_CTX))],
        compiler_params=pltpu.CompilerParams(
            collective_id=10, has_side_effects=True, vmem_limit_bytes=48 << 20
        ),
        name="reduce_ctx",
    )(*arrays)


def rms_scale(values, gain):
    return values * lax.rsqrt(jnp.mean(values * values, axis=-1, keepdims=True) + eps) * gain


def norm_back(values, gain, grad_normed):
    inverse = lax.rsqrt(jnp.mean(values * values, axis=-1, keepdims=True) + eps)
    scaled = grad_normed * gain
    return inverse * scaled - values * inverse**3 * jnp.mean(
        scaled * values, axis=-1, keepdims=True
    )


def doc_layout(doc_lengths, positions):
    ends = jnp.cumsum(doc_lengths, axis=1)
    passed = positions[None, :, None] >= ends[:, None, :]
    doc_ids = jnp.sum(passed.astype(jnp.int32), axis=2)
    starting = jnp.sum(jnp.where(passed, doc_lengths[:, None, :], 0), axis=2)
    inside = positions[None, :] < ends[:, -1:]
    doc_ids = jnp.where(inside, doc_ids, -1 - positions[None, :])
    return (doc_ids, positions[None, :] - starting)


def dot(a, b, ca=1, cb=0):
    return lax.dot_general(a, b, (((ca,), (cb,)), ((), ())), preferred_element_type=f32)


def rope(x, cosine, sine, sign):
    half = HEAD_DIM // 2
    x1, x2 = x[..., :half], x[..., half:]
    s = sine * sign
    return jnp.concatenate([x1 * cosine - x2 * s, x2 * cosine + x1 * s], axis=-1)


def gates_of(logits, onehot):
    chosen = jnp.sum(logits[:, None, :] * onehot, axis=-1)
    return jax.nn.softmax(chosen, axis=-1)


def gates_back(gates, grad_gates, onehot):
    inner = gates * (grad_gates - jnp.sum(gates * grad_gates, axis=-1, keepdims=True))
    return jnp.sum(inner[..., None] * onehot, axis=1)


def dot_nt(a, b):
    return dot(a, b, 1, 1)


def dot_tn(a, b):
    return dot(a, b, 0, 0)


def by_seq(rows, f):
    half = rows.shape[0] // 2
    return jnp.concatenate([f(0, rows[:half]), f(1, rows[half:])], axis=0)


def column_of(values, lane, e):
    return jnp.sum(jnp.where(lane == e, values, 0.0), axis=1, keepdims=True)


def greet(targets):
    barrier = pltpu.get_barrier_semaphore()
    for device in targets:
        pl.semaphore_signal(barrier, inc=1, device_id=device, device_id_type=MESH)
    pl.semaphore_wait(barrier, len(targets))


def masked_gates(logits, hot):
    largest = jnp.max(jnp.where(hot > 0, logits, big_negative), axis=1, keepdims=True)
    powers = jnp.where(hot > 0, jnp.exp(logits - largest), 0.0)
    return powers / jnp.sum(powers, axis=1, keepdims=True)


def ffn_kernel(
    x0, attn, dy, gain, wide, router, hot, b_gu, a_d, z_o, w_gu_hbm, w_d_hbm,
    mixed, dx1, dx1_own, n2, z_sum, g_gu, g_d,
    w_gu, w_d, hg, dgu, dh_tmp, z_gu, dz_d, z_part, parts, own, held, z_held, dots, tails,
    load, send, recv,
):
    me, tp = lax.axis_index("ctx"), lax.axis_index("tp")
    rows, model = x0.shape
    experts = w_gu.shape[0]
    part = model // N_TP
    greet([(me, tp ^ d) for d in range(1, N_TP)])

    def fetch(e):
        return (
            pltpu.make_async_copy(w_gu_hbm.at[e], w_gu.at[e], load.at[0, e]),
            pltpu.make_async_copy(w_d_hbm.at[e], w_d.at[e], load.at[1, e]),
        )

    for e in range(experts):
        for c in fetch(e):
            c.start()

    step = 32

    def normalize(i, carry):
        at = pl.ds(pl.multiple_of(i * step, step), step)
        x = x0[at, :].astype(f32) + attn[at, :].astype(f32)
        n2[at, :] = rms_scale(x, gain[...]).astype(bf16)
        return carry

    lax.fori_loop(0, rows // step, normalize, 0)
    lane = lax.broadcasted_iota(jnp.int32, (rows, 128), 1)
    gates = masked_gates(dot(n2[...], router[...]), hot[...])
    z_gu[...] = by_seq(n2[...], lambda s, v: dot(v, wide[:, 128 * s : 128 * s + 128])).astype(bf16)
    dz_d[...] = by_seq(dy[...], lambda s, v: dot(v, wide[:, 256 + 128 * s : 384 + 128 * s])).astype(bf16)
    g_gu[...] = jnp.zeros_like(g_gu)
    g_d[...] = jnp.zeros_like(g_d)
    zero = jnp.zeros((rows, 128), f32)

    def expert(e, carry):
        d_gates, dz_gu, z_d = carry
        for c in fetch(e):
            c.wait()
        gate = column_of(gates, lane, e)
        z_in = jnp.where(lane // 32 == e, z_gu[...].astype(f32), 0.0).astype(bf16)
        dz_in = jnp.where(lane // 16 == 4 + e, dz_d[...].astype(f32), 0.0).astype(bf16)
        dh_tmp[:, :704] = dot_nt(dy[...], w_d[e]) + by_seq(dz_in, lambda s, v: dot(v, a_d[s]))
        pre = dot(n2[...], w_gu[e]) + by_seq(z_in, lambda s, v: dot(v, b_gu[s]))

        def tile(g, u, d):
            sg = jax.nn.sigmoid(g)
            silu = g * sg
            h = silu * u
            dg = d * gate
            return h, (dg * u * sg * (1.0 + g * (1.0 - sg))), dg * silu, h * d

        h, dgp, dup, hd = tile(pre[:, :640], pre[:, 640:1280], dh_tmp[:, :640])
        hg[e, :, :640] = (h * gate).astype(bf16)
        dgu[e, :, :640] = dgp.astype(bf16)
        dgu[e, :, 640:1280] = dup.astype(bf16)
        dgf = jnp.sum(hd, axis=1, keepdims=True)
        last = pre[:, 1280:]
        h, dgp, dup, hd = tile(last, pltpu.roll(last, 64, 1), dh_tmp[:, 640:])
        hg[e, :, 640:] = (h * gate).astype(bf16)[:, :64]
        dgu[e, :, 1280:] = jnp.where(lane < 64, dgp, pltpu.roll(dup, 64, 1)).astype(bf16)
        dgf = dgf + jnp.sum(jnp.where(lane < 64, hd, 0.0), axis=1, keepdims=True)
        d_gates = d_gates + jnp.where(lane == e, dgf, 0.0)
        back = by_seq(dgu[e], lambda s, v: dot_nt(v, b_gu[s]))
        dz_gu = dz_gu + jnp.where(lane // 32 == e, back, 0.0)
        low = by_seq(hg[e], lambda s, v: dot_nt(v, a_d[s]))
        z_d = z_d + jnp.where(lane // 16 == 4 + e, low, 0.0)
        half = rows // 2
        for s in range(2):
            at = slice(s * half, s * half + half)
            g_gu[s] += dot_tn(z_in[at], dgu[e, at, :])
            g_d[s] += dot_tn(dz_in[at], hg[e, at, :])
        return d_gates, dz_gu, z_d

    d_gates, dz_gu, z_d = lax.fori_loop(0, experts, expert, (zero, zero, zero))
    d_logits = gates * (d_gates - jnp.sum(gates * d_gates, axis=1, keepdims=True))
    d_logits = d_logits.astype(bf16)
    dz_gu, z_d = dz_gu.astype(bf16), z_d.astype(bf16)
    z_part[:, :128] = dz_gu
    z_part[:, 128:] = z_o[...] + z_d

    def scatter(i, d):
        return pltpu.make_async_remote_copy(
            src_ref=parts.at[i, d],
            dst_ref=held.at[i, d],
            send_sem=send.at[i, d],
            recv_sem=recv.at[i, d],
            device_id=(me, tp ^ d),
            device_id_type=MESH,
        )

    def piece(j, carry):
        d = lax.rem(j, N_TP)
        peer = tp ^ d
        at = pl.ds(pl.multiple_of(peer * part, part), part)
        w_rows = wide[at, :]
        dn = dot_nt(d_logits, router[at, :])
        dn = dn + by_seq(dz_gu, lambda s, v: dot_nt(v, w_rows[:, 128 * s : 128 * s + 128]))
        ff = by_seq(z_d, lambda s, v: dot_nt(v, w_rows[:, 256 + 128 * s : 384 + 128 * s]))
        for e in range(experts):
            dn = dn + dot_nt(dgu[e], w_gu[e, at, :])
            ff = ff + dot(hg[e], w_d[e, :, at])

        @pl.when(j < N_TP)
        def _():
            parts[0, d] = dn.astype(bf16)
            parts[1, d] = ff.astype(bf16)
            scatter(0, d).start()
            scatter(1, d).start()

        @pl.when(j == N_TP)
        def _():
            own[0] = dn
            own[1] = ff

        return carry

    z_rows = rows // N_TP

    def z_region(ref, rank):
        return ref.at[pl.ds(pl.multiple_of(rank * z_rows, z_rows), z_rows), :]

    def z_scatter(d):
        return pltpu.make_async_remote_copy(
            src_ref=z_region(z_part, tp ^ d),
            dst_ref=z_held.at[d],
            send_sem=send.at[2, d],
            recv_sem=recv.at[2, d],
            device_id=(me, tp ^ d),
            device_id_type=MESH,
        )

    def z_spread(d, rank):
        return pltpu.make_async_remote_copy(
            src_ref=z_region(z_sum, rank),
            dst_ref=z_region(z_sum, rank),
            send_sem=send.at[3, d],
            recv_sem=recv.at[3, d],
            device_id=(me, tp ^ d),
            device_id_type=MESH,
        )

    def columns(ref, rank):
        return ref.at[:, pl.ds(pl.multiple_of(rank * part, part), part)]

    def spread(d, rank):
        return pltpu.make_async_remote_copy(
            src_ref=columns(dx1, rank),
            dst_ref=columns(dx1, rank),
            send_sem=send.at[4, d],
            recv_sem=recv.at[4, d],
            device_id=(me, tp ^ d),
            device_id_type=MESH,
        )

    def tail(d, rank):
        return pltpu.make_async_remote_copy(
            src_ref=tails.at[rank],
            dst_ref=tails.at[rank],
            send_sem=send.at[5, d],
            recv_sem=recv.at[5, d],
            device_id=(me, tp ^ d),
            device_id_type=MESH,
        )

    def x_own():
        return x0[:, at].astype(f32) + attn[:, at].astype(f32)

    lax.fori_loop(1, N_TP + 1, piece, 0)
    for d in range(1, N_TP):
        z_scatter(d).start()
    total = own[0]
    for d in range(1, N_TP):
        scatter(0, d).wait_recv()
        total = total + held[0, d].astype(f32)
    at = pl.ds(pl.multiple_of(tp * part, part), part)
    total = total * gain[:, at]
    own[0] = total
    columns(dx1, tp)[...] = total.astype(bf16)
    for d in range(1, N_TP):
        spread(d, tp).start()
    dots[...] = jnp.broadcast_to(jnp.sum(total * x_own(), axis=1, keepdims=True), dots.shape)
    tails[tp] = jnp.transpose(dots[...])[:8, :]
    for d in range(1, N_TP):
        tail(d, tp).start()
    total = own[1] + x_own()
    for d in range(1, N_TP):
        scatter(1, d).wait_recv()
        total = total + held[1, d].astype(f32)
    mixed[...] = total.astype(bf16)
    total = z_region(z_part, tp)[...].astype(f32)
    for d in range(1, N_TP):
        z_scatter(d).wait_recv()
        total = total + z_held[d].astype(f32)
    z_region(z_sum, tp)[...] = total.astype(bf16)
    for d in range(1, N_TP):
        z_spread(d, tp).start()
    for d in range(1, N_TP):
        tail(d, tp ^ d).wait_recv()
    whole = tails[0]
    for d in range(1, N_TP):
        whole = whole + tails[d]
    dots[...] = jnp.transpose(jnp.broadcast_to(whole[:1], (128, rows)))
    for d in range(1, N_TP):
        spread(d, tp ^ d).wait_recv()
        spread(d, tp).wait_send()

    def back(i, carry):
        rows_at = pl.ds(pl.multiple_of(i * step, step), step)
        x = x0[rows_at, :].astype(f32) + attn[rows_at, :].astype(f32)
        inverse = lax.rsqrt(jnp.mean(x * x, axis=1, keepdims=True) + eps)
        mean = dots[rows_at, :1] * (1.0 / model)
        got = dy[rows_at, :].astype(f32) + inverse * dx1[rows_at, :].astype(f32) - x * inverse**3 * mean
        dx1[rows_at, :] = got.astype(bf16)
        dx1_own[rows_at, :] = (
            dy[rows_at, at].astype(f32) + inverse * own[0, rows_at, :]
            - (x0[rows_at, at].astype(f32) + attn[rows_at, at].astype(f32)) * inverse**3 * mean
        )
        return carry

    lax.fori_loop(0, rows // step, back, 0)
    for d in range(1, N_TP):
        scatter(0, d).wait_send()
        scatter(1, d).wait_send()
        z_scatter(d).wait_send()
        z_spread(d, tp ^ d).wait_recv()
        z_spread(d, tp).wait_send()
        tail(d, tp).wait_send()


def feed_forward(x0, attn, dy, gain, wide, router, hot, b_gu, a_d, z_o, w_gu, w_d):
    rows, model = x0.shape
    part = model // N_TP
    experts, _, cols = w_gu.shape
    hidden = w_d.shape[1]
    shape = jax.ShapeDtypeStruct
    return pl.pallas_call(
        ffn_kernel,
        out_shape=(
            shape((rows, part), bf16),
            shape((rows, model), bf16),
            shape((rows, part), f32),
            shape((rows, model), bf16),
            shape((rows, 256), bf16),
            shape(b_gu.shape, f32),
            shape(a_d.shape, f32),
        ),
        in_specs=[VMEM] * 10 + [ANY] * 2,
        out_specs=tuple([VMEM] * 7),
        scratch_shapes=[
            pltpu.VMEM(w_gu.shape, bf16),
            pltpu.VMEM(w_d.shape, bf16),
            pltpu.VMEM((experts, rows, hidden), bf16),
            pltpu.VMEM((experts, rows, cols), bf16),
            pltpu.VMEM((rows, 768), f32),
            pltpu.VMEM((rows, 128), bf16),
            pltpu.VMEM((rows, 128), bf16),
            pltpu.VMEM((rows, 256), bf16),
            pltpu.VMEM((2, N_TP, rows, part), bf16),
            pltpu.VMEM((2, rows, part), f32),
            pltpu.VMEM((2, N_TP, rows, part), bf16),
            pltpu.VMEM((N_TP, rows // N_TP, 256), bf16),
            pltpu.VMEM((rows, 128), f32),
            pltpu.VMEM((N_TP, 8, rows), f32),
            pltpu.SemaphoreType.DMA((2, experts)),
            pltpu.SemaphoreType.DMA((6, N_TP)),
            pltpu.SemaphoreType.DMA((6, N_TP)),
        ],
        compiler_params=pltpu.CompilerParams(
            collective_id=2, has_side_effects=True, vmem_limit_bytes=62 << 20
        ),
        name="feed_forward",
    )(x0, attn, dy, gain, wide, router, hot, b_gu, a_d, z_o, w_gu, w_d)


def widen_routes(routes, experts):
    lane = jnp.arange(128, dtype=jnp.int32)
    return jnp.sum((routes[..., None] == lane).astype(f32), axis=1)


def gate_up_columns(gate, up):
    return jnp.concatenate([gate[..., :640], up[..., :640], gate[..., 640:], up[..., 640:]], axis=-1)


def attention_kernel(
    s_q, s_kv, s_o, s_gu, s_d, tokens, cotangent, s_wide,
    gain, router, hot0, hot1, cosine, sine, q_doc, k_doc, b_q, b_kv, a_o,
    g_q, g_kv, g_o, g_gu, g_d, g_wide, wide_mid, dy,
    x0, attn, n1, kv_all, q_all, probs, ob, z_o, z_q, z_kv, gates,
    w_q, w_kv, w_o, wide, parts, own, held,
    send, recv, local, tp_send, tp_recv, tp_local, kv_send, kv_recv, load, sum_send, sum_recv,
):
    me, tp = lax.axis_index("ctx"), lax.axis_index("tp")
    core, side = me ^ 1, me ^ 2
    up, down, far = lax.rem(me + 4, 16), lax.rem(me + 12, 16), lax.rem(me + 8, 16)
    on_core, on_side = lax.rem(me, 2), lax.rem(me // 2, 2)
    rows, model = x0.shape
    part = model // N_TP
    half = rows // 2
    experts = w_q.shape[0]
    width = w_q.shape[2]
    heads = width // HEAD_DIM
    span = (PAST + 1) * half
    greet([(d, tp) for d in (core, side, up, down, far)] + [(me, tp ^ d) for d in range(1, N_TP)])

    kinds = ["flat", "flat", "rows", "cols", "rows", "cols"]
    src = [s_kv, wide_mid, s_q, s_o, s_gu, s_d]
    dst = [g_kv, g_wide, g_q, g_o, g_gu, g_d]
    tp_src, tp_dst, tp_kinds = [tokens, s_wide, cotangent], [x0, wide_mid, dy], ["cols", "rows", "cols"]
    started, staying = [], []
    counter = [0] * len(kinds)

    def tp_copy(i, d, rank):
        size = tp_src[i].shape[1 if tp_kinds[i] == "cols" else 0]
        return pltpu.make_async_remote_copy(
            src_ref=tp_src[i],
            dst_ref=tp_part(tp_kinds[i], tp_dst[i], rank, size),
            send_sem=tp_send.at[i, d],
            recv_sem=tp_recv.at[i, d],
            device_id=(me, tp ^ d),
            device_id_type=MESH,
        )

    def tp_own(i):
        size = tp_src[i].shape[1 if tp_kinds[i] == "cols" else 0]
        return pltpu.make_async_copy(
            tp_src[i], tp_part(tp_kinds[i], tp_dst[i], tp, size), tp_local.at[i]
        )

    def tp_wait(i):
        for d in range(1, N_TP):
            tp_copy(i, d, tp ^ d).wait_recv()
        tp_own(i).wait()

    def copy(t, item, owner, low, high, to, slot, own_shard):
        there = region(kinds[t], dst[t], owner, low, high)
        return pltpu.make_async_remote_copy(
            src_ref=own_part(kinds[t], src[t], low, high) if own_shard else there,
            dst_ref=there,
            send_sem=send.at[t, slot],
            recv_sem=recv.at[t, item],
            device_id=(to, tp),
            device_id_type=MESH,
        )

    def go(t, item, owner, low, high, to, own_shard=False):
        c = copy(t, item, owner, low, high, to, counter[t], own_shard)
        counter[t] += 1
        c.start()
        started.append(c)

    arrive = {
        0: (side, 0, 4),
        1: (down, 0, 4),
        2: (up, 0, 4),
        3: (down ^ 2, 0, 2),
        4: (up ^ 2, 0, 2),
        5: (far, 1, 3),
        6: (far, 0, 1),
        7: (far, 3, 4),
        8: (far ^ 2, 1, 2),
        9: (far ^ 2, 0, 1),
        10: (down ^ 2, 2, 4),
        11: (up ^ 2, 2, 4),
        12: (far ^ 2, 2, 4),
    }

    def got(t, item):
        owner, low, high = arrive[item]
        copy(t, item, owner, low, high, core, 0, False).wait_recv()
        go(t, 13 + item, owner, low, high, core)

    def first(t):
        go(t, 0, me, 0, 4, side, True)
        go(t, 2, me, 0, 4, down, True)
        go(t, 1, me, 0, 4, up, True)
        go(t, 26, me, 0, 4, core, True)
        c = pltpu.make_async_copy(src[t], region(kinds[t], dst[t], me, 0, 4), local.at[t])
        c.start()
        staying.append(c)

    def second(t):
        got(t, 0)
        go(t, 3, side, 0, 2, up)
        go(t, 4, side, 0, 2, down)
        got(t, 1)
        go(t, 5, down, 1, 3, up)
        go(t, 10, down, 2, 4, side)
        got(t, 2)
        go(t, 6, up, 0, 1, down)
        go(t, 7, up, 3, 4, down)
        go(t, 11, up, 2, 4, side)

    def third(t):
        got(t, 3)
        go(t, 8, down ^ 2, 1, 2, up)
        got(t, 4)
        go(t, 9, up ^ 2, 0, 1, down)
        got(t, 5)
        got(t, 6)
        got(t, 7)
        go(t, 12, far, 2, 4, side)

    def fourth(t):
        for item in range(8, 13):
            got(t, item)

    def finish(t):
        for item in range(13):
            owner, low, high = arrive[item]
            copy(t, 13 + item, owner ^ 1, low, high, core, 0, False).wait_recv()
        copy(t, 26, core, 0, 4, core, 0, False).wait_recv()

    for i in range(3):
        for d in range(1, N_TP):
            c = tp_copy(i, d, tp)
            c.start()
            started.append(c)
        tp_own(i).start()
    for t in (0, 2, 3):
        first(t)
    tp_wait(1)
    first(1)
    tp_wait(0)
    step = 32

    def normalize(i, carry):
        at = pl.ds(pl.multiple_of(i * step, step), step)
        n1[at, :] = rms_scale(x0[at, :].astype(f32), gain[...]).astype(bf16)
        return carry

    lax.fori_loop(0, rows // step, normalize, 0)
    gates[...] = masked_gates(dot(n1[...], router[...]), hot0[...] + hot1[...])
    for t in (0, 2, 1, 3):
        second(t)
    for t in (0, 2, 1, 3):
        third(t)
    first(4)
    first(5)
    for t in (0, 2, 1, 3):
        fourth(t)

    for c in staying[:4]:
        c.wait()
    fetches = []
    for i, (t, ref) in enumerate([(0, w_kv), (1, wide), (2, w_q), (3, w_o)]):
        finish(t)
        c = pltpu.make_async_copy(dst[t], ref, load.at[i])
        c.start()
        fetches.append(c)

    lane = lax.broadcasted_iota(jnp.int32, (rows, 128), 1)
    seq = lax.broadcasted_iota(jnp.int32, (rows, 128), 0) // half

    def rotary(x):
        return x * cosine[...] + pltpu.roll(x, HEAD_DIM // 2, 1) * sine[...]

    fetches[0].wait()
    fetches[1].wait()
    z = dot(n1[...], wide[:, 512:640])
    z_q[...] = jnp.where(lane // 64 == seq, z, 0.0).astype(bf16)
    z = dot(n1[...], wide[:, 640:704])
    z_kv[...] = jnp.where((lane // 16) % 2 == seq, jnp.pad(z, ((0, 0), (0, 64))), 0.0).astype(bf16)
    kv = dot(n1[...], w_kv[...]) + dot(z_kv[:, :64], b_kv[...])
    for h in range(heads):
        at = slice(HEAD_DIM * h, HEAD_DIM * h + HEAD_DIM)
        turned = rotary(kv[:, at]).astype(bf16)
        kv_all[PAST, 0, :, at] = turned[:half]
        kv_all[PAST, 1, :, at] = turned[half:]
    for s in range(2):
        kv_all[PAST, s, :, width:] = kv[half * s : half * s + half, width:].astype(bf16)

    def kv_copy(slot, back, to, to_back):
        return pltpu.make_async_remote_copy(
            src_ref=kv_all.at[PAST - back],
            dst_ref=kv_all.at[PAST - to_back],
            send_sem=kv_send.at[slot],
            recv_sem=kv_recv.at[to_back],
            device_id=(to, tp),
            device_id_type=MESH,
        )

    def kv_arrived(back):
        kv_copy(0, back, core, back).wait_recv()

    def when(condition, c):
        if condition is None:
            c.start()
        else:
            pl.when(condition)(c.start)
        kv_started.append((condition, c))

    kv_started = []
    when(None, kv_copy(0, 0, up, 4))
    when(None, kv_copy(1, 0, far, 8))
    when(on_side == 0, kv_copy(2, 0, side, 2))
    when(on_core == 0, kv_copy(3, 0, core, 1))

    fetches[2].wait()
    queries = [jnp.zeros((rows, width), f32), jnp.zeros((rows, width), f32)]
    for e in range(experts):
        z_e = jnp.where((lane % 64) // 16 == e, z_q[...].astype(f32), 0.0).astype(bf16)
        q_e = dot(n1[...], w_q[e]) + dot(z_e, b_q[...])
        for k, hot in enumerate((hot0, hot1)):
            queries[k] = queries[k] + jnp.where(hot[:, e : e + 1] > 0, q_e, 0.0)
    for k in range(2):
        for h in range(heads):
            turned = rotary(queries[k][:, HEAD_DIM * h : HEAD_DIM * h + HEAD_DIM]).astype(bf16)
            for s in range(2):
                q_all[s * heads + h, k * half : k * half + half, :] = turned[half * s : half * s + half]

    kv_arrived(4)
    when(on_side == 0, kv_copy(4, 4, side, 6))
    when(on_side == 1, kv_copy(5, 4, side, 2))
    when(on_core == 0, kv_copy(6, 4, core, 5))
    when(on_core == 1, kv_copy(7, 4, core, 3))
    kv_arrived(8)
    when(on_side == 1, kv_copy(8, 8, side, 6))
    when(on_core == 1, kv_copy(9, 8, core, 7))
    kv_arrived(2)
    when(on_core == 0, kv_copy(10, 2, core, 3))
    when(on_core == 1, kv_copy(11, 2, core, 1))
    kv_arrived(6)
    when(on_core == 0, kv_copy(12, 6, core, 7))
    when(on_core == 1, kv_copy(13, 6, core, 5))
    for back in (1, 3, 5, 7):
        kv_arrived(back)

    row = lax.broadcasted_iota(jnp.int32, (half, span), 0)
    key = lax.broadcasted_iota(jnp.int32, (half, span), 1)
    near = (key > row) & (key <= row + PAST * half)

    def attend(i, carry):
        s = i // heads
        h = lax.rem(i, heads)
        at = pl.ds(pl.multiple_of(h * HEAD_DIM, HEAD_DIM), HEAD_DIM)
        v_at = pl.ds(pl.multiple_of(width + h * HEAD_DIM, HEAD_DIM), HEAD_DIM)
        keys = kv_all[:, s, :, at].reshape(span, HEAD_DIM)
        values = kv_all[:, s, :, v_at].reshape(span, HEAD_DIM)
        seq_rows = pl.ds(pl.multiple_of(s * half, half), half)
        allowed = near & (q_doc[seq_rows, :1] == k_doc[s, :1, :])
        for k in range(2):
            q = q_all[i, k * half : k * half + half, :]
            scores = dot_nt(q, keys) * HEAD_DIM**-0.5
            scores = jnp.where(allowed, scores, big_negative)
            peak = jnp.max(scores, axis=1, keepdims=True)
            powers = jnp.exp(scores - peak)
            p = (powers * (1.0 / jnp.sum(powers, axis=1, keepdims=True))).astype(bf16)
            probs[i, k * half : k * half + half, :] = p
            ob[k, seq_rows, at] = dot(p, values).astype(bf16)
        return carry

    lax.fori_loop(0, 2 * heads, attend, 0)
    second(4)

    fetches[3].wait()
    z_acc = jnp.zeros((rows, 128), f32)
    chosen = []
    for e in range(experts):
        o_e = jnp.where(hot0[:, e : e + 1] > 0, ob[0].astype(f32), 0.0)
        o_e = o_e + jnp.where(hot1[:, e : e + 1] > 0, ob[1].astype(f32), 0.0)
        o_e = o_e.astype(bf16)
        chosen.append(o_e)
        low = by_seq(o_e, lambda s, v: dot_nt(v, a_o[s]))
        z_acc = z_acc + jnp.where(lane // 16 == e, low * gates[:, e : e + 1], 0.0)
    z_o[...] = z_acc.astype(bf16)

    def columns(ref, rank):
        return ref.at[:, pl.ds(pl.multiple_of(rank * part, part), part)]

    def scatter(d):
        return pltpu.make_async_remote_copy(
            src_ref=parts.at[d],
            dst_ref=held.at[d],
            send_sem=sum_send.at[0, d],
            recv_sem=sum_recv.at[0, d],
            device_id=(me, tp ^ d),
            device_id_type=MESH,
        )

    def spread(d, rank):
        return pltpu.make_async_remote_copy(
            src_ref=columns(attn, rank),
            dst_ref=columns(attn, rank),
            send_sem=sum_send.at[1, d],
            recv_sem=sum_recv.at[1, d],
            device_id=(me, tp ^ d),
            device_id_type=MESH,
        )

    for j in range(1, N_TP + 1):
        d = j % N_TP
        at = pl.ds(pl.multiple_of((tp ^ d) * part, part), part)
        w_rows = wide[at, 256:512]
        total = by_seq(z_o[...], lambda s, v: dot_nt(v, w_rows[:, 128 * s : 128 * s + 128]))
        for e in range(experts):
            total = total + dot(chosen[e], w_o[e, :, at]) * gates[:, e : e + 1]
        if d:
            parts[d] = total.astype(bf16)
            scatter(d).start()
        else:
            own[...] = total
    second(5)
    total = own[...]
    for d in range(1, N_TP):
        scatter(d).wait_recv()
        total = total + held[d].astype(f32)
    columns(attn, tp)[...] = total.astype(bf16)
    for d in range(1, N_TP):
        spread(d, tp).start()
    third(4)
    third(5)
    for d in range(1, N_TP):
        spread(d, tp ^ d).wait_recv()
    fourth(4)
    fourth(5)
    tp_wait(2)
    for t in (4, 5):
        finish(t)
    for c in started:
        c.wait_send()
    for c in staying[4:]:
        c.wait()
    for condition, c in kv_started:
        if condition is None:
            c.wait_send()
        else:
            pl.when(condition)(c.wait_send)
    for d in range(1, N_TP):
        scatter(d).wait_send()
        spread(d, tp).wait_send()


def attention(shards_in, tp_shards, small):
    s_q, s_kv, s_o, s_gu, s_d = shards_in
    tokens, cotangent, s_wide = tp_shards
    rows, part = tokens.shape
    model = part * N_TP
    experts, _, width = s_q.shape
    half = rows // 2
    heads = width // HEAD_DIM
    shape = jax.ShapeDtypeStruct

    def grown(a, d):
        return shape(tuple(n * (N_CTX if i == d else 1) for i, n in enumerate(a.shape)), a.dtype)

    gathered = (grown(s_q, 1), grown(s_kv, 0), grown(s_o, 2), grown(s_gu, 1), grown(s_d, 2))
    wide_mid = shape((s_wide.shape[0] * N_TP, s_wide.shape[1]), bf16)
    wide = grown(wide_mid, 0)
    vmem_out = (
        shape((rows, model), bf16),
        shape((rows, model), bf16),
        shape((rows, model), bf16),
        shape((PAST + 1, 2, half, 2 * width), bf16),
        shape((2 * heads, rows, HEAD_DIM), bf16),
        shape((2 * heads, rows, (PAST + 1) * half), bf16),
        shape((2, rows, width), bf16),
        shape((rows, 128), bf16),
        shape((rows, 128), bf16),
        shape((rows, 128), bf16),
        shape((rows, 128), f32),
    )
    any_out = gathered + (wide, wide_mid, shape((rows, model), bf16))
    return pl.pallas_call(
        attention_kernel,
        out_shape=any_out + vmem_out,
        in_specs=[ANY] * 8 + [VMEM] * len(small),
        out_specs=tuple([ANY] * len(any_out) + [VMEM] * len(vmem_out)),
        scratch_shapes=[
            pltpu.VMEM(gathered[0].shape, bf16),
            pltpu.VMEM(gathered[1].shape, bf16),
            pltpu.VMEM(gathered[2].shape, bf16),
            pltpu.VMEM(wide.shape, bf16),
            pltpu.VMEM((N_TP, rows, part), bf16),
            pltpu.VMEM((rows, part), f32),
            pltpu.VMEM((N_TP, rows, part), bf16),
            pltpu.SemaphoreType.DMA((6, 32)),
            pltpu.SemaphoreType.DMA((6, 27)),
            pltpu.SemaphoreType.DMA((6,)),
            pltpu.SemaphoreType.DMA((3, N_TP)),
            pltpu.SemaphoreType.DMA((3, N_TP)),
            pltpu.SemaphoreType.DMA((3,)),
            pltpu.SemaphoreType.DMA((14,)),
            pltpu.SemaphoreType.DMA((PAST + 1,)),
            pltpu.SemaphoreType.DMA((4,)),
            pltpu.SemaphoreType.DMA((2, N_TP)),
            pltpu.SemaphoreType.DMA((2, N_TP)),
        ],
        compiler_params=pltpu.CompilerParams(
            collective_id=0, has_side_effects=True, vmem_limit_bytes=60 << 20
        ),
        name="attention",
    )(*shards_in, *tp_shards, *small)


def shards(
    tokens,
    norm1_gain,
    router_attn,
    w_query,
    w_key_value,
    w_out,
    norm2_gain,
    router_ffn,
    w_gate_up,
    w_down,
    adapt_wide,
    adapt_heads,
    adapt_ffn,
    attention_routes,
    feedforward_routes,
    doc_lengths,
    adapter_index,
    cotangent,
):
    seqs, block, part = tokens.shape
    rows = seqs * block
    n_ctx = lax.axis_size("ctx")
    n_tp = lax.axis_size("tp")
    model = part * n_tp
    experts = w_query.shape[0]
    width = w_query.shape[2]
    heads = width // HEAD_DIM
    hidden = w_down.shape[1]
    rank = adapt_heads.shape[2]
    wide_slots = adapt_wide.shape[1]
    ctx_rank = lax.axis_index("ctx")
    tp_rank = lax.axis_index("tp")

    def split(a):
        return a.reshape((seqs, block) + a.shape[1:])

    def merge(a):
        return a.reshape((rows,) + a.shape[2:])

    wide_own = adapt_wide.astype(bf16)[adapter_index]
    groups = [[6, 10, 7, 11, 8, 12, 9, 13], list(range(14, 22)), [0, 1, 2, 3], [4, 5]]
    order = [(q, s) for g in groups[:3] for q in range(seqs) for s in g]
    order += [(q, s) for s in groups[3] for q in range(seqs)]
    wide_cols = wide_own.reshape(seqs * wide_slots, rank, -1)[
        np.array([q * wide_slots + s for q, s in order])
    ].reshape(seqs * wide_slots * rank, -1).T
    heads_low = adapt_heads.astype(bf16)[adapter_index]
    ffn_low = adapt_ffn.astype(bf16)[adapter_index]
    route_a = attention_routes.reshape(rows, -1)
    route_f = feedforward_routes.reshape(rows, -1)
    hot_a = jax.nn.one_hot(route_a, experts, dtype=f32)
    hot_f = jax.nn.one_hot(route_f, experts, dtype=f32)

    positions = ctx_rank * block + jnp.arange(block, dtype=jnp.int32)
    doc_ids, offsets = doc_layout(doc_lengths, positions)
    half = HEAD_DIM // 2
    frequency = 10000.0 ** (-2.0 * jnp.arange(half, dtype=f32) / HEAD_DIM)
    angles = offsets.astype(f32).reshape(rows)[:, None] * frequency
    cosine, sine = jnp.cos(angles), jnp.sin(angles)

    def low_in(v, first, count):
        return merge(
            jnp.einsum(
                "sbd,dscr->sbcr", split(v), wide[:, :, first : first + count],
                preferred_element_type=f32,
            )
        )

    def low_out(z, factor):
        return merge(
            jnp.einsum("sbcr,scrh->sbch", split(z).astype(bf16), factor, preferred_element_type=f32)
        )

    def low_sum(z, factor):
        return merge(
            jnp.einsum("sbcr,scrh->sbh", split(z).astype(bf16), factor, preferred_element_type=f32)
        )

    def low_back(dp, factor):
        return merge(
            jnp.einsum("sbch,scrh->sbcr", split(dp), factor, preferred_element_type=f32)
        )

    def low_grad(z, dp):
        return jnp.einsum(
            "sbcr,sbch->scrh", split(z).astype(bf16), split(dp), preferred_element_type=f32
        )

    b_q, b_kv, a_o = heads_low[:, :experts], heads_low[:, experts : experts + 2], heads_low[:, experts + 2 :]
    key_pos = (ctx_rank - PAST) * block + jnp.arange((PAST + 1) * block, dtype=jnp.int32)
    key_doc = doc_layout(doc_lengths, jnp.maximum(key_pos, 0))[0]
    key_doc = jnp.where(key_pos[None, :] >= 0, key_doc, -(1 << 20))
    blank = jnp.zeros((seqs, rank, width), bf16)
    b_kv_wide = jnp.concatenate(
        [
            jnp.concatenate([b_kv[:, 0], blank], axis=-1).reshape(seqs * rank, 2 * width),
            jnp.concatenate([blank, b_kv[:, 1]], axis=-1).reshape(seqs * rank, 2 * width),
        ],
        axis=0,
    )
    a_o_wide = jnp.pad(a_o.reshape(seqs, experts * rank, width), ((0, 0), (0, 64), (0, 0)))
    router_wide = jnp.pad(router_attn, ((0, 0), (0, 128 - experts)))
    (
        w_query, w_key_value, w_out, w_gate_up, w_down, wide, _, dy,
        x0, sum_out, n1, kv_all, q_all, probs, ob, z_o_gated, z_q, z_kv, gates,
    ) = attention(
        [
            w_query,
            w_key_value.reshape(-1, 2 * width),
            w_out,
            gate_up_columns(w_gate_up[:, :, 0], w_gate_up[:, :, 1]),
            w_down,
        ],
        [tokens.reshape(rows, part), cotangent.reshape(rows, part), wide_cols],
        [
            norm1_gain[None],
            router_wide,
            widen_routes(route_a[:, :1], experts),
            widen_routes(route_a[:, 1:], experts),
            jnp.concatenate([cosine, cosine], axis=1),
            jnp.concatenate([-sine, sine], axis=1),
            jnp.broadcast_to(doc_ids.reshape(rows, 1), (rows, 128)),
            jnp.broadcast_to(key_doc[:, None, :], (seqs, 8, key_doc.shape[1])),
            b_q.reshape(seqs * experts * rank, width),
            b_kv_wide,
            a_o_wide,
        ],
    )
    wide_low = wide
    place = {qs: rank * i for i, qs in enumerate(order)}
    wide = jnp.stack([jnp.stack([wide[:, place[q, s] : place[q, s] + rank] for s in range(wide_slots)], axis=1) for q in range(seqs)], axis=1)
    ga_e = gates[:, :experts]
    ga = jnp.sum(ga_e[:, None, :] * hot_a, axis=-1)
    scale = HEAD_DIM ** (-0.5)
    length = (PAST + 1) * block
    kv_all = jnp.swapaxes(kv_all, 0, 1).reshape(seqs, length, 2, heads, HEAD_DIM)
    probs = jnp.swapaxes(probs.reshape(seqs, heads, 2, block, length), 1, 2).astype(f32)
    q_s = jnp.transpose(q_all.reshape(seqs, heads, 2, block, HEAD_DIM), (0, 3, 2, 1, 4))
    ob = jnp.swapaxes(ob, 0, 1)
    o = ob.reshape(seqs, block, 2, heads, HEAD_DIM).astype(f32)
    ob_e = jnp.einsum("rke,rkh->reh", hot_a.astype(bf16), ob, preferred_element_type=f32).astype(bf16)
    xf = x0.astype(f32)
    z_q = jnp.where(jnp.arange(rows)[:, None] < block, z_q[:, :64], z_q[:, 64:]).reshape(rows, experts, rank).astype(f32)
    z_kv = z_kv[:, :64].reshape(rows, 2, 2, rank)
    z_kv = jnp.where(jnp.arange(rows)[:, None, None] < block, z_kv[:, :, 0], z_kv[:, :, 1]).astype(f32)
    blank = jnp.zeros((seqs, experts, rank, hidden), bf16)
    b_gu = jnp.stack(
        [gate_up_columns(ffn_low[:, :experts], blank), gate_up_columns(blank, ffn_low[:, experts : 2 * experts])],
        axis=2,
    ).reshape(seqs, 2 * experts * rank, 2 * hidden)
    a_d = jnp.pad(ffn_low[:, 2 * experts :].reshape(seqs, experts * rank, hidden), ((0, 0), (64, 0), (0, 0)))
    mixed, dx1b, dx1_own, n2, z_sum, g_gu, g_d = feed_forward(
        x0, sum_out, dy, norm2_gain[None], wide_low,
        jnp.pad(router_ffn, ((0, 0), (0, 128 - experts))),
        widen_routes(route_f, experts), b_gu, a_d, z_o_gated, w_gate_up, w_down,
    )
    g_gu = g_gu.reshape(seqs, experts, 2, rank, 2 * hidden)
    grad_ffn = jnp.concatenate(
        [
            jnp.concatenate([g_gu[:, :, 0, :, :640], g_gu[:, :, 0, :, 1280:1344]], axis=-1),
            jnp.concatenate([g_gu[:, :, 1, :, 640:1280], g_gu[:, :, 1, :, 1344:]], axis=-1),
            g_d[:, 64:].reshape(seqs, experts, rank, hidden),
        ],
        axis=1,
    )
    dz_o = low_in(dx1b, 14, experts)
    g_e = jnp.stack([dot(dx1b, w_out[e], 1, 1) for e in range(experts)], axis=1) + low_out(dz_o, a_o)
    g_k = jnp.einsum("rke,reh->rkh", hot_a, g_e, precision=lax.Precision.HIGHEST)
    dga = jnp.sum(g_k * ob.astype(f32), axis=-1)
    dob = (g_k * ga[..., None]).astype(bf16)
    dob_s = dob.reshape(seqs, block, -1, heads, HEAD_DIM)
    delta = jnp.sum(dob_s.astype(f32) * o, axis=-1)
    delta = jnp.transpose(delta, (0, 2, 3, 1))[..., None]
    d_p = jnp.einsum("sqthd,skhd->sthqk", dob_s, kv_all[:, :, 1], preferred_element_type=f32)
    d_s = (probs * (d_p - delta)).astype(bf16)
    dqr = jnp.einsum("sthqk,skhd->sqthd", d_s, kv_all[:, :, 0], preferred_element_type=f32) * scale
    dkr = jnp.einsum("sthqk,sqthd->skhd", d_s, q_s, preferred_element_type=f32) * scale
    dvv = jnp.einsum("sthqk,sqthd->skhd", probs.astype(bf16), dob_s, preferred_element_type=f32)
    dkv = jnp.concatenate([dkr, dvv], axis=2).reshape(seqs, length, 2 * width).astype(bf16)
    dkv = halo_back(dkv)
    dkv = dkv.reshape(rows, 2, heads, HEAD_DIM)
    dkp = rope(dkv[:, 0], cosine[:, None], sine[:, None], -1.0).astype(bf16).reshape(rows, width)
    dvp = dkv[:, 1].astype(bf16).reshape(rows, width)
    dqp = rope(
        dqr.reshape(rows, -1, heads, HEAD_DIM), cosine[:, None, None], sine[:, None, None], -1.0
    ).astype(bf16).reshape(rows, -1, width)
    dq_e = jnp.einsum("rke,rkh->reh", hot_a.astype(bf16), dqp, preferred_element_type=f32).astype(bf16)
    dkv_p = jnp.stack([dkp, dvp], axis=1)
    dz_q = low_back(dq_e, b_q)
    dz_kv = low_back(dkv_p, b_kv)
    a_qkv = jnp.transpose(wide[:, :, :6], (1, 2, 3, 0))
    dz_qkv = jnp.concatenate([dz_q, dz_kv], axis=1)
    dla = gates_back(ga, dga, hot_a)
    dn1 = sum(dot(dq_e[:, e], w_query[e], 1, 1) for e in range(experts))
    dn1 = dn1 + dot(dkv_p.reshape(rows, 2 * width), w_key_value.reshape(model, 2 * width), 1, 1)
    dn1 = dn1 + low_sum(dz_qkv, a_qkv) + dot(dla.astype(bf16), router_attn, 1, 1)
    back1 = norm_back(xf, norm1_gain, dn1)
    dz_part = jnp.pad(dz_qkv.reshape(rows, -1).astype(bf16), ((0, 0), (0, 32)))
    back_own, dz_sum = exchange([back1.astype(bf16), dz_part], ["rs_cols", "ar_rows"], 3)
    dz_sum = dz_sum[:, :96].reshape(rows, 6, rank)
    grad_tokens = (back_own + dx1_own).astype(bf16)
    grad_heads = jnp.concatenate(
        [low_grad(z_q, dq_e), low_grad(z_kv, dkv_p), low_grad(dz_o * ga_e[..., None], ob_e)], axis=1
    )
    def strided(a):
        return lax.dynamic_slice_in_dim(
            a.reshape(rows, n_ctx, n_tp, model // (n_ctx * n_tp)), tp_rank, 1, 2
        ).reshape(seqs, block, -1)

    def wide_grad(z, v):
        return jnp.einsum("sbcr,sbm->mscr", split(z).astype(bf16), strided(v), preferred_element_type=f32)

    wide_terms = jnp.concatenate(
        [
            wide_grad(dz_sum, n1),
            wide_grad(z_sum[:, :128].reshape(rows, experts, 2, rank).swapaxes(1, 2).reshape(rows, 2 * experts, rank), n2),
            wide_grad(z_sum[:, 128:192].reshape(rows, experts, rank), dx1b),
            wide_grad(z_sum[:, 192:].reshape(rows, experts, rank), dy),
        ],
        axis=2,
    ).reshape(-1, seqs * wide_slots * rank)
    head_rows = seqs * grad_heads.shape[1] * rank // N_CTX
    head_terms = jnp.pad(
        grad_heads.reshape(N_CTX, head_rows, width).astype(bf16), ((0, 0), (0, 32 - head_rows), (0, 0))
    )
    grad_wide, head_sum = reduce_ctx(
        [wide_terms.reshape(N_CTX, -1, seqs * wide_slots * rank).astype(bf16), head_terms],
        [False, True],
    )
    grad_wide = grad_wide.T.reshape(seqs, wide_slots, rank, -1)[adapter_index]
    grad_heads = head_sum[:, :head_rows].astype(f32).reshape(grad_heads.shape)[adapter_index]
    grad_ffn = lax.psum(grad_ffn.astype(bf16), "ctx").astype(f32)[adapter_index]
    mixed = mixed.reshape(seqs, block, part)
    grad_tokens = grad_tokens.reshape(seqs, block, part)
    return (mixed, grad_tokens, grad_wide, grad_heads, grad_ffn)


def solution(mesh):
    placed = (
        P(None, "ctx", "tp"),
        P(),
        P(),
        P(None, "ctx", "tp"),
        P("ctx", None, "tp"),
        P(None, "tp", "ctx"),
        P(),
        P(),
        P(None, "ctx", None, "tp"),
        P(None, "tp", "ctx"),
        P(None, None, None, ("ctx", "tp")),
        P(None, None, None, "tp"),
        P(None, None, None, "tp"),
        P(None, "ctx", None),
        P(None, "ctx", None),
        P(),
        P(),
        P(None, "ctx", "tp"),
    )
    return jax.shard_map(
        shards,
        mesh=mesh,
        in_specs=placed,
        out_specs=(
            P(None, "ctx", "tp"),
            P(None, "ctx", "tp"),
            P(None, None, None, ("ctx", "tp")),
            P(None, None, None, "tp"),
            P(None, None, None, "tp"),
        ),
        check_vma=False,
    )
```

```python
import functools

import jax
import numpy as np
import jax.numpy as jnp
from jax import lax
from jax.experimental import pallas as pl
from jax.experimental.pallas import tpu as pltpu
from jax.sharding import PartitionSpec as P

HEAD_DIM = 128
WINDOW = 1024
eps = 1e-06
big_negative = -1e30
bf16 = jnp.bfloat16
f32 = jnp.float32

MESH = pl.DeviceIdType.MESH
ANY = pl.BlockSpec(memory_space=pl.ANY)
VMEM = pl.BlockSpec(memory_space=pltpu.VMEM)
N_CTX, N_TP = 16, 8
PAST = 8


def region(kind, ref, owner, low, high):
    if kind == "rows":
        return ref.at[pl.ds(low, high - low), pl.ds(pl.multiple_of(owner * 128, 128), 128), :]
    if kind == "flat":
        return ref.at[pl.ds(pl.multiple_of(owner * 128 + 32 * low, 32), 32 * (high - low)), :]
    return ref.at[pl.ds(low, high - low), :, pl.ds(pl.multiple_of(owner * 128, 128), 128)]


def own_part(kind, ref, low, high):
    if kind == "flat":
        return ref.at[pl.ds(32 * low, 32 * (high - low)), :]
    return ref.at[pl.ds(low, high - low)]


def tp_part(kind, ref, rank, size):
    if kind == "cols":
        return ref.at[:, pl.ds(pl.multiple_of(rank * size, size), size)]
    return ref.at[pl.ds(pl.multiple_of(rank * size, size), size), :]


def rms_scale(values, gain):
    return values * lax.rsqrt(jnp.mean(values * values, axis=-1, keepdims=True) + eps) * gain


def doc_layout(doc_lengths, positions):
    ends = jnp.cumsum(doc_lengths, axis=1)
    passed = positions[None, :, None] >= ends[:, None, :]
    doc_ids = jnp.sum(passed.astype(jnp.int32), axis=2)
    starting = jnp.sum(jnp.where(passed, doc_lengths[:, None, :], 0), axis=2)
    inside = positions[None, :] < ends[:, -1:]
    doc_ids = jnp.where(inside, doc_ids, -1 - positions[None, :])
    return (doc_ids, positions[None, :] - starting)


def dot(a, b, ca=1, cb=0):
    return lax.dot_general(a, b, (((ca,), (cb,)), ((), ())), preferred_element_type=f32)


def dot_nt(a, b):
    return dot(a, b, 1, 1)


def dot_tn(a, b):
    return dot(a, b, 0, 0)


def by_seq(rows, f):
    half = rows.shape[0] // 2
    return jnp.concatenate([f(0, rows[:half]), f(1, rows[half:])], axis=0)


def column_of(values, lane, e):
    return jnp.sum(jnp.where(lane == e, values, 0.0), axis=1, keepdims=True)


def greet(targets):
    barrier = pltpu.get_barrier_semaphore()
    for device in targets:
        pl.semaphore_signal(barrier, inc=1, device_id=device, device_id_type=MESH)
    pl.semaphore_wait(barrier, len(targets))


def masked_gates(logits, hot):
    largest = jnp.max(jnp.where(hot > 0, logits, big_negative), axis=1, keepdims=True)
    powers = jnp.where(hot > 0, jnp.exp(logits - largest), 0.0)
    return powers / jnp.sum(powers, axis=1, keepdims=True)


def ffn_kernel(
    x0, attn, dy, gain, wide, router, hot, b_gu, a_d, z_o, w_gu_hbm, w_d_hbm,
    mixed, dx1, dx1_own, n2, z_sum, g_gu, g_d,
    w_gu, w_d, hg, dgu, dh_tmp, z_gu, dz_d, z_part, parts, own, held, z_held, dots, tails,
    load, send, recv,
):
    me, tp = lax.axis_index("ctx"), lax.axis_index("tp")
    rows, model = x0.shape
    experts = w_gu.shape[0]
    part = model // N_TP
    greet([(me, tp ^ d) for d in range(1, N_TP)])

    def fetch(e):
        return (
            pltpu.make_async_copy(w_gu_hbm.at[e], w_gu.at[e], load.at[0, e]),
            pltpu.make_async_copy(w_d_hbm.at[e], w_d.at[e], load.at[1, e]),
        )

    for e in range(experts):
        for c in fetch(e):
            c.start()

    step = 32

    def normalize(i, carry):
        at = pl.ds(pl.multiple_of(i * step, step), step)
        x = x0[at, :].astype(f32) + attn[at, :].astype(f32)
        n2[at, :] = rms_scale(x, gain[...]).astype(bf16)
        return carry

    lax.fori_loop(0, rows // step, normalize, 0)
    lane = lax.broadcasted_iota(jnp.int32, (rows, 128), 1)
    gates = masked_gates(dot(n2[...], router[...]), hot[...])
    z_gu[...] = by_seq(n2[...], lambda s, v: dot(v, wide[:, 128 * s : 128 * s + 128])).astype(bf16)
    dz_d[...] = by_seq(dy[...], lambda s, v: dot(v, wide[:, 256 + 128 * s : 384 + 128 * s])).astype(bf16)
    g_gu[...] = jnp.zeros_like(g_gu)
    g_d[...] = jnp.zeros_like(g_d)
    zero = jnp.zeros((rows, 128), f32)

    def expert(e, carry):
        d_gates, dz_gu, z_d = carry
        for c in fetch(e):
            c.wait()
        gate = column_of(gates, lane, e)
        z_in = jnp.where(lane // 32 == e, z_gu[...].astype(f32), 0.0).astype(bf16)
        dz_in = jnp.where(lane // 16 == 4 + e, dz_d[...].astype(f32), 0.0).astype(bf16)
        dh_tmp[:, :704] = dot_nt(dy[...], w_d[e]) + by_seq(dz_in, lambda s, v: dot(v, a_d[s]))
        pre = dot(n2[...], w_gu[e]) + by_seq(z_in, lambda s, v: dot(v, b_gu[s]))

        def tile(g, u, d):
            sg = jax.nn.sigmoid(g)
            silu = g * sg
            h = silu * u
            dg = d * gate
            return h, (dg * u * sg * (1.0 + g * (1.0 - sg))), dg * silu, h * d

        h, dgp, dup, hd = tile(pre[:, :640], pre[:, 640:1280], dh_tmp[:, :640])
        hg[e, :, :640] = (h * gate).astype(bf16)
        dgu[e, :, :640] = dgp.astype(bf16)
        dgu[e, :, 640:1280] = dup.astype(bf16)
        dgf = jnp.sum(hd, axis=1, keepdims=True)
        last = pre[:, 1280:]
        h, dgp, dup, hd = tile(last, pltpu.roll(last, 64, 1), dh_tmp[:, 640:])
        hg[e, :, 640:] = (h * gate).astype(bf16)[:, :64]
        dgu[e, :, 1280:] = jnp.where(lane < 64, dgp, pltpu.roll(dup, 64, 1)).astype(bf16)
        dgf = dgf + jnp.sum(jnp.where(lane < 64, hd, 0.0), axis=1, keepdims=True)
        d_gates = d_gates + jnp.where(lane == e, dgf, 0.0)
        back = by_seq(dgu[e], lambda s, v: dot_nt(v, b_gu[s]))
        dz_gu = dz_gu + jnp.where(lane // 32 == e, back, 0.0)
        low = by_seq(hg[e], lambda s, v: dot_nt(v, a_d[s]))
        z_d = z_d + jnp.where(lane // 16 == 4 + e, low, 0.0)
        half = rows // 2
        for s in range(2):
            at = slice(s * half, s * half + half)
            g_gu[s] += dot_tn(z_in[at], dgu[e, at, :])
            g_d[s] += dot_tn(dz_in[at], hg[e, at, :])
        return d_gates, dz_gu, z_d

    d_gates, dz_gu, z_d = lax.fori_loop(0, experts, expert, (zero, zero, zero))
    d_logits = gates * (d_gates - jnp.sum(gates * d_gates, axis=1, keepdims=True))
    d_logits = d_logits.astype(bf16)
    dz_gu, z_d = dz_gu.astype(bf16), z_d.astype(bf16)
    z_part[:, :128] = dz_gu
    z_part[:, 128:] = z_o[...] + z_d

    def scatter(i, d):
        return pltpu.make_async_remote_copy(
            src_ref=parts.at[i, d],
            dst_ref=held.at[i, d],
            send_sem=send.at[i, d],
            recv_sem=recv.at[i, d],
            device_id=(me, tp ^ d),
            device_id_type=MESH,
        )

    def piece(j, carry):
        d = lax.rem(j, N_TP)
        peer = tp ^ d
        at = pl.ds(pl.multiple_of(peer * part, part), part)
        w_rows = wide[at, :]
        dn = dot_nt(d_logits, router[at, :])
        dn = dn + by_seq(dz_gu, lambda s, v: dot_nt(v, w_rows[:, 128 * s : 128 * s + 128]))
        ff = by_seq(z_d, lambda s, v: dot_nt(v, w_rows[:, 256 + 128 * s : 384 + 128 * s]))
        for e in range(experts):
            dn = dn + dot_nt(dgu[e], w_gu[e, at, :])
            ff = ff + dot(hg[e], w_d[e, :, at])

        @pl.when(j < N_TP)
        def _():
            parts[0, d] = dn.astype(bf16)
            parts[1, d] = ff.astype(bf16)
            scatter(0, d).start()
            scatter(1, d).start()

        @pl.when(j == N_TP)
        def _():
            own[0] = dn
            own[1] = ff

        return carry

    z_rows = rows // N_TP

    def z_region(ref, rank):
        return ref.at[pl.ds(pl.multiple_of(rank * z_rows, z_rows), z_rows), :]

    def z_scatter(d):
        return pltpu.make_async_remote_copy(
            src_ref=z_region(z_part, tp ^ d),
            dst_ref=z_held.at[d],
            send_sem=send.at[2, d],
            recv_sem=recv.at[2, d],
            device_id=(me, tp ^ d),
            device_id_type=MESH,
        )

    def z_spread(d, rank):
        return pltpu.make_async_remote_copy(
            src_ref=z_region(z_sum, rank),
            dst_ref=z_region(z_sum, rank),
            send_sem=send.at[3, d],
            recv_sem=recv.at[3, d],
            device_id=(me, tp ^ d),
            device_id_type=MESH,
        )

    def columns(ref, rank):
        return ref.at[:, pl.ds(pl.multiple_of(rank * part, part), part)]

    def spread(d, rank):
        return pltpu.make_async_remote_copy(
            src_ref=columns(dx1, rank),
            dst_ref=columns(dx1, rank),
            send_sem=send.at[4, d],
            recv_sem=recv.at[4, d],
            device_id=(me, tp ^ d),
            device_id_type=MESH,
        )

    def tail(d, rank):
        return pltpu.make_async_remote_copy(
            src_ref=tails.at[rank],
            dst_ref=tails.at[rank],
            send_sem=send.at[5, d],
            recv_sem=recv.at[5, d],
            device_id=(me, tp ^ d),
            device_id_type=MESH,
        )

    def x_own():
        return x0[:, at].astype(f32) + attn[:, at].astype(f32)

    lax.fori_loop(1, N_TP + 1, piece, 0)
    for d in range(1, N_TP):
        z_scatter(d).start()
    total = own[0]
    for d in range(1, N_TP):
        scatter(0, d).wait_recv()
        total = total + held[0, d].astype(f32)
    at = pl.ds(pl.multiple_of(tp * part, part), part)
    total = total * gain[:, at]
    own[0] = total
    columns(dx1, tp)[...] = total.astype(bf16)
    for d in range(1, N_TP):
        spread(d, tp).start()
    dots[...] = jnp.broadcast_to(jnp.sum(total * x_own(), axis=1, keepdims=True), dots.shape)
    tails[tp] = jnp.transpose(dots[...])[:8, :]
    for d in range(1, N_TP):
        tail(d, tp).start()
    total = own[1] + x_own()
    for d in range(1, N_TP):
        scatter(1, d).wait_recv()
        total = total + held[1, d].astype(f32)
    mixed[...] = total.astype(bf16)
    total = z_region(z_part, tp)[...].astype(f32)
    for d in range(1, N_TP):
        z_scatter(d).wait_recv()
        total = total + z_held[d].astype(f32)
    z_region(z_sum, tp)[...] = total.astype(bf16)
    for d in range(1, N_TP):
        z_spread(d, tp).start()
    for d in range(1, N_TP):
        tail(d, tp ^ d).wait_recv()
    whole = tails[0]
    for d in range(1, N_TP):
        whole = whole + tails[d]
    dots[...] = jnp.transpose(jnp.broadcast_to(whole[:1], (128, rows)))
    for d in range(1, N_TP):
        spread(d, tp ^ d).wait_recv()
        spread(d, tp).wait_send()

    def back(i, carry):
        rows_at = pl.ds(pl.multiple_of(i * step, step), step)
        x = x0[rows_at, :].astype(f32) + attn[rows_at, :].astype(f32)
        inverse = lax.rsqrt(jnp.mean(x * x, axis=1, keepdims=True) + eps)
        mean = dots[rows_at, :1] * (1.0 / model)
        got = dy[rows_at, :].astype(f32) + inverse * dx1[rows_at, :].astype(f32) - x * inverse**3 * mean
        dx1[rows_at, :] = got.astype(bf16)
        dx1_own[rows_at, :] = (
            dy[rows_at, at].astype(f32) + inverse * own[0, rows_at, :]
            - (x0[rows_at, at].astype(f32) + attn[rows_at, at].astype(f32)) * inverse**3 * mean
        )
        return carry

    lax.fori_loop(0, rows // step, back, 0)
    for d in range(1, N_TP):
        scatter(0, d).wait_send()
        scatter(1, d).wait_send()
        z_scatter(d).wait_send()
        z_spread(d, tp ^ d).wait_recv()
        z_spread(d, tp).wait_send()
        tail(d, tp).wait_send()


def feed_forward(x0, attn, dy, gain, wide, router, hot, b_gu, a_d, z_o, w_gu, w_d):
    rows, model = x0.shape
    part = model // N_TP
    experts, _, cols = w_gu.shape
    hidden = w_d.shape[1]
    shape = jax.ShapeDtypeStruct
    return pl.pallas_call(
        ffn_kernel,
        out_shape=(
            shape((rows, part), bf16),
            shape((rows, model), bf16),
            shape((rows, part), f32),
            shape((rows, model), bf16),
            shape((rows, 256), bf16),
            shape(b_gu.shape, f32),
            shape(a_d.shape, f32),
        ),
        in_specs=[VMEM] * 10 + [ANY] * 2,
        out_specs=tuple([VMEM] * 7),
        scratch_shapes=[
            pltpu.VMEM(w_gu.shape, bf16),
            pltpu.VMEM(w_d.shape, bf16),
            pltpu.VMEM((experts, rows, hidden), bf16),
            pltpu.VMEM((experts, rows, cols), bf16),
            pltpu.VMEM((rows, 768), f32),
            pltpu.VMEM((rows, 128), bf16),
            pltpu.VMEM((rows, 128), bf16),
            pltpu.VMEM((rows, 256), bf16),
            pltpu.VMEM((2, N_TP, rows, part), bf16),
            pltpu.VMEM((2, rows, part), f32),
            pltpu.VMEM((2, N_TP, rows, part), bf16),
            pltpu.VMEM((N_TP, rows // N_TP, 256), bf16),
            pltpu.VMEM((rows, 128), f32),
            pltpu.VMEM((N_TP, 8, rows), f32),
            pltpu.SemaphoreType.DMA((2, experts)),
            pltpu.SemaphoreType.DMA((6, N_TP)),
            pltpu.SemaphoreType.DMA((6, N_TP)),
        ],
        compiler_params=pltpu.CompilerParams(
            collective_id=2, has_side_effects=True, vmem_limit_bytes=62 << 20
        ),
        name="feed_forward",
    )(x0, attn, dy, gain, wide, router, hot, b_gu, a_d, z_o, w_gu, w_d)


def widen_routes(routes, experts):
    lane = jnp.arange(128, dtype=jnp.int32)
    return jnp.sum((routes[..., None] == lane).astype(f32), axis=1)


def gate_up_columns(gate, up):
    return jnp.concatenate([gate[..., :640], up[..., :640], gate[..., 640:], up[..., 640:]], axis=-1)


def attention_kernel(
    s_q, s_kv, s_o, s_gu, s_d, tokens, cotangent, s_wide,
    gain, router, hot0, hot1, cosine, sine, q_doc, k_doc, b_q, b_kv, a_o,
    g_q, g_kv, g_o, g_gu, g_d, g_wide, wide_mid, dy,
    x0, attn, n1, kv_all, q_all, probs, ob, z_o, z_q, z_kv, gates,
    w_q, w_kv, w_o, wide, parts, own, held,
    send, recv, local, tp_send, tp_recv, tp_local, kv_send, kv_recv, load, sum_send, sum_recv,
):
    me, tp = lax.axis_index("ctx"), lax.axis_index("tp")
    core, side = me ^ 1, me ^ 2
    up, down, far = lax.rem(me + 4, 16), lax.rem(me + 12, 16), lax.rem(me + 8, 16)
    on_core, on_side = lax.rem(me, 2), lax.rem(me // 2, 2)
    rows, model = x0.shape
    part = model // N_TP
    half = rows // 2
    experts = w_q.shape[0]
    width = w_q.shape[2]
    heads = width // HEAD_DIM
    span = (PAST + 1) * half
    greet([(d, tp) for d in (core, side, up, down, far)] + [(me, tp ^ d) for d in range(1, N_TP)])

    kinds = ["flat", "flat", "rows", "cols", "rows", "cols"]
    src = [s_kv, wide_mid, s_q, s_o, s_gu, s_d]
    dst = [g_kv, g_wide, g_q, g_o, g_gu, g_d]
    tp_src, tp_dst, tp_kinds = [tokens, s_wide, cotangent], [x0, wide_mid, dy], ["cols", "rows", "cols"]
    started, staying = [], []
    counter = [0] * len(kinds)

    def tp_copy(i, d, rank):
        size = tp_src[i].shape[1 if tp_kinds[i] == "cols" else 0]
        return pltpu.make_async_remote_copy(
            src_ref=tp_src[i],
            dst_ref=tp_part(tp_kinds[i], tp_dst[i], rank, size),
            send_sem=tp_send.at[i, d],
            recv_sem=tp_recv.at[i, d],
            device_id=(me, tp ^ d),
            device_id_type=MESH,
        )

    def tp_own(i):
        size = tp_src[i].shape[1 if tp_kinds[i] == "cols" else 0]
        return pltpu.make_async_copy(
            tp_src[i], tp_part(tp_kinds[i], tp_dst[i], tp, size), tp_local.at[i]
        )

    def tp_wait(i):
        for d in range(1, N_TP):
            tp_copy(i, d, tp ^ d).wait_recv()
        tp_own(i).wait()

    def copy(t, item, owner, low, high, to, slot, own_shard):
        there = region(kinds[t], dst[t], owner, low, high)
        return pltpu.make_async_remote_copy(
            src_ref=own_part(kinds[t], src[t], low, high) if own_shard else there,
            dst_ref=there,
            send_sem=send.at[t, slot],
            recv_sem=recv.at[t, item],
            device_id=(to, tp),
            device_id_type=MESH,
        )

    def go(t, item, owner, low, high, to, own_shard=False):
        c = copy(t, item, owner, low, high, to, counter[t], own_shard)
        counter[t] += 1
        c.start()
        started.append(c)

    arrive = {
        0: (side, 0, 4),
        1: (down, 0, 4),
        2: (up, 0, 4),
        3: (down ^ 2, 0, 2),
        4: (up ^ 2, 0, 2),
        5: (far, 1, 3),
        6: (far, 0, 1),
        7: (far, 3, 4),
        8: (far ^ 2, 1, 2),
        9: (far ^ 2, 0, 1),
        10: (down ^ 2, 2, 4),
        11: (up ^ 2, 2, 4),
        12: (far ^ 2, 2, 4),
    }

    def got(t, item):
        owner, low, high = arrive[item]
        copy(t, item, owner, low, high, core, 0, False).wait_recv()
        go(t, 13 + item, owner, low, high, core)

    def first(t):
        go(t, 0, me, 0, 4, side, True)
        go(t, 2, me, 0, 4, down, True)
        go(t, 1, me, 0, 4, up, True)
        go(t, 26, me, 0, 4, core, True)
        c = pltpu.make_async_copy(src[t], region(kinds[t], dst[t], me, 0, 4), local.at[t])
        c.start()
        staying.append(c)

    def second(t):
        got(t, 0)
        go(t, 3, side, 0, 2, up)
        go(t, 4, side, 0, 2, down)
        got(t, 1)
        go(t, 5, down, 1, 3, up)
        go(t, 10, down, 2, 4, side)
        got(t, 2)
        go(t, 6, up, 0, 1, down)
        go(t, 7, up, 3, 4, down)
        go(t, 11, up, 2, 4, side)

    def third(t):
        got(t, 3)
        go(t, 8, down ^ 2, 1, 2, up)
        got(t, 4)
        go(t, 9, up ^ 2, 0, 1, down)
        got(t, 5)
        got(t, 6)
        got(t, 7)
        go(t, 12, far, 2, 4, side)

    def fourth(t):
        for item in range(8, 13):
            got(t, item)

    def finish(t):
        for item in range(13):
            owner, low, high = arrive[item]
            copy(t, 13 + item, owner ^ 1, low, high, core, 0, False).wait_recv()
        copy(t, 26, core, 0, 4, core, 0, False).wait_recv()

    for i in range(3):
        for d in range(1, N_TP):
            c = tp_copy(i, d, tp)
            c.start()
            started.append(c)
        tp_own(i).start()
    for t in (0, 2, 3):
        first(t)
    tp_wait(1)
    first(1)
    tp_wait(0)
    step = 32

    def normalize(i, carry):
        at = pl.ds(pl.multiple_of(i * step, step), step)
        n1[at, :] = rms_scale(x0[at, :].astype(f32), gain[...]).astype(bf16)
        return carry

    lax.fori_loop(0, rows // step, normalize, 0)
    gates[...] = masked_gates(dot(n1[...], router[...]), hot0[...] + hot1[...])
    for t in (0, 2, 1, 3):
        second(t)
    for t in (0, 2, 1, 3):
        third(t)
    first(4)
    first(5)
    for t in (0, 2, 1, 3):
        fourth(t)

    for c in staying[:4]:
        c.wait()
    fetches = []
    for i, (t, ref) in enumerate([(0, w_kv), (1, wide), (2, w_q), (3, w_o)]):
        finish(t)
        c = pltpu.make_async_copy(dst[t], ref, load.at[i])
        c.start()
        fetches.append(c)

    lane = lax.broadcasted_iota(jnp.int32, (rows, 128), 1)
    seq = lax.broadcasted_iota(jnp.int32, (rows, 128), 0) // half

    def rotary(x):
        return x * cosine[...] + pltpu.roll(x, HEAD_DIM // 2, 1) * sine[...]

    fetches[0].wait()
    fetches[1].wait()
    z = dot(n1[...], wide[:, 512:640])
    z_q[...] = jnp.where(lane // 64 == seq, z, 0.0).astype(bf16)
    z = dot(n1[...], wide[:, 640:704])
    z_kv[...] = jnp.where((lane // 16) % 2 == seq, jnp.pad(z, ((0, 0), (0, 64))), 0.0).astype(bf16)
    kv = dot(n1[...], w_kv[...]) + dot(z_kv[:, :64], b_kv[...])
    for h in range(heads):
        at = slice(HEAD_DIM * h, HEAD_DIM * h + HEAD_DIM)
        turned = rotary(kv[:, at]).astype(bf16)
        kv_all[PAST, 0, :, at] = turned[:half]
        kv_all[PAST, 1, :, at] = turned[half:]
    for s in range(2):
        kv_all[PAST, s, :, width:] = kv[half * s : half * s + half, width:].astype(bf16)

    def kv_copy(slot, back, to, to_back):
        return pltpu.make_async_remote_copy(
            src_ref=kv_all.at[PAST - back],
            dst_ref=kv_all.at[PAST - to_back],
            send_sem=kv_send.at[slot],
            recv_sem=kv_recv.at[to_back],
            device_id=(to, tp),
            device_id_type=MESH,
        )

    def kv_arrived(back):
        kv_copy(0, back, core, back).wait_recv()

    def when(condition, c):
        if condition is None:
            c.start()
        else:
            pl.when(condition)(c.start)
        kv_started.append((condition, c))

    kv_started = []
    when(None, kv_copy(0, 0, up, 4))
    when(None, kv_copy(1, 0, far, 8))
    when(on_side == 0, kv_copy(2, 0, side, 2))
    when(on_core == 0, kv_copy(3, 0, core, 1))

    fetches[2].wait()
    queries = [jnp.zeros((rows, width), f32), jnp.zeros((rows, width), f32)]
    for e in range(experts):
        z_e = jnp.where((lane % 64) // 16 == e, z_q[...].astype(f32), 0.0).astype(bf16)
        q_e = dot(n1[...], w_q[e]) + dot(z_e, b_q[...])
        for k, hot in enumerate((hot0, hot1)):
            queries[k] = queries[k] + jnp.where(hot[:, e : e + 1] > 0, q_e, 0.0)
    for k in range(2):
        for h in range(heads):
            turned = rotary(queries[k][:, HEAD_DIM * h : HEAD_DIM * h + HEAD_DIM]).astype(bf16)
            for s in range(2):
                q_all[s * heads + h, k * half : k * half + half, :] = turned[half * s : half * s + half]

    kv_arrived(4)
    when(on_side == 0, kv_copy(4, 4, side, 6))
    when(on_side == 1, kv_copy(5, 4, side, 2))
    when(on_core == 0, kv_copy(6, 4, core, 5))
    when(on_core == 1, kv_copy(7, 4, core, 3))
    kv_arrived(8)
    when(on_side == 1, kv_copy(8, 8, side, 6))
    when(on_core == 1, kv_copy(9, 8, core, 7))
    kv_arrived(2)
    when(on_core == 0, kv_copy(10, 2, core, 3))
    when(on_core == 1, kv_copy(11, 2, core, 1))
    kv_arrived(6)
    when(on_core == 0, kv_copy(12, 6, core, 7))
    when(on_core == 1, kv_copy(13, 6, core, 5))
    for back in (1, 3, 5, 7):
        kv_arrived(back)

    row = lax.broadcasted_iota(jnp.int32, (half, span), 0)
    key = lax.broadcasted_iota(jnp.int32, (half, span), 1)
    near = (key > row) & (key <= row + PAST * half)

    def attend(i, carry):
        s = i // heads
        h = lax.rem(i, heads)
        at = pl.ds(pl.multiple_of(h * HEAD_DIM, HEAD_DIM), HEAD_DIM)
        v_at = pl.ds(pl.multiple_of(width + h * HEAD_DIM, HEAD_DIM), HEAD_DIM)
        keys = kv_all[:, s, :, at].reshape(span, HEAD_DIM)
        values = kv_all[:, s, :, v_at].reshape(span, HEAD_DIM)
        seq_rows = pl.ds(pl.multiple_of(s * half, half), half)
        allowed = near & (q_doc[seq_rows, :1] == k_doc[s, :1, :])
        for k in range(2):
            q = q_all[i, k * half : k * half + half, :]
            scores = dot_nt(q, keys) * HEAD_DIM**-0.5
            scores = jnp.where(allowed, scores, big_negative)
            peak = jnp.max(scores, axis=1, keepdims=True)
            powers = jnp.exp(scores - peak)
            p = (powers * (1.0 / jnp.sum(powers, axis=1, keepdims=True))).astype(bf16)
            probs[i, k * half : k * half + half, :] = p
            ob[k, seq_rows, at] = dot(p, values).astype(bf16)
        return carry

    lax.fori_loop(0, 2 * heads, attend, 0)
    second(4)

    fetches[3].wait()
    z_acc = jnp.zeros((rows, 128), f32)
    chosen = []
    for e in range(experts):
        o_e = jnp.where(hot0[:, e : e + 1] > 0, ob[0].astype(f32), 0.0)
        o_e = o_e + jnp.where(hot1[:, e : e + 1] > 0, ob[1].astype(f32), 0.0)
        o_e = o_e.astype(bf16)
        chosen.append(o_e)
        low = by_seq(o_e, lambda s, v: dot_nt(v, a_o[s]))
        z_acc = z_acc + jnp.where(lane // 16 == e, low * gates[:, e : e + 1], 0.0)
    z_o[...] = z_acc.astype(bf16)

    def columns(ref, rank):
        return ref.at[:, pl.ds(pl.multiple_of(rank * part, part), part)]

    def scatter(d):
        return pltpu.make_async_remote_copy(
            src_ref=parts.at[d],
            dst_ref=held.at[d],
            send_sem=sum_send.at[0, d],
            recv_sem=sum_recv.at[0, d],
            device_id=(me, tp ^ d),
            device_id_type=MESH,
        )

    def spread(d, rank):
        return pltpu.make_async_remote_copy(
            src_ref=columns(attn, rank),
            dst_ref=columns(attn, rank),
            send_sem=sum_send.at[1, d],
            recv_sem=sum_recv.at[1, d],
            device_id=(me, tp ^ d),
            device_id_type=MESH,
        )

    for j in range(1, N_TP + 1):
        d = j % N_TP
        at = pl.ds(pl.multiple_of((tp ^ d) * part, part), part)
        w_rows = wide[at, 256:512]
        total = by_seq(z_o[...], lambda s, v: dot_nt(v, w_rows[:, 128 * s : 128 * s + 128]))
        for e in range(experts):
            total = total + dot(chosen[e], w_o[e, :, at]) * gates[:, e : e + 1]
        if d:
            parts[d] = total.astype(bf16)
            scatter(d).start()
        else:
            own[...] = total
    second(5)
    total = own[...]
    for d in range(1, N_TP):
        scatter(d).wait_recv()
        total = total + held[d].astype(f32)
    columns(attn, tp)[...] = total.astype(bf16)
    for d in range(1, N_TP):
        spread(d, tp).start()
    third(4)
    third(5)
    for d in range(1, N_TP):
        spread(d, tp ^ d).wait_recv()
    fourth(4)
    fourth(5)
    tp_wait(2)
    for t in (4, 5):
        finish(t)
    for c in started:
        c.wait_send()
    for c in staying[4:]:
        c.wait()
    for condition, c in kv_started:
        if condition is None:
            c.wait_send()
        else:
            pl.when(condition)(c.wait_send)
    for d in range(1, N_TP):
        scatter(d).wait_send()
        spread(d, tp).wait_send()


def attention(shards_in, tp_shards, small):
    s_q, s_kv, s_o, s_gu, s_d = shards_in
    tokens, cotangent, s_wide = tp_shards
    rows, part = tokens.shape
    model = part * N_TP
    experts, _, width = s_q.shape
    half = rows // 2
    heads = width // HEAD_DIM
    shape = jax.ShapeDtypeStruct

    def grown(a, d):
        return shape(tuple(n * (N_CTX if i == d else 1) for i, n in enumerate(a.shape)), a.dtype)

    gathered = (grown(s_q, 1), grown(s_kv, 0), grown(s_o, 2), grown(s_gu, 1), grown(s_d, 2))
    wide_mid = shape((s_wide.shape[0] * N_TP, s_wide.shape[1]), bf16)
    wide = grown(wide_mid, 0)
    vmem_out = (
        shape((rows, model), bf16),
        shape((rows, model), bf16),
        shape((rows, model), bf16),
        shape((PAST + 1, 2, half, 2 * width), bf16),
        shape((2 * heads, rows, HEAD_DIM), bf16),
        shape((2 * heads, rows, (PAST + 1) * half), bf16),
        shape((2, rows, width), bf16),
        shape((rows, 128), bf16),
        shape((rows, 128), bf16),
        shape((rows, 128), bf16),
        shape((rows, 128), f32),
    )
    any_out = gathered + (wide, wide_mid, shape((rows, model), bf16))
    return pl.pallas_call(
        attention_kernel,
        out_shape=any_out + vmem_out,
        in_specs=[ANY] * 8 + [VMEM] * len(small),
        out_specs=tuple([ANY] * len(any_out) + [VMEM] * len(vmem_out)),
        scratch_shapes=[
            pltpu.VMEM(gathered[0].shape, bf16),
            pltpu.VMEM(gathered[1].shape, bf16),
            pltpu.VMEM(gathered[2].shape, bf16),
            pltpu.VMEM(wide.shape, bf16),
            pltpu.VMEM((N_TP, rows, part), bf16),
            pltpu.VMEM((rows, part), f32),
            pltpu.VMEM((N_TP, rows, part), bf16),
            pltpu.SemaphoreType.DMA((6, 32)),
            pltpu.SemaphoreType.DMA((6, 27)),
            pltpu.SemaphoreType.DMA((6,)),
            pltpu.SemaphoreType.DMA((3, N_TP)),
            pltpu.SemaphoreType.DMA((3, N_TP)),
            pltpu.SemaphoreType.DMA((3,)),
            pltpu.SemaphoreType.DMA((14,)),
            pltpu.SemaphoreType.DMA((PAST + 1,)),
            pltpu.SemaphoreType.DMA((4,)),
            pltpu.SemaphoreType.DMA((2, N_TP)),
            pltpu.SemaphoreType.DMA((2, N_TP)),
        ],
        compiler_params=pltpu.CompilerParams(
            collective_id=0, has_side_effects=True, vmem_limit_bytes=60 << 20
        ),
        name="attention",
    )(*shards_in, *tp_shards, *small)


def backward_kernel(
    dx1, dx1_own, x0, n1, n2, dy, kv_all, q_all, probs, ob, gates, z_q, z_kv, z_sum,
    hot0, hot1, cosine, sine, gain, router, b_q, b_kv, a_o, f_gu, f_d,
    h_q, h_kv, h_o, h_wide,
    grad_tokens, wide_a, wide_b, heads_out, gu_out, d_out,
    w_q, w_kv, w_o, wide, dob, dkv, dkv_held, dq, dkv_own, dn, parts, own, held, z_part, z_held, z_done,
    dots, tails, gu_src, d_src, a_src, b_src, heads_src, gu_held, d_held, a_held, b_held, heads_held,
    load, tp_send, tp_recv, core_send, core_recv, kv_send, kv_recv, ctx_send, ctx_recv,
):
    me, tp = lax.axis_index("ctx"), lax.axis_index("tp")
    core = me ^ 1
    on_core = lax.rem(me, 2)
    rows, model = x0.shape
    part = model // N_TP
    half = rows // 2
    experts = w_q.shape[0]
    width = w_q.shape[2]
    heads = width // HEAD_DIM
    span = (PAST + 1) * half
    greet([(me ^ d, tp) for d in range(1, N_CTX)] + [(me, tp ^ d) for d in range(1, N_TP)])
    loads = []
    for i, (h, w) in enumerate(((h_wide, wide), (h_o, w_o), (h_q, w_q), (h_kv, w_kv))):
        c = pltpu.make_async_copy(h, w, load.at[i])
        c.start()
        loads.append(c)

    ctx_src = [gu_src, d_src, a_src, b_src, heads_src]
    ctx_held = [gu_held, d_held, a_held, b_held, heads_held]
    ctx_dst = [gu_out, d_out, None, None, heads_out]

    def ctx_scatter(i, d):
        return pltpu.make_async_remote_copy(
            src_ref=ctx_src[i].at[me ^ d],
            dst_ref=ctx_held[i].at[d],
            send_sem=ctx_send.at[i, d],
            recv_sem=ctx_recv.at[i, d],
            device_id=(me ^ d, tp),
            device_id_type=MESH,
        )

    def ctx_spread(i, d, rank):
        return pltpu.make_async_remote_copy(
            src_ref=ctx_dst[i].at[rank],
            dst_ref=ctx_dst[i].at[rank],
            send_sem=ctx_send.at[i, N_CTX + d],
            recv_sem=ctx_recv.at[i, N_CTX + d],
            device_id=(me ^ d, tp),
            device_id_type=MESH,
        )

    def ctx_start(i):
        for d in range(1, N_CTX):
            ctx_scatter(i, d).start()

    def ctx_total(i):
        total = ctx_src[i][me].astype(f32)
        for d in range(1, N_CTX):
            ctx_scatter(i, d).wait_recv()
            total = total + ctx_held[i][d].astype(f32)
        return total

    def ctx_again(i):
        ctx_dst[i][me] = ctx_total(i).astype(ctx_dst[i].dtype)
        for d in range(1, N_CTX):
            ctx_spread(i, d, me).start()

    def ctx_end(i):
        for d in range(1, N_CTX):
            ctx_scatter(i, d).wait_send()
            if ctx_dst[i] is not None:
                ctx_spread(i, d, me ^ d).wait_recv()
                ctx_spread(i, d, me).wait_send()

    for i in range(N_CTX):
        s, slot = i // 8, i % 8
        at = slice(16 * slot, 16 * slot + 16)
        first = 640 * (slot % 2)
        gu_src[i, :, :640] = f_gu[s, at, first : first + 640].astype(bf16)
        gu_src[i, :, 640:] = f_gu[s, at, 1280:].astype(bf16)
        d_src[i] = f_d[s, 64 + 8 * slot : 72 + 8 * slot, :]
    ctx_start(0)
    ctx_start(1)

    lane = lax.broadcasted_iota(jnp.int32, (rows, 128), 1)
    seq = lax.broadcasted_iota(jnp.int32, (rows, 128), 0) // half
    hots = (hot0, hot1)

    loads[0].wait()
    dz_o = by_seq(dx1[...], lambda s, v: dot(v, wide[:, 256 + 128 * s : 384 + 128 * s]))
    loads[1].wait()
    g = [jnp.zeros((rows, width), f32), jnp.zeros((rows, width), f32)]
    g_ao = [jnp.zeros((128, width), f32), jnp.zeros((128, width), f32)]
    for e in range(experts):
        dz_e = jnp.where(lane // 16 == e, dz_o, 0.0)
        g_e = dot_nt(dx1[...], w_o[e]) + by_seq(dz_e.astype(bf16), lambda s, v: dot(v, a_o[s]))
        o_e = jnp.where(hot0[:, e : e + 1] > 0, ob[0].astype(f32), 0.0)
        o_e = o_e + jnp.where(hot1[:, e : e + 1] > 0, ob[1].astype(f32), 0.0)
        o_e = o_e.astype(bf16)
        dz_e = (dz_e * gates[:, e : e + 1]).astype(bf16)
        for s in range(2):
            at = slice(half * s, half * s + half)
            g_ao[s] = g_ao[s] + dot_tn(dz_e[at], o_e[at])
        for k in range(2):
            g[k] = g[k] + jnp.where(hots[k][:, e : e + 1] > 0, g_e, 0.0)
    d_gates = jnp.zeros((rows, 128), f32)
    for k in range(2):
        d_gate = jnp.sum(g[k] * ob[k].astype(f32), axis=1, keepdims=True)
        d_gates = d_gates + jnp.where(hots[k][...] > 0, d_gate, 0.0)
        gate = jnp.sum(hots[k][...] * gates[...], axis=1, keepdims=True)
        d_out = (g[k] * gate).astype(bf16)
        for s in range(2):
            for h in range(heads):
                dob[s * heads + h, k * half : k * half + half, :] = d_out[
                    half * s : half * s + half, HEAD_DIM * h : HEAD_DIM * h + HEAD_DIM
                ]
    d_logits = gates[...] * (d_gates - jnp.sum(gates[...] * d_gates, axis=1, keepdims=True))
    d_logits = d_logits.astype(bf16)

    def attend_back(i, carry):
        s = i // heads
        h = lax.rem(i, heads)
        at = pl.ds(pl.multiple_of(h * HEAD_DIM, HEAD_DIM), HEAD_DIM)
        v_at = pl.ds(pl.multiple_of(width + h * HEAD_DIM, HEAD_DIM), HEAD_DIM)
        keys = kv_all[:, s, :, at].reshape(span, HEAD_DIM)
        values = kv_all[:, s, :, v_at].reshape(span, HEAD_DIM)
        seq_rows = pl.ds(pl.multiple_of(s * half, half), half)
        d_keys = jnp.zeros((span, HEAD_DIM), f32)
        d_values = jnp.zeros((span, HEAD_DIM), f32)
        for k in range(2):
            k_rows = slice(k * half, k * half + half)
            d_o = dob[i, k_rows, :]
            p = probs[i, k_rows, :]
            delta = jnp.sum(d_o.astype(f32) * ob[k, seq_rows, at].astype(f32), axis=1, keepdims=True)
            d_s = (p.astype(f32) * (dot_nt(d_o, values) - delta)).astype(bf16)
            d_q = dot(d_s, keys) * HEAD_DIM**-0.5
            turned = d_q * cosine[seq_rows, :] - pltpu.roll(d_q, HEAD_DIM // 2, 1) * sine[seq_rows, :]
            dq[k, seq_rows, at] = turned.astype(bf16)
            d_keys = d_keys + dot_tn(d_s, q_all[i, k_rows, :])
            d_values = d_values + dot_tn(p, d_o)
        d_keys = (d_keys * HEAD_DIM**-0.5).astype(bf16)
        dkv[:, s, :, at] = d_keys.reshape(PAST + 1, half, HEAD_DIM)
        dkv[:, s, :, v_at] = d_values.astype(bf16).reshape(PAST + 1, half, HEAD_DIM)
        return carry

    lax.fori_loop(0, 2 * heads, attend_back, 0)

    def to_core(back):
        return pltpu.make_async_remote_copy(
            src_ref=dkv.at[PAST - back],
            dst_ref=dkv_held.at[back // 2],
            send_sem=core_send.at[back // 2],
            recv_sem=core_recv.at[back // 2],
            device_id=(core, tp),
            device_id_type=MESH,
        )

    def to_owner(back):
        return pltpu.make_async_remote_copy(
            src_ref=dkv.at[PAST - back],
            dst_ref=dkv_held.at[3 + back // 2],
            send_sem=kv_send.at[back // 2],
            recv_sem=kv_recv.at[back // 2],
            device_id=(lax.rem(me + N_CTX - back, N_CTX), tp),
            device_id_type=MESH,
        )

    for back in (1, 3, 5, 7):
        to_core(back).start()
    for back in (1, 3, 5, 7):
        to_core(back).wait_recv()
        mine = PAST - (back - 1) - 2 * on_core
        dkv[mine] = (dkv[mine].astype(f32) + dkv_held[back // 2].astype(f32)).astype(bf16)
    for back in (2, 4, 6, 8):
        to_owner(back).start()

    loads[2].wait()
    dz_q = jnp.zeros((rows, 128), f32)
    g_bq = jnp.zeros((128, width), f32)
    chosen = []
    for e in range(experts):
        dq_e = jnp.where(hot0[:, e : e + 1] > 0, dq[0].astype(f32), 0.0)
        dq_e = dq_e + jnp.where(hot1[:, e : e + 1] > 0, dq[1].astype(f32), 0.0)
        dq_e = dq_e.astype(bf16)
        chosen.append(dq_e)
        mine = (lane // 64 == seq) & ((lane % 64) // 16 == e)
        dz_q = dz_q + jnp.where(mine, dot_nt(dq_e, b_q[...]), 0.0)
        z_e = jnp.where(mine, z_q[...].astype(f32), 0.0).astype(bf16)
        g_bq = g_bq + dot_tn(z_e, dq_e)
    dz_q = dz_q.astype(bf16)
    z_part[:, :128] = dz_q
    for j in range(N_TP):
        at = slice(part * j, part * j + part)
        total = dot_nt(dz_q, wide[at, 512:640]) + dot_nt(d_logits, router[at, :])
        for e in range(experts):
            total = total + dot_nt(chosen[e], w_q[e, at, :])
        dn[j] = total
    own_columns = lax.broadcasted_iota(jnp.int32, (model, part), 1)
    own_columns = (own_columns // 16) * 128 + tp * 16 + own_columns % 16
    pick = (lax.broadcasted_iota(jnp.int32, (model, part), 0) == own_columns).astype(bf16)
    n2_own = dot(n2[...], pick).astype(bf16)
    dx1_cols = dot(dx1[...], pick).astype(bf16)
    dy_own = dot(dy[...], pick).astype(bf16)
    n1_own = dot(n1[...], pick).astype(bf16)
    lane_m = lax.broadcasted_iota(jnp.int32, (part, 128), 1)
    for s in range(2):
        at = slice(half * s, half * s + half)
        a_src[:, :, 128 * s : 128 * s + 128] = (
            dot_tn(n2_own[at], z_sum[at, :128]).astype(bf16).reshape(N_CTX, 16, 128)
        )
        low = jnp.where(
            lane_m < 64, dot_tn(dx1_cols[at], z_sum[at, 128:]), dot_tn(dy_own[at], z_sum[at, 128:])
        )
        a_src[:, :, 256 + 128 * s : 384 + 128 * s] = low.astype(bf16).reshape(N_CTX, 16, 128)

    total = dkv[PAST].astype(f32)
    for back in (2, 4, 6, 8):
        to_owner(back).wait_recv()
        total = total + dkv_held[3 + back // 2].astype(f32)
    ctx_start(2)
    ctx_again(0)
    ctx_again(1)
    for h in range(heads):
        at = slice(HEAD_DIM * h, HEAD_DIM * h + HEAD_DIM)
        d_k = jnp.concatenate([total[0, :, at], total[1, :, at]], axis=0)
        turned = d_k * cosine[...] - pltpu.roll(d_k, HEAD_DIM // 2, 1) * sine[...]
        dkv_own[:, at] = turned.astype(bf16)
    dkv_own[:, width:] = jnp.concatenate([total[0, :, width:], total[1, :, width:]], axis=0).astype(bf16)
    loads[3].wait()
    dz_kv = dot_nt(dkv_own[...], b_kv[...])
    keep = (lane[:, :64] // 16) % 2 == seq[:, :64]
    dz_kv = jnp.where(keep, dz_kv, 0.0).astype(bf16)
    z_part[:, 128:] = jnp.pad(dz_kv.astype(f32), ((0, 0), (0, 64))).astype(bf16)

    def scatter(d):
        return pltpu.make_async_remote_copy(
            src_ref=parts.at[d],
            dst_ref=held.at[d],
            send_sem=tp_send.at[0, d],
            recv_sem=tp_recv.at[0, d],
            device_id=(me, tp ^ d),
            device_id_type=MESH,
        )

    z_rows = rows // N_TP

    def z_region(ref, rank):
        return ref.at[pl.ds(pl.multiple_of(rank * z_rows, z_rows), z_rows), :]

    def z_scatter(d):
        return pltpu.make_async_remote_copy(
            src_ref=z_region(z_part, tp ^ d),
            dst_ref=z_held.at[d],
            send_sem=tp_send.at[1, d],
            recv_sem=tp_recv.at[1, d],
            device_id=(me, tp ^ d),
            device_id_type=MESH,
        )

    def z_spread(d, rank):
        return pltpu.make_async_remote_copy(
            src_ref=z_region(z_done, rank),
            dst_ref=z_region(z_done, rank),
            send_sem=tp_send.at[2, d],
            recv_sem=tp_recv.at[2, d],
            device_id=(me, tp ^ d),
            device_id_type=MESH,
        )

    def tail(d, rank):
        return pltpu.make_async_remote_copy(
            src_ref=tails.at[rank],
            dst_ref=tails.at[rank],
            send_sem=tp_send.at[3, d],
            recv_sem=tp_recv.at[3, d],
            device_id=(me, tp ^ d),
            device_id_type=MESH,
        )

    for d in range(1, N_TP):
        z_scatter(d).start()
    along = jnp.zeros((rows, 1), f32)
    for j in range(1, N_TP + 1):
        d = j % N_TP
        peer = tp ^ d
        at = pl.ds(pl.multiple_of(peer * part, part), part)
        total = dn[peer] + dot_nt(dz_kv, wide[at, 640:704]) + dot_nt(dkv_own[...], w_kv[at, :])
        scaled = total * gain[:, at]
        along = along + jnp.sum(scaled * x0[:, at].astype(f32), axis=1, keepdims=True)
        if d:
            parts[d] = total.astype(bf16)
            scatter(d).start()
        else:
            own[...] = total
    dots[...] = jnp.broadcast_to(along, dots.shape)
    tails[tp] = jnp.transpose(dots[...])[:8, :]
    for d in range(1, N_TP):
        tail(d, tp).start()
    total = z_region(z_part, tp)[...].astype(f32)
    for d in range(1, N_TP):
        z_scatter(d).wait_recv()
        total = total + z_held[d].astype(f32)
    z_region(z_done, tp)[...] = total.astype(bf16)
    for d in range(1, N_TP):
        z_spread(d, tp).start()
    g_bkv = dot_tn(z_kv[...], dkv_own[...])
    heads_src[:4] = g_bq.astype(bf16).reshape(4, 32, width)
    heads_src[4] = g_bkv[:32, :width].astype(bf16)
    heads_src[5] = g_bkv[32:64, width:].astype(bf16)
    for s in range(2):
        heads_src[6 + 2 * s : 8 + 2 * s] = g_ao[s][:64].astype(bf16).reshape(2, 32, width)
    heads_src[10:] = jnp.zeros((6, 32, width), bf16)
    ctx_start(4)
    for d in range(1, N_TP):
        z_spread(d, tp ^ d).wait_recv()
    b_src[...] = dot_tn(n1_own, z_done[...]).astype(bf16).reshape(N_CTX, 16, part)
    ctx_start(3)
    total = own[...]
    for d in range(1, N_TP):
        scatter(d).wait_recv()
        total = total + held[d].astype(f32)
    for d in range(1, N_TP):
        tail(d, tp ^ d).wait_recv()
    whole = tails[0]
    for d in range(1, N_TP):
        whole = whole + tails[d]
    dots[...] = jnp.transpose(jnp.broadcast_to(whole[:1], (128, rows)))
    own_at = pl.ds(pl.multiple_of(tp * part, part), part)
    own[...] = total * gain[:, own_at]
    step = 32

    def finish(i, carry):
        at = pl.ds(pl.multiple_of(i * step, step), step)
        x = x0[at, :].astype(f32)
        inverse = lax.rsqrt(jnp.mean(x * x, axis=1, keepdims=True) + eps)
        mean = dots[at, :1] * (1.0 / model)
        back = inverse * own[at, :] - x0[at, own_at].astype(f32) * inverse**3 * mean
        grad_tokens[at, :] = (dx1_own[at, :] + back).astype(bf16)
        return carry

    lax.fori_loop(0, rows // step, finish, 0)
    ctx_again(4)
    wide_a[...] = ctx_total(2)
    wide_b[...] = ctx_total(3)
    for i in range(5):
        ctx_end(i)
    for back in (1, 3, 5, 7):
        to_core(back).wait_send()
        to_owner(back + 1).wait_send()
    for d in range(1, N_TP):
        scatter(d).wait_send()
        z_scatter(d).wait_send()
        z_spread(d, tp).wait_send()
        tail(d, tp).wait_send()


def backward(vmem, hbm):
    dx1, dx1_own, kv_all, f_gu = vmem[0], vmem[1], vmem[6], vmem[23]
    w_q, w_kv, w_o, wide = hbm
    rows, model = dx1.shape
    part = model // N_TP
    width = w_q.shape[2]
    heads = width // HEAD_DIM
    half = rows // 2
    hidden = vmem[24].shape[2]
    shape = jax.ShapeDtypeStruct
    reduced = [
        ((N_CTX, 16, 768), bf16),
        ((N_CTX, 8, hidden), f32),
        ((N_CTX, 16, 512), bf16),
        ((N_CTX, 16, part), bf16),
        ((N_CTX, 32, width), bf16),
    ]
    return pl.pallas_call(
        backward_kernel,
        out_shape=(
            shape((rows, part), bf16),
            shape((16, 512), f32),
            shape((16, part), f32),
            shape(*reduced[4]),
            shape(*reduced[0]),
            shape(*reduced[1]),
        ),
        in_specs=[VMEM] * len(vmem) + [ANY] * 4,
        out_specs=tuple([VMEM] * 6),
        scratch_shapes=[
            pltpu.VMEM(w_q.shape, bf16),
            pltpu.VMEM(w_kv.shape, bf16),
            pltpu.VMEM(w_o.shape, bf16),
            pltpu.VMEM(wide.shape, bf16),
            pltpu.VMEM((2 * heads, rows, HEAD_DIM), bf16),
            pltpu.VMEM(kv_all.shape, bf16),
            pltpu.VMEM((8,) + kv_all.shape[1:], bf16),
            pltpu.VMEM((2, rows, width), bf16),
            pltpu.VMEM((rows, 2 * width), bf16),
            pltpu.VMEM((N_TP, rows, part), f32),
            pltpu.VMEM((N_TP, rows, part), bf16),
            pltpu.VMEM((rows, part), f32),
            pltpu.VMEM((N_TP, rows, part), bf16),
            pltpu.VMEM((rows, 256), bf16),
            pltpu.VMEM((N_TP, rows // N_TP, 256), bf16),
            pltpu.VMEM((rows, 256), bf16),
            pltpu.VMEM((rows, 128), f32),
            pltpu.VMEM((N_TP, 8, rows), f32),
        ]
        + [pltpu.VMEM(*a) for a in reduced + reduced]
        + [
            pltpu.SemaphoreType.DMA((4,)),
            pltpu.SemaphoreType.DMA((4, N_TP)),
            pltpu.SemaphoreType.DMA((4, N_TP)),
            pltpu.SemaphoreType.DMA((4,)),
            pltpu.SemaphoreType.DMA((4,)),
            pltpu.SemaphoreType.DMA((5,)),
            pltpu.SemaphoreType.DMA((5,)),
            pltpu.SemaphoreType.DMA((5, 2 * N_CTX)),
            pltpu.SemaphoreType.DMA((5, 2 * N_CTX)),
        ],
        compiler_params=pltpu.CompilerParams(
            collective_id=3, has_side_effects=True, vmem_limit_bytes=60 << 20
        ),
        name="backward",
    )(*vmem, *hbm)


def shards(
    tokens,
    norm1_gain,
    router_attn,
    w_query,
    w_key_value,
    w_out,
    norm2_gain,
    router_ffn,
    w_gate_up,
    w_down,
    adapt_wide,
    adapt_heads,
    adapt_ffn,
    attention_routes,
    feedforward_routes,
    doc_lengths,
    adapter_index,
    cotangent,
):
    seqs, block, part = tokens.shape
    rows = seqs * block
    n_tp = lax.axis_size("tp")
    model = part * n_tp
    experts = w_query.shape[0]
    width = w_query.shape[2]
    heads = width // HEAD_DIM
    hidden = w_down.shape[1]
    rank = adapt_heads.shape[2]
    wide_slots = adapt_wide.shape[1]
    ctx_rank = lax.axis_index("ctx")

    wide_own = adapt_wide.astype(bf16)[adapter_index]
    groups = [[6, 10, 7, 11, 8, 12, 9, 13], list(range(14, 22)), [0, 1, 2, 3], [4, 5]]
    order = [(q, s) for g in groups[:3] for q in range(seqs) for s in g]
    order += [(q, s) for s in groups[3] for q in range(seqs)]
    wide_cols = wide_own.reshape(seqs * wide_slots, rank, -1)[
        np.array([q * wide_slots + s for q, s in order])
    ].reshape(seqs * wide_slots * rank, -1).T
    heads_low = adapt_heads.astype(bf16)[adapter_index]
    ffn_low = adapt_ffn.astype(bf16)[adapter_index]
    route_a = attention_routes.reshape(rows, -1)
    route_f = feedforward_routes.reshape(rows, -1)

    positions = ctx_rank * block + jnp.arange(block, dtype=jnp.int32)
    doc_ids, offsets = doc_layout(doc_lengths, positions)
    half = HEAD_DIM // 2
    frequency = 10000.0 ** (-2.0 * jnp.arange(half, dtype=f32) / HEAD_DIM)
    angles = offsets.astype(f32).reshape(rows)[:, None] * frequency
    cosine, sine = jnp.cos(angles), jnp.sin(angles)
    cosine = jnp.concatenate([cosine, cosine], axis=1)
    sine = jnp.concatenate([-sine, sine], axis=1)

    b_q, b_kv, a_o = heads_low[:, :experts], heads_low[:, experts : experts + 2], heads_low[:, experts + 2 :]
    key_pos = (ctx_rank - PAST) * block + jnp.arange((PAST + 1) * block, dtype=jnp.int32)
    key_doc = doc_layout(doc_lengths, jnp.maximum(key_pos, 0))[0]
    key_doc = jnp.where(key_pos[None, :] >= 0, key_doc, -(1 << 20))
    blank = jnp.zeros((seqs, rank, width), bf16)
    b_kv_wide = jnp.concatenate(
        [
            jnp.concatenate([b_kv[:, 0], blank], axis=-1).reshape(seqs * rank, 2 * width),
            jnp.concatenate([blank, b_kv[:, 1]], axis=-1).reshape(seqs * rank, 2 * width),
        ],
        axis=0,
    )
    a_o_wide = jnp.pad(a_o.reshape(seqs, experts * rank, width), ((0, 0), (0, 64), (0, 0)))
    b_q = b_q.reshape(seqs * experts * rank, width)
    hot0, hot1 = widen_routes(route_a[:, :1], experts), widen_routes(route_a[:, 1:], experts)
    router_wide = jnp.pad(router_attn, ((0, 0), (0, 128 - experts)))
    (
        w_query, w_key_value, w_out, w_gate_up, w_down, wide, _, dy,
        x0, sum_out, n1, kv_all, q_all, probs, ob, z_o_gated, z_q, z_kv, gates,
    ) = attention(
        [
            w_query,
            w_key_value.reshape(-1, 2 * width),
            w_out,
            gate_up_columns(w_gate_up[:, :, 0], w_gate_up[:, :, 1]),
            w_down,
        ],
        [tokens.reshape(rows, part), cotangent.reshape(rows, part), wide_cols],
        [
            norm1_gain[None],
            router_wide,
            hot0,
            hot1,
            cosine,
            sine,
            jnp.broadcast_to(doc_ids.reshape(rows, 1), (rows, 128)),
            jnp.broadcast_to(key_doc[:, None, :], (seqs, 8, key_doc.shape[1])),
            b_q,
            b_kv_wide,
            a_o_wide,
        ],
    )
    blank = jnp.zeros((seqs, experts, rank, hidden), bf16)
    b_gu = jnp.stack(
        [gate_up_columns(ffn_low[:, :experts], blank), gate_up_columns(blank, ffn_low[:, experts : 2 * experts])],
        axis=2,
    ).reshape(seqs, 2 * experts * rank, 2 * hidden)
    a_d = jnp.pad(ffn_low[:, 2 * experts :].reshape(seqs, experts * rank, hidden), ((0, 0), (64, 0), (0, 0)))
    mixed, dx1b, dx1_own, n2, z_sum, g_gu, g_d = feed_forward(
        x0, sum_out, dy, norm2_gain[None], wide,
        jnp.pad(router_ffn, ((0, 0), (0, 128 - experts))),
        widen_routes(route_f, experts), b_gu, a_d, z_o_gated, w_gate_up, w_down,
    )
    grad_tokens, wide_a, wide_b, head_sum, gu_sum, d_sum = backward(
        [
            dx1b, dx1_own, x0, n1, n2, dy, kv_all, q_all, probs, ob, gates, z_q, z_kv, z_sum,
            hot0, hot1, cosine, sine, norm1_gain[None], router_wide, b_q, b_kv_wide, a_o_wide, g_gu, g_d,
        ],
        [w_query, w_key_value, w_out, wide],
    )
    grad_wide = jnp.concatenate([wide_a, wide_b[:, : 704 - 512]], axis=1).T
    back_order = np.argsort(np.array([q * wide_slots + s for q, s in order]))
    grad_wide = grad_wide.reshape(seqs * wide_slots, rank, -1)[back_order]
    grad_wide = grad_wide.reshape(seqs, wide_slots, rank, -1)[adapter_index]
    head_sum = head_sum.reshape(-1, rank, width).astype(f32)
    grad_heads = jnp.concatenate(
        [
            head_sum[: seqs * experts].reshape(seqs, experts, rank, width),
            jnp.swapaxes(head_sum[8:12].reshape(2, seqs, rank, width), 0, 1),
            head_sum[12:20].reshape(seqs, experts, rank, width),
        ],
        axis=1,
    )[adapter_index]
    gu_sum = gu_sum.reshape(seqs, experts, 2, rank, 768).astype(f32)
    grad_ffn = jnp.concatenate(
        [
            gu_sum[:, :, 0, :, :704],
            jnp.concatenate([gu_sum[:, :, 1, :, :640], gu_sum[:, :, 1, :, 704:]], axis=-1),
            d_sum.reshape(seqs, experts, rank, hidden),
        ],
        axis=1,
    )[adapter_index]
    mixed = mixed.reshape(seqs, block, part)
    grad_tokens = grad_tokens.reshape(seqs, block, part)
    return (mixed, grad_tokens, grad_wide, grad_heads, grad_ffn)


def solution(mesh):
    placed = (
        P(None, "ctx", "tp"),
        P(),
        P(),
        P(None, "ctx", "tp"),
        P("ctx", None, "tp"),
        P(None, "tp", "ctx"),
        P(),
        P(),
        P(None, "ctx", None, "tp"),
        P(None, "tp", "ctx"),
        P(None, None, None, ("ctx", "tp")),
        P(None, None, None, "tp"),
        P(None, None, None, "tp"),
        P(None, "ctx", None),
        P(None, "ctx", None),
        P(),
        P(),
        P(None, "ctx", "tp"),
    )
    return jax.shard_map(
        shards,
        mesh=mesh,
        in_specs=placed,
        out_specs=(
            P(None, "ctx", "tp"),
            P(None, "ctx", "tp"),
            P(None, None, None, ("ctx", "tp")),
            P(None, None, None, "tp"),
            P(None, None, None, "tp"),
        ),
        check_vma=False,
    )
```

```python
import functools

import jax
import numpy as np
import jax.numpy as jnp
from jax import lax
from jax.experimental import pallas as pl
from jax.experimental.pallas import tpu as pltpu
from jax.sharding import PartitionSpec as P

HEAD_DIM = 128
WINDOW = 1024
eps = 1e-06
big_negative = -1e30
bf16 = jnp.bfloat16
f32 = jnp.float32

MESH = pl.DeviceIdType.MESH
ANY = pl.BlockSpec(memory_space=pl.ANY)
VMEM = pl.BlockSpec(memory_space=pltpu.VMEM)
N_CTX, N_TP = 16, 8
FAR = 4
PAST = 8


def region(kind, ref, owner, low, high):
    rows = pl.ds(pl.multiple_of(owner * 128 + 32 * low, 32), 32 * (high - low))
    cols = pl.ds(pl.multiple_of(owner * 128, 128), 128)
    if kind == "rows":
        return ref.at[pl.ds(low, high - low), cols, :]
    if kind == "flat":
        return ref.at[rows, :]
    if kind == "cols":
        return ref.at[pl.ds(low, high - low), :, cols]
    if high - low == 1:
        half = ref.shape[1] // 2
        return ref.at[low // 2, pl.ds(half * (low % 2), half), cols]
    return ref.at[pl.ds(low // 2, (high - low) // 2), :, cols]


def own_part(kind, ref, low, high):
    if kind == "flat":
        return ref.at[pl.ds(32 * low, 32 * (high - low)), :]
    if kind == "pair":
        return ref
    return ref.at[pl.ds(low, high - low)]


def tp_part(kind, ref, rank, size):
    if kind == "cols":
        return ref.at[:, pl.ds(pl.multiple_of(rank * size, size), size)]
    return ref.at[pl.ds(pl.multiple_of(rank * size, size), size), :]


def rms_scale(values, gain):
    return values * lax.rsqrt(jnp.mean(values * values, axis=-1, keepdims=True) + eps) * gain


def doc_layout(doc_lengths, positions):
    docs = doc_lengths.shape[1]
    upto = np.tril(np.ones((docs, docs), np.int32))
    ends = jnp.sum(doc_lengths[:, None, :] * upto[None], axis=2)
    passed = positions[None, :, None] >= ends[:, None, :]
    doc_ids = jnp.sum(passed.astype(jnp.int32), axis=2)
    starting = jnp.sum(jnp.where(passed, doc_lengths[:, None, :], 0), axis=2)
    inside = positions[None, :] < ends[:, -1:]
    doc_ids = jnp.where(inside, doc_ids, -1 - positions[None, :])
    return (doc_ids, positions[None, :] - starting)


def dot(a, b, ca=1, cb=0):
    return lax.dot_general(a, b, (((ca,), (cb,)), ((), ())), preferred_element_type=f32)


class Scatter:
    def __init__(self, parts, held, relay, send, recv, row):
        self.me, self.tp = lax.axis_index("ctx"), lax.axis_index("tp")
        self.parts, self.held, self.relay_buffer = parts, held, relay
        self.send, self.recv, self.row = send, recv, row

    def copy_to(self, d, to):
        return pltpu.make_async_remote_copy(
            src_ref=self.parts.at[d],
            dst_ref=self.held.at[d],
            send_sem=self.send.at[self.row, d],
            recv_sem=self.recv.at[self.row, d],
            device_id=(self.me, self.tp ^ to),
            device_id_type=MESH,
        )

    def copy(self, d):
        if d != FAR:
            return self.copy_to(d, d % FAR)
        return pltpu.make_async_remote_copy(
            src_ref=self.relay_buffer,
            dst_ref=self.held.at[FAR],
            send_sem=self.send.at[self.row, FAR],
            recv_sem=self.recv.at[self.row, FAR],
            device_id=(self.me, self.tp ^ FAR),
            device_id_type=MESH,
        )

    def relay(self):
        total = self.parts[FAR].astype(f32)
        for d in range(FAR + 1, N_TP):
            self.copy(d).wait_recv()
            total = total + self.held[d].astype(f32)
        self.relay_buffer[...] = total.astype(bf16)
        self.copy(FAR).start()

    def total(self, own):
        for d in range(1, FAR + 1):
            self.copy(d).wait_recv()
            own = own + self.held[d].astype(f32)
        return own

    def sent(self):
        for d in range(1, N_TP):
            self.copy(d).wait_send()


class Spread:
    def __init__(self, source, place, send, recv, row):
        self.me, self.tp = lax.axis_index("ctx"), lax.axis_index("tp")
        self.source, self.place = source, place
        self.send, self.recv, self.row = send, recv, row

    def copy(self, d, owner, to, source=None):
        return pltpu.make_async_remote_copy(
            src_ref=self.place(owner) if source is None else source,
            dst_ref=self.place(owner),
            send_sem=self.send.at[self.row, d],
            recv_sem=self.recv.at[self.row, d],
            device_id=(self.me, self.tp ^ to),
            device_id_type=MESH,
        )

    def start(self):
        for d in (FAR, 1, 2, 3):
            self.copy(d, self.tp, d, self.source).start()

    def relay(self):
        self.copy(FAR, self.tp ^ FAR, FAR).wait_recv()
        for d in (1, 2, 3):
            self.copy(FAR + d, self.tp ^ FAR, d).start()

    def wait(self):
        for d in (1, 2, 3):
            self.copy(d, self.tp ^ d, d).wait_recv()
            self.copy(FAR + d, self.tp ^ (FAR + d), d).wait_recv()

    def sent(self):
        for d in (FAR, 1, 2, 3):
            self.copy(d, self.tp, d, self.source).wait_send()
        for d in (1, 2, 3):
            self.copy(FAR + d, self.tp ^ FAR, d).wait_send()


class CtxSum:
    def __init__(self, source, core_held, held, out, send, recv, row):
        self.me, self.tp = lax.axis_index("ctx"), lax.axis_index("tp")
        self.core, self.chip = lax.rem(self.me, 2), self.me // 2
        self.source, self.core_held, self.held, self.out = source, core_held, held, out
        self.send, self.recv, self.row = send, recv, row

    def copy(self, item, src, dst, to):
        return pltpu.make_async_remote_copy(
            src_ref=src,
            dst_ref=dst,
            send_sem=self.send.at[self.row, item],
            recv_sem=self.recv.at[self.row, item],
            device_id=(to, self.tp),
            device_id_type=MESH,
        )

    def to_core(self):
        return self.copy(0, self.source.at[1 - self.core], self.core_held, self.me ^ 1)

    def to_chip(self, d):
        return self.copy(
            d, self.source.at[self.core, self.chip ^ d], self.held.at[d], self.me ^ (2 * d)
        )

    def spread(self, d, chip):
        there = self.out.at[self.core, chip]
        return self.copy(7 + d, there, there, self.me ^ (2 * d))

    def back_to_core(self, core):
        return self.copy(15, self.out.at[core], self.out.at[core], self.me ^ 1)

    def start(self):
        self.to_core().start()

    def chips(self):
        self.to_core().wait()
        self.source[self.core] = (
            self.source[self.core].astype(f32) + self.core_held[...].astype(f32)
        ).astype(self.source.dtype)
        for d in range(1, 8):
            self.to_chip(d).start()

    def total(self):
        total = self.source[self.core, self.chip].astype(f32)
        for d in range(1, 8):
            self.to_chip(d).wait_recv()
            total = total + self.held[d].astype(f32)
        for d in range(1, 8):
            self.to_chip(d).wait_send()
        return total

    def again(self):
        self.out[self.core, self.chip] = self.total().astype(self.out.dtype)
        for d in range(1, 8):
            self.spread(d, self.chip).start()

    def other_core(self):
        for d in range(1, 8):
            self.spread(d, self.chip ^ d).wait_recv()
            self.spread(d, self.chip).wait_send()
        self.back_to_core(self.core).start()

    def finish(self):
        self.back_to_core(1 - self.core).wait_recv()
        self.back_to_core(self.core).wait_send()


def dot_nt(a, b):
    return dot(a, b, 1, 1)


def dot_tn(a, b):
    return dot(a, b, 0, 0)


def by_seq(rows, f):
    half = rows.shape[0] // 2
    return jnp.concatenate([f(0, rows[:half]), f(1, rows[half:])], axis=0)


def column_of(values, lane, e):
    return jnp.sum(jnp.where(lane == e, values, 0.0), axis=1, keepdims=True)


def greet(targets):
    barrier = pltpu.get_barrier_semaphore()
    for device in targets:
        pl.semaphore_signal(barrier, inc=1, device_id=device, device_id_type=MESH)
    pl.semaphore_wait(barrier, len(targets))


def masked_gates(logits, hot):
    largest = jnp.max(jnp.where(hot > 0, logits, big_negative), axis=1, keepdims=True)
    powers = jnp.where(hot > 0, jnp.exp(logits - largest), 0.0)
    return powers / jnp.sum(powers, axis=1, keepdims=True)


def ffn_kernel(
    x0, attn, dy, gain, wide, router, table, b_gu, a_d, z_o, w_gu_hbm, w_d_hbm,
    ff_parts, ff_own, dx1, dx1_own, n2, z_sum, gu_out, d_out,
    w_gu, w_d, hg, dgu, dh_tmp, z_gu, dz_d, z_part, parts, relay, own, held, z_held, dots, tails, inverse,
    g_gu, g_d, gu_src, gu_core, gu_held, d_src, d_core, d_held,
    load, send, recv, ctx_send, ctx_recv,
):
    me, tp = lax.axis_index("ctx"), lax.axis_index("tp")
    hot = table.at[:, 512:640]
    rows, model = x0.shape
    experts = w_gu.shape[0]
    part = model // N_TP
    greet([(me ^ d, tp) for d in range(1, N_CTX)] + [(me, tp ^ d) for d in range(1, N_TP)])

    def fetch(e):
        return (
            pltpu.make_async_copy(w_gu_hbm.at[e], w_gu.at[e], load.at[0, e]),
            pltpu.make_async_copy(w_d_hbm.at[e], w_d.at[e], load.at[1, e]),
        )

    for e in range(experts):
        for c in fetch(e):
            c.start()

    step = 32

    def normalize(i, carry):
        at = pl.ds(pl.multiple_of(i * step, step), step)
        x = x0[at, :].astype(f32) + attn[at, :].astype(f32)
        r = lax.rsqrt(jnp.mean(x * x, axis=1, keepdims=True) + eps)
        inverse[at, :] = jnp.broadcast_to(r, (step, 128))
        n2[at, :] = (x * r * gain[...]).astype(bf16)
        return carry

    lax.fori_loop(0, rows // step, normalize, 0)
    lane = lax.broadcasted_iota(jnp.int32, (rows, 128), 1)
    gates = masked_gates(dot(n2[...], router[...]), hot[...])
    pair_lane = lax.broadcasted_iota(jnp.int32, (rows, 256), 1)
    mine = pair_lane // 128 == lax.broadcasted_iota(jnp.int32, (rows, 256), 0) // (rows // 2)
    pair_lane = pair_lane % 128
    z_gu[...] = jnp.where(mine, dot(n2[...], wide[:, :256]), 0.0).astype(bf16)
    dz_d[...] = jnp.where(mine, dot(dy[...], wide[:, 256:512]), 0.0).astype(bf16)
    g_gu[...] = jnp.zeros_like(g_gu)
    g_d[...] = jnp.zeros_like(g_d)
    zero = jnp.zeros((rows, 256), f32)

    def expert(e, carry):
        d_gates, dz_gu, z_d = carry
        for c in fetch(e):
            c.wait()
        gate = column_of(gates, lane, e)
        z_in = jnp.where(pair_lane // 32 == e, z_gu[...].astype(f32), 0.0).astype(bf16)
        dz_in = jnp.where(pair_lane // 16 == 4 + e, dz_d[...].astype(f32), 0.0).astype(bf16)
        dh_tmp[:, :704] = dot_nt(dy[...], w_d[e]) + dot(dz_in, a_d[...])
        pre = dot(n2[...], w_gu[e]) + dot(z_in, b_gu[...])

        def tile(g, u, d):
            sg = jax.nn.sigmoid(g)
            silu = g * sg
            h = silu * u
            dg = d * gate
            return h, (dg * u * sg * (1.0 + g * (1.0 - sg))), dg * silu, h * d

        h, dgp, dup, hd = tile(pre[:, :640], pre[:, 640:1280], dh_tmp[:, :640])
        hg[e, :, :640] = (h * gate).astype(bf16)
        dgu[e, :, :640] = dgp.astype(bf16)
        dgu[e, :, 640:1280] = dup.astype(bf16)
        dgf = jnp.sum(hd, axis=1, keepdims=True)
        last = pre[:, 1280:]
        h, dgp, dup, hd = tile(last, pltpu.roll(last, 64, 1), dh_tmp[:, 640:])
        hg[e, :, 640:] = (h * gate).astype(bf16)[:, :64]
        dgu[e, :, 1280:] = jnp.where(lane < 64, dgp, pltpu.roll(dup, 64, 1)).astype(bf16)
        dgf = dgf + jnp.sum(jnp.where(lane < 64, hd, 0.0), axis=1, keepdims=True)
        d_gates = d_gates + jnp.where(lane == e, dgf, 0.0)
        keep = mine & (pair_lane // 32 == e)
        dz_gu = dz_gu + jnp.where(keep, dot_nt(dgu[e], b_gu[...]), 0.0)
        keep = mine & (pair_lane // 16 == 4 + e)
        z_d = z_d + jnp.where(keep, dot_nt(hg[e], a_d[...]), 0.0)
        g_gu[...] += dot_tn(z_in, dgu[e])
        g_d[...] += dot_tn(dz_in, hg[e])
        return d_gates, dz_gu, z_d

    d_gates, dz_gu, z_d = lax.fori_loop(
        0, experts, expert, (jnp.zeros((rows, 128), f32), zero, zero)
    )
    d_logits = gates * (d_gates - jnp.sum(gates * d_gates, axis=1, keepdims=True))
    d_logits = d_logits.astype(bf16)
    dz_gu, z_d = dz_gu.astype(bf16), z_d.astype(bf16)
    z_part[:, :128] = dz_gu[:, :128] + dz_gu[:, 128:]
    z_part[:, 128:] = z_o[...] + z_d[:, :128] + z_d[:, 128:]

    for i in range(N_CTX):
        s, slot = i // 8, i % 8
        at = slice(128 * s + 16 * slot, 128 * s + 16 * slot + 16)
        cols = 640 * (slot % 2)
        gu_src[i % 2, i // 2, :, :640] = g_gu[at, cols : cols + 640].astype(bf16)
        gu_src[i % 2, i // 2, :, 640:] = g_gu[at, 1280:].astype(bf16)
        first = 128 * s + 64 + 8 * slot
        d_src[i % 2, i // 2] = g_d[first : first + 8, :]
    gu_sum = CtxSum(gu_src, gu_core, gu_held, gu_out, ctx_send, ctx_recv, 0)
    d_sum = CtxSum(d_src, d_core, d_held, d_out, ctx_send, ctx_recv, 1)
    gu_sum.start()
    d_sum.start()
    scatter = Scatter(parts, held, relay, send, recv, 0)

    def x_at(at):
        return x0[:, at].astype(f32) + attn[:, at].astype(f32)

    def piece(j, along):
        d = lax.rem(j + FAR + 1, N_TP)
        peer = tp ^ d
        at = pl.ds(pl.multiple_of(peer * part, part), part)
        w_rows = wide[at, :256]
        dn = dot_nt(d_logits, router[at, :])
        dn = dn + dot_nt(dz_gu, w_rows)
        for e in range(experts):
            dn = dn + dot_nt(dgu[e], w_gu[e, at, :])
        parts[d] = dn.astype(bf16)

        @pl.when((d != 0) & (d != FAR))
        def _():
            scatter.copy_to(d, lax.rem(d, FAR)).start()

        @pl.when(d == 0)
        def _():
            own[...] = dn

        return along + jnp.sum(dn * gain[:, at] * x_at(at), axis=1, keepdims=True)

    def out_piece(d, carry):
        peer = tp ^ d
        at = pl.ds(pl.multiple_of(peer * part, part), part)
        w_rows = wide[at, 256:512]
        ff = dot_nt(z_d, w_rows)
        for e in range(experts):
            ff = ff + dot(hg[e], w_d[e, :, at])
        ff_parts[d] = ff.astype(bf16)

        @pl.when(d == 0)
        def _():
            ff_own[...] = ff + x_at(at)

        return carry

    z_rows = rows // N_TP

    def z_region(ref, rank):
        return ref.at[pl.ds(pl.multiple_of(rank * z_rows, z_rows), z_rows), :]

    def z_scatter(d):
        return pltpu.make_async_remote_copy(
            src_ref=z_region(z_part, tp ^ d),
            dst_ref=z_held.at[d],
            send_sem=send.at[2, d],
            recv_sem=recv.at[2, d],
            device_id=(me, tp ^ d),
            device_id_type=MESH,
        )

    def z_spread(d, rank):
        return pltpu.make_async_remote_copy(
            src_ref=z_region(z_sum, rank),
            dst_ref=z_region(z_sum, rank),
            send_sem=send.at[3, d],
            recv_sem=recv.at[3, d],
            device_id=(me, tp ^ d),
            device_id_type=MESH,
        )

    def columns(ref, rank):
        return ref.at[:, pl.ds(pl.multiple_of(rank * part, part), part)]

    def tail(d, rank):
        return pltpu.make_async_remote_copy(
            src_ref=tails.at[rank],
            dst_ref=tails.at[rank],
            send_sem=send.at[5, d],
            recv_sem=recv.at[5, d],
            device_id=(me, tp ^ d),
            device_id_type=MESH,
        )

    along = lax.fori_loop(0, N_TP, piece, jnp.zeros((rows, 1), f32))
    dots[...] = jnp.broadcast_to(along, dots.shape)
    tails[tp] = jnp.transpose(dots[...])[:8, :]
    for d in range(1, N_TP):
        tail(d, tp).start()
        z_scatter(d).start()
    scatter.relay()
    gu_sum.chips()
    d_sum.chips()
    lax.fori_loop(0, N_TP, out_piece, 0)
    at = pl.ds(pl.multiple_of(tp * part, part), part)
    total = scatter.total(own[...]) * gain[:, at]
    for d in range(1, N_TP):
        tail(d, tp ^ d).wait_recv()
    whole = tails[0]
    for d in range(1, N_TP):
        whole = whole + tails[d]
    dots[...] = jnp.transpose(jnp.broadcast_to(whole[:1], (128, rows)))
    r = inverse[:, :1]
    total = dy[:, at].astype(f32) + r * total - x_at(at) * r**3 * (dots[:, :1] * (1.0 / model))
    dx1_own[...] = total
    columns(dx1, tp)[...] = total.astype(bf16)
    spread = Spread(None, lambda rank: columns(dx1, rank), send, recv, 4)
    spread.start()
    gu_sum.again()
    d_sum.again()
    total = z_region(z_part, tp)[...].astype(f32)
    for d in range(1, N_TP):
        z_scatter(d).wait_recv()
        total = total + z_held[d].astype(f32)
    z_region(z_sum, tp)[...] = total.astype(bf16)
    for d in range(1, N_TP):
        z_spread(d, tp).start()
    spread.relay()
    gu_sum.other_core()
    d_sum.other_core()
    spread.wait()
    gu_sum.finish()
    d_sum.finish()
    scatter.sent()
    spread.sent()
    for d in range(1, N_TP):
        z_scatter(d).wait_send()
        z_spread(d, tp ^ d).wait_recv()
        z_spread(d, tp).wait_send()
        tail(d, tp).wait_send()


def feed_forward(x0, attn, dy, gain, wide, router, table, b_gu, a_d, z_o, w_gu, w_d):
    rows, model = x0.shape
    part = model // N_TP
    experts, _, cols = w_gu.shape
    hidden = w_d.shape[1]
    shape = jax.ShapeDtypeStruct
    return pl.pallas_call(
        ffn_kernel,
        out_shape=(
            shape((N_TP, rows, part), bf16),
            shape((rows, part), f32),
            shape((rows, model), bf16),
            shape((rows, part), f32),
            shape((rows, model), bf16),
            shape((rows, 256), bf16),
            shape((2, 8, 16, 768), bf16),
            shape((2, 8, 8, hidden), f32),
        ),
        in_specs=[VMEM] * 10 + [ANY] * 2,
        out_specs=tuple([VMEM] * 8),
        scratch_shapes=[
            pltpu.VMEM(w_gu.shape, bf16),
            pltpu.VMEM(w_d.shape, bf16),
            pltpu.VMEM((experts, rows, hidden), bf16),
            pltpu.VMEM((experts, rows, cols), bf16),
            pltpu.VMEM((rows, 768), f32),
            pltpu.VMEM((rows, 256), bf16),
            pltpu.VMEM((rows, 256), bf16),
            pltpu.VMEM((rows, 256), bf16),
            pltpu.VMEM((N_TP, rows, part), bf16),
            pltpu.VMEM((rows, part), bf16),
            pltpu.VMEM((rows, part), f32),
            pltpu.VMEM((N_TP, rows, part), bf16),
            pltpu.VMEM((N_TP, rows // N_TP, 256), bf16),
            pltpu.VMEM((rows, 128), f32),
            pltpu.VMEM((N_TP, 8, rows), f32),
            pltpu.VMEM((rows, 128), f32),
            pltpu.VMEM(b_gu.shape, f32),
            pltpu.VMEM(a_d.shape, f32),
            pltpu.VMEM((2, 8, 16, 768), bf16),
            pltpu.VMEM((8, 16, 768), bf16),
            pltpu.VMEM((8, 16, 768), bf16),
            pltpu.VMEM((2, 8, 8, hidden), f32),
            pltpu.VMEM((8, 8, hidden), f32),
            pltpu.VMEM((8, 8, hidden), f32),
            pltpu.SemaphoreType.DMA((2, experts)),
            pltpu.SemaphoreType.DMA((6, N_TP)),
            pltpu.SemaphoreType.DMA((6, N_TP)),
            pltpu.SemaphoreType.DMA((2, 16)),
            pltpu.SemaphoreType.DMA((2, 16)),
        ],
        compiler_params=pltpu.CompilerParams(
            collective_id=2, has_side_effects=True, vmem_limit_bytes=63 << 20
        ),
        name="feed_forward",
    )(x0, attn, dy, gain, wide, router, table, b_gu, a_d, z_o, w_gu, w_d)


def widen_routes(routes, experts):
    lane = jnp.arange(128, dtype=jnp.int32)
    return jnp.sum((routes[..., None] == lane).astype(f32), axis=1)


def gate_up_columns(gate, up):
    return jnp.concatenate([gate[..., :640], up[..., :640], gate[..., 640:], up[..., 640:]], axis=-1)


def attention_kernel(
    s_q, s_kv, s_o, s_gu, s_d, tokens, cotangent, s_wide,
    gain, router, table, k_doc, b_q, b_kv, a_o,
    g_q, g_kv, g_o, g_gu, g_d, g_wide, wide_mid, dy,
    x0, attn, n1, kv_all, q_all, probs, ob, z_o, z_q, z_kv, gates,
    w_q, w_kv, w_o, wide, parts, relay, own, held,
    send, recv, local, tp_send, tp_recv, tp_local, kv_send, kv_recv, load, sum_send, sum_recv,
):
    me, tp = lax.axis_index("ctx"), lax.axis_index("tp")
    core, side = me ^ 1, me ^ 2
    up, down, far = lax.rem(me + 4, 16), lax.rem(me + 12, 16), lax.rem(me + 8, 16)
    on_core, on_side = lax.rem(me, 2), lax.rem(me // 2, 2)
    cosine, sine, hot0, hot1 = (table.at[:, 128 * i : 128 * i + 128] for i in range(4))
    q_doc = table.at[:, 640:768]
    rows, model = x0.shape
    part = model // N_TP
    half = rows // 2
    experts = w_q.shape[0]
    width = w_q.shape[2]
    heads = width // HEAD_DIM
    span = (PAST + 1) * half
    greet([(d, tp) for d in (core, side, up, down, far)] + [(me, tp ^ d) for d in range(1, N_TP)])

    kinds = ["flat", "flat", "rows", "cols"] + ["flat"] * experts + ["pair"] * (experts // 2)
    src = [s_kv, wide_mid, s_q, s_o] + [s_gu.at[e] for e in range(experts)]
    dst = [g_kv, g_wide, g_q, g_o] + [g_gu.at[e] for e in range(experts)]
    src += [s_d.at[pl.ds(e, 2)] for e in range(0, experts, 2)]
    dst += [g_d.at[pl.ds(e, 2)] for e in range(0, experts, 2)]
    tp_src, tp_dst, tp_kinds = [tokens, s_wide, cotangent], [x0, wide_mid, dy], ["cols", "rows", "cols"]
    started, staying = [], [None] * len(kinds)
    counter = [0] * len(kinds)

    def place_of(i):
        size = tp_src[i].shape[1 if tp_kinds[i] == "cols" else 0]
        return lambda rank: tp_part(tp_kinds[i], tp_dst[i], rank, size)

    tp_all = [Spread(tp_src[i], place_of(i), tp_send, tp_recv, i) for i in range(3)]

    def tp_own(i):
        return pltpu.make_async_copy(tp_src[i], place_of(i)(tp), tp_local.at[i])

    def tp_start(i):
        tp_all[i].start()
        tp_own(i).start()

    def tp_wait(i):
        tp_all[i].wait()
        tp_own(i).wait()

    def copy(t, item, owner, low, high, to, slot, own_shard):
        there = region(kinds[t], dst[t], owner, low, high)
        return pltpu.make_async_remote_copy(
            src_ref=own_part(kinds[t], src[t], low, high) if own_shard else there,
            dst_ref=there,
            send_sem=send.at[t, slot],
            recv_sem=recv.at[t, item],
            device_id=(to, tp),
            device_id_type=MESH,
        )

    def go(t, item, owner, low, high, to, own_shard=False):
        c = copy(t, item, owner, low, high, to, counter[t], own_shard)
        counter[t] += 1
        c.start()
        started.append(c)

    cuts = [2, 2, 3, 3] + [2] * 6

    def arrive(t, item):
        cut = cuts[t]
        mid = cut // 2 if t % 2 else (cut + 1) // 2
        return {
            0: (side, 0, 4),
            1: (down, 0, 4),
            2: (up, 0, 4),
            3: (down ^ 2, 0, cut),
            4: (up ^ 2, 0, cut),
            5: (far, 2, 4),
            6: (far, 0, 2),
            7: (far ^ 2, mid, cut),
            8: (far ^ 2, 0, mid),
            9: (down ^ 2, cut, 4),
            10: (up ^ 2, cut, 4),
            11: (far ^ 2, cut, 4),
        }[item]

    def got(t, item):
        owner, low, high = arrive(t, item)
        copy(t, item, owner, low, high, core, 0, False).wait_recv()
        go(t, 12 + item, owner, low, high, core)

    def first(t):
        go(t, 0, me, 0, 4, side, True)
        go(t, 2, me, 0, 4, down, True)
        go(t, 1, me, 0, 4, up, True)
        go(t, 24, me, 0, 4, core, True)
        c = pltpu.make_async_copy(src[t], region(kinds[t], dst[t], me, 0, 4), local.at[t])
        c.start()
        staying[t] = c

    def second(t):
        got(t, 0)
        go(t, 3, side, 0, cuts[t], up)
        go(t, 4, side, 0, cuts[t], down)
        got(t, 1)
        go(t, 5, down, 2, 4, up)
        go(t, 9, down, cuts[t], 4, side)
        got(t, 2)
        go(t, 6, up, 0, 2, down)
        go(t, 10, up, cuts[t], 4, side)

    def third(t):
        got(t, 3)
        _, low, high = arrive(t, 7)
        go(t, 7, down ^ 2, low, high, up)
        got(t, 4)
        _, low, high = arrive(t, 8)
        go(t, 8, up ^ 2, low, high, down)
        got(t, 5)
        got(t, 6)
        go(t, 11, far, cuts[t], 4, side)

    def fourth(t):
        for item in range(7, 12):
            got(t, item)

    def finish(t):
        for item in range(12):
            owner, low, high = arrive(t, item)
            copy(t, 12 + item, owner ^ 1, low, high, core, 0, False).wait_recv()
        copy(t, 24, core, 0, 4, core, 0, False).wait_recv()

    tp_start(0)
    tp_start(1)
    for t in (0, 2):
        first(t)
    tp_all[0].relay()
    tp_all[1].relay()
    tp_wait(1)
    first(1)
    tp_wait(0)
    step = 32

    def normalize(i, carry):
        at = pl.ds(pl.multiple_of(i * step, step), step)
        n1[at, :] = rms_scale(x0[at, :].astype(f32), gain[...]).astype(bf16)
        return carry

    lax.fori_loop(0, rows // step, normalize, 0)
    gates[...] = masked_gates(dot(n1[...], router[...]), hot0[...] + hot1[...])

    second(0)
    second(2)
    second(1)
    first(3)
    third(0)
    third(2)
    third(1)
    first(4)
    first(5)
    fourth(0)
    fourth(2)
    fourth(1)

    def fetch(t, ref):
        finish(t)
        staying[t].wait()
        c = pltpu.make_async_copy(dst[t], ref, load.at[t])
        c.start()
        return c

    fetches = [fetch(0, w_kv), fetch(1, wide), fetch(2, w_q)]

    lane = lax.broadcasted_iota(jnp.int32, (rows, 128), 1)
    seq = lax.broadcasted_iota(jnp.int32, (rows, 128), 0) // half

    def rotary(x):
        return x * cosine[...] + pltpu.roll(x, HEAD_DIM // 2, 1) * sine[...]

    fetches[0].wait()
    fetches[1].wait()
    z = dot(n1[...], wide[:, 512:640])
    z_q[...] = jnp.where(lane // 64 == seq, z, 0.0).astype(bf16)
    z = dot(n1[...], wide[:, 640:704])
    z_kv[...] = jnp.where((lane // 16) % 2 == seq, jnp.pad(z, ((0, 0), (0, 64))), 0.0).astype(bf16)
    kv = dot(n1[...], w_kv[...]) + dot(z_kv[:, :64], b_kv[...])
    for h in range(heads):
        at = slice(HEAD_DIM * h, HEAD_DIM * h + HEAD_DIM)
        turned = rotary(kv[:, at]).astype(bf16)
        kv_all[PAST, 0, :, at] = turned[:half]
        kv_all[PAST, 1, :, at] = turned[half:]
    for s in range(2):
        kv_all[PAST, s, :, width:] = kv[half * s : half * s + half, width:].astype(bf16)

    def kv_copy(slot, back, to, to_back):
        return pltpu.make_async_remote_copy(
            src_ref=kv_all.at[PAST - back],
            dst_ref=kv_all.at[PAST - to_back],
            send_sem=kv_send.at[slot],
            recv_sem=kv_recv.at[to_back],
            device_id=(to, tp),
            device_id_type=MESH,
        )

    def kv_arrived(back):
        kv_copy(0, back, core, back).wait_recv()

    def when(condition, c):
        if condition is None:
            c.start()
        else:
            pl.when(condition)(c.start)
        kv_started.append((condition, c))

    kv_started = []
    when(None, kv_copy(0, 0, up, 4))
    when(None, kv_copy(1, 0, far, 8))
    when(on_side == 0, kv_copy(2, 0, side, 2))
    when(on_core == 0, kv_copy(3, 0, core, 1))
    second(3)
    first(6)
    first(7)

    fetches[2].wait()
    queries = [jnp.zeros((rows, width), f32), jnp.zeros((rows, width), f32)]
    for e in range(experts):
        z_e = jnp.where((lane % 64) // 16 == e, z_q[...].astype(f32), 0.0).astype(bf16)
        q_e = dot(n1[...], w_q[e]) + dot(z_e, b_q[...])
        for k, hot in enumerate((hot0, hot1)):
            queries[k] = queries[k] + jnp.where(hot[:, e : e + 1] > 0, q_e, 0.0)
    for k in range(2):
        for h in range(heads):
            turned = rotary(queries[k][:, HEAD_DIM * h : HEAD_DIM * h + HEAD_DIM]).astype(bf16)
            for s in range(2):
                q_all[s * heads + h, k * half : k * half + half, :] = turned[half * s : half * s + half]

    tp_start(2)
    second(4)
    kv_arrived(4)
    when(on_side == 0, kv_copy(4, 4, side, 6))
    when(on_side == 1, kv_copy(5, 4, side, 2))
    when(on_core == 0, kv_copy(6, 4, core, 5))
    when(on_core == 1, kv_copy(7, 4, core, 3))
    kv_arrived(8)
    when(on_side == 1, kv_copy(8, 8, side, 6))
    when(on_core == 1, kv_copy(9, 8, core, 7))
    first(8)
    second(5)
    kv_arrived(2)
    when(on_core == 0, kv_copy(10, 2, core, 3))
    when(on_core == 1, kv_copy(11, 2, core, 1))
    kv_arrived(6)
    when(on_core == 0, kv_copy(12, 6, core, 7))
    when(on_core == 1, kv_copy(13, 6, core, 5))
    third(3)
    first(9)
    for back in (1, 3, 5, 7):
        kv_arrived(back)
    tp_all[2].relay()
    second(6)

    row = lax.broadcasted_iota(jnp.int32, (half, span), 0)
    key = lax.broadcasted_iota(jnp.int32, (half, span), 1)
    near = (key > row) & (key <= row + PAST * half)

    def attend(i, carry):
        s = i // heads
        h = lax.rem(i, heads)
        at = pl.ds(pl.multiple_of(h * HEAD_DIM, HEAD_DIM), HEAD_DIM)
        v_at = pl.ds(pl.multiple_of(width + h * HEAD_DIM, HEAD_DIM), HEAD_DIM)
        keys = kv_all[:, s, :, at].reshape(span, HEAD_DIM)
        values = kv_all[:, s, :, v_at].reshape(span, HEAD_DIM)
        seq_rows = pl.ds(pl.multiple_of(s * half, half), half)
        allowed = near & (q_doc[seq_rows, :1] == k_doc[s, :1, :])
        for k in range(2):
            q = q_all[i, k * half : k * half + half, :]
            scores = dot_nt(q, keys) * HEAD_DIM**-0.5
            scores = jnp.where(allowed, scores, big_negative)
            peak = jnp.max(scores, axis=1, keepdims=True)
            powers = jnp.exp(scores - peak)
            p = (powers * (1.0 / jnp.sum(powers, axis=1, keepdims=True))).astype(bf16)
            probs[i, k * half : k * half + half, :] = p
            ob[k, seq_rows, at] = dot(p, values).astype(bf16)
        return carry

    lax.fori_loop(0, 2 * heads, attend, 0)
    fourth(3)
    third(4)
    fetches.append(fetch(3, w_o))

    fetches[3].wait()
    z_acc = jnp.zeros((rows, 256), f32)
    pair_lane = lax.broadcasted_iota(jnp.int32, (rows, 256), 1)
    mine = pair_lane // 128 == lax.broadcasted_iota(jnp.int32, (rows, 256), 0) // half
    chosen = []
    for e in range(experts):
        o_e = jnp.where(hot0[:, e : e + 1] > 0, ob[0].astype(f32), 0.0)
        o_e = o_e + jnp.where(hot1[:, e : e + 1] > 0, ob[1].astype(f32), 0.0)
        o_e = o_e.astype(bf16)
        chosen.append(o_e)
        low = dot_nt(o_e, a_o[...]) * gates[:, e : e + 1]
        z_acc = z_acc + jnp.where(mine & ((pair_lane % 128) // 16 == e), low, 0.0)
    z_acc = z_acc.astype(bf16)
    z_o[...] = z_acc[:, :128] + z_acc[:, 128:]

    def columns(ref, rank):
        return ref.at[:, pl.ds(pl.multiple_of(rank * part, part), part)]

    scatter = Scatter(parts, held, relay, sum_send, sum_recv, 0)
    spread = Spread(None, lambda rank: columns(attn, rank), sum_send, sum_recv, 1)
    for d in (5, 6, 7, 4, 1, 2, 3, 0):
        at = pl.ds(pl.multiple_of((tp ^ d) * part, part), part)
        total = dot_nt(z_acc, wide[at, 256:512])
        for e in range(experts):
            total = total + dot(chosen[e], w_o[e, :, at]) * gates[:, e : e + 1]
        if d:
            parts[d] = total.astype(bf16)
            if d != FAR:
                scatter.copy(d).start()
        else:
            own[...] = total
    second(7)
    scatter.relay()
    second(8)
    third(5)
    columns(attn, tp)[...] = scatter.total(own[...]).astype(bf16)
    spread.start()
    second(9)
    third(6)
    spread.relay()
    third(7)
    third(8)
    spread.wait()
    fourth(4)
    fourth(5)
    third(9)
    fourth(6)
    fourth(7)
    fourth(8)
    fourth(9)
    tp_wait(2)
    for t in range(4, len(kinds)):
        finish(t)
    for c in started:
        c.wait_send()
    for t, c in enumerate(staying):
        if t > 3:
            c.wait()
    for condition, c in kv_started:
        if condition is None:
            c.wait_send()
        else:
            pl.when(condition)(c.wait_send)
    scatter.sent()
    spread.sent()
    for c in tp_all:
        c.sent()


def attention(shards_in, tp_shards, small):
    s_q, s_kv, s_o, s_gu, s_d = shards_in
    tokens, cotangent, s_wide = tp_shards
    rows, part = tokens.shape
    model = part * N_TP
    experts, _, width = s_q.shape
    half = rows // 2
    heads = width // HEAD_DIM
    shape = jax.ShapeDtypeStruct

    def grown(a, d):
        return shape(tuple(n * (N_CTX if i == d else 1) for i, n in enumerate(a.shape)), a.dtype)

    gathered = (grown(s_q, 1), grown(s_kv, 0), grown(s_o, 2), grown(s_gu, 1), grown(s_d, 2))
    wide_mid = shape((s_wide.shape[0] * N_TP, s_wide.shape[1]), bf16)
    wide = grown(wide_mid, 0)
    vmem_out = (
        shape((rows, model), bf16),
        shape((rows, model), bf16),
        shape((rows, model), bf16),
        shape((PAST + 1, 2, half, 2 * width), bf16),
        shape((2 * heads, rows, HEAD_DIM), bf16),
        shape((2 * heads, rows, (PAST + 1) * half), bf16),
        shape((2, rows, width), bf16),
        shape((rows, 128), bf16),
        shape((rows, 128), bf16),
        shape((rows, 128), bf16),
        shape((rows, 128), f32),
    )
    any_out = gathered + (wide, wide_mid, shape((rows, model), bf16))
    return pl.pallas_call(
        attention_kernel,
        out_shape=any_out + vmem_out,
        in_specs=[ANY] * 8 + [VMEM] * len(small),
        out_specs=tuple([ANY] * len(any_out) + [VMEM] * len(vmem_out)),
        scratch_shapes=[
            pltpu.VMEM(gathered[0].shape, bf16),
            pltpu.VMEM(gathered[1].shape, bf16),
            pltpu.VMEM(gathered[2].shape, bf16),
            pltpu.VMEM(wide.shape, bf16),
            pltpu.VMEM((N_TP, rows, part), bf16),
            pltpu.VMEM((rows, part), bf16),
            pltpu.VMEM((rows, part), f32),
            pltpu.VMEM((N_TP, rows, part), bf16),
            pltpu.SemaphoreType.DMA((10, 25)),
            pltpu.SemaphoreType.DMA((10, 25)),
            pltpu.SemaphoreType.DMA((10,)),
            pltpu.SemaphoreType.DMA((3, N_TP)),
            pltpu.SemaphoreType.DMA((3, N_TP)),
            pltpu.SemaphoreType.DMA((3,)),
            pltpu.SemaphoreType.DMA((14,)),
            pltpu.SemaphoreType.DMA((PAST + 1,)),
            pltpu.SemaphoreType.DMA((4,)),
            pltpu.SemaphoreType.DMA((2, N_TP)),
            pltpu.SemaphoreType.DMA((2, N_TP)),
        ],
        compiler_params=pltpu.CompilerParams(
            collective_id=0, has_side_effects=True, vmem_limit_bytes=60 << 20
        ),
        name="attention",
    )(*shards_in, *tp_shards, *small)


def backward_kernel(
    dx1, dx1_own, ob, gates, z_q, z_kv, z_sum, table, gain, router, b_q, b_kv, a_o, ff_parts, ff_own,
    h_q, h_kv, h_o, h_wide, h_x0, h_n1, h_n2, h_dy, h_kv_all, h_q_all, h_probs,
    mixed, grad_tokens, wide_a, wide_b, heads_out,
    w_q, w_kv, w_o, wide, x0, n1, n2, dy, kv_all, q_all, probs, dob, dkv, dkv_held, dq, dkv_own, dn, parts, relay, own, held, ff_held, ff_relay,
    z_part, z_held, z_done, dots, tails, a_src, b_src, heads_src, a_core, b_core, heads_core, a_held, b_held, heads_held,
    load, tp_send, tp_recv, core_send, core_recv, kv_send, kv_recv, ctx_send, ctx_recv,
):
    me, tp = lax.axis_index("ctx"), lax.axis_index("tp")
    core = me ^ 1
    on_core = lax.rem(me, 2)
    rows, model = x0.shape
    cosine, sine, hot0, hot1 = (table.at[:, 128 * i : 128 * i + 128] for i in range(4))
    part = model // N_TP
    half = rows // 2
    experts = w_q.shape[0]
    width = w_q.shape[2]
    heads = width // HEAD_DIM
    span = (PAST + 1) * half
    loads = []
    for i, (h, w) in enumerate(
        (
            (h_wide, wide),
            (h_o, w_o),
            (h_kv_all, kv_all),
            (h_probs, probs),
            (h_q_all, q_all),
            (h_q, w_q),
            (h_n2, n2),
            (h_dy, dy),
            (h_n1, n1),
            (h_kv, w_kv),
            (h_x0, x0),
        )
    ):
        c = pltpu.make_async_copy(h, w, load.at[i])
        c.start()
        loads.append(c)
    greet([(me ^ d, tp) for d in range(1, N_CTX)] + [(me, tp ^ d) for d in range(1, N_TP)])
    a_sum = CtxSum(a_src, a_core, a_held, None, ctx_send, ctx_recv, 0)
    b_sum = CtxSum(b_src, b_core, b_held, None, ctx_send, ctx_recv, 1)
    heads_sum = CtxSum(heads_src, heads_core, heads_held, heads_out, ctx_send, ctx_recv, 2)
    ff = Scatter(ff_parts, ff_held, ff_relay, tp_send, tp_recv, 4)
    for d in (5, 6, 7, 1, 2, 3):
        ff.copy(d).start()

    lane = lax.broadcasted_iota(jnp.int32, (rows, 128), 1)
    seq = lax.broadcasted_iota(jnp.int32, (rows, 128), 0) // half
    hots = (hot0, hot1)

    loads[0].wait()
    pair_lane = lax.broadcasted_iota(jnp.int32, (rows, 256), 1)
    mine = pair_lane // 128 == lax.broadcasted_iota(jnp.int32, (rows, 256), 0) // half
    dz_o = dot(dx1[...], wide[:, 256:512])
    loads[1].wait()
    g = [jnp.zeros((rows, width), f32), jnp.zeros((rows, width), f32)]
    g_ao = jnp.zeros((256, width), f32)
    for e in range(experts):
        dz_e = jnp.where(mine & ((pair_lane % 128) // 16 == e), dz_o, 0.0)
        g_e = dot_nt(dx1[...], w_o[e]) + dot(dz_e.astype(bf16), a_o[...])
        o_e = jnp.where(hot0[:, e : e + 1] > 0, ob[0].astype(f32), 0.0)
        o_e = o_e + jnp.where(hot1[:, e : e + 1] > 0, ob[1].astype(f32), 0.0)
        o_e = o_e.astype(bf16)
        dz_e = (dz_e * gates[:, e : e + 1]).astype(bf16)
        g_ao = g_ao + dot_tn(dz_e, o_e)
        for k in range(2):
            g[k] = g[k] + jnp.where(hots[k][:, e : e + 1] > 0, g_e, 0.0)
    d_gates = jnp.zeros((rows, 128), f32)
    for k in range(2):
        d_gate = jnp.sum(g[k] * ob[k].astype(f32), axis=1, keepdims=True)
        d_gates = d_gates + jnp.where(hots[k][...] > 0, d_gate, 0.0)
        gate = jnp.sum(hots[k][...] * gates[...], axis=1, keepdims=True)
        d_out = (g[k] * gate).astype(bf16)
        for s in range(2):
            for h in range(heads):
                dob[s * heads + h, k * half : k * half + half, :] = d_out[
                    half * s : half * s + half, HEAD_DIM * h : HEAD_DIM * h + HEAD_DIM
                ]
    d_logits = gates[...] * (d_gates - jnp.sum(gates[...] * d_gates, axis=1, keepdims=True))
    d_logits = d_logits.astype(bf16)

    def attend_back(i, carry):
        s = i // heads
        h = lax.rem(i, heads)
        at = pl.ds(pl.multiple_of(h * HEAD_DIM, HEAD_DIM), HEAD_DIM)
        v_at = pl.ds(pl.multiple_of(width + h * HEAD_DIM, HEAD_DIM), HEAD_DIM)
        keys = kv_all[:, s, :, at].reshape(span, HEAD_DIM)
        values = kv_all[:, s, :, v_at].reshape(span, HEAD_DIM)
        seq_rows = pl.ds(pl.multiple_of(s * half, half), half)
        d_keys = jnp.zeros((span, HEAD_DIM), f32)
        d_values = jnp.zeros((span, HEAD_DIM), f32)
        for k in range(2):
            k_rows = slice(k * half, k * half + half)
            d_o = dob[i, k_rows, :]
            p = probs[i, k_rows, :]
            delta = jnp.sum(d_o.astype(f32) * ob[k, seq_rows, at].astype(f32), axis=1, keepdims=True)
            d_s = (p.astype(f32) * (dot_nt(d_o, values) - delta)).astype(bf16)
            d_q = dot(d_s, keys) * HEAD_DIM**-0.5
            turned = d_q * cosine[seq_rows, :] - pltpu.roll(d_q, HEAD_DIM // 2, 1) * sine[seq_rows, :]
            dq[k, seq_rows, at] = turned.astype(bf16)
            d_keys = d_keys + dot_tn(d_s, q_all[i, k_rows, :])
            d_values = d_values + dot_tn(p, d_o)
        d_keys = (d_keys * HEAD_DIM**-0.5).astype(bf16)
        dkv[:, s, :, at] = d_keys.reshape(PAST + 1, half, HEAD_DIM)
        dkv[:, s, :, v_at] = d_values.astype(bf16).reshape(PAST + 1, half, HEAD_DIM)
        return carry

    ff.relay()
    for i in (2, 3, 4):
        loads[i].wait()
    lax.fori_loop(0, 2 * heads, attend_back, 0)

    def to_core(back):
        return pltpu.make_async_remote_copy(
            src_ref=dkv.at[PAST - back],
            dst_ref=dkv_held.at[back // 2],
            send_sem=core_send.at[back // 2],
            recv_sem=core_recv.at[back // 2],
            device_id=(core, tp),
            device_id_type=MESH,
        )

    def to_owner(back):
        return pltpu.make_async_remote_copy(
            src_ref=dkv.at[PAST - back],
            dst_ref=dkv_held.at[3 + back // 2],
            send_sem=kv_send.at[back // 2],
            recv_sem=kv_recv.at[back // 2],
            device_id=(lax.rem(me + N_CTX - back, N_CTX), tp),
            device_id_type=MESH,
        )

    for back in (1, 3, 5, 7):
        to_core(back).start()
    for back in (1, 3, 5, 7):
        to_core(back).wait_recv()
        slot = PAST - (back - 1) - 2 * on_core
        dkv[slot] = (dkv[slot].astype(f32) + dkv_held[back // 2].astype(f32)).astype(bf16)
    for back in (2, 4, 6, 8):
        to_owner(back).start()

    mixed[...] = ff.total(ff_own[...]).astype(bf16)
    loads[5].wait()
    dz_q = jnp.zeros((rows, 128), f32)
    g_bq = jnp.zeros((128, width), f32)
    chosen = []
    for e in range(experts):
        dq_e = jnp.where(hot0[:, e : e + 1] > 0, dq[0].astype(f32), 0.0)
        dq_e = dq_e + jnp.where(hot1[:, e : e + 1] > 0, dq[1].astype(f32), 0.0)
        dq_e = dq_e.astype(bf16)
        chosen.append(dq_e)
        keep = (lane // 64 == seq) & ((lane % 64) // 16 == e)
        dz_q = dz_q + jnp.where(keep, dot_nt(dq_e, b_q[...]), 0.0)
        z_e = jnp.where(keep, z_q[...].astype(f32), 0.0).astype(bf16)
        g_bq = g_bq + dot_tn(z_e, dq_e)
    dz_q = dz_q.astype(bf16)
    z_part[:, :128] = dz_q
    for j in range(N_TP):
        at = slice(part * j, part * j + part)
        total = dot_nt(dz_q, wide[at, 512:640]) + dot_nt(d_logits, router[at, :])
        for e in range(experts):
            total = total + dot_nt(chosen[e], w_q[e, at, :])
        dn[j] = total
    for i in (6, 7, 8):
        loads[i].wait()
    own_columns = lax.broadcasted_iota(jnp.int32, (model, part), 1)
    own_columns = (own_columns // 16) * 128 + tp * 16 + own_columns % 16
    pick = (lax.broadcasted_iota(jnp.int32, (model, part), 0) == own_columns).astype(bf16)

    def to_pairs(ref, at, values):
        values = values.astype(bf16).reshape(8, 2, 16, values.shape[1])
        for c in range(2):
            ref[c, :, :, at] = values[:, c]

    n2_own = dot(n2[...], pick).astype(bf16)
    dx1_cols = dot(dx1[...], pick).astype(bf16)
    dy_own = dot(dy[...], pick).astype(bf16)
    n1_own = dot(n1[...], pick).astype(bf16)
    lane_m = lax.broadcasted_iota(jnp.int32, (part, 128), 1)
    for s in range(2):
        at = slice(half * s, half * s + half)
        to_pairs(a_src, slice(128 * s, 128 * s + 128), dot_tn(n2_own[at], z_sum[at, :128]))
        low = jnp.where(
            lane_m < 64, dot_tn(dx1_cols[at], z_sum[at, 128:]), dot_tn(dy_own[at], z_sum[at, 128:])
        )
        to_pairs(a_src, slice(256 + 128 * s, 384 + 128 * s), low)
    a_sum.start()

    total = dkv[PAST].astype(f32)
    for back in (2, 4, 6, 8):
        to_owner(back).wait_recv()
        total = total + dkv_held[3 + back // 2].astype(f32)
    a_sum.chips()
    for h in range(heads):
        at = slice(HEAD_DIM * h, HEAD_DIM * h + HEAD_DIM)
        d_k = jnp.concatenate([total[0, :, at], total[1, :, at]], axis=0)
        turned = d_k * cosine[...] - pltpu.roll(d_k, HEAD_DIM // 2, 1) * sine[...]
        dkv_own[:, at] = turned.astype(bf16)
    dkv_own[:, width:] = jnp.concatenate([total[0, :, width:], total[1, :, width:]], axis=0).astype(bf16)
    loads[9].wait()
    loads[10].wait()
    dz_kv = dot_nt(dkv_own[...], b_kv[...])
    keep = (lane[:, :64] // 16) % 2 == seq[:, :64]
    dz_kv = jnp.where(keep, dz_kv, 0.0).astype(bf16)
    z_part[:, 128:] = jnp.pad(dz_kv.astype(f32), ((0, 0), (0, 64))).astype(bf16)

    scatter = Scatter(parts, held, relay, tp_send, tp_recv, 0)
    z_rows = rows // N_TP

    def z_region(ref, rank):
        return ref.at[pl.ds(pl.multiple_of(rank * z_rows, z_rows), z_rows), :]

    def z_scatter(d):
        return pltpu.make_async_remote_copy(
            src_ref=z_region(z_part, tp ^ d),
            dst_ref=z_held.at[d],
            send_sem=tp_send.at[1, d],
            recv_sem=tp_recv.at[1, d],
            device_id=(me, tp ^ d),
            device_id_type=MESH,
        )

    def z_spread(d, rank):
        return pltpu.make_async_remote_copy(
            src_ref=z_region(z_done, rank),
            dst_ref=z_region(z_done, rank),
            send_sem=tp_send.at[2, d],
            recv_sem=tp_recv.at[2, d],
            device_id=(me, tp ^ d),
            device_id_type=MESH,
        )

    def tail(d, rank):
        return pltpu.make_async_remote_copy(
            src_ref=tails.at[rank],
            dst_ref=tails.at[rank],
            send_sem=tp_send.at[3, d],
            recv_sem=tp_recv.at[3, d],
            device_id=(me, tp ^ d),
            device_id_type=MESH,
        )

    for d in range(1, N_TP):
        z_scatter(d).start()
    g_bkv = dot_tn(z_kv[...], dkv_own[...])
    blocks = [g_bq[32 * i : 32 * i + 32] for i in range(4)] + [g_bkv[:32, :width], g_bkv[32:64, width:]]
    blocks += [g_ao[128 * s + 32 * i : 128 * s + 32 * i + 32] for s in range(2) for i in range(2)]
    blocks += [jnp.zeros((32, width), f32)] * 6
    for i in range(N_CTX):
        heads_src[i % 2, i // 2] = blocks[i].astype(bf16)
    heads_sum.start()
    along = jnp.zeros((rows, 1), f32)
    for d in (5, 6, 7, 4, 1, 2, 3, 0):
        peer = tp ^ d
        at = pl.ds(pl.multiple_of(peer * part, part), part)
        total = dn[peer] + dot_nt(dz_kv, wide[at, 640:704]) + dot_nt(dkv_own[...], w_kv[at, :])
        scaled = total * gain[:, at]
        along = along + jnp.sum(scaled * x0[:, at].astype(f32), axis=1, keepdims=True)
        if d:
            parts[d] = total.astype(bf16)
            if d != FAR:
                scatter.copy(d).start()
        else:
            own[...] = total
    dots[...] = jnp.broadcast_to(along, dots.shape)
    tails[tp] = jnp.transpose(dots[...])[:8, :]
    for d in range(1, N_TP):
        tail(d, tp).start()
    total = z_region(z_part, tp)[...].astype(f32)
    for d in range(1, N_TP):
        z_scatter(d).wait_recv()
        total = total + z_held[d].astype(f32)
    z_region(z_done, tp)[...] = total.astype(bf16)
    for d in range(1, N_TP):
        z_spread(d, tp).start()
    heads_sum.chips()
    scatter.relay()
    for d in range(1, N_TP):
        z_spread(d, tp ^ d).wait_recv()
    to_pairs(b_src, slice(0, part), dot_tn(n1_own, z_done[...]))
    b_sum.start()
    heads_sum.again()
    total = scatter.total(own[...])
    b_sum.chips()
    for d in range(1, N_TP):
        tail(d, tp ^ d).wait_recv()
    whole = tails[0]
    for d in range(1, N_TP):
        whole = whole + tails[d]
    dots[...] = jnp.transpose(jnp.broadcast_to(whole[:1], (128, rows)))
    own_at = pl.ds(pl.multiple_of(tp * part, part), part)
    own[...] = total * gain[:, own_at]
    step = 32

    def finish(i, carry):
        at = pl.ds(pl.multiple_of(i * step, step), step)
        x = x0[at, :].astype(f32)
        inverse = lax.rsqrt(jnp.mean(x * x, axis=1, keepdims=True) + eps)
        mean = dots[at, :1] * (1.0 / model)
        back = inverse * own[at, :] - x0[at, own_at].astype(f32) * inverse**3 * mean
        grad_tokens[at, :] = (dx1_own[at, :] + back).astype(bf16)
        return carry

    lax.fori_loop(0, rows // step, finish, 0)
    wide_a[...] = a_sum.total()
    heads_sum.other_core()
    wide_b[...] = b_sum.total()
    heads_sum.finish()
    for back in (1, 3, 5, 7):
        to_core(back).wait_send()
        to_owner(back + 1).wait_send()
    scatter.sent()
    ff.sent()
    for d in range(1, N_TP):
        z_scatter(d).wait_send()
        z_spread(d, tp).wait_send()
        tail(d, tp).wait_send()


def backward(vmem, hbm):
    dx1 = vmem[0]
    w_q, w_kv, w_o, wide, x0, n1, n2, dy, kv_all, q_all, probs = hbm
    rows, model = dx1.shape
    part = model // N_TP
    width = w_q.shape[2]
    heads = width // HEAD_DIM
    half = rows // 2
    shape = jax.ShapeDtypeStruct
    reduced = [(2, 8, 16, 512), (2, 8, 16, part), (2, 8, 32, width)]
    return pl.pallas_call(
        backward_kernel,
        out_shape=(
            shape((rows, part), bf16),
            shape((rows, part), bf16),
            shape((16, 512), f32),
            shape((16, part), f32),
            shape(reduced[2], bf16),
        ),
        in_specs=[VMEM] * len(vmem) + [ANY] * len(hbm),
        out_specs=tuple([VMEM] * 5),
        scratch_shapes=[
            pltpu.VMEM(a.shape, bf16) for a in hbm
        ]
        + [
            pltpu.VMEM((2 * heads, rows, HEAD_DIM), bf16),
            pltpu.VMEM(kv_all.shape, bf16),
            pltpu.VMEM((8,) + kv_all.shape[1:], bf16),
            pltpu.VMEM((2, rows, width), bf16),
            pltpu.VMEM((rows, 2 * width), bf16),
            pltpu.VMEM((N_TP, rows, part), f32),
            pltpu.VMEM((N_TP, rows, part), bf16),
            pltpu.VMEM((rows, part), bf16),
            pltpu.VMEM((rows, part), f32),
            pltpu.VMEM((N_TP, rows, part), bf16),
            pltpu.VMEM((N_TP, rows, part), bf16),
            pltpu.VMEM((rows, part), bf16),
            pltpu.VMEM((rows, 256), bf16),
            pltpu.VMEM((N_TP, rows // N_TP, 256), bf16),
            pltpu.VMEM((rows, 256), bf16),
            pltpu.VMEM((rows, 128), f32),
            pltpu.VMEM((N_TP, 8, rows), f32),
        ]
        + [pltpu.VMEM(a, bf16) for a in reduced]
        + [pltpu.VMEM(a[1:], bf16) for a in reduced + reduced]
        + [
            pltpu.SemaphoreType.DMA((len(hbm),)),
            pltpu.SemaphoreType.DMA((5, N_TP)),
            pltpu.SemaphoreType.DMA((5, N_TP)),
            pltpu.SemaphoreType.DMA((4,)),
            pltpu.SemaphoreType.DMA((4,)),
            pltpu.SemaphoreType.DMA((5,)),
            pltpu.SemaphoreType.DMA((5,)),
            pltpu.SemaphoreType.DMA((3, 16)),
            pltpu.SemaphoreType.DMA((3, 16)),
        ],
        compiler_params=pltpu.CompilerParams(
            collective_id=3, has_side_effects=True, vmem_limit_bytes=60 << 20
        ),
        name="backward",
    )(*vmem, *hbm)


def shards(
    tokens,
    norm1_gain,
    router_attn,
    w_query,
    w_key_value,
    w_out,
    norm2_gain,
    router_ffn,
    w_gate_up,
    w_down,
    adapt_wide,
    adapt_heads,
    adapt_ffn,
    attention_routes,
    feedforward_routes,
    doc_lengths,
    adapter_index,
    cotangent,
):
    seqs, block, part = tokens.shape
    rows = seqs * block
    n_tp = lax.axis_size("tp")
    model = part * n_tp
    experts = w_query.shape[0]
    width = w_query.shape[2]
    heads = width // HEAD_DIM
    hidden = w_down.shape[1]
    rank = adapt_heads.shape[2]
    wide_slots = adapt_wide.shape[1]
    ctx_rank = lax.axis_index("ctx")


    def by_sequence(a):
        return jnp.where(adapter_index[0] == 0, a, a[::-1])

    wide_own = by_sequence(adapt_wide.astype(bf16))
    groups = [[6, 10, 7, 11, 8, 12, 9, 13], list(range(14, 22)), [0, 1, 2, 3], [4, 5]]
    order = [(q, s) for g in groups[:3] for q in range(seqs) for s in g]
    order += [(q, s) for s in groups[3] for q in range(seqs)]
    wide_cols = wide_own.reshape(seqs * wide_slots, rank, -1)[
        np.array([q * wide_slots + s for q, s in order])
    ].reshape(seqs * wide_slots * rank, -1).T
    heads_low = by_sequence(adapt_heads.astype(bf16))
    ffn_low = by_sequence(adapt_ffn.astype(bf16))
    route_a = attention_routes.reshape(rows, -1)
    route_f = feedforward_routes.reshape(rows, -1)

    positions = ctx_rank * block + jnp.arange(block, dtype=jnp.int32)
    doc_ids, offsets = doc_layout(doc_lengths, positions)
    half = HEAD_DIM // 2
    frequency = 10000.0 ** (-2.0 * jnp.arange(half, dtype=f32) / HEAD_DIM)
    angles = offsets.astype(f32).reshape(rows)[:, None] * frequency
    cosine, sine = jnp.cos(angles), jnp.sin(angles)
    cosine = jnp.concatenate([cosine, cosine], axis=1)
    sine = jnp.concatenate([-sine, sine], axis=1)

    b_q, b_kv, a_o = heads_low[:, :experts], heads_low[:, experts : experts + 2], heads_low[:, experts + 2 :]
    key_pos = (ctx_rank - PAST) * block + jnp.arange((PAST + 1) * block, dtype=jnp.int32)
    key_doc = doc_layout(doc_lengths, jnp.maximum(key_pos, 0))[0]
    key_doc = jnp.where(key_pos[None, :] >= 0, key_doc, -(1 << 20))
    blank = jnp.zeros((seqs, rank, width), bf16)
    b_kv_wide = jnp.concatenate(
        [
            jnp.concatenate([b_kv[:, 0], blank], axis=-1).reshape(seqs * rank, 2 * width),
            jnp.concatenate([blank, b_kv[:, 1]], axis=-1).reshape(seqs * rank, 2 * width),
        ],
        axis=0,
    )
    a_o_wide = jnp.pad(a_o.reshape(seqs, experts * rank, width), ((0, 0), (0, 64), (0, 0))).reshape(256, width)
    b_q = b_q.reshape(seqs * experts * rank, width)
    table = jnp.concatenate(
        [
            cosine,
            sine,
            widen_routes(route_a[:, :1], experts),
            widen_routes(route_a[:, 1:], experts),
            widen_routes(route_f, experts),
            jnp.broadcast_to(doc_ids.reshape(rows, 1).astype(f32), (rows, 128)),
        ],
        axis=1,
    )
    router_wide = jnp.pad(router_attn, ((0, 0), (0, 128 - experts)))
    (
        w_query, w_key_value, w_out, w_gate_up, w_down, wide, _, dy,
        x0, sum_out, n1, kv_all, q_all, probs, ob, z_o_gated, z_q, z_kv, gates,
    ) = attention(
        [
            w_query,
            w_key_value.reshape(-1, 2 * width),
            w_out,
            gate_up_columns(w_gate_up[:, :, 0], w_gate_up[:, :, 1]),
            w_down,
        ],
        [tokens.reshape(rows, part), cotangent.reshape(rows, part), wide_cols],
        [
            norm1_gain[None],
            router_wide,
            table,
            jnp.broadcast_to(key_doc[:, None, :], (seqs, 8, key_doc.shape[1])).astype(f32),
            b_q,
            b_kv_wide,
            a_o_wide,
        ],
    )
    blank = jnp.zeros((seqs, experts, rank, hidden), bf16)
    b_gu = jnp.stack(
        [gate_up_columns(ffn_low[:, :experts], blank), gate_up_columns(blank, ffn_low[:, experts : 2 * experts])],
        axis=2,
    ).reshape(seqs, 2 * experts * rank, 2 * hidden)
    a_d = jnp.pad(ffn_low[:, 2 * experts :].reshape(seqs, experts * rank, hidden), ((0, 0), (64, 0), (0, 0)))
    ff_parts, ff_own, dx1b, dx1_own, n2, z_sum, gu_sum, d_sum = feed_forward(
        x0, sum_out, dy, norm2_gain[None], wide,
        jnp.pad(router_ffn, ((0, 0), (0, 128 - experts))),
        table, b_gu.reshape(256, 2 * hidden), a_d.reshape(256, hidden), z_o_gated, w_gate_up, w_down,
    )
    mixed, grad_tokens, wide_a, wide_b, head_sum = backward(
        [
            dx1b, dx1_own, ob, gates, z_q, z_kv, z_sum, table, norm1_gain[None], router_wide, b_q, b_kv_wide, a_o_wide, ff_parts, ff_own,
        ],
        [w_query, w_key_value, w_out, wide, x0, n1, n2, dy, kv_all, q_all, probs],
    )
    grad_wide = jnp.concatenate([wide_a, wide_b[:, : 704 - 512]], axis=1).T
    back_order = np.argsort(np.array([q * wide_slots + s for q, s in order]))
    grad_wide = grad_wide.reshape(seqs * wide_slots, rank, -1)[back_order]
    grad_wide = by_sequence(grad_wide.reshape(seqs, wide_slots, rank, -1))
    head_sum = jnp.swapaxes(head_sum, 0, 1).reshape(-1, rank, width).astype(f32)
    grad_heads = by_sequence(jnp.concatenate(
        [
            head_sum[: seqs * experts].reshape(seqs, experts, rank, width),
            jnp.swapaxes(head_sum[8:12].reshape(2, seqs, rank, width), 0, 1),
            head_sum[12:20].reshape(seqs, experts, rank, width),
        ],
        axis=1,
    ))
    gu_sum = jnp.swapaxes(gu_sum, 0, 1).reshape(seqs, experts, 2, rank, 768).astype(f32)
    grad_ffn = by_sequence(jnp.concatenate(
        [
            gu_sum[:, :, 0, :, :704],
            jnp.concatenate([gu_sum[:, :, 1, :, :640], gu_sum[:, :, 1, :, 704:]], axis=-1),
            jnp.swapaxes(d_sum, 0, 1).reshape(seqs, experts, rank, hidden),
        ],
        axis=1,
    ))
    mixed = mixed.reshape(seqs, block, part)
    grad_tokens = grad_tokens.reshape(seqs, block, part)
    return (mixed, grad_tokens, grad_wide, grad_heads, grad_ffn)


def solution(mesh):
    placed = (
        P(None, "ctx", "tp"),
        P(),
        P(),
        P(None, "ctx", "tp"),
        P("ctx", None, "tp"),
        P(None, "tp", "ctx"),
        P(),
        P(),
        P(None, "ctx", None, "tp"),
        P(None, "tp", "ctx"),
        P(None, None, None, ("ctx", "tp")),
        P(None, None, None, "tp"),
        P(None, None, None, "tp"),
        P(None, "ctx", None),
        P(None, "ctx", None),
        P(),
        P(),
        P(None, "ctx", "tp"),
    )
    return jax.shard_map(
        shards,
        mesh=mesh,
        in_specs=placed,
        out_specs=(
            P(None, "ctx", "tp"),
            P(None, "ctx", "tp"),
            P(None, None, None, ("ctx", "tp")),
            P(None, None, None, "tp"),
            P(None, None, None, "tp"),
        ),
        check_vma=False,
    )
```

```python
import functools

import jax
import numpy as np
import jax.numpy as jnp
from jax import lax
from jax.experimental import pallas as pl
from jax.experimental.pallas import tpu as pltpu
from jax.sharding import PartitionSpec as P

HEAD_DIM = 128
WINDOW = 1024
eps = 1e-06
big_negative = -1e30
bf16 = jnp.bfloat16
f32 = jnp.float32

MESH = pl.DeviceIdType.MESH
ANY = pl.BlockSpec(memory_space=pl.ANY)
VMEM = pl.BlockSpec(memory_space=pltpu.VMEM)
N_CTX, N_TP = 16, 8
FAR = 4
PAST = 8


def region(kind, ref, owner, low, high):
    rows = pl.ds(pl.multiple_of(owner * 128 + 32 * low, 32), 32 * (high - low))
    cols = pl.ds(pl.multiple_of(owner * 128, 128), 128)
    if kind == "rows":
        return ref.at[pl.ds(low, high - low), cols, :]
    if kind == "flat":
        return ref.at[rows, :]
    if kind == "cols":
        return ref.at[pl.ds(low, high - low), :, cols]
    if high - low == 1:
        half = ref.shape[1] // 2
        return ref.at[low // 2, pl.ds(half * (low % 2), half), cols]
    return ref.at[pl.ds(low // 2, (high - low) // 2), :, cols]


def own_part(kind, ref, low, high):
    if kind == "flat":
        return ref.at[pl.ds(32 * low, 32 * (high - low)), :]
    if kind == "pair":
        return ref
    return ref.at[pl.ds(low, high - low)]


def tp_part(kind, ref, rank, size):
    if kind == "cols":
        return ref.at[:, pl.ds(pl.multiple_of(rank * size, size), size)]
    return ref.at[pl.ds(pl.multiple_of(rank * size, size), size), :]


def rms_scale(values, gain):
    return values * lax.rsqrt(jnp.mean(values * values, axis=-1, keepdims=True) + eps) * gain


def doc_layout(doc_lengths, positions):
    docs = doc_lengths.shape[1]
    upto = np.tril(np.ones((docs, docs), np.int32))
    ends = jnp.sum(doc_lengths[:, None, :] * upto[None], axis=2)
    passed = positions[None, :, None] >= ends[:, None, :]
    doc_ids = jnp.sum(passed.astype(jnp.int32), axis=2)
    starting = jnp.sum(jnp.where(passed, doc_lengths[:, None, :], 0), axis=2)
    inside = positions[None, :] < ends[:, -1:]
    doc_ids = jnp.where(inside, doc_ids, -1 - positions[None, :])
    return (doc_ids, positions[None, :] - starting)


def dot(a, b, ca=1, cb=0):
    return lax.dot_general(a, b, (((ca,), (cb,)), ((), ())), preferred_element_type=f32)


class Scatter:
    def __init__(self, parts, held, relay, send, recv, row):
        self.me, self.tp = lax.axis_index("ctx"), lax.axis_index("tp")
        self.parts, self.held, self.relay_buffer = parts, held, relay
        self.send, self.recv, self.row = send, recv, row

    def copy_to(self, d, to):
        return pltpu.make_async_remote_copy(
            src_ref=self.parts.at[d],
            dst_ref=self.held.at[d],
            send_sem=self.send.at[self.row, d],
            recv_sem=self.recv.at[self.row, d],
            device_id=(self.me, self.tp ^ to),
            device_id_type=MESH,
        )

    def copy(self, d):
        if d != FAR:
            return self.copy_to(d, d % FAR)
        return pltpu.make_async_remote_copy(
            src_ref=self.relay_buffer,
            dst_ref=self.held.at[FAR],
            send_sem=self.send.at[self.row, FAR],
            recv_sem=self.recv.at[self.row, FAR],
            device_id=(self.me, self.tp ^ FAR),
            device_id_type=MESH,
        )

    def relay(self):
        total = self.parts[FAR].astype(f32)
        for d in range(FAR + 1, N_TP):
            self.copy(d).wait_recv()
            total = total + self.held[d].astype(f32)
        self.relay_buffer[...] = total.astype(bf16)
        self.copy(FAR).start()

    def total(self, own):
        for d in range(1, FAR + 1):
            self.copy(d).wait_recv()
            own = own + self.held[d].astype(f32)
        return own

    def sent(self):
        for d in range(1, N_TP):
            self.copy(d).wait_send()


class Spread:
    def __init__(self, source, place, send, recv, row):
        self.me, self.tp = lax.axis_index("ctx"), lax.axis_index("tp")
        self.source, self.place = source, place
        self.send, self.recv, self.row = send, recv, row

    def copy(self, d, owner, to, source=None):
        return pltpu.make_async_remote_copy(
            src_ref=self.place(owner) if source is None else source,
            dst_ref=self.place(owner),
            send_sem=self.send.at[self.row, d],
            recv_sem=self.recv.at[self.row, d],
            device_id=(self.me, self.tp ^ to),
            device_id_type=MESH,
        )

    def start(self):
        for d in (FAR, 1, 2, 3):
            self.copy(d, self.tp, d, self.source).start()

    def relay(self):
        self.copy(FAR, self.tp ^ FAR, FAR).wait_recv()
        for d in (1, 2, 3):
            self.copy(FAR + d, self.tp ^ FAR, d).start()

    def wait(self):
        for d in (1, 2, 3):
            self.copy(d, self.tp ^ d, d).wait_recv()
            self.copy(FAR + d, self.tp ^ (FAR + d), d).wait_recv()

    def sent(self):
        for d in (FAR, 1, 2, 3):
            self.copy(d, self.tp, d, self.source).wait_send()
        for d in (1, 2, 3):
            self.copy(FAR + d, self.tp ^ FAR, d).wait_send()


class CtxSum:
    def __init__(self, source, core_held, held, out, send, recv, row):
        self.me, self.tp = lax.axis_index("ctx"), lax.axis_index("tp")
        self.core, self.chip = lax.rem(self.me, 2), self.me // 2
        self.source, self.core_held, self.held, self.out = source, core_held, held, out
        self.send, self.recv, self.row = send, recv, row

    def copy(self, item, src, dst, to):
        return pltpu.make_async_remote_copy(
            src_ref=src,
            dst_ref=dst,
            send_sem=self.send.at[self.row, item],
            recv_sem=self.recv.at[self.row, item],
            device_id=(to, self.tp),
            device_id_type=MESH,
        )

    def to_core(self):
        return self.copy(0, self.source.at[1 - self.core], self.core_held, self.me ^ 1)

    def to_chip(self, d):
        return self.copy(
            d, self.source.at[self.core, self.chip ^ d], self.held.at[d], self.me ^ (2 * d)
        )

    def spread(self, d, chip):
        there = self.out.at[self.core, chip]
        return self.copy(7 + d, there, there, self.me ^ (2 * d))

    def back_to_core(self, core):
        return self.copy(15, self.out.at[core], self.out.at[core], self.me ^ 1)

    def start(self):
        self.to_core().start()

    def chips(self):
        self.to_core().wait()
        self.source[self.core] = (
            self.source[self.core].astype(f32) + self.core_held[...].astype(f32)
        ).astype(self.source.dtype)
        for d in range(1, 8):
            self.to_chip(d).start()

    def total(self):
        total = self.source[self.core, self.chip].astype(f32)
        for d in range(1, 8):
            self.to_chip(d).wait_recv()
            total = total + self.held[d].astype(f32)
        for d in range(1, 8):
            self.to_chip(d).wait_send()
        return total

    def again(self):
        self.out[self.core, self.chip] = self.total().astype(self.out.dtype)
        for d in range(1, 8):
            self.spread(d, self.chip).start()

    def other_core(self):
        for d in range(1, 8):
            self.spread(d, self.chip ^ d).wait_recv()
            self.spread(d, self.chip).wait_send()
        self.back_to_core(self.core).start()

    def finish(self):
        self.back_to_core(1 - self.core).wait_recv()
        self.back_to_core(self.core).wait_send()


def dot_nt(a, b):
    return dot(a, b, 1, 1)


def dot_tn(a, b):
    return dot(a, b, 0, 0)


def by_seq(rows, f):
    half = rows.shape[0] // 2
    return jnp.concatenate([f(0, rows[:half]), f(1, rows[half:])], axis=0)


def column_of(values, lane, e):
    return jnp.sum(jnp.where(lane == e, values, 0.0), axis=1, keepdims=True)


def greet(targets):
    barrier = pltpu.get_barrier_semaphore()
    for device in targets:
        pl.semaphore_signal(barrier, inc=1, device_id=device, device_id_type=MESH)
    pl.semaphore_wait(barrier, len(targets))


def masked_gates(logits, hot):
    largest = jnp.max(jnp.where(hot > 0, logits, big_negative), axis=1, keepdims=True)
    powers = jnp.where(hot > 0, jnp.exp(logits - largest), 0.0)
    return powers / jnp.sum(powers, axis=1, keepdims=True)


def ffn_kernel(
    x0, attn, dy, gain, wide, router, table, b_gu, a_d, z_o, w_gu_hbm, w_d_hbm,
    ff_parts, ff_own, dx1, dx1_own, n2, z_sum, gu_out, d_out,
    w_gu, w_d, hg, dgu, dh_tmp, z_gu, dz_d, z_part, parts, relay, own, held, z_held, dots, tails, inverse,
    g_gu, g_d, gu_src, gu_core, gu_held, d_src, d_core, d_held,
    load, send, recv, ctx_send, ctx_recv,
):
    me, tp = lax.axis_index("ctx"), lax.axis_index("tp")
    hot = table.at[:, 512:640]
    rows, model = x0.shape
    experts = w_gu.shape[0]
    part = model // N_TP
    greet([(me ^ d, tp) for d in range(1, N_CTX)] + [(me, tp ^ d) for d in range(1, N_TP)])

    def fetch(e):
        return (
            pltpu.make_async_copy(w_gu_hbm.at[e], w_gu.at[e], load.at[0, e]),
            pltpu.make_async_copy(w_d_hbm.at[e], w_d.at[e], load.at[1, e]),
        )

    for e in range(experts):
        for c in fetch(e):
            c.start()

    step = 32

    def normalize(i, carry):
        at = pl.ds(pl.multiple_of(i * step, step), step)
        x = x0[at, :].astype(f32) + attn[at, :].astype(f32)
        r = lax.rsqrt(jnp.mean(x * x, axis=1, keepdims=True) + eps)
        inverse[at, :] = jnp.broadcast_to(r, (step, 128))
        n2[at, :] = (x * r * gain[...]).astype(bf16)
        return carry

    lax.fori_loop(0, rows // step, normalize, 0)
    lane = lax.broadcasted_iota(jnp.int32, (rows, 128), 1)
    gates = masked_gates(dot(n2[...], router[...]), hot[...])
    pair_lane = lax.broadcasted_iota(jnp.int32, (rows, 256), 1)
    mine = pair_lane // 128 == lax.broadcasted_iota(jnp.int32, (rows, 256), 0) // (rows // 2)
    pair_lane = pair_lane % 128
    z_gu[...] = jnp.where(mine, dot(n2[...], wide[:, :256]), 0.0).astype(bf16)
    dz_d[...] = jnp.where(mine, dot(dy[...], wide[:, 256:512]), 0.0).astype(bf16)
    g_gu[...] = jnp.zeros_like(g_gu)
    g_d[...] = jnp.zeros_like(g_d)
    zero = jnp.zeros((rows, 256), f32)

    def expert(e, carry):
        d_gates, dz_gu, z_d = carry
        for c in fetch(e):
            c.wait()
        gate = column_of(gates, lane, e)
        z_in = jnp.where(pair_lane // 32 == e, z_gu[...].astype(f32), 0.0).astype(bf16)
        dz_in = jnp.where(pair_lane // 16 == 4 + e, dz_d[...].astype(f32), 0.0).astype(bf16)
        dh_tmp[:, :704] = dot_nt(dy[...], w_d[e]) + dot(dz_in, a_d[...])
        pre = dot(n2[...], w_gu[e]) + dot(z_in, b_gu[...])

        def tile(g, u, d):
            sg = jax.nn.sigmoid(g)
            silu = g * sg
            h = silu * u
            dg = d * gate
            return h, (dg * u * sg * (1.0 + g * (1.0 - sg))), dg * silu, h * d

        h, dgp, dup, hd = tile(pre[:, :640], pre[:, 640:1280], dh_tmp[:, :640])
        hg[e, :, :640] = (h * gate).astype(bf16)
        dgu[e, :, :640] = dgp.astype(bf16)
        dgu[e, :, 640:1280] = dup.astype(bf16)
        dgf = jnp.sum(hd, axis=1, keepdims=True)
        last = pre[:, 1280:]
        h, dgp, dup, hd = tile(last, pltpu.roll(last, 64, 1), dh_tmp[:, 640:])
        hg[e, :, 640:] = (h * gate).astype(bf16)[:, :64]
        dgu[e, :, 1280:] = jnp.where(lane < 64, dgp, pltpu.roll(dup, 64, 1)).astype(bf16)
        dgf = dgf + jnp.sum(jnp.where(lane < 64, hd, 0.0), axis=1, keepdims=True)
        d_gates = d_gates + jnp.where(lane == e, dgf, 0.0)
        keep = mine & (pair_lane // 32 == e)
        dz_gu = dz_gu + jnp.where(keep, dot_nt(dgu[e], b_gu[...]), 0.0)
        keep = mine & (pair_lane // 16 == 4 + e)
        z_d = z_d + jnp.where(keep, dot_nt(hg[e], a_d[...]), 0.0)
        g_gu[...] += dot_tn(z_in, dgu[e])
        g_d[...] += dot_tn(dz_in, hg[e])
        return d_gates, dz_gu, z_d

    d_gates, dz_gu, z_d = lax.fori_loop(
        0, experts, expert, (jnp.zeros((rows, 128), f32), zero, zero)
    )
    d_logits = gates * (d_gates - jnp.sum(gates * d_gates, axis=1, keepdims=True))
    d_logits = d_logits.astype(bf16)
    dz_gu, z_d = dz_gu.astype(bf16), z_d.astype(bf16)
    z_part[:, :128] = dz_gu[:, :128] + dz_gu[:, 128:]
    z_part[:, 128:] = z_o[...] + z_d[:, :128] + z_d[:, 128:]

    for i in range(N_CTX):
        s, slot = i // 8, i % 8
        at = slice(128 * s + 16 * slot, 128 * s + 16 * slot + 16)
        cols = 640 * (slot % 2)
        gu_src[i % 2, i // 2, :, :640] = g_gu[at, cols : cols + 640].astype(bf16)
        gu_src[i % 2, i // 2, :, 640:] = g_gu[at, 1280:].astype(bf16)
        first = 128 * s + 64 + 8 * slot
        d_src[i % 2, i // 2] = g_d[first : first + 8, :]
    gu_sum = CtxSum(gu_src, gu_core, gu_held, gu_out, ctx_send, ctx_recv, 0)
    d_sum = CtxSum(d_src, d_core, d_held, d_out, ctx_send, ctx_recv, 1)
    gu_sum.start()
    d_sum.start()
    scatter = Scatter(parts, held, relay, send, recv, 0)

    def x_at(at):
        return x0[:, at].astype(f32) + attn[:, at].astype(f32)

    def piece(j, along):
        d = lax.rem(j + FAR + 1, N_TP)
        peer = tp ^ d
        at = pl.ds(pl.multiple_of(peer * part, part), part)
        w_rows = wide[at, :256]
        dn = dot_nt(d_logits, router[at, :])
        dn = dn + dot_nt(dz_gu, w_rows)
        for e in range(experts):
            dn = dn + dot_nt(dgu[e], w_gu[e, at, :])
        parts[d] = dn.astype(bf16)

        @pl.when((d != 0) & (d != FAR))
        def _():
            scatter.copy_to(d, lax.rem(d, FAR)).start()

        @pl.when(d == 0)
        def _():
            own[...] = dn

        return along + jnp.sum(dn * gain[:, at] * x_at(at), axis=1, keepdims=True)

    def out_piece(d, carry):
        peer = tp ^ d
        at = pl.ds(pl.multiple_of(peer * part, part), part)
        w_rows = wide[at, 256:512]
        ff = dot_nt(z_d, w_rows)
        for e in range(experts):
            ff = ff + dot(hg[e], w_d[e, :, at])
        ff_parts[d] = ff.astype(bf16)

        @pl.when(d == 0)
        def _():
            ff_own[...] = ff + x_at(at)

        return carry

    z_rows = rows // N_TP

    def z_region(ref, rank):
        return ref.at[pl.ds(pl.multiple_of(rank * z_rows, z_rows), z_rows), :]

    def z_scatter(d):
        return pltpu.make_async_remote_copy(
            src_ref=z_region(z_part, tp ^ d),
            dst_ref=z_held.at[d],
            send_sem=send.at[2, d],
            recv_sem=recv.at[2, d],
            device_id=(me, tp ^ d),
            device_id_type=MESH,
        )

    def z_spread(d, rank):
        return pltpu.make_async_remote_copy(
            src_ref=z_region(z_sum, rank),
            dst_ref=z_region(z_sum, rank),
            send_sem=send.at[3, d],
            recv_sem=recv.at[3, d],
            device_id=(me, tp ^ d),
            device_id_type=MESH,
        )

    def columns(ref, rank):
        return ref.at[:, pl.ds(pl.multiple_of(rank * part, part), part)]

    def tail(d, rank):
        return pltpu.make_async_remote_copy(
            src_ref=tails.at[rank],
            dst_ref=tails.at[rank],
            send_sem=send.at[5, d],
            recv_sem=recv.at[5, d],
            device_id=(me, tp ^ d),
            device_id_type=MESH,
        )

    along = lax.fori_loop(0, N_TP, piece, jnp.zeros((rows, 1), f32))
    dots[...] = jnp.broadcast_to(along, dots.shape)
    tails[tp] = jnp.transpose(dots[...])[:8, :]
    for d in range(1, N_TP):
        tail(d, tp).start()
        z_scatter(d).start()
    scatter.relay()
    gu_sum.chips()
    d_sum.chips()
    lax.fori_loop(0, N_TP, out_piece, 0)
    at = pl.ds(pl.multiple_of(tp * part, part), part)
    total = scatter.total(own[...]) * gain[:, at]
    for d in range(1, N_TP):
        tail(d, tp ^ d).wait_recv()
    whole = tails[0]
    for d in range(1, N_TP):
        whole = whole + tails[d]
    dots[...] = jnp.transpose(jnp.broadcast_to(whole[:1], (128, rows)))
    r = inverse[:, :1]
    total = dy[:, at].astype(f32) + r * total - x_at(at) * r**3 * (dots[:, :1] * (1.0 / model))
    dx1_own[...] = total
    columns(dx1, tp)[...] = total.astype(bf16)
    spread = Spread(None, lambda rank: columns(dx1, rank), send, recv, 4)
    spread.start()
    gu_sum.again()
    d_sum.again()
    total = z_region(z_part, tp)[...].astype(f32)
    for d in range(1, N_TP):
        z_scatter(d).wait_recv()
        total = total + z_held[d].astype(f32)
    z_region(z_sum, tp)[...] = total.astype(bf16)
    for d in range(1, N_TP):
        z_spread(d, tp).start()
    spread.relay()
    gu_sum.other_core()
    d_sum.other_core()
    spread.wait()
    gu_sum.finish()
    d_sum.finish()
    scatter.sent()
    spread.sent()
    for d in range(1, N_TP):
        z_scatter(d).wait_send()
        z_spread(d, tp ^ d).wait_recv()
        z_spread(d, tp).wait_send()
        tail(d, tp).wait_send()


def feed_forward(x0, attn, dy, gain, wide, router, table, b_gu, a_d, z_o, w_gu, w_d):
    rows, model = x0.shape
    part = model // N_TP
    experts, _, cols = w_gu.shape
    hidden = w_d.shape[1]
    shape = jax.ShapeDtypeStruct
    return pl.pallas_call(
        ffn_kernel,
        out_shape=(
            shape((N_TP, rows, part), bf16),
            shape((rows, part), f32),
            shape((rows, model), bf16),
            shape((rows, part), f32),
            shape((rows, model), bf16),
            shape((rows, 256), bf16),
            shape((2, 8, 16, 768), bf16),
            shape((2, 8, 8, hidden), f32),
        ),
        in_specs=[VMEM] * 10 + [ANY] * 2,
        out_specs=tuple([VMEM] * 8),
        scratch_shapes=[
            pltpu.VMEM(w_gu.shape, bf16),
            pltpu.VMEM(w_d.shape, bf16),
            pltpu.VMEM((experts, rows, hidden), bf16),
            pltpu.VMEM((experts, rows, cols), bf16),
            pltpu.VMEM((rows, 768), f32),
            pltpu.VMEM((rows, 256), bf16),
            pltpu.VMEM((rows, 256), bf16),
            pltpu.VMEM((rows, 256), bf16),
            pltpu.VMEM((N_TP, rows, part), bf16),
            pltpu.VMEM((rows, part), bf16),
            pltpu.VMEM((rows, part), f32),
            pltpu.VMEM((N_TP, rows, part), bf16),
            pltpu.VMEM((N_TP, rows // N_TP, 256), bf16),
            pltpu.VMEM((rows, 128), f32),
            pltpu.VMEM((N_TP, 8, rows), f32),
            pltpu.VMEM((rows, 128), f32),
            pltpu.VMEM(b_gu.shape, f32),
            pltpu.VMEM(a_d.shape, f32),
            pltpu.VMEM((2, 8, 16, 768), bf16),
            pltpu.VMEM((8, 16, 768), bf16),
            pltpu.VMEM((8, 16, 768), bf16),
            pltpu.VMEM((2, 8, 8, hidden), f32),
            pltpu.VMEM((8, 8, hidden), f32),
            pltpu.VMEM((8, 8, hidden), f32),
            pltpu.SemaphoreType.DMA((2, experts)),
            pltpu.SemaphoreType.DMA((6, N_TP)),
            pltpu.SemaphoreType.DMA((6, N_TP)),
            pltpu.SemaphoreType.DMA((2, 16)),
            pltpu.SemaphoreType.DMA((2, 16)),
        ],
        compiler_params=pltpu.CompilerParams(
            collective_id=2, has_side_effects=True, vmem_limit_bytes=63 << 20
        ),
        name="feed_forward",
    )(x0, attn, dy, gain, wide, router, table, b_gu, a_d, z_o, w_gu, w_d)


def widen_routes(routes, experts):
    lane = jnp.arange(128, dtype=jnp.int32)
    return jnp.sum((routes[..., None] == lane).astype(f32), axis=1)


def gate_up_columns(gate, up):
    def put(part, before, after):
        sides = [(0, 0, 0)] * (part.ndim - 1) + [(before, after, 0)]
        return lax.pad(part, jnp.zeros((), part.dtype), sides)

    return (
        put(gate[..., :640], 0, 768) + put(up[..., :640], 640, 128)
    ) + (put(gate[..., 640:], 1280, 64) + put(up[..., 640:], 1344, 0))


def attention_kernel(
    s_q, s_kv, s_o, s_gu, s_d, tokens, cotangent, s_wide,
    gain, router, table, k_doc, b_q, b_kv, a_o,
    g_q, g_kv, g_o, g_gu, g_d, g_wide, wide_mid, dy,
    x0, attn, n1, kv_all, q_all, probs, ob, z_o, z_q, z_kv, gates,
    w_q, w_kv, w_o, wide, parts, relay, own, held,
    send, recv, local, tp_send, tp_recv, tp_local, kv_send, kv_recv, load, sum_send, sum_recv,
):
    me, tp = lax.axis_index("ctx"), lax.axis_index("tp")
    core, side = me ^ 1, me ^ 2
    up, down, far = lax.rem(me + 4, 16), lax.rem(me + 12, 16), lax.rem(me + 8, 16)
    on_core, on_side = lax.rem(me, 2), lax.rem(me // 2, 2)
    cosine, sine, hot0, hot1 = (table.at[:, 128 * i : 128 * i + 128] for i in range(4))
    q_doc = table.at[:, 640:768]
    rows, model = x0.shape
    part = model // N_TP
    half = rows // 2
    experts = w_q.shape[0]
    width = w_q.shape[2]
    heads = width // HEAD_DIM
    span = (PAST + 1) * half
    greet([(d, tp) for d in (core, side, up, down, far)] + [(me, tp ^ d) for d in range(1, N_TP)])

    kinds = ["flat", "flat", "rows", "cols"] + ["flat"] * experts + ["pair"] * (experts // 2)
    src = [s_kv, wide_mid, s_q, s_o] + [s_gu.at[e] for e in range(experts)]
    dst = [g_kv, g_wide, g_q, g_o] + [g_gu.at[e] for e in range(experts)]
    src += [s_d.at[pl.ds(e, 2)] for e in range(0, experts, 2)]
    dst += [g_d.at[pl.ds(e, 2)] for e in range(0, experts, 2)]
    tp_src, tp_dst, tp_kinds = [tokens, s_wide, cotangent], [x0, wide_mid, dy], ["cols", "rows", "cols"]
    started, staying = [], [None] * len(kinds)
    counter = [0] * len(kinds)

    def place_of(i):
        size = tp_src[i].shape[1 if tp_kinds[i] == "cols" else 0]
        return lambda rank: tp_part(tp_kinds[i], tp_dst[i], rank, size)

    tp_all = [Spread(tp_src[i], place_of(i), tp_send, tp_recv, i) for i in range(3)]

    def tp_own(i):
        return pltpu.make_async_copy(tp_src[i], place_of(i)(tp), tp_local.at[i])

    def tp_start(i):
        tp_all[i].start()
        tp_own(i).start()

    def tp_wait(i):
        tp_all[i].wait()
        tp_own(i).wait()

    def copy(t, item, owner, low, high, to, slot, own_shard):
        there = region(kinds[t], dst[t], owner, low, high)
        return pltpu.make_async_remote_copy(
            src_ref=own_part(kinds[t], src[t], low, high) if own_shard else there,
            dst_ref=there,
            send_sem=send.at[t, slot],
            recv_sem=recv.at[t, item],
            device_id=(to, tp),
            device_id_type=MESH,
        )

    def go(t, item, owner, low, high, to, own_shard=False):
        c = copy(t, item, owner, low, high, to, counter[t], own_shard)
        counter[t] += 1
        c.start()
        started.append(c)

    cuts = [2, 2, 3, 3, 3, 3, 3, 2, 2, 2]

    def arrive(t, item):
        cut = cuts[t]
        mid = cut // 2 if t % 2 else (cut + 1) // 2
        return {
            0: (side, 0, 4),
            1: (down, 0, 4),
            2: (up, 0, 4),
            3: (down ^ 2, 0, cut),
            4: (up ^ 2, 0, cut),
            5: (far, 2, 4),
            6: (far, 0, 2),
            7: (far ^ 2, mid, cut),
            8: (far ^ 2, 0, mid),
            9: (down ^ 2, cut, 4),
            10: (up ^ 2, cut, 4),
            11: (far ^ 2, cut, 4),
        }[item]

    def got(t, item):
        owner, low, high = arrive(t, item)
        copy(t, item, owner, low, high, core, 0, False).wait_recv()
        go(t, 12 + item, owner, low, high, core)

    def first(t):
        go(t, 0, me, 0, 4, side, True)
        go(t, 2, me, 0, 4, down, True)
        go(t, 1, me, 0, 4, up, True)
        go(t, 24, me, 0, 4, core, True)
        c = pltpu.make_async_copy(src[t], region(kinds[t], dst[t], me, 0, 4), local.at[t])
        c.start()
        staying[t] = c

    def second(t):
        got(t, 0)
        go(t, 3, side, 0, cuts[t], up)
        go(t, 4, side, 0, cuts[t], down)
        got(t, 1)
        go(t, 5, down, 2, 4, up)
        go(t, 9, down, cuts[t], 4, side)
        got(t, 2)
        go(t, 6, up, 0, 2, down)
        go(t, 10, up, cuts[t], 4, side)

    def third(t):
        got(t, 3)
        _, low, high = arrive(t, 7)
        go(t, 7, down ^ 2, low, high, up)
        got(t, 4)
        _, low, high = arrive(t, 8)
        go(t, 8, up ^ 2, low, high, down)
        got(t, 5)
        got(t, 6)
        go(t, 11, far, cuts[t], 4, side)

    def fourth(t):
        for item in range(7, 12):
            got(t, item)

    def finish(t):
        for item in range(12):
            owner, low, high = arrive(t, item)
            copy(t, 12 + item, owner ^ 1, low, high, core, 0, False).wait_recv()
        copy(t, 24, core, 0, 4, core, 0, False).wait_recv()

    tp_start(1)
    tp_start(0)
    for t in (0, 2):
        first(t)
    tp_all[1].relay()
    tp_all[0].relay()
    tp_wait(1)
    first(1)
    second(0)
    second(2)
    first(3)
    second(1)
    tp_wait(0)
    step = 32

    def normalize(i, carry):
        at = pl.ds(pl.multiple_of(i * step, step), step)
        n1[at, :] = rms_scale(x0[at, :].astype(f32), gain[...]).astype(bf16)
        return carry

    lax.fori_loop(0, rows // step, normalize, 0)
    gates[...] = masked_gates(dot(n1[...], router[...]), hot0[...] + hot1[...])

    third(0)
    third(2)
    third(1)
    first(4)
    first(5)
    fourth(0)
    fourth(2)
    fourth(1)

    def fetch(t, ref):
        finish(t)
        staying[t].wait()
        c = pltpu.make_async_copy(dst[t], ref, load.at[t])
        c.start()
        return c

    fetches = [fetch(0, w_kv), fetch(1, wide), fetch(2, w_q)]

    lane = lax.broadcasted_iota(jnp.int32, (rows, 128), 1)
    seq = lax.broadcasted_iota(jnp.int32, (rows, 128), 0) // half

    def rotary(x):
        return x * cosine[...] + pltpu.roll(x, HEAD_DIM // 2, 1) * sine[...]

    fetches[0].wait()
    fetches[1].wait()
    z = dot(n1[...], wide[:, 512:640])
    z_q[...] = jnp.where(lane // 64 == seq, z, 0.0).astype(bf16)
    z = dot(n1[...], wide[:, 640:704])
    z_kv[...] = jnp.where((lane // 16) % 2 == seq, jnp.pad(z, ((0, 0), (0, 64))), 0.0).astype(bf16)
    kv = dot(n1[...], w_kv[...]) + dot(z_kv[:, :64], b_kv[...])
    for h in range(heads):
        at = slice(HEAD_DIM * h, HEAD_DIM * h + HEAD_DIM)
        turned = rotary(kv[:, at]).astype(bf16)
        kv_all[PAST, 0, :, at] = turned[:half]
        kv_all[PAST, 1, :, at] = turned[half:]
    for s in range(2):
        kv_all[PAST, s, :, width:] = kv[half * s : half * s + half, width:].astype(bf16)

    def kv_copy(slot, back, to, to_back):
        return pltpu.make_async_remote_copy(
            src_ref=kv_all.at[PAST - back],
            dst_ref=kv_all.at[PAST - to_back],
            send_sem=kv_send.at[slot],
            recv_sem=kv_recv.at[to_back],
            device_id=(to, tp),
            device_id_type=MESH,
        )

    def kv_arrived(back):
        kv_copy(0, back, core, back).wait_recv()

    def when(condition, c):
        if condition is None:
            c.start()
        else:
            pl.when(condition)(c.start)
        kv_started.append((condition, c))

    kv_started = []
    when(None, kv_copy(0, 0, up, 4))
    when(None, kv_copy(1, 0, far, 8))
    when(on_side == 0, kv_copy(2, 0, side, 2))
    when(on_core == 0, kv_copy(3, 0, core, 1))
    second(3)
    first(6)
    first(7)

    fetches[2].wait()
    queries = [jnp.zeros((rows, width), f32), jnp.zeros((rows, width), f32)]
    for e in range(experts):
        z_e = jnp.where((lane % 64) // 16 == e, z_q[...].astype(f32), 0.0).astype(bf16)
        q_e = dot(n1[...], w_q[e]) + dot(z_e, b_q[...])
        for k, hot in enumerate((hot0, hot1)):
            queries[k] = queries[k] + jnp.where(hot[:, e : e + 1] > 0, q_e, 0.0)
    for k in range(2):
        for h in range(heads):
            turned = rotary(queries[k][:, HEAD_DIM * h : HEAD_DIM * h + HEAD_DIM]).astype(bf16)
            for s in range(2):
                q_all[s * heads + h, k * half : k * half + half, :] = turned[half * s : half * s + half]

    tp_start(2)
    second(4)
    kv_arrived(4)
    when(on_side == 0, kv_copy(4, 4, side, 6))
    when(on_side == 1, kv_copy(5, 4, side, 2))
    when(on_core == 0, kv_copy(6, 4, core, 5))
    when(on_core == 1, kv_copy(7, 4, core, 3))
    kv_arrived(8)
    when(on_side == 1, kv_copy(8, 8, side, 6))
    when(on_core == 1, kv_copy(9, 8, core, 7))
    first(8)
    second(5)
    kv_arrived(2)
    when(on_core == 0, kv_copy(10, 2, core, 3))
    when(on_core == 1, kv_copy(11, 2, core, 1))
    kv_arrived(6)
    when(on_core == 0, kv_copy(12, 6, core, 7))
    when(on_core == 1, kv_copy(13, 6, core, 5))
    third(3)
    first(9)
    for back in (1, 3, 5, 7):
        kv_arrived(back)
    tp_all[2].relay()
    second(6)

    row = lax.broadcasted_iota(jnp.int32, (half, span), 0)
    key = lax.broadcasted_iota(jnp.int32, (half, span), 1)
    near = (key > row) & (key <= row + PAST * half)

    def attend(i, carry):
        s = i // heads
        h = lax.rem(i, heads)
        at = pl.ds(pl.multiple_of(h * HEAD_DIM, HEAD_DIM), HEAD_DIM)
        v_at = pl.ds(pl.multiple_of(width + h * HEAD_DIM, HEAD_DIM), HEAD_DIM)
        keys = kv_all[:, s, :, at].reshape(span, HEAD_DIM)
        values = kv_all[:, s, :, v_at].reshape(span, HEAD_DIM)
        seq_rows = pl.ds(pl.multiple_of(s * half, half), half)
        allowed = near & (q_doc[seq_rows, :1] == k_doc[s, :1, :])
        for k in range(2):
            q = q_all[i, k * half : k * half + half, :]
            scores = dot_nt(q, keys) * HEAD_DIM**-0.5
            scores = jnp.where(allowed, scores, big_negative)
            peak = jnp.max(scores, axis=1, keepdims=True)
            powers = jnp.exp(scores - peak)
            p = (powers * (1.0 / jnp.sum(powers, axis=1, keepdims=True))).astype(bf16)
            probs[i, k * half : k * half + half, :] = p
            ob[k, seq_rows, at] = dot(p, values).astype(bf16)
        return carry

    lax.fori_loop(0, 2 * heads, attend, 0)
    fourth(3)
    third(4)
    fetches.append(fetch(3, w_o))

    fetches[3].wait()
    z_acc = jnp.zeros((rows, 256), f32)
    pair_lane = lax.broadcasted_iota(jnp.int32, (rows, 256), 1)
    mine = pair_lane // 128 == lax.broadcasted_iota(jnp.int32, (rows, 256), 0) // half
    chosen = []
    for e in range(experts):
        o_e = jnp.where(hot0[:, e : e + 1] > 0, ob[0].astype(f32), 0.0)
        o_e = o_e + jnp.where(hot1[:, e : e + 1] > 0, ob[1].astype(f32), 0.0)
        o_e = o_e.astype(bf16)
        chosen.append(o_e)
        low = dot_nt(o_e, a_o[...]) * gates[:, e : e + 1]
        z_acc = z_acc + jnp.where(mine & ((pair_lane % 128) // 16 == e), low, 0.0)
    z_acc = z_acc.astype(bf16)
    z_o[...] = z_acc[:, :128] + z_acc[:, 128:]

    def columns(ref, rank):
        return ref.at[:, pl.ds(pl.multiple_of(rank * part, part), part)]

    scatter = Scatter(parts, held, relay, sum_send, sum_recv, 0)
    spread = Spread(None, lambda rank: columns(attn, rank), sum_send, sum_recv, 1)
    for d in (5, 6, 7, 4, 1, 2, 3, 0):
        at = pl.ds(pl.multiple_of((tp ^ d) * part, part), part)
        total = dot_nt(z_acc, wide[at, 256:512])
        for e in range(experts):
            total = total + dot(chosen[e], w_o[e, :, at]) * gates[:, e : e + 1]
        if d:
            parts[d] = total.astype(bf16)
            if d != FAR:
                scatter.copy(d).start()
        else:
            own[...] = total
    second(7)
    scatter.relay()
    second(8)
    third(5)
    columns(attn, tp)[...] = scatter.total(own[...]).astype(bf16)
    spread.start()
    second(9)
    third(6)
    spread.relay()
    third(7)
    third(8)
    spread.wait()
    fourth(4)
    fourth(5)
    third(9)
    fourth(6)
    fourth(7)
    fourth(8)
    fourth(9)
    tp_wait(2)
    for t in range(4, len(kinds)):
        finish(t)
    for c in started:
        c.wait_send()
    for t, c in enumerate(staying):
        if t > 3:
            c.wait()
    for condition, c in kv_started:
        if condition is None:
            c.wait_send()
        else:
            pl.when(condition)(c.wait_send)
    scatter.sent()
    spread.sent()
    for c in tp_all:
        c.sent()


def attention(shards_in, tp_shards, small):
    s_q, s_kv, s_o, s_gu, s_d = shards_in
    tokens, cotangent, s_wide = tp_shards
    rows, part = tokens.shape
    model = part * N_TP
    experts, _, width = s_q.shape
    half = rows // 2
    heads = width // HEAD_DIM
    shape = jax.ShapeDtypeStruct

    def grown(a, d):
        return shape(tuple(n * (N_CTX if i == d else 1) for i, n in enumerate(a.shape)), a.dtype)

    gathered = (grown(s_q, 1), grown(s_kv, 0), grown(s_o, 2), grown(s_gu, 1), grown(s_d, 2))
    wide_mid = shape((s_wide.shape[0] * N_TP, s_wide.shape[1]), bf16)
    wide = grown(wide_mid, 0)
    vmem_out = (
        shape((rows, model), bf16),
        shape((rows, model), bf16),
        shape((rows, model), bf16),
        shape((PAST + 1, 2, half, 2 * width), bf16),
        shape((2 * heads, rows, HEAD_DIM), bf16),
        shape((2 * heads, rows, (PAST + 1) * half), bf16),
        shape((2, rows, width), bf16),
        shape((rows, 128), bf16),
        shape((rows, 128), bf16),
        shape((rows, 128), bf16),
        shape((rows, 128), f32),
    )
    any_out = gathered + (wide, wide_mid, shape((rows, model), bf16))
    return pl.pallas_call(
        attention_kernel,
        out_shape=any_out + vmem_out,
        in_specs=[ANY] * 8 + [VMEM] * len(small),
        out_specs=tuple([ANY] * len(any_out) + [VMEM] * len(vmem_out)),
        scratch_shapes=[
            pltpu.VMEM(gathered[0].shape, bf16),
            pltpu.VMEM(gathered[1].shape, bf16),
            pltpu.VMEM(gathered[2].shape, bf16),
            pltpu.VMEM(wide.shape, bf16),
            pltpu.VMEM((N_TP, rows, part), bf16),
            pltpu.VMEM((rows, part), bf16),
            pltpu.VMEM((rows, part), f32),
            pltpu.VMEM((N_TP, rows, part), bf16),
            pltpu.SemaphoreType.DMA((10, 25)),
            pltpu.SemaphoreType.DMA((10, 25)),
            pltpu.SemaphoreType.DMA((10,)),
            pltpu.SemaphoreType.DMA((3, N_TP)),
            pltpu.SemaphoreType.DMA((3, N_TP)),
            pltpu.SemaphoreType.DMA((3,)),
            pltpu.SemaphoreType.DMA((14,)),
            pltpu.SemaphoreType.DMA((PAST + 1,)),
            pltpu.SemaphoreType.DMA((4,)),
            pltpu.SemaphoreType.DMA((2, N_TP)),
            pltpu.SemaphoreType.DMA((2, N_TP)),
        ],
        compiler_params=pltpu.CompilerParams(
            collective_id=0, has_side_effects=True, vmem_limit_bytes=60 << 20
        ),
        name="attention",
    )(*shards_in, *tp_shards, *small)


def backward_kernel(
    dx1, dx1_own, ob, gates, z_q, z_kv, z_sum, table, gain, router, b_q, b_kv, a_o, ff_parts, ff_own,
    h_q, h_kv, h_o, h_wide, h_x0, h_n1, h_n2, h_dy, h_kv_all, h_q_all, h_probs,
    mixed, grad_tokens, wide_a, wide_b, heads_out,
    w_q, w_kv, w_o, wide, x0, n1, n2, dy, kv_all, q_all, probs, dob, dkv, dkv_held, dq, dkv_own, dn, parts, relay, own, held, ff_held, ff_relay,
    z_part, z_held, z_done, dots, tails, a_src, b_src, heads_src, a_core, b_core, heads_core, a_held, b_held, heads_held,
    load, tp_send, tp_recv, core_send, core_recv, kv_send, kv_recv, ctx_send, ctx_recv,
):
    me, tp = lax.axis_index("ctx"), lax.axis_index("tp")
    core = me ^ 1
    on_core = lax.rem(me, 2)
    rows, model = x0.shape
    cosine, sine, hot0, hot1 = (table.at[:, 128 * i : 128 * i + 128] for i in range(4))
    part = model // N_TP
    half = rows // 2
    experts = w_q.shape[0]
    width = w_q.shape[2]
    heads = width // HEAD_DIM
    span = (PAST + 1) * half
    loads = []
    for i, (h, w) in enumerate(
        (
            (h_wide, wide),
            (h_o, w_o),
            (h_kv_all, kv_all),
            (h_probs, probs),
            (h_q_all, q_all),
            (h_q, w_q),
            (h_n2, n2),
            (h_dy, dy),
            (h_n1, n1),
            (h_kv, w_kv),
            (h_x0, x0),
        )
    ):
        c = pltpu.make_async_copy(h, w, load.at[i])
        c.start()
        loads.append(c)
    greet([(me ^ d, tp) for d in range(1, N_CTX)] + [(me, tp ^ d) for d in range(1, N_TP)])
    a_sum = CtxSum(a_src, a_core, a_held, None, ctx_send, ctx_recv, 0)
    b_sum = CtxSum(b_src, b_core, b_held, None, ctx_send, ctx_recv, 1)
    heads_sum = CtxSum(heads_src, heads_core, heads_held, heads_out, ctx_send, ctx_recv, 2)
    ff = Scatter(ff_parts, ff_held, ff_relay, tp_send, tp_recv, 4)
    for d in (5, 6, 7, 1, 2, 3):
        ff.copy(d).start()

    lane = lax.broadcasted_iota(jnp.int32, (rows, 128), 1)
    seq = lax.broadcasted_iota(jnp.int32, (rows, 128), 0) // half
    hots = (hot0, hot1)

    loads[0].wait()
    pair_lane = lax.broadcasted_iota(jnp.int32, (rows, 256), 1)
    mine = pair_lane // 128 == lax.broadcasted_iota(jnp.int32, (rows, 256), 0) // half
    dz_o = dot(dx1[...], wide[:, 256:512])
    loads[1].wait()
    g = [jnp.zeros((rows, width), f32), jnp.zeros((rows, width), f32)]
    g_ao = jnp.zeros((256, width), f32)
    for e in range(experts):
        dz_e = jnp.where(mine & ((pair_lane % 128) // 16 == e), dz_o, 0.0)
        g_e = dot_nt(dx1[...], w_o[e]) + dot(dz_e.astype(bf16), a_o[...])
        o_e = jnp.where(hot0[:, e : e + 1] > 0, ob[0].astype(f32), 0.0)
        o_e = o_e + jnp.where(hot1[:, e : e + 1] > 0, ob[1].astype(f32), 0.0)
        o_e = o_e.astype(bf16)
        dz_e = (dz_e * gates[:, e : e + 1]).astype(bf16)
        g_ao = g_ao + dot_tn(dz_e, o_e)
        for k in range(2):
            g[k] = g[k] + jnp.where(hots[k][:, e : e + 1] > 0, g_e, 0.0)
    d_gates = jnp.zeros((rows, 128), f32)
    for k in range(2):
        d_gate = jnp.sum(g[k] * ob[k].astype(f32), axis=1, keepdims=True)
        d_gates = d_gates + jnp.where(hots[k][...] > 0, d_gate, 0.0)
        gate = jnp.sum(hots[k][...] * gates[...], axis=1, keepdims=True)
        d_out = (g[k] * gate).astype(bf16)
        for s in range(2):
            for h in range(heads):
                dob[s * heads + h, k * half : k * half + half, :] = d_out[
                    half * s : half * s + half, HEAD_DIM * h : HEAD_DIM * h + HEAD_DIM
                ]
    d_logits = gates[...] * (d_gates - jnp.sum(gates[...] * d_gates, axis=1, keepdims=True))
    d_logits = d_logits.astype(bf16)

    def attend_back(i, carry):
        s = i // heads
        h = lax.rem(i, heads)
        at = pl.ds(pl.multiple_of(h * HEAD_DIM, HEAD_DIM), HEAD_DIM)
        v_at = pl.ds(pl.multiple_of(width + h * HEAD_DIM, HEAD_DIM), HEAD_DIM)
        keys = kv_all[:, s, :, at].reshape(span, HEAD_DIM)
        values = kv_all[:, s, :, v_at].reshape(span, HEAD_DIM)
        seq_rows = pl.ds(pl.multiple_of(s * half, half), half)
        d_keys = jnp.zeros((span, HEAD_DIM), f32)
        d_values = jnp.zeros((span, HEAD_DIM), f32)
        for k in range(2):
            k_rows = slice(k * half, k * half + half)
            d_o = dob[i, k_rows, :]
            p = probs[i, k_rows, :]
            delta = jnp.sum(d_o.astype(f32) * ob[k, seq_rows, at].astype(f32), axis=1, keepdims=True)
            d_s = (p.astype(f32) * (dot_nt(d_o, values) - delta)).astype(bf16)
            d_q = dot(d_s, keys) * HEAD_DIM**-0.5
            turned = d_q * cosine[seq_rows, :] - pltpu.roll(d_q, HEAD_DIM // 2, 1) * sine[seq_rows, :]
            dq[k, seq_rows, at] = turned.astype(bf16)
            d_keys = d_keys + dot_tn(d_s, q_all[i, k_rows, :])
            d_values = d_values + dot_tn(p, d_o)
        d_keys = (d_keys * HEAD_DIM**-0.5).astype(bf16)
        dkv[:, s, :, at] = d_keys.reshape(PAST + 1, half, HEAD_DIM)
        dkv[:, s, :, v_at] = d_values.astype(bf16).reshape(PAST + 1, half, HEAD_DIM)
        return carry

    for i in (2, 3, 4):
        loads[i].wait()
    lax.fori_loop(0, 2 * heads, attend_back, 0)

    def to_core(back):
        return pltpu.make_async_remote_copy(
            src_ref=dkv.at[PAST - back],
            dst_ref=dkv_held.at[back // 2],
            send_sem=core_send.at[back // 2],
            recv_sem=core_recv.at[back // 2],
            device_id=(core, tp),
            device_id_type=MESH,
        )

    def to_owner(back):
        return pltpu.make_async_remote_copy(
            src_ref=dkv.at[PAST - back],
            dst_ref=dkv_held.at[3 + back // 2],
            send_sem=kv_send.at[back // 2],
            recv_sem=kv_recv.at[back // 2],
            device_id=(lax.rem(me + N_CTX - back, N_CTX), tp),
            device_id_type=MESH,
        )

    for back in (1, 3, 5, 7):
        to_core(back).start()
    for back in (1, 3, 5, 7):
        to_core(back).wait_recv()
        slot = PAST - (back - 1) - 2 * on_core
        dkv[slot] = (dkv[slot].astype(f32) + dkv_held[back // 2].astype(f32)).astype(bf16)
    for back in (2, 4, 6, 8):
        to_owner(back).start()

    ff.relay()
    loads[5].wait()
    dz_q = jnp.zeros((rows, 128), f32)
    g_bq = jnp.zeros((128, width), f32)
    chosen = []
    for e in range(experts):
        dq_e = jnp.where(hot0[:, e : e + 1] > 0, dq[0].astype(f32), 0.0)
        dq_e = dq_e + jnp.where(hot1[:, e : e + 1] > 0, dq[1].astype(f32), 0.0)
        dq_e = dq_e.astype(bf16)
        chosen.append(dq_e)
        keep = (lane // 64 == seq) & ((lane % 64) // 16 == e)
        dz_q = dz_q + jnp.where(keep, dot_nt(dq_e, b_q[...]), 0.0)
        z_e = jnp.where(keep, z_q[...].astype(f32), 0.0).astype(bf16)
        g_bq = g_bq + dot_tn(z_e, dq_e)
    dz_q = dz_q.astype(bf16)
    z_part[:, :128] = dz_q
    for j in range(N_TP):
        at = slice(part * j, part * j + part)
        total = dot_nt(dz_q, wide[at, 512:640]) + dot_nt(d_logits, router[at, :])
        for e in range(experts):
            total = total + dot_nt(chosen[e], w_q[e, at, :])
        dn[j] = total
    for i in (6, 7, 8):
        loads[i].wait()
    own_columns = lax.broadcasted_iota(jnp.int32, (model, part), 1)
    own_columns = (own_columns // 16) * 128 + tp * 16 + own_columns % 16
    pick = (lax.broadcasted_iota(jnp.int32, (model, part), 0) == own_columns).astype(bf16)

    def to_pairs(ref, at, values):
        values = values.astype(bf16).reshape(8, 2, 16, values.shape[1])
        for c in range(2):
            ref[c, :, :, at] = values[:, c]

    n2_own = dot(n2[...], pick).astype(bf16)
    dx1_cols = dot(dx1[...], pick).astype(bf16)
    dy_own = dot(dy[...], pick).astype(bf16)
    n1_own = dot(n1[...], pick).astype(bf16)
    lane_m = lax.broadcasted_iota(jnp.int32, (part, 128), 1)
    for s in range(2):
        at = slice(half * s, half * s + half)
        to_pairs(a_src, slice(128 * s, 128 * s + 128), dot_tn(n2_own[at], z_sum[at, :128]))
        low = jnp.where(
            lane_m < 64, dot_tn(dx1_cols[at], z_sum[at, 128:]), dot_tn(dy_own[at], z_sum[at, 128:])
        )
        to_pairs(a_src, slice(256 + 128 * s, 384 + 128 * s), low)
    a_sum.start()

    total = dkv[PAST].astype(f32)
    for back in (2, 4, 6, 8):
        to_owner(back).wait_recv()
        total = total + dkv_held[3 + back // 2].astype(f32)
    a_sum.chips()
    for h in range(heads):
        at = slice(HEAD_DIM * h, HEAD_DIM * h + HEAD_DIM)
        d_k = jnp.concatenate([total[0, :, at], total[1, :, at]], axis=0)
        turned = d_k * cosine[...] - pltpu.roll(d_k, HEAD_DIM // 2, 1) * sine[...]
        dkv_own[:, at] = turned.astype(bf16)
    dkv_own[:, width:] = jnp.concatenate([total[0, :, width:], total[1, :, width:]], axis=0).astype(bf16)
    loads[9].wait()
    loads[10].wait()
    dz_kv = dot_nt(dkv_own[...], b_kv[...])
    keep = (lane[:, :64] // 16) % 2 == seq[:, :64]
    dz_kv = jnp.where(keep, dz_kv, 0.0).astype(bf16)
    z_part[:, 128:] = jnp.pad(dz_kv.astype(f32), ((0, 0), (0, 64))).astype(bf16)

    scatter = Scatter(parts, held, relay, tp_send, tp_recv, 0)
    z_rows = rows // N_TP

    def z_region(ref, rank):
        return ref.at[pl.ds(pl.multiple_of(rank * z_rows, z_rows), z_rows), :]

    def z_scatter(d):
        return pltpu.make_async_remote_copy(
            src_ref=z_region(z_part, tp ^ d),
            dst_ref=z_held.at[d],
            send_sem=tp_send.at[1, d],
            recv_sem=tp_recv.at[1, d],
            device_id=(me, tp ^ d),
            device_id_type=MESH,
        )

    def z_spread(d, rank):
        return pltpu.make_async_remote_copy(
            src_ref=z_region(z_done, rank),
            dst_ref=z_region(z_done, rank),
            send_sem=tp_send.at[2, d],
            recv_sem=tp_recv.at[2, d],
            device_id=(me, tp ^ d),
            device_id_type=MESH,
        )

    def tail(d, rank):
        return pltpu.make_async_remote_copy(
            src_ref=tails.at[rank],
            dst_ref=tails.at[rank],
            send_sem=tp_send.at[3, d],
            recv_sem=tp_recv.at[3, d],
            device_id=(me, tp ^ d),
            device_id_type=MESH,
        )

    for d in range(1, N_TP):
        z_scatter(d).start()
    g_bkv = dot_tn(z_kv[...], dkv_own[...])
    blocks = [g_bq[32 * i : 32 * i + 32] for i in range(4)] + [g_bkv[:32, :width], g_bkv[32:64, width:]]
    blocks += [g_ao[128 * s + 32 * i : 128 * s + 32 * i + 32] for s in range(2) for i in range(2)]
    blocks += [jnp.zeros((32, width), f32)] * 6
    for i in range(N_CTX):
        heads_src[i % 2, i // 2] = blocks[i].astype(bf16)
    heads_sum.start()
    def finish_z():
        total = z_region(z_part, tp)[...].astype(f32)
        for d in range(1, N_TP):
            z_scatter(d).wait_recv()
            total = total + z_held[d].astype(f32)
        z_region(z_done, tp)[...] = total.astype(bf16)
        for d in range(1, N_TP):
            z_spread(d, tp).start()

    along = jnp.zeros((rows, 1), f32)
    for d in (5, 6, 7, 4, 1, 2, 3, 0):
        if d == FAR:
            finish_z()
        peer = tp ^ d
        at = pl.ds(pl.multiple_of(peer * part, part), part)
        total = dn[peer] + dot_nt(dz_kv, wide[at, 640:704]) + dot_nt(dkv_own[...], w_kv[at, :])
        scaled = total * gain[:, at]
        along = along + jnp.sum(scaled * x0[:, at].astype(f32), axis=1, keepdims=True)
        if d:
            parts[d] = total.astype(bf16)
            if d != FAR:
                scatter.copy(d).start()
        else:
            own[...] = total
    dots[...] = jnp.broadcast_to(along, dots.shape)
    tails[tp] = jnp.transpose(dots[...])[:8, :]
    for d in range(1, N_TP):
        tail(d, tp).start()
    heads_sum.chips()
    mixed[...] = ff.total(ff_own[...]).astype(bf16)
    scatter.relay()
    heads_sum.again()
    for d in range(1, N_TP):
        z_spread(d, tp ^ d).wait_recv()
    to_pairs(b_src, slice(0, part), dot_tn(n1_own, z_done[...]))
    b_sum.start()
    total = scatter.total(own[...])
    b_sum.chips()
    for d in range(1, N_TP):
        tail(d, tp ^ d).wait_recv()
    whole = tails[0]
    for d in range(1, N_TP):
        whole = whole + tails[d]
    dots[...] = jnp.transpose(jnp.broadcast_to(whole[:1], (128, rows)))
    own_at = pl.ds(pl.multiple_of(tp * part, part), part)
    own[...] = total * gain[:, own_at]
    step = 32

    def finish(i, carry):
        at = pl.ds(pl.multiple_of(i * step, step), step)
        x = x0[at, :].astype(f32)
        inverse = lax.rsqrt(jnp.mean(x * x, axis=1, keepdims=True) + eps)
        mean = dots[at, :1] * (1.0 / model)
        back = inverse * own[at, :] - x0[at, own_at].astype(f32) * inverse**3 * mean
        grad_tokens[at, :] = (dx1_own[at, :] + back).astype(bf16)
        return carry

    lax.fori_loop(0, rows // step, finish, 0)
    wide_a[...] = a_sum.total()
    heads_sum.other_core()
    wide_b[...] = b_sum.total()
    heads_sum.finish()
    for back in (1, 3, 5, 7):
        to_core(back).wait_send()
        to_owner(back + 1).wait_send()
    scatter.sent()
    ff.sent()
    for d in range(1, N_TP):
        z_scatter(d).wait_send()
        z_spread(d, tp).wait_send()
        tail(d, tp).wait_send()


def backward(vmem, hbm):
    dx1 = vmem[0]
    w_q, w_kv, w_o, wide, x0, n1, n2, dy, kv_all, q_all, probs = hbm
    rows, model = dx1.shape
    part = model // N_TP
    width = w_q.shape[2]
    heads = width // HEAD_DIM
    half = rows // 2
    shape = jax.ShapeDtypeStruct
    reduced = [(2, 8, 16, 512), (2, 8, 16, part), (2, 8, 32, width)]
    return pl.pallas_call(
        backward_kernel,
        out_shape=(
            shape((rows, part), bf16),
            shape((rows, part), bf16),
            shape((16, 512), f32),
            shape((16, part), f32),
            shape(reduced[2], bf16),
        ),
        in_specs=[VMEM] * len(vmem) + [ANY] * len(hbm),
        out_specs=tuple([VMEM] * 5),
        scratch_shapes=[
            pltpu.VMEM(a.shape, bf16) for a in hbm
        ]
        + [
            pltpu.VMEM((2 * heads, rows, HEAD_DIM), bf16),
            pltpu.VMEM(kv_all.shape, bf16),
            pltpu.VMEM((8,) + kv_all.shape[1:], bf16),
            pltpu.VMEM((2, rows, width), bf16),
            pltpu.VMEM((rows, 2 * width), bf16),
            pltpu.VMEM((N_TP, rows, part), f32),
            pltpu.VMEM((N_TP, rows, part), bf16),
            pltpu.VMEM((rows, part), bf16),
            pltpu.VMEM((rows, part), f32),
            pltpu.VMEM((N_TP, rows, part), bf16),
            pltpu.VMEM((N_TP, rows, part), bf16),
            pltpu.VMEM((rows, part), bf16),
            pltpu.VMEM((rows, 256), bf16),
            pltpu.VMEM((N_TP, rows // N_TP, 256), bf16),
            pltpu.VMEM((rows, 256), bf16),
            pltpu.VMEM((rows, 128), f32),
            pltpu.VMEM((N_TP, 8, rows), f32),
        ]
        + [pltpu.VMEM(a, bf16) for a in reduced]
        + [pltpu.VMEM(a[1:], bf16) for a in reduced + reduced]
        + [
            pltpu.SemaphoreType.DMA((len(hbm),)),
            pltpu.SemaphoreType.DMA((5, N_TP)),
            pltpu.SemaphoreType.DMA((5, N_TP)),
            pltpu.SemaphoreType.DMA((4,)),
            pltpu.SemaphoreType.DMA((4,)),
            pltpu.SemaphoreType.DMA((5,)),
            pltpu.SemaphoreType.DMA((5,)),
            pltpu.SemaphoreType.DMA((3, 16)),
            pltpu.SemaphoreType.DMA((3, 16)),
        ],
        compiler_params=pltpu.CompilerParams(
            collective_id=3, has_side_effects=True, vmem_limit_bytes=60 << 20
        ),
        name="backward",
    )(*vmem, *hbm)


def shards(
    tokens,
    norm1_gain,
    router_attn,
    w_query,
    w_key_value,
    w_out,
    norm2_gain,
    router_ffn,
    w_gate_up,
    w_down,
    adapt_wide,
    adapt_heads,
    adapt_ffn,
    attention_routes,
    feedforward_routes,
    doc_lengths,
    adapter_index,
    cotangent,
):
    seqs, block, part = tokens.shape
    rows = seqs * block
    n_tp = lax.axis_size("tp")
    model = part * n_tp
    experts = w_query.shape[0]
    width = w_query.shape[2]
    heads = width // HEAD_DIM
    hidden = w_down.shape[1]
    rank = adapt_heads.shape[2]
    wide_slots = adapt_wide.shape[1]
    ctx_rank = lax.axis_index("ctx")


    def by_sequence(a):
        first = adapter_index[0] == 0
        return jnp.stack([jnp.where(first, a[0], a[1]), jnp.where(first, a[1], a[0])])

    wide_own = by_sequence(adapt_wide.astype(bf16))
    groups = [[6, 10, 7, 11, 8, 12, 9, 13], list(range(14, 22)), [0, 1, 2, 3], [4, 5]]
    order = [(q, s) for g in groups[:3] for q in range(seqs) for s in g]
    order += [(q, s) for s in groups[3] for q in range(seqs)]
    wide_cols = wide_own.reshape(seqs * wide_slots, rank, -1)[
        np.array([q * wide_slots + s for q, s in order])
    ].reshape(seqs * wide_slots * rank, -1).T
    heads_low = by_sequence(adapt_heads.astype(bf16))
    ffn_low = by_sequence(adapt_ffn.astype(bf16))
    route_a = attention_routes.reshape(rows, -1)
    route_f = feedforward_routes.reshape(rows, -1)

    positions = ctx_rank * block + jnp.arange(block, dtype=jnp.int32)
    doc_ids, offsets = doc_layout(doc_lengths, positions)
    half = HEAD_DIM // 2
    frequency = 10000.0 ** (-2.0 * jnp.arange(half, dtype=f32) / HEAD_DIM)
    angles = offsets.astype(f32).reshape(rows)[:, None] * frequency
    cosine, sine = jnp.cos(angles), jnp.sin(angles)
    cosine = jnp.concatenate([cosine, cosine], axis=1)
    sine = jnp.concatenate([-sine, sine], axis=1)

    b_q, b_kv, a_o = heads_low[:, :experts], heads_low[:, experts : experts + 2], heads_low[:, experts + 2 :]
    key_pos = (ctx_rank - PAST) * block + jnp.arange((PAST + 1) * block, dtype=jnp.int32)
    key_doc = doc_layout(doc_lengths, jnp.maximum(key_pos, 0))[0]
    key_doc = jnp.where(key_pos[None, :] >= 0, key_doc, -(1 << 20))
    blank = jnp.zeros((seqs, rank, width), bf16)
    b_kv_wide = jnp.concatenate(
        [
            jnp.concatenate([b_kv[:, 0], blank], axis=-1).reshape(seqs * rank, 2 * width),
            jnp.concatenate([blank, b_kv[:, 1]], axis=-1).reshape(seqs * rank, 2 * width),
        ],
        axis=0,
    )
    a_o_wide = jnp.pad(a_o.reshape(seqs, experts * rank, width), ((0, 0), (0, 64), (0, 0))).reshape(256, width)
    b_q = b_q.reshape(seqs * experts * rank, width)
    table = jnp.concatenate(
        [
            cosine,
            sine,
            widen_routes(route_a[:, :1], experts),
            widen_routes(route_a[:, 1:], experts),
            widen_routes(route_f, experts),
            jnp.broadcast_to(doc_ids.reshape(rows, 1).astype(f32), (rows, 128)),
        ],
        axis=1,
    )
    router_wide = jnp.pad(router_attn, ((0, 0), (0, 128 - experts)))
    (
        w_query, w_key_value, w_out, w_gate_up, w_down, wide, _, dy,
        x0, sum_out, n1, kv_all, q_all, probs, ob, z_o_gated, z_q, z_kv, gates,
    ) = attention(
        [
            w_query,
            w_key_value.reshape(-1, 2 * width),
            w_out,
            gate_up_columns(w_gate_up[:, :, 0], w_gate_up[:, :, 1]),
            w_down,
        ],
        [tokens.reshape(rows, part), cotangent.reshape(rows, part), wide_cols],
        [
            norm1_gain[None],
            router_wide,
            table,
            jnp.broadcast_to(key_doc[:, None, :], (seqs, 8, key_doc.shape[1])).astype(f32),
            b_q,
            b_kv_wide,
            a_o_wide,
        ],
    )
    blank = jnp.zeros((seqs, experts, rank, hidden), bf16)
    b_gu = jnp.stack(
        [gate_up_columns(ffn_low[:, :experts], blank), gate_up_columns(blank, ffn_low[:, experts : 2 * experts])],
        axis=2,
    ).reshape(seqs, 2 * experts * rank, 2 * hidden)
    a_d = jnp.pad(ffn_low[:, 2 * experts :].reshape(seqs, experts * rank, hidden), ((0, 0), (64, 0), (0, 0)))
    ff_parts, ff_own, dx1b, dx1_own, n2, z_sum, gu_sum, d_sum = feed_forward(
        x0, sum_out, dy, norm2_gain[None], wide,
        jnp.pad(router_ffn, ((0, 0), (0, 128 - experts))),
        table, b_gu.reshape(256, 2 * hidden), a_d.reshape(256, hidden), z_o_gated, w_gate_up, w_down,
    )
    mixed, grad_tokens, wide_a, wide_b, head_sum = backward(
        [
            dx1b, dx1_own, ob, gates, z_q, z_kv, z_sum, table, norm1_gain[None], router_wide, b_q, b_kv_wide, a_o_wide, ff_parts, ff_own,
        ],
        [w_query, w_key_value, w_out, wide, x0, n1, n2, dy, kv_all, q_all, probs],
    )
    grad_wide = jnp.concatenate([wide_a, wide_b[:, : 704 - 512]], axis=1).T
    back_order = np.argsort(np.array([q * wide_slots + s for q, s in order]))
    grad_wide = grad_wide.reshape(seqs * wide_slots, rank, -1)[back_order]
    grad_wide = by_sequence(grad_wide.reshape(seqs, wide_slots, rank, -1))
    head_sum = jnp.swapaxes(head_sum, 0, 1).reshape(-1, rank, width).astype(f32)
    grad_heads = by_sequence(jnp.concatenate(
        [
            head_sum[: seqs * experts].reshape(seqs, experts, rank, width),
            jnp.swapaxes(head_sum[8:12].reshape(2, seqs, rank, width), 0, 1),
            head_sum[12:20].reshape(seqs, experts, rank, width),
        ],
        axis=1,
    ))
    gu_sum = jnp.swapaxes(gu_sum, 0, 1).reshape(seqs, experts, 2, rank, 768).astype(f32)
    grad_ffn = by_sequence(jnp.concatenate(
        [
            gu_sum[:, :, 0, :, :704],
            jnp.concatenate([gu_sum[:, :, 1, :, :640], gu_sum[:, :, 1, :, 704:]], axis=-1),
            jnp.swapaxes(d_sum, 0, 1).reshape(seqs, experts, rank, hidden),
        ],
        axis=1,
    ))
    mixed = mixed.reshape(seqs, block, part)
    grad_tokens = grad_tokens.reshape(seqs, block, part)
    return (mixed, grad_tokens, grad_wide, grad_heads, grad_ffn)


def solution(mesh):
    placed = (
        P(None, "ctx", "tp"),
        P(),
        P(),
        P(None, "ctx", "tp"),
        P("ctx", None, "tp"),
        P(None, "tp", "ctx"),
        P(),
        P(),
        P(None, "ctx", None, "tp"),
        P(None, "tp", "ctx"),
        P(None, None, None, ("ctx", "tp")),
        P(None, None, None, "tp"),
        P(None, None, None, "tp"),
        P(None, "ctx", None),
        P(None, "ctx", None),
        P(),
        P(),
        P(None, "ctx", "tp"),
    )
    return jax.shard_map(
        shards,
        mesh=mesh,
        in_specs=placed,
        out_specs=(
            P(None, "ctx", "tp"),
            P(None, "ctx", "tp"),
            P(None, None, None, ("ctx", "tp")),
            P(None, None, None, "tp"),
            P(None, None, None, "tp"),
        ),
        check_vma=False,
    )
```

```python
import functools

import jax
import numpy as np
import jax.numpy as jnp
from jax import lax
from jax.experimental import pallas as pl
from jax.experimental.pallas import tpu as pltpu
from jax.sharding import PartitionSpec as P

HEAD_DIM = 128
WINDOW = 1024
eps = 1e-06
big_negative = -1e30
bf16 = jnp.bfloat16
f32 = jnp.float32

MESH = pl.DeviceIdType.MESH
ANY = pl.BlockSpec(memory_space=pl.ANY)
VMEM = pl.BlockSpec(memory_space=pltpu.VMEM)
N_CTX, N_TP = 16, 8
FAR = 4
PAST = 8


def region(kind, ref, owner, low, high):
    rows = pl.ds(pl.multiple_of(owner * 128 + 32 * low, 32), 32 * (high - low))
    cols = pl.ds(pl.multiple_of(owner * 128, 128), 128)
    if kind == "rows":
        return ref.at[pl.ds(low, high - low), cols, :]
    if kind == "flat":
        return ref.at[rows, :]
    if kind == "cols":
        return ref.at[pl.ds(low, high - low), :, cols]
    if high - low == 1:
        half = ref.shape[1] // 2
        return ref.at[low // 2, pl.ds(half * (low % 2), half), cols]
    return ref.at[pl.ds(low // 2, (high - low) // 2), :, cols]


def own_part(kind, ref, low, high):
    if kind == "flat":
        return ref.at[pl.ds(32 * low, 32 * (high - low)), :]
    if kind == "pair":
        return ref
    return ref.at[pl.ds(low, high - low)]


def tp_part(kind, ref, rank, size):
    if kind == "cols":
        return ref.at[:, pl.ds(pl.multiple_of(rank * size, size), size)]
    return ref.at[pl.ds(pl.multiple_of(rank * size, size), size), :]


def rms_scale(values, gain):
    return values * lax.rsqrt(jnp.mean(values * values, axis=-1, keepdims=True) + eps) * gain


def doc_layout(doc_lengths, positions):
    docs = doc_lengths.shape[1]
    upto = np.tril(np.ones((docs, docs), np.int32))
    ends = jnp.sum(doc_lengths[:, None, :] * upto[None], axis=2)
    passed = positions[None, :, None] >= ends[:, None, :]
    doc_ids = jnp.sum(passed.astype(jnp.int32), axis=2)
    starting = jnp.sum(jnp.where(passed, doc_lengths[:, None, :], 0), axis=2)
    inside = positions[None, :] < ends[:, -1:]
    doc_ids = jnp.where(inside, doc_ids, -1 - positions[None, :])
    return (doc_ids, positions[None, :] - starting)


def dot(a, b, ca=1, cb=0):
    return lax.dot_general(a, b, (((ca,), (cb,)), ((), ())), preferred_element_type=f32)


class Scatter:
    def __init__(self, parts, held, relay, send, recv, row):
        self.me, self.tp = lax.axis_index("ctx"), lax.axis_index("tp")
        self.parts, self.held, self.relay_buffer = parts, held, relay
        self.send, self.recv, self.row = send, recv, row

    def copy_to(self, d, to):
        return pltpu.make_async_remote_copy(
            src_ref=self.parts.at[d],
            dst_ref=self.held.at[d],
            send_sem=self.send.at[self.row, d],
            recv_sem=self.recv.at[self.row, d],
            device_id=(self.me, self.tp ^ to),
            device_id_type=MESH,
        )

    def copy(self, d):
        if d != FAR:
            return self.copy_to(d, d % FAR)
        return pltpu.make_async_remote_copy(
            src_ref=self.relay_buffer,
            dst_ref=self.held.at[FAR],
            send_sem=self.send.at[self.row, FAR],
            recv_sem=self.recv.at[self.row, FAR],
            device_id=(self.me, self.tp ^ FAR),
            device_id_type=MESH,
        )

    def relay(self):
        total = self.parts[FAR].astype(f32)
        for d in range(FAR + 1, N_TP):
            self.copy(d).wait_recv()
            total = total + self.held[d].astype(f32)
        self.relay_buffer[...] = total.astype(bf16)
        self.copy(FAR).start()

    def total(self, own):
        for d in range(1, FAR + 1):
            self.copy(d).wait_recv()
            own = own + self.held[d].astype(f32)
        return own

    def sent(self):
        for d in range(1, N_TP):
            self.copy(d).wait_send()


class Spread:
    def __init__(self, source, place, send, recv, row):
        self.me, self.tp = lax.axis_index("ctx"), lax.axis_index("tp")
        self.source, self.place = source, place
        self.send, self.recv, self.row = send, recv, row

    def copy(self, d, owner, to, source=None):
        return pltpu.make_async_remote_copy(
            src_ref=self.place(owner) if source is None else source,
            dst_ref=self.place(owner),
            send_sem=self.send.at[self.row, d],
            recv_sem=self.recv.at[self.row, d],
            device_id=(self.me, self.tp ^ to),
            device_id_type=MESH,
        )

    def start(self):
        for d in (FAR, 1, 2, 3):
            self.copy(d, self.tp, d, self.source).start()

    def relay(self):
        self.copy(FAR, self.tp ^ FAR, FAR).wait_recv()
        for d in (1, 2, 3):
            self.copy(FAR + d, self.tp ^ FAR, d).start()

    def wait(self):
        for d in (1, 2, 3):
            self.copy(d, self.tp ^ d, d).wait_recv()
            self.copy(FAR + d, self.tp ^ (FAR + d), d).wait_recv()

    def sent(self):
        for d in (FAR, 1, 2, 3):
            self.copy(d, self.tp, d, self.source).wait_send()
        for d in (1, 2, 3):
            self.copy(FAR + d, self.tp ^ FAR, d).wait_send()


class CtxSum:
    def __init__(self, source, core_held, held, out, send, recv, row):
        self.me, self.tp = lax.axis_index("ctx"), lax.axis_index("tp")
        self.core, self.chip = lax.rem(self.me, 2), self.me // 2
        self.source, self.core_held, self.held, self.out = source, core_held, held, out
        self.send, self.recv, self.row = send, recv, row

    def copy(self, item, src, dst, to):
        return pltpu.make_async_remote_copy(
            src_ref=src,
            dst_ref=dst,
            send_sem=self.send.at[self.row, item],
            recv_sem=self.recv.at[self.row, item],
            device_id=(to, self.tp),
            device_id_type=MESH,
        )

    def to_core(self):
        return self.copy(0, self.source.at[1 - self.core], self.core_held, self.me ^ 1)

    def to_chip(self, d):
        return self.copy(
            d, self.source.at[self.core, self.chip ^ d], self.held.at[d], self.me ^ (2 * d)
        )

    def spread(self, d, chip):
        there = self.out.at[self.core, chip]
        return self.copy(7 + d, there, there, self.me ^ (2 * d))

    def back_to_core(self, core):
        return self.copy(15, self.out.at[core], self.out.at[core], self.me ^ 1)

    def start(self):
        self.to_core().start()

    def chips(self):
        self.to_core().wait()
        self.source[self.core] = (
            self.source[self.core].astype(f32) + self.core_held[...].astype(f32)
        ).astype(self.source.dtype)
        for d in range(1, 8):
            self.to_chip(d).start()

    def total(self):
        total = self.source[self.core, self.chip].astype(f32)
        for d in range(1, 8):
            self.to_chip(d).wait_recv()
            total = total + self.held[d].astype(f32)
        for d in range(1, 8):
            self.to_chip(d).wait_send()
        return total

    def again(self):
        self.out[self.core, self.chip] = self.total().astype(self.out.dtype)
        for d in range(1, 8):
            self.spread(d, self.chip).start()

    def other_core(self):
        for d in range(1, 8):
            self.spread(d, self.chip ^ d).wait_recv()
            self.spread(d, self.chip).wait_send()
        self.back_to_core(self.core).start()

    def finish(self):
        self.back_to_core(1 - self.core).wait_recv()
        self.back_to_core(self.core).wait_send()


def dot_nt(a, b):
    return dot(a, b, 1, 1)


def dot_tn(a, b):
    return dot(a, b, 0, 0)


def by_seq(rows, f):
    half = rows.shape[0] // 2
    return jnp.concatenate([f(0, rows[:half]), f(1, rows[half:])], axis=0)


def column_of(values, lane, e):
    return jnp.sum(jnp.where(lane == e, values, 0.0), axis=1, keepdims=True)


def greet(targets):
    barrier = pltpu.get_barrier_semaphore()
    for device in targets:
        pl.semaphore_signal(barrier, inc=1, device_id=device, device_id_type=MESH)
    pl.semaphore_wait(barrier, len(targets))


def masked_gates(logits, hot):
    largest = jnp.max(jnp.where(hot > 0, logits, big_negative), axis=1, keepdims=True)
    powers = jnp.where(hot > 0, jnp.exp(logits - largest), 0.0)
    return powers / jnp.sum(powers, axis=1, keepdims=True)


def ffn_kernel(
    gain, router, table, b_gu, a_d, z_o, h_x0, h_attn, h_wide, h_dy, w_gu_hbm, w_d_hbm,
    ff_parts, ff_own, dx1, dx1_own, n2, z_sum, gu_out, d_out,
    x0, attn, wide, dy, w_gu, w_d, hg, dgu, dh_tmp, z_gu, dz_d, z_part, parts, relay, own, held, z_held, dots, tails, inverse,
    g_gu, g_d, gu_src, gu_core, gu_held, d_src, d_core, d_held,
    load, small_load, send, recv, ctx_send, ctx_recv,
):
    me, tp = lax.axis_index("ctx"), lax.axis_index("tp")
    hot = table.at[:, 512:640]
    rows, model = x0.shape
    experts = w_gu.shape[0]
    part = model // N_TP
    smalls = []
    for i, (h, v) in enumerate(((h_x0, x0), (h_attn, attn), (h_wide, wide), (h_dy, dy))):
        c = pltpu.make_async_copy(h, v, small_load.at[i])
        c.start()
        smalls.append(c)

    def fetch(e):
        return (
            pltpu.make_async_copy(w_gu_hbm.at[e], w_gu.at[e], load.at[0, e]),
            pltpu.make_async_copy(w_d_hbm.at[e], w_d.at[e], load.at[1, e]),
        )


    greet([(me ^ d, tp) for d in range(1, N_CTX)] + [(me, tp ^ d) for d in range(1, N_TP)])
    for e in range(experts):
        for c in fetch(e):
            c.start()
    for c in smalls:
        c.wait()
    step = 32

    def normalize(i, carry):
        at = pl.ds(pl.multiple_of(i * step, step), step)
        x = x0[at, :].astype(f32) + attn[at, :].astype(f32)
        r = lax.rsqrt(jnp.mean(x * x, axis=1, keepdims=True) + eps)
        inverse[at, :] = jnp.broadcast_to(r, (step, 128))
        n2[at, :] = (x * r * gain[...]).astype(bf16)
        return carry

    lax.fori_loop(0, rows // step, normalize, 0)
    lane = lax.broadcasted_iota(jnp.int32, (rows, 128), 1)
    gates = masked_gates(dot(n2[...], router[...]), hot[...])
    pair_lane = lax.broadcasted_iota(jnp.int32, (rows, 256), 1)
    mine = pair_lane // 128 == lax.broadcasted_iota(jnp.int32, (rows, 256), 0) // (rows // 2)
    pair_lane = pair_lane % 128
    z_gu[...] = jnp.where(mine, dot(n2[...], wide[:, :256]), 0.0).astype(bf16)
    dz_d[...] = jnp.where(mine, dot(dy[...], wide[:, 256:512]), 0.0).astype(bf16)
    g_gu[...] = jnp.zeros_like(g_gu)
    g_d[...] = jnp.zeros_like(g_d)
    zero = jnp.zeros((rows, 256), f32)

    def expert(e, carry):
        d_gates, dz_gu, z_d = carry
        for c in fetch(e):
            c.wait()
        gate = column_of(gates, lane, e)
        z_in = jnp.where(pair_lane // 32 == e, z_gu[...].astype(f32), 0.0).astype(bf16)
        dz_in = jnp.where(pair_lane // 16 == 4 + e, dz_d[...].astype(f32), 0.0).astype(bf16)
        dh_tmp[:, :704] = dot_nt(dy[...], w_d[e]) + dot(dz_in, a_d[...])
        pre = dot(n2[...], w_gu[e]) + dot(z_in, b_gu[...])

        def tile(g, u, d):
            sg = jax.nn.sigmoid(g)
            silu = g * sg
            h = silu * u
            dg = d * gate
            return h, (dg * u * sg * (1.0 + g * (1.0 - sg))), dg * silu, h * d

        h, dgp, dup, hd = tile(pre[:, :640], pre[:, 640:1280], dh_tmp[:, :640])
        hg[e, :, :640] = (h * gate).astype(bf16)
        dgu[e, :, :640] = dgp.astype(bf16)
        dgu[e, :, 640:1280] = dup.astype(bf16)
        dgf = jnp.sum(hd, axis=1, keepdims=True)
        last = pre[:, 1280:]
        h, dgp, dup, hd = tile(last, pltpu.roll(last, 64, 1), dh_tmp[:, 640:])
        hg[e, :, 640:] = (h * gate).astype(bf16)[:, :64]
        dgu[e, :, 1280:] = jnp.where(lane < 64, dgp, pltpu.roll(dup, 64, 1)).astype(bf16)
        dgf = dgf + jnp.sum(jnp.where(lane < 64, hd, 0.0), axis=1, keepdims=True)
        d_gates = d_gates + jnp.where(lane == e, dgf, 0.0)
        keep = mine & (pair_lane // 32 == e)
        dz_gu = dz_gu + jnp.where(keep, dot_nt(dgu[e], b_gu[...]), 0.0)
        keep = mine & (pair_lane // 16 == 4 + e)
        z_d = z_d + jnp.where(keep, dot_nt(hg[e], a_d[...]), 0.0)
        g_gu[...] += dot_tn(z_in, dgu[e])
        g_d[...] += dot_tn(dz_in, hg[e])
        return d_gates, dz_gu, z_d

    d_gates, dz_gu, z_d = lax.fori_loop(
        0, experts, expert, (jnp.zeros((rows, 128), f32), zero, zero)
    )
    d_logits = gates * (d_gates - jnp.sum(gates * d_gates, axis=1, keepdims=True))
    d_logits = d_logits.astype(bf16)
    dz_gu, z_d = dz_gu.astype(bf16), z_d.astype(bf16)
    z_part[:, :128] = dz_gu[:, :128] + dz_gu[:, 128:]
    z_part[:, 128:] = z_o[...] + z_d[:, :128] + z_d[:, 128:]

    for i in range(N_CTX):
        s, slot = i // 8, i % 8
        at = slice(128 * s + 16 * slot, 128 * s + 16 * slot + 16)
        cols = 640 * (slot % 2)
        gu_src[i % 2, i // 2, :, :640] = g_gu[at, cols : cols + 640].astype(bf16)
        gu_src[i % 2, i // 2, :, 640:] = g_gu[at, 1280:].astype(bf16)
        first = 128 * s + 64 + 8 * slot
        d_src[i % 2, i // 2] = g_d[first : first + 8, :]
    gu_sum = CtxSum(gu_src, gu_core, gu_held, gu_out, ctx_send, ctx_recv, 0)
    d_sum = CtxSum(d_src, d_core, d_held, d_out, ctx_send, ctx_recv, 1)
    gu_sum.start()
    d_sum.start()
    scatter = Scatter(parts, held, relay, send, recv, 0)

    def x_at(at):
        return x0[:, at].astype(f32) + attn[:, at].astype(f32)

    def piece(j, along):
        d = lax.rem(j + FAR + 1, N_TP)
        peer = tp ^ d
        at = pl.ds(pl.multiple_of(peer * part, part), part)
        w_rows = wide[at, :256]
        dn = dot_nt(d_logits, router[at, :])
        dn = dn + dot_nt(dz_gu, w_rows)
        for e in range(experts):
            dn = dn + dot_nt(dgu[e], w_gu[e, at, :])
        parts[d] = dn.astype(bf16)

        @pl.when((d != 0) & (d != FAR))
        def _():
            scatter.copy_to(d, lax.rem(d, FAR)).start()

        @pl.when(d == 0)
        def _():
            own[...] = dn

        return along + jnp.sum(dn * gain[:, at] * x_at(at), axis=1, keepdims=True)

    def out_piece(d, carry):
        peer = tp ^ d
        at = pl.ds(pl.multiple_of(peer * part, part), part)
        w_rows = wide[at, 256:512]
        ff = dot_nt(z_d, w_rows)
        for e in range(experts):
            ff = ff + dot(hg[e], w_d[e, :, at])
        ff_parts[d] = ff.astype(bf16)

        @pl.when(d == 0)
        def _():
            ff_own[...] = ff + x_at(at)

        return carry

    z_rows = rows // N_TP

    def z_region(ref, rank):
        return ref.at[pl.ds(pl.multiple_of(rank * z_rows, z_rows), z_rows), :]

    def z_scatter(d):
        return pltpu.make_async_remote_copy(
            src_ref=z_region(z_part, tp ^ d),
            dst_ref=z_held.at[d],
            send_sem=send.at[2, d],
            recv_sem=recv.at[2, d],
            device_id=(me, tp ^ d),
            device_id_type=MESH,
        )

    def z_spread(d, rank):
        return pltpu.make_async_remote_copy(
            src_ref=z_region(z_sum, rank),
            dst_ref=z_region(z_sum, rank),
            send_sem=send.at[3, d],
            recv_sem=recv.at[3, d],
            device_id=(me, tp ^ d),
            device_id_type=MESH,
        )

    def columns(ref, rank):
        return ref.at[:, pl.ds(pl.multiple_of(rank * part, part), part)]

    def tail(d, rank):
        return pltpu.make_async_remote_copy(
            src_ref=tails.at[rank],
            dst_ref=tails.at[rank],
            send_sem=send.at[5, d],
            recv_sem=recv.at[5, d],
            device_id=(me, tp ^ d),
            device_id_type=MESH,
        )

    along = lax.fori_loop(0, N_TP, piece, jnp.zeros((rows, 1), f32))
    dots[...] = jnp.broadcast_to(along, dots.shape)
    tails[tp] = jnp.transpose(dots[...])[:8, :]
    for d in range(1, N_TP):
        tail(d, tp).start()
        z_scatter(d).start()
    scatter.relay()
    gu_sum.chips()
    d_sum.chips()
    lax.fori_loop(0, N_TP, out_piece, 0)
    at = pl.ds(pl.multiple_of(tp * part, part), part)
    total = scatter.total(own[...]) * gain[:, at]
    for d in range(1, N_TP):
        tail(d, tp ^ d).wait_recv()
    whole = tails[0]
    for d in range(1, N_TP):
        whole = whole + tails[d]
    dots[...] = jnp.transpose(jnp.broadcast_to(whole[:1], (128, rows)))
    r = inverse[:, :1]
    total = dy[:, at].astype(f32) + r * total - x_at(at) * r**3 * (dots[:, :1] * (1.0 / model))
    dx1_own[...] = total
    columns(dx1, tp)[...] = total.astype(bf16)
    spread = Spread(None, lambda rank: columns(dx1, rank), send, recv, 4)
    spread.start()
    gu_sum.again()
    d_sum.again()
    total = z_region(z_part, tp)[...].astype(f32)
    for d in range(1, N_TP):
        z_scatter(d).wait_recv()
        total = total + z_held[d].astype(f32)
    z_region(z_sum, tp)[...] = total.astype(bf16)
    for d in range(1, N_TP):
        z_spread(d, tp).start()
    spread.relay()
    gu_sum.other_core()
    d_sum.other_core()
    spread.wait()
    gu_sum.finish()
    d_sum.finish()
    scatter.sent()
    spread.sent()
    for d in range(1, N_TP):
        z_scatter(d).wait_send()
        z_spread(d, tp ^ d).wait_recv()
        z_spread(d, tp).wait_send()
        tail(d, tp).wait_send()


def feed_forward(small, large):
    x0, attn, wide, dy, w_gu, w_d = large
    rows, model = x0.shape
    b_gu, a_d = small[3], small[4]
    part = model // N_TP
    experts, _, cols = w_gu.shape
    hidden = w_d.shape[1]
    shape = jax.ShapeDtypeStruct
    return pl.pallas_call(
        ffn_kernel,
        out_shape=(
            shape((N_TP, rows, part), bf16),
            shape((rows, part), f32),
            shape((rows, model), bf16),
            shape((rows, part), f32),
            shape((rows, model), bf16),
            shape((rows, 256), bf16),
            shape((2, 8, 16, 768), bf16),
            shape((2, 8, 8, hidden), f32),
        ),
        in_specs=[VMEM] * len(small) + [ANY] * len(large),
        out_specs=tuple([VMEM] * 8),
        scratch_shapes=[
            pltpu.VMEM(a.shape, bf16) for a in large
        ]
        + [
            pltpu.VMEM((experts, rows, hidden), bf16),
            pltpu.VMEM((experts, rows, cols), bf16),
            pltpu.VMEM((rows, 768), f32),
            pltpu.VMEM((rows, 256), bf16),
            pltpu.VMEM((rows, 256), bf16),
            pltpu.VMEM((rows, 256), bf16),
            pltpu.VMEM((N_TP, rows, part), bf16),
            pltpu.VMEM((rows, part), bf16),
            pltpu.VMEM((rows, part), f32),
            pltpu.VMEM((N_TP, rows, part), bf16),
            pltpu.VMEM((N_TP, rows // N_TP, 256), bf16),
            pltpu.VMEM((rows, 128), f32),
            pltpu.VMEM((N_TP, 8, rows), f32),
            pltpu.VMEM((rows, 128), f32),
            pltpu.VMEM(b_gu.shape, f32),
            pltpu.VMEM(a_d.shape, f32),
            pltpu.VMEM((2, 8, 16, 768), bf16),
            pltpu.VMEM((8, 16, 768), bf16),
            pltpu.VMEM((8, 16, 768), bf16),
            pltpu.VMEM((2, 8, 8, hidden), f32),
            pltpu.VMEM((8, 8, hidden), f32),
            pltpu.VMEM((8, 8, hidden), f32),
            pltpu.SemaphoreType.DMA((2, experts)),
            pltpu.SemaphoreType.DMA((4,)),
            pltpu.SemaphoreType.DMA((6, N_TP)),
            pltpu.SemaphoreType.DMA((6, N_TP)),
            pltpu.SemaphoreType.DMA((2, 16)),
            pltpu.SemaphoreType.DMA((2, 16)),
        ],
        compiler_params=pltpu.CompilerParams(
            collective_id=2, has_side_effects=True, vmem_limit_bytes=63 << 20
        ),
        name="feed_forward",
    )(*small, *large)


def widen_routes(routes, experts):
    lane = jnp.arange(128, dtype=jnp.int32)
    return jnp.sum((routes[..., None] == lane).astype(f32), axis=1)


def gate_up_columns(gate, up):
    def put(part, before, after):
        sides = [(0, 0, 0)] * (part.ndim - 1) + [(before, after, 0)]
        return lax.pad(part, jnp.zeros((), part.dtype), sides)

    return (
        put(gate[..., :640], 0, 768) + put(up[..., :640], 640, 128)
    ) + (put(gate[..., 640:], 1280, 64) + put(up[..., 640:], 1344, 0))


def attention_kernel(
    s_q, s_kv, s_o, s_gu, s_d, tokens, cotangent, s_wide, s_rest,
    gain, router, table, k_doc, b_q, b_kv, a_o,
    g_q, g_kv, g_o, g_gu, g_d, g_wide, wide_mid, dy, g_rest,
    h_n1, h_kv_all, h_q_all, h_probs, x0, attn, ob, z_o, z_q, z_kv, gates,
    n1, kv_all, q_all, probs, w_q, w_kv, w_o, wide, rest, parts, relay, own, held,
    send, recv, local, tp_send, tp_recv, tp_local, kv_send, kv_recv, load, store, rest_send, rest_recv, sum_send, sum_recv,
):
    me, tp = lax.axis_index("ctx"), lax.axis_index("tp")
    core, side = me ^ 1, me ^ 2
    up, down, far = lax.rem(me + 4, 16), lax.rem(me + 12, 16), lax.rem(me + 8, 16)
    on_core, on_side = lax.rem(me, 2), lax.rem(me // 2, 2)
    cosine, sine, hot0, hot1 = (table.at[:, 128 * i : 128 * i + 128] for i in range(4))
    q_doc = table.at[:, 640:768]
    rows, model = x0.shape
    part = model // N_TP
    half = rows // 2
    experts = w_q.shape[0]
    width = w_q.shape[2]
    heads = width // HEAD_DIM
    span = (PAST + 1) * half
    greet([(core, tp)] + [(me ^ (2 * d), tp) for d in range(1, 8)] + [(me, tp ^ d) for d in range(1, N_TP)])

    kinds = ["flat", "flat", "rows", "cols"] + ["flat"] * experts + ["pair"] * (experts // 2)
    src = [s_kv, wide_mid, s_q, s_o] + [s_gu.at[e] for e in range(experts)]
    dst = [g_kv, g_wide, g_q, g_o] + [g_gu.at[e] for e in range(experts)]
    src += [s_d.at[pl.ds(e, 2)] for e in range(0, experts, 2)]
    dst += [g_d.at[pl.ds(e, 2)] for e in range(0, experts, 2)]
    tp_src, tp_dst, tp_kinds = [tokens, s_wide, cotangent], [x0, wide_mid, dy], ["cols", "rows", "cols"]
    started, staying = [], [None] * len(kinds)
    counter = [0] * len(kinds)

    def place_of(i):
        size = tp_src[i].shape[1 if tp_kinds[i] == "cols" else 0]
        return lambda rank: tp_part(tp_kinds[i], tp_dst[i], rank, size)

    tp_all = [Spread(tp_src[i], place_of(i), tp_send, tp_recv, i) for i in range(3)]

    def tp_own(i):
        return pltpu.make_async_copy(tp_src[i], place_of(i)(tp), tp_local.at[i])

    def tp_start(i):
        tp_all[i].start()
        tp_own(i).start()

    def tp_wait(i):
        tp_all[i].wait()
        tp_own(i).wait()

    def copy(t, item, owner, low, high, to, slot, own_shard):
        there = region(kinds[t], dst[t], owner, low, high)
        return pltpu.make_async_remote_copy(
            src_ref=own_part(kinds[t], src[t], low, high) if own_shard else there,
            dst_ref=there,
            send_sem=send.at[t, slot],
            recv_sem=recv.at[t, item],
            device_id=(to, tp),
            device_id_type=MESH,
        )

    def go(t, item, owner, low, high, to, own_shard=False):
        c = copy(t, item, owner, low, high, to, counter[t], own_shard)
        counter[t] += 1
        c.start()
        started.append(c)

    cuts = [2, 2, 3, 3, 3, 3, 3, 2, 2, 2]

    def arrive(t, item):
        cut = cuts[t]
        mid = cut // 2 if t % 2 else (cut + 1) // 2
        return {
            0: (side, 0, 4),
            1: (down, 0, 4),
            2: (up, 0, 4),
            3: (down ^ 2, 0, cut),
            4: (up ^ 2, 0, cut),
            5: (far, 2, 4),
            6: (far, 0, 2),
            7: (far ^ 2, mid, cut),
            8: (far ^ 2, 0, mid),
            9: (down ^ 2, cut, 4),
            10: (up ^ 2, cut, 4),
            11: (far ^ 2, cut, 4),
        }[item]

    def got(t, item):
        owner, low, high = arrive(t, item)
        copy(t, item, owner, low, high, core, 0, False).wait_recv()
        go(t, 12 + item, owner, low, high, core)

    def first(t):
        go(t, 0, me, 0, 4, side, True)
        go(t, 2, me, 0, 4, down, True)
        go(t, 1, me, 0, 4, up, True)
        go(t, 24, me, 0, 4, core, True)
        c = pltpu.make_async_copy(src[t], region(kinds[t], dst[t], me, 0, 4), local.at[t])
        c.start()
        staying[t] = c

    def second(t):
        got(t, 0)
        go(t, 3, side, 0, cuts[t], up)
        go(t, 4, side, 0, cuts[t], down)
        got(t, 1)
        go(t, 5, down, 2, 4, up)
        go(t, 9, down, cuts[t], 4, side)
        got(t, 2)
        go(t, 6, up, 0, 2, down)
        go(t, 10, up, cuts[t], 4, side)

    def third(t):
        got(t, 3)
        _, low, high = arrive(t, 7)
        go(t, 7, down ^ 2, low, high, up)
        got(t, 4)
        _, low, high = arrive(t, 8)
        go(t, 8, up ^ 2, low, high, down)
        got(t, 5)
        got(t, 6)
        go(t, 11, far, cuts[t], 4, side)

    def fourth(t):
        for item in range(7, 12):
            got(t, item)

    def finish(t):
        for item in range(12):
            owner, low, high = arrive(t, item)
            copy(t, 12 + item, owner ^ 1, low, high, core, 0, False).wait_recv()
        copy(t, 24, core, 0, 4, core, 0, False).wait_recv()

    def rest_copy(item, owner, to, source=None):
        there = g_rest.at[owner, tp]
        return pltpu.make_async_remote_copy(
            src_ref=there if source is None else source,
            dst_ref=there,
            send_sem=rest_send.at[item],
            recv_sem=rest_recv.at[item],
            device_id=(to, tp),
            device_id_type=MESH,
        )

    rest_all = Spread(None, lambda rank: g_rest.at[:, rank], tp_send, tp_recv, 3)
    rest_own = pltpu.make_async_copy(s_rest, g_rest.at[me, tp], tp_local.at[3])

    def rest_start():
        rest_own.start()
        for d in range(1, 8):
            rest_copy(d, me, me ^ (2 * d), s_rest).start()
        rest_copy(8, me, core, s_rest).start()

    def rest_core():
        for d in range(1, 8):
            rest_copy(d, me ^ (2 * d), core).wait_recv()
            rest_copy(8 + d, me ^ (2 * d), core).start()

    def rest_spread():
        for d in range(8):
            rest_copy(8 + d, core ^ (2 * d), core).wait_recv()
        rest_own.wait()
        rest_all.start()

    tp_start(1)
    tp_start(0)
    for t in (0, 2):
        first(t)
    tp_all[1].relay()
    tp_all[0].relay()
    tp_wait(1)
    first(1)
    rest_start()
    second(0)
    second(2)
    first(3)
    second(1)
    tp_wait(0)
    step = 32

    def normalize(i, carry):
        at = pl.ds(pl.multiple_of(i * step, step), step)
        n1[at, :] = rms_scale(x0[at, :].astype(f32), gain[...]).astype(bf16)
        return carry

    lax.fori_loop(0, rows // step, normalize, 0)
    gates[...] = masked_gates(dot(n1[...], router[...]), hot0[...] + hot1[...])

    third(0)
    third(2)
    third(1)
    first(4)
    first(5)
    fourth(0)
    fourth(2)
    fourth(1)

    def fetch(t, ref):
        finish(t)
        staying[t].wait()
        c = pltpu.make_async_copy(dst[t], ref, load.at[t])
        c.start()
        return c

    fetches = [fetch(0, w_kv), fetch(1, wide), fetch(2, w_q)]

    lane = lax.broadcasted_iota(jnp.int32, (rows, 128), 1)
    seq = lax.broadcasted_iota(jnp.int32, (rows, 128), 0) // half

    def rotary(x):
        return x * cosine[...] + pltpu.roll(x, HEAD_DIM // 2, 1) * sine[...]

    rest_core()
    fetches[0].wait()
    fetches[1].wait()
    z = dot(n1[...], wide[:, :128])
    z_q[...] = jnp.where(lane // 64 == seq, z, 0.0).astype(bf16)
    z = dot(n1[...], wide[:, 128:192])
    z_kv[...] = jnp.where((lane // 16) % 2 == seq, jnp.pad(z, ((0, 0), (0, 64))), 0.0).astype(bf16)
    kv = dot(n1[...], w_kv[...]) + dot(z_kv[:, :64], b_kv[...])
    for h in range(heads):
        at = slice(HEAD_DIM * h, HEAD_DIM * h + HEAD_DIM)
        turned = rotary(kv[:, at]).astype(bf16)
        kv_all[PAST, 0, :, at] = turned[:half]
        kv_all[PAST, 1, :, at] = turned[half:]
    for s in range(2):
        kv_all[PAST, s, :, width:] = kv[half * s : half * s + half, width:].astype(bf16)

    def kv_copy(slot, back, to, to_back):
        return pltpu.make_async_remote_copy(
            src_ref=kv_all.at[PAST - back],
            dst_ref=kv_all.at[PAST - to_back],
            send_sem=kv_send.at[slot],
            recv_sem=kv_recv.at[to_back],
            device_id=(to, tp),
            device_id_type=MESH,
        )

    def kv_arrived(back):
        kv_copy(0, back, core, back).wait_recv()

    def when(condition, c):
        if condition is None:
            c.start()
        else:
            pl.when(condition)(c.start)
        kv_started.append((condition, c))

    kv_started = []
    when(None, kv_copy(0, 0, up, 4))
    when(None, kv_copy(1, 0, far, 8))
    when(on_side == 0, kv_copy(2, 0, side, 2))
    when(on_core == 0, kv_copy(3, 0, core, 1))
    second(3)
    first(6)
    first(7)

    fetches[2].wait()
    queries = [jnp.zeros((rows, width), f32), jnp.zeros((rows, width), f32)]
    for e in range(experts):
        z_e = jnp.where((lane % 64) // 16 == e, z_q[...].astype(f32), 0.0).astype(bf16)
        q_e = dot(n1[...], w_q[e]) + dot(z_e, b_q[...])
        for k, hot in enumerate((hot0, hot1)):
            queries[k] = queries[k] + jnp.where(hot[:, e : e + 1] > 0, q_e, 0.0)
    for k in range(2):
        for h in range(heads):
            turned = rotary(queries[k][:, HEAD_DIM * h : HEAD_DIM * h + HEAD_DIM]).astype(bf16)
            for s in range(2):
                q_all[s * heads + h, k * half : k * half + half, :] = turned[half * s : half * s + half]

    rest_spread()
    tp_start(2)
    second(4)
    kv_arrived(4)
    when(on_side == 0, kv_copy(4, 4, side, 6))
    when(on_side == 1, kv_copy(5, 4, side, 2))
    when(on_core == 0, kv_copy(6, 4, core, 5))
    when(on_core == 1, kv_copy(7, 4, core, 3))
    kv_arrived(8)
    when(on_side == 1, kv_copy(8, 8, side, 6))
    when(on_core == 1, kv_copy(9, 8, core, 7))
    first(8)
    second(5)
    kv_arrived(2)
    when(on_core == 0, kv_copy(10, 2, core, 3))
    when(on_core == 1, kv_copy(11, 2, core, 1))
    kv_arrived(6)
    when(on_core == 0, kv_copy(12, 6, core, 7))
    when(on_core == 1, kv_copy(13, 6, core, 5))
    third(3)
    first(9)
    for back in (1, 3, 5, 7):
        kv_arrived(back)
    rest_all.relay()
    tp_all[2].relay()
    second(6)

    row = lax.broadcasted_iota(jnp.int32, (half, span), 0)
    key = lax.broadcasted_iota(jnp.int32, (half, span), 1)
    near = (key > row) & (key <= row + PAST * half)

    def attend(i, carry):
        s = i // heads
        h = lax.rem(i, heads)
        at = pl.ds(pl.multiple_of(h * HEAD_DIM, HEAD_DIM), HEAD_DIM)
        v_at = pl.ds(pl.multiple_of(width + h * HEAD_DIM, HEAD_DIM), HEAD_DIM)
        keys = kv_all[:, s, :, at].reshape(span, HEAD_DIM)
        values = kv_all[:, s, :, v_at].reshape(span, HEAD_DIM)
        seq_rows = pl.ds(pl.multiple_of(s * half, half), half)
        allowed = near & (q_doc[seq_rows, :1] == k_doc[s, :1, :])
        for k in range(2):
            q = q_all[i, k * half : k * half + half, :]
            scores = dot_nt(q, keys) * HEAD_DIM**-0.5
            scores = jnp.where(allowed, scores, big_negative)
            peak = jnp.max(scores, axis=1, keepdims=True)
            powers = jnp.exp(scores - peak)
            p = (powers * (1.0 / jnp.sum(powers, axis=1, keepdims=True))).astype(bf16)
            probs[i, k * half : k * half + half, :] = p
            ob[k, seq_rows, at] = dot(p, values).astype(bf16)
        return carry

    lax.fori_loop(0, 2 * heads, attend, 0)
    stores = []
    for i, (v, h) in enumerate(((n1, h_n1), (kv_all, h_kv_all), (q_all, h_q_all), (probs, h_probs))):
        c = pltpu.make_async_copy(v, h, store.at[i])
        c.start()
        stores.append(c)
    fourth(3)
    third(4)
    fetches.append(fetch(3, w_o))
    rest_all.wait()
    rest_load = pltpu.make_async_copy(g_rest, rest, load.at[4])
    rest_load.start()

    fetches[3].wait()
    rest_load.wait()
    z_acc = jnp.zeros((rows, 256), f32)
    pair_lane = lax.broadcasted_iota(jnp.int32, (rows, 256), 1)
    mine = pair_lane // 128 == lax.broadcasted_iota(jnp.int32, (rows, 256), 0) // half
    chosen = []
    for e in range(experts):
        o_e = jnp.where(hot0[:, e : e + 1] > 0, ob[0].astype(f32), 0.0)
        o_e = o_e + jnp.where(hot1[:, e : e + 1] > 0, ob[1].astype(f32), 0.0)
        o_e = o_e.astype(bf16)
        chosen.append(o_e)
        low = dot_nt(o_e, a_o[...]) * gates[:, e : e + 1]
        z_acc = z_acc + jnp.where(mine & ((pair_lane % 128) // 16 == e), low, 0.0)
    z_acc = z_acc.astype(bf16)
    z_o[...] = z_acc[:, :128] + z_acc[:, 128:]

    def columns(ref, rank):
        return ref.at[:, pl.ds(pl.multiple_of(rank * part, part), part)]

    scatter = Scatter(parts, held, relay, sum_send, sum_recv, 0)
    spread = Spread(None, lambda rank: columns(attn, rank), sum_send, sum_recv, 1)
    for d in (5, 6, 7, 4, 1, 2, 3, 0):
        at = pl.ds(pl.multiple_of((tp ^ d) * part, part), part)
        total = dot_nt(z_acc, rest[pl.ds(2 * (tp ^ d), 2), :, :, 256:512].reshape(part, 256))
        for e in range(experts):
            total = total + dot(chosen[e], w_o[e, :, at]) * gates[:, e : e + 1]
        if d:
            parts[d] = total.astype(bf16)
            if d != FAR:
                scatter.copy(d).start()
        else:
            own[...] = total
    second(7)
    scatter.relay()
    second(8)
    third(5)
    columns(attn, tp)[...] = scatter.total(own[...]).astype(bf16)
    spread.start()
    second(9)
    third(6)
    spread.relay()
    third(7)
    third(8)
    spread.wait()
    fourth(4)
    fourth(5)
    third(9)
    fourth(6)
    fourth(7)
    fourth(8)
    fourth(9)
    tp_wait(2)
    for t in range(4, len(kinds)):
        finish(t)
    for c in stores:
        c.wait()
    for c in started:
        c.wait_send()
    for t, c in enumerate(staying):
        if t > 3:
            c.wait()
    for condition, c in kv_started:
        if condition is None:
            c.wait_send()
        else:
            pl.when(condition)(c.wait_send)
    scatter.sent()
    spread.sent()
    for c in tp_all + [rest_all]:
        c.sent()
    for d in range(1, 8):
        rest_copy(d, me, me ^ (2 * d), s_rest).wait_send()
        rest_copy(8 + d, me ^ (2 * d), core).wait_send()
    rest_copy(8, me, core, s_rest).wait_send()


def attention(shards_in, tp_shards, small):
    s_q, s_kv, s_o, s_gu, s_d = shards_in
    tokens, cotangent, s_wide, s_rest = tp_shards
    rows, part = tokens.shape
    model = part * N_TP
    experts, _, width = s_q.shape
    half = rows // 2
    heads = width // HEAD_DIM
    shape = jax.ShapeDtypeStruct

    def grown(a, d):
        return shape(tuple(n * (N_CTX if i == d else 1) for i, n in enumerate(a.shape)), a.dtype)

    gathered = (grown(s_q, 1), grown(s_kv, 0), grown(s_o, 2), grown(s_gu, 1), grown(s_d, 2))
    wide_mid = shape((s_wide.shape[0] * N_TP, s_wide.shape[1]), bf16)
    wide = grown(wide_mid, 0)
    rest = shape((N_CTX, N_TP) + s_rest.shape, bf16)
    kept = (
        shape((rows, model), bf16),
        shape((PAST + 1, 2, half, 2 * width), bf16),
        shape((2 * heads, rows, HEAD_DIM), bf16),
        shape((2 * heads, rows, (PAST + 1) * half), bf16),
    )
    vmem_out = (
        shape((rows, model), bf16),
        shape((rows, model), bf16),
        shape((2, rows, width), bf16),
        shape((rows, 128), bf16),
        shape((rows, 128), bf16),
        shape((rows, 128), bf16),
        shape((rows, 128), f32),
    )
    any_out = gathered + (wide, wide_mid, shape((rows, model), bf16), rest) + kept
    return pl.pallas_call(
        attention_kernel,
        out_shape=any_out + vmem_out,
        in_specs=[ANY] * 9 + [VMEM] * len(small),
        out_specs=tuple([ANY] * len(any_out) + [VMEM] * len(vmem_out)),
        scratch_shapes=[pltpu.VMEM(a.shape, bf16) for a in kept]
        + [
            pltpu.VMEM(gathered[0].shape, bf16),
            pltpu.VMEM(gathered[1].shape, bf16),
            pltpu.VMEM(gathered[2].shape, bf16),
            pltpu.VMEM(wide.shape, bf16),
            pltpu.VMEM(rest.shape, bf16),
            pltpu.VMEM((N_TP, rows, part), bf16),
            pltpu.VMEM((rows, part), bf16),
            pltpu.VMEM((rows, part), f32),
            pltpu.VMEM((N_TP, rows, part), bf16),
            pltpu.SemaphoreType.DMA((10, 25)),
            pltpu.SemaphoreType.DMA((10, 25)),
            pltpu.SemaphoreType.DMA((10,)),
            pltpu.SemaphoreType.DMA((4, N_TP)),
            pltpu.SemaphoreType.DMA((4, N_TP)),
            pltpu.SemaphoreType.DMA((4,)),
            pltpu.SemaphoreType.DMA((14,)),
            pltpu.SemaphoreType.DMA((PAST + 1,)),
            pltpu.SemaphoreType.DMA((5,)),
            pltpu.SemaphoreType.DMA((4,)),
            pltpu.SemaphoreType.DMA((16,)),
            pltpu.SemaphoreType.DMA((16,)),
            pltpu.SemaphoreType.DMA((2, N_TP)),
            pltpu.SemaphoreType.DMA((2, N_TP)),
        ],
        compiler_params=pltpu.CompilerParams(
            collective_id=0, has_side_effects=True, vmem_limit_bytes=60 << 20
        ),
        name="attention",
    )(*shards_in, *tp_shards, *small)


def backward_kernel(
    dx1, dx1_own, ob, gates, z_q, z_kv, z_sum, table, gain, router, b_q, b_kv, a_o, ff_parts, ff_own,
    h_q, h_kv, h_o, h_wide, h_rest, h_x0, h_n1, h_n2, h_dy, h_kv_all, h_q_all, h_probs,
    mixed, grad_tokens, wide_a, wide_b, heads_out,
    w_q, w_kv, w_o, wide, rest, x0, n1, n2, dy, kv_all, q_all, probs, dob, dkv, dkv_held, dq, dkv_own, dn, parts, relay, own, held, ff_held, ff_relay,
    z_part, z_held, z_done, dots, tails, a_src, b_src, heads_src, a_core, b_core, heads_core, a_held, b_held, heads_held,
    load, tp_send, tp_recv, core_send, core_recv, kv_send, kv_recv, ctx_send, ctx_recv,
):
    me, tp = lax.axis_index("ctx"), lax.axis_index("tp")
    core = me ^ 1
    on_core = lax.rem(me, 2)
    rows, model = x0.shape
    cosine, sine, hot0, hot1 = (table.at[:, 128 * i : 128 * i + 128] for i in range(4))
    part = model // N_TP
    half = rows // 2
    experts = w_q.shape[0]
    width = w_q.shape[2]
    heads = width // HEAD_DIM
    span = (PAST + 1) * half
    loads = []
    for i, (h, w) in enumerate(
        (
            (h_rest, rest),
            (h_o, w_o),
            (h_kv_all, kv_all),
            (h_probs, probs),
            (h_q_all, q_all),
            (h_q, w_q),
            (h_n2, n2),
            (h_dy, dy),
            (h_n1, n1),
            (h_kv, w_kv),
            (h_x0, x0),
            (h_wide, wide),
        )
    ):
        c = pltpu.make_async_copy(h, w, load.at[i])
        c.start()
        loads.append(c)
    greet([(me ^ d, tp) for d in range(1, N_CTX)] + [(me, tp ^ d) for d in range(1, N_TP)])
    a_sum = CtxSum(a_src, a_core, a_held, None, ctx_send, ctx_recv, 0)
    b_sum = CtxSum(b_src, b_core, b_held, None, ctx_send, ctx_recv, 1)
    heads_sum = CtxSum(heads_src, heads_core, heads_held, heads_out, ctx_send, ctx_recv, 2)
    ff = Scatter(ff_parts, ff_held, ff_relay, tp_send, tp_recv, 4)
    for d in (5, 6, 7, 1, 2, 3):
        ff.copy(d).start()

    lane = lax.broadcasted_iota(jnp.int32, (rows, 128), 1)
    seq = lax.broadcasted_iota(jnp.int32, (rows, 128), 0) // half
    hots = (hot0, hot1)

    loads[0].wait()
    pair_lane = lax.broadcasted_iota(jnp.int32, (rows, 256), 1)
    mine = pair_lane // 128 == lax.broadcasted_iota(jnp.int32, (rows, 256), 0) // half
    dz_o = dot(dx1[...], rest[:, 256:512])
    loads[1].wait()
    g = [jnp.zeros((rows, width), f32), jnp.zeros((rows, width), f32)]
    g_ao = jnp.zeros((256, width), f32)
    for e in range(experts):
        dz_e = jnp.where(mine & ((pair_lane % 128) // 16 == e), dz_o, 0.0)
        g_e = dot_nt(dx1[...], w_o[e]) + dot(dz_e.astype(bf16), a_o[...])
        o_e = jnp.where(hot0[:, e : e + 1] > 0, ob[0].astype(f32), 0.0)
        o_e = o_e + jnp.where(hot1[:, e : e + 1] > 0, ob[1].astype(f32), 0.0)
        o_e = o_e.astype(bf16)
        dz_e = (dz_e * gates[:, e : e + 1]).astype(bf16)
        g_ao = g_ao + dot_tn(dz_e, o_e)
        for k in range(2):
            g[k] = g[k] + jnp.where(hots[k][:, e : e + 1] > 0, g_e, 0.0)
    d_gates = jnp.zeros((rows, 128), f32)
    for k in range(2):
        d_gate = jnp.sum(g[k] * ob[k].astype(f32), axis=1, keepdims=True)
        d_gates = d_gates + jnp.where(hots[k][...] > 0, d_gate, 0.0)
        gate = jnp.sum(hots[k][...] * gates[...], axis=1, keepdims=True)
        d_out = (g[k] * gate).astype(bf16)
        for s in range(2):
            for h in range(heads):
                dob[s * heads + h, k * half : k * half + half, :] = d_out[
                    half * s : half * s + half, HEAD_DIM * h : HEAD_DIM * h + HEAD_DIM
                ]
    d_logits = gates[...] * (d_gates - jnp.sum(gates[...] * d_gates, axis=1, keepdims=True))
    d_logits = d_logits.astype(bf16)

    def attend_back(i, carry):
        s = i // heads
        h = lax.rem(i, heads)
        at = pl.ds(pl.multiple_of(h * HEAD_DIM, HEAD_DIM), HEAD_DIM)
        v_at = pl.ds(pl.multiple_of(width + h * HEAD_DIM, HEAD_DIM), HEAD_DIM)
        keys = kv_all[:, s, :, at].reshape(span, HEAD_DIM)
        values = kv_all[:, s, :, v_at].reshape(span, HEAD_DIM)
        seq_rows = pl.ds(pl.multiple_of(s * half, half), half)
        d_keys = jnp.zeros((span, HEAD_DIM), f32)
        d_values = jnp.zeros((span, HEAD_DIM), f32)
        for k in range(2):
            k_rows = slice(k * half, k * half + half)
            d_o = dob[i, k_rows, :]
            p = probs[i, k_rows, :]
            delta = jnp.sum(d_o.astype(f32) * ob[k, seq_rows, at].astype(f32), axis=1, keepdims=True)
            d_s = (p.astype(f32) * (dot_nt(d_o, values) - delta)).astype(bf16)
            d_q = dot(d_s, keys) * HEAD_DIM**-0.5
            turned = d_q * cosine[seq_rows, :] - pltpu.roll(d_q, HEAD_DIM // 2, 1) * sine[seq_rows, :]
            dq[k, seq_rows, at] = turned.astype(bf16)
            d_keys = d_keys + dot_tn(d_s, q_all[i, k_rows, :])
            d_values = d_values + dot_tn(p, d_o)
        d_keys = (d_keys * HEAD_DIM**-0.5).astype(bf16)
        dkv[:, s, :, at] = d_keys.reshape(PAST + 1, half, HEAD_DIM)
        dkv[:, s, :, v_at] = d_values.astype(bf16).reshape(PAST + 1, half, HEAD_DIM)
        return carry

    for i in (2, 3, 4):
        loads[i].wait()
    lax.fori_loop(0, 2 * heads, attend_back, 0)

    def to_core(back):
        return pltpu.make_async_remote_copy(
            src_ref=dkv.at[PAST - back],
            dst_ref=dkv_held.at[back // 2],
            send_sem=core_send.at[back // 2],
            recv_sem=core_recv.at[back // 2],
            device_id=(core, tp),
            device_id_type=MESH,
        )

    def to_owner(back):
        return pltpu.make_async_remote_copy(
            src_ref=dkv.at[PAST - back],
            dst_ref=dkv_held.at[3 + back // 2],
            send_sem=kv_send.at[back // 2],
            recv_sem=kv_recv.at[back // 2],
            device_id=(lax.rem(me + N_CTX - back, N_CTX), tp),
            device_id_type=MESH,
        )

    for back in (1, 3, 5, 7):
        to_core(back).start()
    for back in (1, 3, 5, 7):
        to_core(back).wait_recv()
        slot = PAST - (back - 1) - 2 * on_core
        dkv[slot] = (dkv[slot].astype(f32) + dkv_held[back // 2].astype(f32)).astype(bf16)
    for back in (2, 4, 6, 8):
        to_owner(back).start()

    ff.relay()
    loads[5].wait()
    loads[11].wait()
    dz_q = jnp.zeros((rows, 128), f32)
    g_bq = jnp.zeros((128, width), f32)
    chosen = []
    for e in range(experts):
        dq_e = jnp.where(hot0[:, e : e + 1] > 0, dq[0].astype(f32), 0.0)
        dq_e = dq_e + jnp.where(hot1[:, e : e + 1] > 0, dq[1].astype(f32), 0.0)
        dq_e = dq_e.astype(bf16)
        chosen.append(dq_e)
        keep = (lane // 64 == seq) & ((lane % 64) // 16 == e)
        dz_q = dz_q + jnp.where(keep, dot_nt(dq_e, b_q[...]), 0.0)
        z_e = jnp.where(keep, z_q[...].astype(f32), 0.0).astype(bf16)
        g_bq = g_bq + dot_tn(z_e, dq_e)
    dz_q = dz_q.astype(bf16)
    z_part[:, :128] = dz_q
    for j in range(N_TP):
        at = slice(part * j, part * j + part)
        total = dot_nt(dz_q, wide[at, :128]) + dot_nt(d_logits, router[at, :])
        for e in range(experts):
            total = total + dot_nt(chosen[e], w_q[e, at, :])
        dn[j] = total
    for i in (6, 7, 8):
        loads[i].wait()
    own_columns = lax.broadcasted_iota(jnp.int32, (model, part), 1)
    own_columns = (own_columns // 16) * 128 + tp * 16 + own_columns % 16
    pick = (lax.broadcasted_iota(jnp.int32, (model, part), 0) == own_columns).astype(bf16)

    def to_pairs(ref, at, values):
        values = values.astype(bf16).reshape(8, 2, 16, values.shape[1])
        for c in range(2):
            ref[c, :, :, at] = values[:, c]

    n2_own = dot(n2[...], pick).astype(bf16)
    dx1_cols = dot(dx1[...], pick).astype(bf16)
    dy_own = dot(dy[...], pick).astype(bf16)
    n1_own = dot(n1[...], pick).astype(bf16)
    lane_m = lax.broadcasted_iota(jnp.int32, (part, 128), 1)
    for s in range(2):
        at = slice(half * s, half * s + half)
        to_pairs(a_src, slice(128 * s, 128 * s + 128), dot_tn(n2_own[at], z_sum[at, :128]))
        low = jnp.where(
            lane_m < 64, dot_tn(dx1_cols[at], z_sum[at, 128:]), dot_tn(dy_own[at], z_sum[at, 128:])
        )
        to_pairs(a_src, slice(256 + 128 * s, 384 + 128 * s), low)
    a_sum.start()

    total = dkv[PAST].astype(f32)
    for back in (2, 4, 6, 8):
        to_owner(back).wait_recv()
        total = total + dkv_held[3 + back // 2].astype(f32)
    a_sum.chips()
    for h in range(heads):
        at = slice(HEAD_DIM * h, HEAD_DIM * h + HEAD_DIM)
        d_k = jnp.concatenate([total[0, :, at], total[1, :, at]], axis=0)
        turned = d_k * cosine[...] - pltpu.roll(d_k, HEAD_DIM // 2, 1) * sine[...]
        dkv_own[:, at] = turned.astype(bf16)
    dkv_own[:, width:] = jnp.concatenate([total[0, :, width:], total[1, :, width:]], axis=0).astype(bf16)
    loads[9].wait()
    loads[10].wait()
    dz_kv = dot_nt(dkv_own[...], b_kv[...])
    keep = (lane[:, :64] // 16) % 2 == seq[:, :64]
    dz_kv = jnp.where(keep, dz_kv, 0.0).astype(bf16)
    z_part[:, 128:] = jnp.pad(dz_kv.astype(f32), ((0, 0), (0, 64))).astype(bf16)

    scatter = Scatter(parts, held, relay, tp_send, tp_recv, 0)
    z_rows = rows // N_TP

    def z_region(ref, rank):
        return ref.at[pl.ds(pl.multiple_of(rank * z_rows, z_rows), z_rows), :]

    def z_scatter(d):
        return pltpu.make_async_remote_copy(
            src_ref=z_region(z_part, tp ^ d),
            dst_ref=z_held.at[d],
            send_sem=tp_send.at[1, d],
            recv_sem=tp_recv.at[1, d],
            device_id=(me, tp ^ d),
            device_id_type=MESH,
        )

    def z_spread(d, rank):
        return pltpu.make_async_remote_copy(
            src_ref=z_region(z_done, rank),
            dst_ref=z_region(z_done, rank),
            send_sem=tp_send.at[2, d],
            recv_sem=tp_recv.at[2, d],
            device_id=(me, tp ^ d),
            device_id_type=MESH,
        )

    def tail(d, rank):
        return pltpu.make_async_remote_copy(
            src_ref=tails.at[rank],
            dst_ref=tails.at[rank],
            send_sem=tp_send.at[3, d],
            recv_sem=tp_recv.at[3, d],
            device_id=(me, tp ^ d),
            device_id_type=MESH,
        )

    for d in range(1, N_TP):
        z_scatter(d).start()
    g_bkv = dot_tn(z_kv[...], dkv_own[...])
    blocks = [g_bq[32 * i : 32 * i + 32] for i in range(4)] + [g_bkv[:32, :width], g_bkv[32:64, width:]]
    blocks += [g_ao[128 * s + 32 * i : 128 * s + 32 * i + 32] for s in range(2) for i in range(2)]
    blocks += [jnp.zeros((32, width), f32)] * 6
    for i in range(N_CTX):
        heads_src[i % 2, i // 2] = blocks[i].astype(bf16)
    heads_sum.start()
    def finish_z():
        total = z_region(z_part, tp)[...].astype(f32)
        for d in range(1, N_TP):
            z_scatter(d).wait_recv()
            total = total + z_held[d].astype(f32)
        z_region(z_done, tp)[...] = total.astype(bf16)
        for d in range(1, N_TP):
            z_spread(d, tp).start()

    along = jnp.zeros((rows, 1), f32)
    for d in (5, 6, 7, 4, 1, 2, 3, 0):
        if d == FAR:
            finish_z()
        peer = tp ^ d
        at = pl.ds(pl.multiple_of(peer * part, part), part)
        total = dn[peer] + dot_nt(dz_kv, wide[at, 128:192]) + dot_nt(dkv_own[...], w_kv[at, :])
        scaled = total * gain[:, at]
        along = along + jnp.sum(scaled * x0[:, at].astype(f32), axis=1, keepdims=True)
        if d:
            parts[d] = total.astype(bf16)
            if d != FAR:
                scatter.copy(d).start()
        else:
            own[...] = total
    dots[...] = jnp.broadcast_to(along, dots.shape)
    tails[tp] = jnp.transpose(dots[...])[:8, :]
    for d in range(1, N_TP):
        tail(d, tp).start()
    heads_sum.chips()
    mixed[...] = ff.total(ff_own[...]).astype(bf16)
    scatter.relay()
    heads_sum.again()
    for d in range(1, N_TP):
        z_spread(d, tp ^ d).wait_recv()
    to_pairs(b_src, slice(0, part), dot_tn(n1_own, z_done[...]))
    b_sum.start()
    total = scatter.total(own[...])
    b_sum.chips()
    for d in range(1, N_TP):
        tail(d, tp ^ d).wait_recv()
    whole = tails[0]
    for d in range(1, N_TP):
        whole = whole + tails[d]
    dots[...] = jnp.transpose(jnp.broadcast_to(whole[:1], (128, rows)))
    own_at = pl.ds(pl.multiple_of(tp * part, part), part)
    own[...] = total * gain[:, own_at]
    step = 32

    def finish(i, carry):
        at = pl.ds(pl.multiple_of(i * step, step), step)
        x = x0[at, :].astype(f32)
        inverse = lax.rsqrt(jnp.mean(x * x, axis=1, keepdims=True) + eps)
        mean = dots[at, :1] * (1.0 / model)
        back = inverse * own[at, :] - x0[at, own_at].astype(f32) * inverse**3 * mean
        grad_tokens[at, :] = (dx1_own[at, :] + back).astype(bf16)
        return carry

    lax.fori_loop(0, rows // step, finish, 0)
    wide_a[...] = a_sum.total()
    heads_sum.other_core()
    wide_b[...] = b_sum.total()
    heads_sum.finish()
    for back in (1, 3, 5, 7):
        to_core(back).wait_send()
        to_owner(back + 1).wait_send()
    scatter.sent()
    ff.sent()
    for d in range(1, N_TP):
        z_scatter(d).wait_send()
        z_spread(d, tp).wait_send()
        tail(d, tp).wait_send()


def backward(vmem, hbm):
    dx1 = vmem[0]
    w_q = hbm[0]
    rows, model = dx1.shape
    part = model // N_TP
    width = w_q.shape[2]
    heads = width // HEAD_DIM
    half = rows // 2
    shape = jax.ShapeDtypeStruct
    reduced = [(2, 8, 16, 512), (2, 8, 16, part), (2, 8, 32, width)]
    return pl.pallas_call(
        backward_kernel,
        out_shape=(
            shape((rows, part), bf16),
            shape((rows, part), bf16),
            shape((16, 512), f32),
            shape((16, part), f32),
            shape(reduced[2], bf16),
        ),
        in_specs=[VMEM] * len(vmem) + [ANY] * len(hbm),
        out_specs=tuple([VMEM] * 5),
        scratch_shapes=[
            pltpu.VMEM(a.shape, bf16) for a in hbm
        ]
        + [
            pltpu.VMEM((2 * heads, rows, HEAD_DIM), bf16),
            pltpu.VMEM(hbm[9].shape, bf16),
            pltpu.VMEM((8,) + hbm[9].shape[1:], bf16),
            pltpu.VMEM((2, rows, width), bf16),
            pltpu.VMEM((rows, 2 * width), bf16),
            pltpu.VMEM((N_TP, rows, part), f32),
            pltpu.VMEM((N_TP, rows, part), bf16),
            pltpu.VMEM((rows, part), bf16),
            pltpu.VMEM((rows, part), f32),
            pltpu.VMEM((N_TP, rows, part), bf16),
            pltpu.VMEM((N_TP, rows, part), bf16),
            pltpu.VMEM((rows, part), bf16),
            pltpu.VMEM((rows, 256), bf16),
            pltpu.VMEM((N_TP, rows // N_TP, 256), bf16),
            pltpu.VMEM((rows, 256), bf16),
            pltpu.VMEM((rows, 128), f32),
            pltpu.VMEM((N_TP, 8, rows), f32),
        ]
        + [pltpu.VMEM(a, bf16) for a in reduced]
        + [pltpu.VMEM(a[1:], bf16) for a in reduced + reduced]
        + [
            pltpu.SemaphoreType.DMA((len(hbm),)),
            pltpu.SemaphoreType.DMA((5, N_TP)),
            pltpu.SemaphoreType.DMA((5, N_TP)),
            pltpu.SemaphoreType.DMA((4,)),
            pltpu.SemaphoreType.DMA((4,)),
            pltpu.SemaphoreType.DMA((5,)),
            pltpu.SemaphoreType.DMA((5,)),
            pltpu.SemaphoreType.DMA((3, 16)),
            pltpu.SemaphoreType.DMA((3, 16)),
        ],
        compiler_params=pltpu.CompilerParams(
            collective_id=3, has_side_effects=True, vmem_limit_bytes=60 << 20
        ),
        name="backward",
    )(*vmem, *hbm)


def shards(
    tokens,
    norm1_gain,
    router_attn,
    w_query,
    w_key_value,
    w_out,
    norm2_gain,
    router_ffn,
    w_gate_up,
    w_down,
    adapt_wide,
    adapt_heads,
    adapt_ffn,
    attention_routes,
    feedforward_routes,
    doc_lengths,
    adapter_index,
    cotangent,
):
    seqs, block, part = tokens.shape
    rows = seqs * block
    n_tp = lax.axis_size("tp")
    model = part * n_tp
    experts = w_query.shape[0]
    width = w_query.shape[2]
    heads = width // HEAD_DIM
    hidden = w_down.shape[1]
    rank = adapt_heads.shape[2]
    wide_slots = adapt_wide.shape[1]
    ctx_rank = lax.axis_index("ctx")


    def by_sequence(a):
        first = adapter_index[0] == 0
        return jnp.stack([jnp.where(first, a[0], a[1]), jnp.where(first, a[1], a[0])])

    wide_own = by_sequence(adapt_wide.astype(bf16))
    groups = [[6, 10, 7, 11, 8, 12, 9, 13], list(range(14, 22)), [0, 1, 2, 3], [4, 5]]
    order = [(q, s) for g in groups[:3] for q in range(seqs) for s in g]
    order += [(q, s) for s in groups[3] for q in range(seqs)]
    wide_cols = wide_own.reshape(seqs * wide_slots, rank, -1)[
        np.array([q * wide_slots + s for q, s in order])
    ].reshape(seqs * wide_slots * rank, -1).T
    heads_low = by_sequence(adapt_heads.astype(bf16))
    ffn_low = by_sequence(adapt_ffn.astype(bf16))
    route_a = attention_routes.reshape(rows, -1)
    route_f = feedforward_routes.reshape(rows, -1)

    positions = ctx_rank * block + jnp.arange(block, dtype=jnp.int32)
    doc_ids, offsets = doc_layout(doc_lengths, positions)
    half = HEAD_DIM // 2
    frequency = 10000.0 ** (-2.0 * jnp.arange(half, dtype=f32) / HEAD_DIM)
    angles = offsets.astype(f32).reshape(rows)[:, None] * frequency
    cosine, sine = jnp.cos(angles), jnp.sin(angles)
    cosine = jnp.concatenate([cosine, cosine], axis=1)
    sine = jnp.concatenate([-sine, sine], axis=1)

    b_q, b_kv, a_o = heads_low[:, :experts], heads_low[:, experts : experts + 2], heads_low[:, experts + 2 :]
    key_pos = (ctx_rank - PAST) * block + jnp.arange((PAST + 1) * block, dtype=jnp.int32)
    key_doc = doc_layout(doc_lengths, jnp.maximum(key_pos, 0))[0]
    key_doc = jnp.where(key_pos[None, :] >= 0, key_doc, -(1 << 20))
    blank = jnp.zeros((seqs, rank, width), bf16)
    b_kv_wide = jnp.concatenate(
        [
            jnp.concatenate([b_kv[:, 0], blank], axis=-1).reshape(seqs * rank, 2 * width),
            jnp.concatenate([blank, b_kv[:, 1]], axis=-1).reshape(seqs * rank, 2 * width),
        ],
        axis=0,
    )
    a_o_wide = jnp.pad(a_o.reshape(seqs, experts * rank, width), ((0, 0), (0, 64), (0, 0))).reshape(256, width)
    b_q = b_q.reshape(seqs * experts * rank, width)
    table = jnp.concatenate(
        [
            cosine,
            sine,
            widen_routes(route_a[:, :1], experts),
            widen_routes(route_a[:, 1:], experts),
            widen_routes(route_f, experts),
            jnp.broadcast_to(doc_ids.reshape(rows, 1).astype(f32), (rows, 128)),
        ],
        axis=1,
    )
    router_wide = jnp.pad(router_attn, ((0, 0), (0, 128 - experts)))
    (
        w_query, w_key_value, w_out, w_gate_up, w_down, wide, _, dy, rest,
        n1, kv_all, q_all, probs, x0, sum_out, ob, z_o_gated, z_q, z_kv, gates,
    ) = attention(
        [
            w_query,
            w_key_value.reshape(-1, 2 * width),
            w_out,
            gate_up_columns(w_gate_up[:, :, 0], w_gate_up[:, :, 1]),
            w_down,
        ],
        [tokens.reshape(rows, part), cotangent.reshape(rows, part), wide_cols[:, 512:], wide_cols[:, :512]],
        [
            norm1_gain[None],
            router_wide,
            table,
            jnp.broadcast_to(key_doc[:, None, :], (seqs, 8, key_doc.shape[1])).astype(f32),
            b_q,
            b_kv_wide,
            a_o_wide,
        ],
    )
    blank = jnp.zeros((seqs, experts, rank, hidden), bf16)
    b_gu = jnp.stack(
        [gate_up_columns(ffn_low[:, :experts], blank), gate_up_columns(blank, ffn_low[:, experts : 2 * experts])],
        axis=2,
    ).reshape(seqs, 2 * experts * rank, 2 * hidden)
    a_d = jnp.pad(ffn_low[:, 2 * experts :].reshape(seqs, experts * rank, hidden), ((0, 0), (64, 0), (0, 0)))
    rest = rest.reshape(model, 512)
    ff_parts, ff_own, dx1b, dx1_own, n2, z_sum, gu_sum, d_sum = feed_forward(
        [
            norm2_gain[None],
            jnp.pad(router_ffn, ((0, 0), (0, 128 - experts))),
            table,
            b_gu.reshape(256, 2 * hidden),
            a_d.reshape(256, hidden),
            z_o_gated,
        ],
        [x0, sum_out, rest, dy, w_gate_up, w_down],
    )
    mixed, grad_tokens, wide_a, wide_b, head_sum = backward(
        [
            dx1b, dx1_own, ob, gates, z_q, z_kv, z_sum, table, norm1_gain[None], router_wide, b_q, b_kv_wide, a_o_wide, ff_parts, ff_own,
        ],
        [w_query, w_key_value, w_out, wide, rest, x0, n1, n2, dy, kv_all, q_all, probs],
    )
    grad_wide = jnp.concatenate([wide_a, wide_b[:, : 704 - 512]], axis=1).T
    back_order = np.argsort(np.array([q * wide_slots + s for q, s in order]))
    grad_wide = grad_wide.reshape(seqs * wide_slots, rank, -1)[back_order]
    grad_wide = by_sequence(grad_wide.reshape(seqs, wide_slots, rank, -1))
    head_sum = jnp.swapaxes(head_sum, 0, 1).reshape(-1, rank, width).astype(f32)
    grad_heads = by_sequence(jnp.concatenate(
        [
            head_sum[: seqs * experts].reshape(seqs, experts, rank, width),
            jnp.swapaxes(head_sum[8:12].reshape(2, seqs, rank, width), 0, 1),
            head_sum[12:20].reshape(seqs, experts, rank, width),
        ],
        axis=1,
    ))
    gu_sum = jnp.swapaxes(gu_sum, 0, 1).reshape(seqs, experts, 2, rank, 768).astype(f32)
    grad_ffn = by_sequence(jnp.concatenate(
        [
            gu_sum[:, :, 0, :, :704],
            jnp.concatenate([gu_sum[:, :, 1, :, :640], gu_sum[:, :, 1, :, 704:]], axis=-1),
            jnp.swapaxes(d_sum, 0, 1).reshape(seqs, experts, rank, hidden),
        ],
        axis=1,
    ))
    mixed = mixed.reshape(seqs, block, part)
    grad_tokens = grad_tokens.reshape(seqs, block, part)
    return (mixed, grad_tokens, grad_wide, grad_heads, grad_ffn)


def solution(mesh):
    placed = (
        P(None, "ctx", "tp"),
        P(),
        P(),
        P(None, "ctx", "tp"),
        P("ctx", None, "tp"),
        P(None, "tp", "ctx"),
        P(),
        P(),
        P(None, "ctx", None, "tp"),
        P(None, "tp", "ctx"),
        P(None, None, None, ("ctx", "tp")),
        P(None, None, None, "tp"),
        P(None, None, None, "tp"),
        P(None, "ctx", None),
        P(None, "ctx", None),
        P(),
        P(),
        P(None, "ctx", "tp"),
    )
    return jax.shard_map(
        shards,
        mesh=mesh,
        in_specs=placed,
        out_specs=(
            P(None, "ctx", "tp"),
            P(None, "ctx", "tp"),
            P(None, None, None, ("ctx", "tp")),
            P(None, None, None, "tp"),
            P(None, None, None, "tp"),
        ),
        check_vma=False,
    )
```

```python
import functools

import jax
import numpy as np
import jax.numpy as jnp
from jax import lax
from jax.experimental import pallas as pl
from jax.experimental.pallas import tpu as pltpu
from jax.sharding import PartitionSpec as P

HEAD_DIM = 128
WINDOW = 1024
eps = 1e-06
big_negative = -1e30
bf16 = jnp.bfloat16
f32 = jnp.float32

MESH = pl.DeviceIdType.MESH
ANY = pl.BlockSpec(memory_space=pl.ANY)
VMEM = pl.BlockSpec(memory_space=pltpu.VMEM)
N_CTX, N_TP = 16, 8
FAR = 4
PAST = 8


def region(kind, ref, owner, low, high):
    rows = pl.ds(pl.multiple_of(owner * 128 + 32 * low, 32), 32 * (high - low))
    cols = pl.ds(pl.multiple_of(owner * 128, 128), 128)
    if kind == "rows":
        return ref.at[pl.ds(low, high - low), cols, :]
    if kind == "flat":
        return ref.at[rows, :]
    if kind == "cols":
        return ref.at[pl.ds(low, high - low), :, cols]
    if high - low == 1:
        half = ref.shape[1] // 2
        return ref.at[low // 2, pl.ds(half * (low % 2), half), cols]
    return ref.at[pl.ds(low // 2, (high - low) // 2), :, cols]


def own_part(kind, ref, low, high):
    if kind == "flat":
        return ref.at[pl.ds(32 * low, 32 * (high - low)), :]
    if kind == "pair":
        return ref
    return ref.at[pl.ds(low, high - low)]


def tp_part(kind, ref, rank, size):
    if kind == "cols":
        return ref.at[:, pl.ds(pl.multiple_of(rank * size, size), size)]
    return ref.at[pl.ds(pl.multiple_of(rank * size, size), size), :]


def rms_scale(values, gain):
    return values * lax.rsqrt(jnp.mean(values * values, axis=-1, keepdims=True) + eps) * gain


def doc_layout(doc_lengths, positions):
    docs = doc_lengths.shape[1]
    upto = np.tril(np.ones((docs, docs), np.int32))
    ends = jnp.sum(doc_lengths[:, None, :] * upto[None], axis=2)
    passed = positions[None, :, None] >= ends[:, None, :]
    doc_ids = jnp.sum(passed.astype(jnp.int32), axis=2)
    starting = jnp.sum(jnp.where(passed, doc_lengths[:, None, :], 0), axis=2)
    inside = positions[None, :] < ends[:, -1:]
    doc_ids = jnp.where(inside, doc_ids, -1 - positions[None, :])
    return (doc_ids, positions[None, :] - starting)


def dot(a, b, ca=1, cb=0):
    return lax.dot_general(a, b, (((ca,), (cb,)), ((), ())), preferred_element_type=f32)


class Scatter:
    def __init__(self, parts, held, relay, send, recv, row):
        self.me, self.tp = lax.axis_index("ctx"), lax.axis_index("tp")
        self.parts, self.held, self.relay_buffer = parts, held, relay
        self.send, self.recv, self.row = send, recv, row

    def copy_to(self, d, to):
        return pltpu.make_async_remote_copy(
            src_ref=self.parts.at[d],
            dst_ref=self.held.at[d],
            send_sem=self.send.at[self.row, d],
            recv_sem=self.recv.at[self.row, d],
            device_id=(self.me, self.tp ^ to),
            device_id_type=MESH,
        )

    def copy(self, d):
        if d != FAR:
            return self.copy_to(d, d % FAR)
        return pltpu.make_async_remote_copy(
            src_ref=self.relay_buffer,
            dst_ref=self.held.at[FAR],
            send_sem=self.send.at[self.row, FAR],
            recv_sem=self.recv.at[self.row, FAR],
            device_id=(self.me, self.tp ^ FAR),
            device_id_type=MESH,
        )

    def relay(self):
        total = self.parts[FAR].astype(f32)
        for d in range(FAR + 1, N_TP):
            self.copy(d).wait_recv()
            total = total + self.held[d].astype(f32)
        self.relay_buffer[...] = total.astype(bf16)
        self.copy(FAR).start()

    def total(self, own):
        for d in range(1, FAR + 1):
            self.copy(d).wait_recv()
            own = own + self.held[d].astype(f32)
        return own

    def sent(self):
        for d in range(1, N_TP):
            self.copy(d).wait_send()


class Spread:
    def __init__(self, source, place, send, recv, row):
        self.me, self.tp = lax.axis_index("ctx"), lax.axis_index("tp")
        self.source, self.place = source, place
        self.send, self.recv, self.row = send, recv, row

    def copy(self, d, owner, to, source=None):
        return pltpu.make_async_remote_copy(
            src_ref=self.place(owner) if source is None else source,
            dst_ref=self.place(owner),
            send_sem=self.send.at[self.row, d],
            recv_sem=self.recv.at[self.row, d],
            device_id=(self.me, self.tp ^ to),
            device_id_type=MESH,
        )

    def start(self):
        for d in (FAR, 1, 2, 3):
            self.copy(d, self.tp, d, self.source).start()

    def relay(self):
        self.copy(FAR, self.tp ^ FAR, FAR).wait_recv()
        for d in (1, 2, 3):
            self.copy(FAR + d, self.tp ^ FAR, d).start()

    def wait(self):
        for d in (1, 2, 3):
            self.copy(d, self.tp ^ d, d).wait_recv()
            self.copy(FAR + d, self.tp ^ (FAR + d), d).wait_recv()

    def sent(self):
        for d in (FAR, 1, 2, 3):
            self.copy(d, self.tp, d, self.source).wait_send()
        for d in (1, 2, 3):
            self.copy(FAR + d, self.tp ^ FAR, d).wait_send()


class CtxSum:
    def __init__(self, source, core_held, held, out, send, recv, row):
        self.me, self.tp = lax.axis_index("ctx"), lax.axis_index("tp")
        self.core, self.chip = lax.rem(self.me, 2), self.me // 2
        self.source, self.core_held, self.held, self.out = source, core_held, held, out
        self.send, self.recv, self.row = send, recv, row

    def copy(self, item, src, dst, to):
        return pltpu.make_async_remote_copy(
            src_ref=src,
            dst_ref=dst,
            send_sem=self.send.at[self.row, item],
            recv_sem=self.recv.at[self.row, item],
            device_id=(to, self.tp),
            device_id_type=MESH,
        )

    def to_core(self):
        return self.copy(0, self.source.at[1 - self.core], self.core_held, self.me ^ 1)

    def to_chip(self, d):
        return self.copy(
            d, self.source.at[self.core, self.chip ^ d], self.held.at[d], self.me ^ (2 * d)
        )

    def spread(self, d, chip):
        there = self.out.at[self.core, chip]
        return self.copy(7 + d, there, there, self.me ^ (2 * d))

    def back_to_core(self, core):
        return self.copy(15, self.out.at[core], self.out.at[core], self.me ^ 1)

    def start(self):
        self.to_core().start()

    def chips(self):
        self.to_core().wait()
        self.source[self.core] = (
            self.source[self.core].astype(f32) + self.core_held[...].astype(f32)
        ).astype(self.source.dtype)
        for d in range(1, 8):
            self.to_chip(d).start()

    def total(self):
        total = self.source[self.core, self.chip].astype(f32)
        for d in range(1, 8):
            self.to_chip(d).wait_recv()
            total = total + self.held[d].astype(f32)
        for d in range(1, 8):
            self.to_chip(d).wait_send()
        return total

    def again(self):
        self.out[self.core, self.chip] = self.total().astype(self.out.dtype)
        for d in range(1, 8):
            self.spread(d, self.chip).start()

    def other_core(self):
        for d in range(1, 8):
            self.spread(d, self.chip ^ d).wait_recv()
            self.spread(d, self.chip).wait_send()
        self.back_to_core(self.core).start()

    def finish(self):
        self.back_to_core(1 - self.core).wait_recv()
        self.back_to_core(self.core).wait_send()


def dot_nt(a, b):
    return dot(a, b, 1, 1)


def dot_tn(a, b):
    return dot(a, b, 0, 0)


def by_seq(rows, f):
    half = rows.shape[0] // 2
    return jnp.concatenate([f(0, rows[:half]), f(1, rows[half:])], axis=0)


def column_of(values, lane, e):
    return jnp.sum(jnp.where(lane == e, values, 0.0), axis=1, keepdims=True)


def greet(targets):
    barrier = pltpu.get_barrier_semaphore()
    for device in targets:
        pl.semaphore_signal(barrier, inc=1, device_id=device, device_id_type=MESH)
    pl.semaphore_wait(barrier, len(targets))


def masked_gates(logits, hot):
    largest = jnp.max(jnp.where(hot > 0, logits, big_negative), axis=1, keepdims=True)
    powers = jnp.where(hot > 0, jnp.exp(logits - largest), 0.0)
    return powers / jnp.sum(powers, axis=1, keepdims=True)


def ffn_kernel(
    gain, router, table, b_gu, a_d, z_o, h_x0, h_attn, h_wide, h_dy, w_gu_hbm, w_d_hbm,
    ff_parts, ff_own, dx1, dx1_own, n2, z_sum, gu_out, d_out,
    x0, attn, wide, dy, w_gu, w_d, hg, dgu, dh_tmp, z_gu, dz_d, z_part, parts, relay, own, held, z_held, dots, tails, inverse,
    g_gu, g_d, gu_src, gu_core, gu_held, d_src, d_core, d_held,
    load, small_load, send, recv, ctx_send, ctx_recv,
):
    me, tp = lax.axis_index("ctx"), lax.axis_index("tp")
    hot = table.at[:, 512:640]
    rows, model = x0.shape
    experts = w_gu.shape[0]
    part = model // N_TP
    smalls = []
    for i, (h, v) in enumerate(((h_x0, x0), (h_attn, attn), (h_wide, wide), (h_dy, dy))):
        c = pltpu.make_async_copy(h, v, small_load.at[i])
        c.start()
        smalls.append(c)

    def fetch(e):
        return (
            pltpu.make_async_copy(w_gu_hbm.at[e], w_gu.at[e], load.at[0, e]),
            pltpu.make_async_copy(w_d_hbm.at[e], w_d.at[e], load.at[1, e]),
        )


    greet([(me ^ d, tp) for d in range(1, N_CTX)] + [(me, tp ^ d) for d in range(1, N_TP)])
    for e in range(experts):
        for c in fetch(e):
            c.start()
    for c in smalls:
        c.wait()
    step = 32

    def normalize(i, carry):
        at = pl.ds(pl.multiple_of(i * step, step), step)
        x = x0[at, :].astype(f32) + attn[at, :].astype(f32)
        r = lax.rsqrt(jnp.mean(x * x, axis=1, keepdims=True) + eps)
        inverse[at, :] = jnp.broadcast_to(r, (step, 128))
        n2[at, :] = (x * r * gain[...]).astype(bf16)
        return carry

    lax.fori_loop(0, rows // step, normalize, 0)
    lane = lax.broadcasted_iota(jnp.int32, (rows, 128), 1)
    gates = masked_gates(dot(n2[...], router[...]), hot[...])
    pair_lane = lax.broadcasted_iota(jnp.int32, (rows, 256), 1)
    mine = pair_lane // 128 == lax.broadcasted_iota(jnp.int32, (rows, 256), 0) // (rows // 2)
    pair_lane = pair_lane % 128
    z_gu[...] = jnp.where(mine, dot(n2[...], wide[:, :256]), 0.0).astype(bf16)
    dz_d[...] = jnp.where(mine, dot(dy[...], wide[:, 256:512]), 0.0).astype(bf16)
    g_gu[...] = jnp.zeros_like(g_gu)
    g_d[...] = jnp.zeros_like(g_d)
    zero = jnp.zeros((rows, 256), f32)

    def expert(e, carry):
        d_gates, dz_gu, z_d = carry
        for c in fetch(e):
            c.wait()
        gate = column_of(gates, lane, e)
        z_in = jnp.where(pair_lane // 32 == e, z_gu[...].astype(f32), 0.0).astype(bf16)
        dz_in = jnp.where(pair_lane // 16 == 4 + e, dz_d[...].astype(f32), 0.0).astype(bf16)
        dh_tmp[:, :704] = dot_nt(dy[...], w_d[e]) + dot(dz_in, a_d[...])
        pre = dot(n2[...], w_gu[e]) + dot(z_in, b_gu[...])

        def tile(g, u, d):
            sg = jax.nn.sigmoid(g)
            silu = g * sg
            h = silu * u
            dg = d * gate
            return h, (dg * u * sg * (1.0 + g * (1.0 - sg))), dg * silu, h * d

        h, dgp, dup, hd = tile(pre[:, :640], pre[:, 640:1280], dh_tmp[:, :640])
        hg[e, :, :640] = (h * gate).astype(bf16)
        dgu[e, :, :640] = dgp.astype(bf16)
        dgu[e, :, 640:1280] = dup.astype(bf16)
        dgf = jnp.sum(hd, axis=1, keepdims=True)
        last = pre[:, 1280:]
        h, dgp, dup, hd = tile(last, pltpu.roll(last, 64, 1), dh_tmp[:, 640:])
        hg[e, :, 640:] = (h * gate).astype(bf16)[:, :64]
        dgu[e, :, 1280:] = jnp.where(lane < 64, dgp, pltpu.roll(dup, 64, 1)).astype(bf16)
        dgf = dgf + jnp.sum(jnp.where(lane < 64, hd, 0.0), axis=1, keepdims=True)
        d_gates = d_gates + jnp.where(lane == e, dgf, 0.0)
        keep = mine & (pair_lane // 32 == e)
        dz_gu = dz_gu + jnp.where(keep, dot_nt(dgu[e], b_gu[...]), 0.0)
        keep = mine & (pair_lane // 16 == 4 + e)
        z_d = z_d + jnp.where(keep, dot_nt(hg[e], a_d[...]), 0.0)
        g_gu[...] += dot_tn(z_in, dgu[e])
        g_d[...] += dot_tn(dz_in, hg[e])
        return d_gates, dz_gu, z_d

    d_gates, dz_gu, z_d = lax.fori_loop(
        0, experts, expert, (jnp.zeros((rows, 128), f32), zero, zero)
    )
    d_logits = gates * (d_gates - jnp.sum(gates * d_gates, axis=1, keepdims=True))
    d_logits = d_logits.astype(bf16)
    dz_gu, z_d = dz_gu.astype(bf16), z_d.astype(bf16)
    z_part[:, :128] = dz_gu[:, :128] + dz_gu[:, 128:]
    z_part[:, 128:] = z_o[...] + z_d[:, :128] + z_d[:, 128:]

    for i in range(N_CTX):
        s, slot = i // 8, i % 8
        at = slice(128 * s + 16 * slot, 128 * s + 16 * slot + 16)
        cols = 640 * (slot % 2)
        gu_src[i % 2, i // 2, :, :640] = g_gu[at, cols : cols + 640].astype(bf16)
        gu_src[i % 2, i // 2, :, 640:] = g_gu[at, 1280:].astype(bf16)
        first = 128 * s + 64 + 8 * slot
        d_src[i % 2, i // 2] = g_d[first : first + 8, :]
    gu_sum = CtxSum(gu_src, gu_core, gu_held, gu_out, ctx_send, ctx_recv, 0)
    d_sum = CtxSum(d_src, d_core, d_held, d_out, ctx_send, ctx_recv, 1)
    gu_sum.start()
    d_sum.start()
    scatter = Scatter(parts, held, relay, send, recv, 0)

    def x_at(at):
        return x0[:, at].astype(f32) + attn[:, at].astype(f32)

    def piece(j, along):
        d = lax.rem(j + FAR + 1, N_TP)
        peer = tp ^ d
        at = pl.ds(pl.multiple_of(peer * part, part), part)
        w_rows = wide[at, :256]
        dn = dot_nt(d_logits, router[at, :])
        dn = dn + dot_nt(dz_gu, w_rows)
        for e in range(experts):
            dn = dn + dot_nt(dgu[e], w_gu[e, at, :])
        parts[d] = dn.astype(bf16)

        @pl.when((d != 0) & (d != FAR))
        def _():
            scatter.copy_to(d, lax.rem(d, FAR)).start()

        @pl.when(d == 0)
        def _():
            own[...] = dn

        return along + jnp.sum(dn * gain[:, at] * x_at(at), axis=1, keepdims=True)

    def out_piece(d, carry):
        peer = tp ^ d
        at = pl.ds(pl.multiple_of(peer * part, part), part)
        w_rows = wide[at, 256:512]
        ff = dot_nt(z_d, w_rows)
        for e in range(experts):
            ff = ff + dot(hg[e], w_d[e, :, at])
        ff_parts[d] = ff.astype(bf16)

        @pl.when(d == 0)
        def _():
            ff_own[...] = ff + x_at(at)

        return carry

    z_rows = rows // N_TP

    def z_region(ref, rank):
        return ref.at[pl.ds(pl.multiple_of(rank * z_rows, z_rows), z_rows), :]

    def z_scatter(d):
        return pltpu.make_async_remote_copy(
            src_ref=z_region(z_part, tp ^ d),
            dst_ref=z_held.at[d],
            send_sem=send.at[2, d],
            recv_sem=recv.at[2, d],
            device_id=(me, tp ^ d),
            device_id_type=MESH,
        )

    def z_spread(d, rank):
        return pltpu.make_async_remote_copy(
            src_ref=z_region(z_sum, rank),
            dst_ref=z_region(z_sum, rank),
            send_sem=send.at[3, d],
            recv_sem=recv.at[3, d],
            device_id=(me, tp ^ d),
            device_id_type=MESH,
        )

    def columns(ref, rank):
        return ref.at[:, pl.ds(pl.multiple_of(rank * part, part), part)]

    def tail(d, rank):
        return pltpu.make_async_remote_copy(
            src_ref=tails.at[rank],
            dst_ref=tails.at[rank],
            send_sem=send.at[5, d],
            recv_sem=recv.at[5, d],
            device_id=(me, tp ^ d),
            device_id_type=MESH,
        )

    along = lax.fori_loop(0, N_TP, piece, jnp.zeros((rows, 1), f32))
    dots[...] = jnp.broadcast_to(along, dots.shape)
    tails[tp] = jnp.transpose(dots[...])[:8, :]
    for d in range(1, N_TP):
        tail(d, tp).start()
        z_scatter(d).start()
    scatter.relay()
    gu_sum.chips()
    d_sum.chips()
    lax.fori_loop(0, N_TP, out_piece, 0)
    at = pl.ds(pl.multiple_of(tp * part, part), part)
    total = scatter.total(own[...]) * gain[:, at]
    for d in range(1, N_TP):
        tail(d, tp ^ d).wait_recv()
    whole = tails[0]
    for d in range(1, N_TP):
        whole = whole + tails[d]
    dots[...] = jnp.transpose(jnp.broadcast_to(whole[:1], (128, rows)))
    r = inverse[:, :1]
    total = dy[:, at].astype(f32) + r * total - x_at(at) * r**3 * (dots[:, :1] * (1.0 / model))
    dx1_own[...] = total
    columns(dx1, tp)[...] = total.astype(bf16)
    spread = Spread(None, lambda rank: columns(dx1, rank), send, recv, 4)
    spread.start()
    gu_sum.again()
    d_sum.again()
    total = z_region(z_part, tp)[...].astype(f32)
    for d in range(1, N_TP):
        z_scatter(d).wait_recv()
        total = total + z_held[d].astype(f32)
    z_region(z_sum, tp)[...] = total.astype(bf16)
    for d in range(1, N_TP):
        z_spread(d, tp).start()
    spread.relay()
    gu_sum.other_core()
    d_sum.other_core()
    spread.wait()
    gu_sum.finish()
    d_sum.finish()
    scatter.sent()
    spread.sent()
    for d in range(1, N_TP):
        z_scatter(d).wait_send()
        z_spread(d, tp ^ d).wait_recv()
        z_spread(d, tp).wait_send()
        tail(d, tp).wait_send()


def feed_forward(small, large):
    x0, attn, wide, dy, w_gu, w_d = large
    rows, model = x0.shape
    b_gu, a_d = small[3], small[4]
    part = model // N_TP
    experts, _, cols = w_gu.shape
    hidden = w_d.shape[1]
    shape = jax.ShapeDtypeStruct
    return pl.pallas_call(
        ffn_kernel,
        out_shape=(
            shape((N_TP, rows, part), bf16),
            shape((rows, part), f32),
            shape((rows, model), bf16),
            shape((rows, part), f32),
            shape((rows, model), bf16),
            shape((rows, 256), bf16),
            shape((2, 8, 16, 768), bf16),
            shape((2, 8, 8, hidden), f32),
        ),
        in_specs=[VMEM] * len(small) + [ANY] * len(large),
        out_specs=tuple([VMEM] * 8),
        scratch_shapes=[
            pltpu.VMEM(a.shape, bf16) for a in large
        ]
        + [
            pltpu.VMEM((experts, rows, hidden), bf16),
            pltpu.VMEM((experts, rows, cols), bf16),
            pltpu.VMEM((rows, 768), f32),
            pltpu.VMEM((rows, 256), bf16),
            pltpu.VMEM((rows, 256), bf16),
            pltpu.VMEM((rows, 256), bf16),
            pltpu.VMEM((N_TP, rows, part), bf16),
            pltpu.VMEM((rows, part), bf16),
            pltpu.VMEM((rows, part), f32),
            pltpu.VMEM((N_TP, rows, part), bf16),
            pltpu.VMEM((N_TP, rows // N_TP, 256), bf16),
            pltpu.VMEM((rows, 128), f32),
            pltpu.VMEM((N_TP, 8, rows), f32),
            pltpu.VMEM((rows, 128), f32),
            pltpu.VMEM(b_gu.shape, f32),
            pltpu.VMEM(a_d.shape, f32),
            pltpu.VMEM((2, 8, 16, 768), bf16),
            pltpu.VMEM((8, 16, 768), bf16),
            pltpu.VMEM((8, 16, 768), bf16),
            pltpu.VMEM((2, 8, 8, hidden), f32),
            pltpu.VMEM((8, 8, hidden), f32),
            pltpu.VMEM((8, 8, hidden), f32),
            pltpu.SemaphoreType.DMA((2, experts)),
            pltpu.SemaphoreType.DMA((4,)),
            pltpu.SemaphoreType.DMA((6, N_TP)),
            pltpu.SemaphoreType.DMA((6, N_TP)),
            pltpu.SemaphoreType.DMA((2, 16)),
            pltpu.SemaphoreType.DMA((2, 16)),
        ],
        compiler_params=pltpu.CompilerParams(
            collective_id=2, has_side_effects=True, vmem_limit_bytes=63 << 20
        ),
        name="feed_forward",
    )(*small, *large)


def widen_routes(routes, experts):
    lane = jnp.arange(128, dtype=jnp.int32)
    return jnp.sum((routes[..., None] == lane).astype(f32), axis=1)


def gate_up_columns(gate, up):
    def put(part, before, after):
        sides = [(0, 0, 0)] * (part.ndim - 1) + [(before, after, 0)]
        return lax.pad(part, jnp.zeros((), part.dtype), sides)

    return (
        put(gate[..., :640], 0, 768) + put(up[..., :640], 640, 128)
    ) + (put(gate[..., 640:], 1280, 64) + put(up[..., 640:], 1344, 0))


def attention_kernel(
    s_q, s_kv, s_o, s_gu, s_d, tokens, cotangent, s_wide, s_rest,
    gain, router, table, k_doc, b_q, b_kv, a_o,
    g_q, g_kv, g_o, g_gu, g_d, g_wide, wide_mid, dy, g_rest,
    h_n1, h_kv_all, h_q_all, h_probs, x0, attn, ob, z_o, z_q, z_kv, gates,
    n1, kv_all, q_all, probs, w_q, w_kv, w_o, wide, rest, parts, relay, own, held,
    send, recv, local, tp_send, tp_recv, tp_local, kv_send, kv_recv, load, store, rest_send, rest_recv, sum_send, sum_recv,
):
    me, tp = lax.axis_index("ctx"), lax.axis_index("tp")
    core, side = me ^ 1, me ^ 2
    up, down, far = lax.rem(me + 4, 16), lax.rem(me + 12, 16), lax.rem(me + 8, 16)
    on_core, on_side = lax.rem(me, 2), lax.rem(me // 2, 2)
    cosine, sine, hot0, hot1 = (table.at[:, 128 * i : 128 * i + 128] for i in range(4))
    q_doc = table.at[:, 640:768]
    rows, model = x0.shape
    part = model // N_TP
    half = rows // 2
    experts = w_q.shape[0]
    width = w_q.shape[2]
    heads = width // HEAD_DIM
    span = (PAST + 1) * half
    greet([(core, tp)] + [(me ^ (2 * d), tp) for d in range(1, 8)] + [(me, tp ^ d) for d in range(1, N_TP)])

    kinds = ["flat", "flat", "rows", "cols"] + ["flat"] * experts + ["pair"] * (experts // 2)
    src = [s_kv, wide_mid, s_q, s_o] + [s_gu.at[e] for e in range(experts)]
    dst = [g_kv, g_wide, g_q, g_o] + [g_gu.at[e] for e in range(experts)]
    src += [s_d.at[pl.ds(e, 2)] for e in range(0, experts, 2)]
    dst += [g_d.at[pl.ds(e, 2)] for e in range(0, experts, 2)]
    tp_src, tp_dst, tp_kinds = [tokens, s_wide, cotangent], [x0, wide_mid, dy], ["cols", "rows", "cols"]
    started, staying = [], [None] * len(kinds)
    counter = [0] * len(kinds)

    def place_of(i):
        size = tp_src[i].shape[1 if tp_kinds[i] == "cols" else 0]
        return lambda rank: tp_part(tp_kinds[i], tp_dst[i], rank, size)

    tp_all = [Spread(tp_src[i], place_of(i), tp_send, tp_recv, i) for i in range(3)]

    def tp_own(i):
        return pltpu.make_async_copy(tp_src[i], place_of(i)(tp), tp_local.at[i])

    def tp_start(i):
        tp_all[i].start()
        tp_own(i).start()

    def tp_wait(i):
        tp_all[i].wait()
        tp_own(i).wait()

    def copy(t, item, owner, low, high, to, slot, own_shard):
        there = region(kinds[t], dst[t], owner, low, high)
        return pltpu.make_async_remote_copy(
            src_ref=own_part(kinds[t], src[t], low, high) if own_shard else there,
            dst_ref=there,
            send_sem=send.at[t, slot],
            recv_sem=recv.at[t, item],
            device_id=(to, tp),
            device_id_type=MESH,
        )

    def go(t, item, owner, low, high, to, own_shard=False):
        c = copy(t, item, owner, low, high, to, counter[t], own_shard)
        counter[t] += 1
        c.start()
        started.append(c)

    cuts = [2, 2, 3, 3, 3, 3, 3, 3, 2, 2]

    def arrive(t, item):
        cut = cuts[t]
        mid = cut // 2 if t % 2 else (cut + 1) // 2
        return {
            0: (side, 0, 4),
            1: (down, 0, 4),
            2: (up, 0, 4),
            3: (down ^ 2, 0, cut),
            4: (up ^ 2, 0, cut),
            5: (far, 2, 4),
            6: (far, 0, 2),
            7: (far ^ 2, mid, cut),
            8: (far ^ 2, 0, mid),
            9: (down ^ 2, cut, 4),
            10: (up ^ 2, cut, 4),
            11: (far ^ 2, cut, 4),
        }[item]

    def got(t, item):
        owner, low, high = arrive(t, item)
        copy(t, item, owner, low, high, core, 0, False).wait_recv()
        go(t, 12 + item, owner, low, high, core)

    def first(t):
        go(t, 0, me, 0, 4, side, True)
        go(t, 2, me, 0, 4, down, True)
        go(t, 1, me, 0, 4, up, True)
        go(t, 24, me, 0, 4, core, True)
        c = pltpu.make_async_copy(src[t], region(kinds[t], dst[t], me, 0, 4), local.at[t])
        c.start()
        staying[t] = c

    def second(t):
        got(t, 0)
        go(t, 3, side, 0, cuts[t], up)
        go(t, 4, side, 0, cuts[t], down)
        got(t, 1)
        go(t, 5, down, 2, 4, up)
        go(t, 9, down, cuts[t], 4, side)
        got(t, 2)
        go(t, 6, up, 0, 2, down)
        go(t, 10, up, cuts[t], 4, side)

    def third(t):
        got(t, 3)
        _, low, high = arrive(t, 7)
        go(t, 7, down ^ 2, low, high, up)
        got(t, 4)
        _, low, high = arrive(t, 8)
        go(t, 8, up ^ 2, low, high, down)
        got(t, 5)
        got(t, 6)
        go(t, 11, far, cuts[t], 4, side)

    def fourth(t):
        for item in range(7, 12):
            got(t, item)

    def finish(t):
        for item in range(12):
            owner, low, high = arrive(t, item)
            copy(t, 12 + item, owner ^ 1, low, high, core, 0, False).wait_recv()
        copy(t, 24, core, 0, 4, core, 0, False).wait_recv()

    def rest_copy(item, owner, to, source=None):
        there = g_rest.at[owner, tp]
        return pltpu.make_async_remote_copy(
            src_ref=there if source is None else source,
            dst_ref=there,
            send_sem=rest_send.at[item],
            recv_sem=rest_recv.at[item],
            device_id=(to, tp),
            device_id_type=MESH,
        )

    rest_all = Spread(None, lambda rank: g_rest.at[:, rank], tp_send, tp_recv, 3)
    rest_own = pltpu.make_async_copy(s_rest, g_rest.at[me, tp], tp_local.at[3])

    def rest_start():
        rest_own.start()
        for d in range(1, 8):
            rest_copy(d, me, me ^ (2 * d), s_rest).start()
        rest_copy(8, me, core, s_rest).start()

    def rest_core():
        for d in range(1, 8):
            rest_copy(d, me ^ (2 * d), core).wait_recv()
            rest_copy(8 + d, me ^ (2 * d), core).start()

    def rest_spread():
        for d in range(8):
            rest_copy(8 + d, core ^ (2 * d), core).wait_recv()
        rest_own.wait()
        rest_all.start()

    tp_start(1)
    tp_start(0)
    for t in (0, 2):
        first(t)
    tp_all[1].relay()
    tp_all[0].relay()
    tp_wait(1)
    first(1)
    rest_start()
    second(0)
    second(2)
    first(3)
    second(1)
    tp_wait(0)
    step = 32

    def normalize(i, carry):
        at = pl.ds(pl.multiple_of(i * step, step), step)
        n1[at, :] = rms_scale(x0[at, :].astype(f32), gain[...]).astype(bf16)
        return carry

    lax.fori_loop(0, rows // step, normalize, 0)
    gates[...] = masked_gates(dot(n1[...], router[...]), hot0[...] + hot1[...])

    third(0)
    third(2)
    third(1)
    first(4)
    first(5)
    fourth(0)
    fourth(2)
    fourth(1)

    def fetch(t, ref):
        finish(t)
        staying[t].wait()
        c = pltpu.make_async_copy(dst[t], ref, load.at[t])
        c.start()
        return c

    fetches = [fetch(0, w_kv), fetch(1, wide), fetch(2, w_q)]

    lane = lax.broadcasted_iota(jnp.int32, (rows, 128), 1)
    seq = lax.broadcasted_iota(jnp.int32, (rows, 128), 0) // half

    def rotary(x):
        return x * cosine[...] + pltpu.roll(x, HEAD_DIM // 2, 1) * sine[...]

    rest_core()
    fetches[0].wait()
    fetches[1].wait()
    z = dot(n1[...], wide[:, :128])
    z_q[...] = jnp.where(lane // 64 == seq, z, 0.0).astype(bf16)
    z = dot(n1[...], wide[:, 128:192])
    z_kv[...] = jnp.where((lane // 16) % 2 == seq, jnp.pad(z, ((0, 0), (0, 64))), 0.0).astype(bf16)
    kv = dot(n1[...], w_kv[...]) + dot(z_kv[:, :64], b_kv[...])
    for h in range(heads):
        at = slice(HEAD_DIM * h, HEAD_DIM * h + HEAD_DIM)
        turned = rotary(kv[:, at]).astype(bf16)
        kv_all[PAST, 0, :, at] = turned[:half]
        kv_all[PAST, 1, :, at] = turned[half:]
    for s in range(2):
        kv_all[PAST, s, :, width:] = kv[half * s : half * s + half, width:].astype(bf16)

    def kv_copy(slot, back, to, to_back):
        return pltpu.make_async_remote_copy(
            src_ref=kv_all.at[PAST - back],
            dst_ref=kv_all.at[PAST - to_back],
            send_sem=kv_send.at[slot],
            recv_sem=kv_recv.at[to_back],
            device_id=(to, tp),
            device_id_type=MESH,
        )

    def kv_arrived(back):
        kv_copy(0, back, core, back).wait_recv()

    def when(condition, c):
        if condition is None:
            c.start()
        else:
            pl.when(condition)(c.start)
        kv_started.append((condition, c))

    kv_started = []
    when(None, kv_copy(0, 0, up, 4))
    when(None, kv_copy(1, 0, far, 8))
    when(on_side == 0, kv_copy(2, 0, side, 2))
    when(on_core == 0, kv_copy(3, 0, core, 1))
    second(3)
    first(6)
    first(7)

    fetches[2].wait()
    queries = [jnp.zeros((rows, width), f32), jnp.zeros((rows, width), f32)]
    for e in range(experts):
        z_e = jnp.where((lane % 64) // 16 == e, z_q[...].astype(f32), 0.0).astype(bf16)
        q_e = dot(n1[...], w_q[e]) + dot(z_e, b_q[...])
        for k, hot in enumerate((hot0, hot1)):
            queries[k] = queries[k] + jnp.where(hot[:, e : e + 1] > 0, q_e, 0.0)
    for k in range(2):
        for h in range(heads):
            turned = rotary(queries[k][:, HEAD_DIM * h : HEAD_DIM * h + HEAD_DIM]).astype(bf16)
            for s in range(2):
                q_all[s * heads + h, k * half : k * half + half, :] = turned[half * s : half * s + half]

    rest_spread()
    tp_start(2)
    second(4)
    kv_arrived(4)
    when(on_side == 0, kv_copy(4, 4, side, 6))
    when(on_side == 1, kv_copy(5, 4, side, 2))
    when(on_core == 0, kv_copy(6, 4, core, 5))
    when(on_core == 1, kv_copy(7, 4, core, 3))
    kv_arrived(8)
    when(on_side == 1, kv_copy(8, 8, side, 6))
    when(on_core == 1, kv_copy(9, 8, core, 7))
    first(8)
    second(5)
    kv_arrived(2)
    when(on_core == 0, kv_copy(10, 2, core, 3))
    when(on_core == 1, kv_copy(11, 2, core, 1))
    kv_arrived(6)
    when(on_core == 0, kv_copy(12, 6, core, 7))
    when(on_core == 1, kv_copy(13, 6, core, 5))
    third(3)
    first(9)
    for back in (1, 3, 5, 7):
        kv_arrived(back)
    rest_all.relay()
    tp_all[2].relay()
    second(6)

    row = lax.broadcasted_iota(jnp.int32, (half, span), 0)
    key = lax.broadcasted_iota(jnp.int32, (half, span), 1)
    near = (key > row) & (key <= row + PAST * half)

    def attend(i, carry):
        s = i // heads
        h = lax.rem(i, heads)
        at = pl.ds(pl.multiple_of(h * HEAD_DIM, HEAD_DIM), HEAD_DIM)
        v_at = pl.ds(pl.multiple_of(width + h * HEAD_DIM, HEAD_DIM), HEAD_DIM)
        keys = kv_all[:, s, :, at].reshape(span, HEAD_DIM)
        values = kv_all[:, s, :, v_at].reshape(span, HEAD_DIM)
        seq_rows = pl.ds(pl.multiple_of(s * half, half), half)
        allowed = near & (q_doc[seq_rows, :1] == k_doc[s, :1, :])
        for k in range(2):
            q = q_all[i, k * half : k * half + half, :]
            scores = dot_nt(q, keys) * HEAD_DIM**-0.5
            scores = jnp.where(allowed, scores, big_negative)
            peak = jnp.max(scores, axis=1, keepdims=True)
            powers = jnp.exp(scores - peak)
            p = (powers * (1.0 / jnp.sum(powers, axis=1, keepdims=True))).astype(bf16)
            probs[i, k * half : k * half + half, :] = p
            ob[k, seq_rows, at] = dot(p, values).astype(bf16)
        return carry

    lax.fori_loop(0, 2 * heads, attend, 0)
    stores = []
    for i, (v, h) in enumerate(((n1, h_n1), (kv_all, h_kv_all), (q_all, h_q_all), (probs, h_probs))):
        c = pltpu.make_async_copy(v, h, store.at[i])
        c.start()
        stores.append(c)
    fourth(3)
    third(4)
    fetches.append(fetch(3, w_o))
    rest_all.wait()
    rest_load = pltpu.make_async_copy(g_rest, rest, load.at[4])
    rest_load.start()

    fetches[3].wait()
    rest_load.wait()
    z_acc = jnp.zeros((rows, 256), f32)
    pair_lane = lax.broadcasted_iota(jnp.int32, (rows, 256), 1)
    mine = pair_lane // 128 == lax.broadcasted_iota(jnp.int32, (rows, 256), 0) // half
    chosen = []
    for e in range(experts):
        o_e = jnp.where(hot0[:, e : e + 1] > 0, ob[0].astype(f32), 0.0)
        o_e = o_e + jnp.where(hot1[:, e : e + 1] > 0, ob[1].astype(f32), 0.0)
        o_e = o_e.astype(bf16)
        chosen.append(o_e)
        low = dot_nt(o_e, a_o[...]) * gates[:, e : e + 1]
        z_acc = z_acc + jnp.where(mine & ((pair_lane % 128) // 16 == e), low, 0.0)
    z_acc = z_acc.astype(bf16)
    z_o[...] = z_acc[:, :128] + z_acc[:, 128:]

    def columns(ref, rank):
        return ref.at[:, pl.ds(pl.multiple_of(rank * part, part), part)]

    scatter = Scatter(parts, held, relay, sum_send, sum_recv, 0)
    spread = Spread(None, lambda rank: columns(attn, rank), sum_send, sum_recv, 1)
    for d in (5, 6, 7, 4, 1, 2, 3, 0):
        at = pl.ds(pl.multiple_of((tp ^ d) * part, part), part)
        total = dot_nt(z_acc, rest[pl.ds(2 * (tp ^ d), 2), :, :, 256:512].reshape(part, 256))
        for e in range(experts):
            total = total + dot(chosen[e], w_o[e, :, at]) * gates[:, e : e + 1]
        if d:
            parts[d] = total.astype(bf16)
            if d != FAR:
                scatter.copy(d).start()
        else:
            own[...] = total
    second(7)
    scatter.relay()
    second(8)
    third(5)
    columns(attn, tp)[...] = scatter.total(own[...]).astype(bf16)
    spread.start()
    second(9)
    third(6)
    spread.relay()
    third(7)
    third(8)
    spread.wait()
    fourth(4)
    fourth(5)
    third(9)
    fourth(6)
    fourth(7)
    fourth(8)
    fourth(9)
    tp_wait(2)
    for t in range(4, len(kinds)):
        finish(t)
    for c in stores:
        c.wait()
    for c in started:
        c.wait_send()
    for t, c in enumerate(staying):
        if t > 3:
            c.wait()
    for condition, c in kv_started:
        if condition is None:
            c.wait_send()
        else:
            pl.when(condition)(c.wait_send)
    scatter.sent()
    spread.sent()
    for c in tp_all + [rest_all]:
        c.sent()
    for d in range(1, 8):
        rest_copy(d, me, me ^ (2 * d), s_rest).wait_send()
        rest_copy(8 + d, me ^ (2 * d), core).wait_send()
    rest_copy(8, me, core, s_rest).wait_send()


def attention(shards_in, tp_shards, small):
    s_q, s_kv, s_o, s_gu, s_d = shards_in
    tokens, cotangent, s_wide, s_rest = tp_shards
    rows, part = tokens.shape
    model = part * N_TP
    experts, _, width = s_q.shape
    half = rows // 2
    heads = width // HEAD_DIM
    shape = jax.ShapeDtypeStruct

    def grown(a, d):
        return shape(tuple(n * (N_CTX if i == d else 1) for i, n in enumerate(a.shape)), a.dtype)

    gathered = (grown(s_q, 1), grown(s_kv, 0), grown(s_o, 2), grown(s_gu, 1), grown(s_d, 2))
    wide_mid = shape((s_wide.shape[0] * N_TP, s_wide.shape[1]), bf16)
    wide = grown(wide_mid, 0)
    rest = shape((N_CTX, N_TP) + s_rest.shape, bf16)
    kept = (
        shape((rows, model), bf16),
        shape((PAST + 1, 2, half, 2 * width), bf16),
        shape((2 * heads, rows, HEAD_DIM), bf16),
        shape((2 * heads, rows, (PAST + 1) * half), bf16),
    )
    vmem_out = (
        shape((rows, model), bf16),
        shape((rows, model), bf16),
        shape((2, rows, width), bf16),
        shape((rows, 128), bf16),
        shape((rows, 128), bf16),
        shape((rows, 128), bf16),
        shape((rows, 128), f32),
    )
    any_out = gathered + (wide, wide_mid, shape((rows, model), bf16), rest) + kept
    return pl.pallas_call(
        attention_kernel,
        out_shape=any_out + vmem_out,
        in_specs=[ANY] * 9 + [VMEM] * len(small),
        out_specs=tuple([ANY] * len(any_out) + [VMEM] * len(vmem_out)),
        scratch_shapes=[pltpu.VMEM(a.shape, bf16) for a in kept]
        + [
            pltpu.VMEM(gathered[0].shape, bf16),
            pltpu.VMEM(gathered[1].shape, bf16),
            pltpu.VMEM(gathered[2].shape, bf16),
            pltpu.VMEM(wide.shape, bf16),
            pltpu.VMEM(rest.shape, bf16),
            pltpu.VMEM((N_TP, rows, part), bf16),
            pltpu.VMEM((rows, part), bf16),
            pltpu.VMEM((rows, part), f32),
            pltpu.VMEM((N_TP, rows, part), bf16),
            pltpu.SemaphoreType.DMA((10, 25)),
            pltpu.SemaphoreType.DMA((10, 25)),
            pltpu.SemaphoreType.DMA((10,)),
            pltpu.SemaphoreType.DMA((4, N_TP)),
            pltpu.SemaphoreType.DMA((4, N_TP)),
            pltpu.SemaphoreType.DMA((4,)),
            pltpu.SemaphoreType.DMA((14,)),
            pltpu.SemaphoreType.DMA((PAST + 1,)),
            pltpu.SemaphoreType.DMA((5,)),
            pltpu.SemaphoreType.DMA((4,)),
            pltpu.SemaphoreType.DMA((16,)),
            pltpu.SemaphoreType.DMA((16,)),
            pltpu.SemaphoreType.DMA((2, N_TP)),
            pltpu.SemaphoreType.DMA((2, N_TP)),
        ],
        compiler_params=pltpu.CompilerParams(
            collective_id=0, has_side_effects=True, vmem_limit_bytes=60 << 20
        ),
        name="attention",
    )(*shards_in, *tp_shards, *small)


def backward_kernel(
    dx1, dx1_own, ob, gates, z_q, z_kv, z_sum, table, gain, router, b_q, b_kv, a_o, ff_parts, ff_own,
    h_q, h_kv, h_o, h_wide, h_rest, h_x0, h_n1, h_n2, h_dy, h_kv_all, h_q_all, h_probs,
    mixed, grad_tokens, wide_a, wide_b, heads_out,
    w_q, w_kv, w_o, wide, rest, x0, n1, n2, dy, kv_all, q_all, probs, dob, dkv, dkv_held, dq, dkv_own, dn, parts, relay, own, held, ff_held, ff_relay,
    z_part, z_held, z_done, dots, tails, a_src, b_src, heads_src, a_core, b_core, heads_core, a_held, b_held, heads_held,
    load, tp_send, tp_recv, core_send, core_recv, kv_send, kv_recv, ctx_send, ctx_recv,
):
    me, tp = lax.axis_index("ctx"), lax.axis_index("tp")
    core = me ^ 1
    on_core = lax.rem(me, 2)
    rows, model = x0.shape
    cosine, sine, hot0, hot1 = (table.at[:, 128 * i : 128 * i + 128] for i in range(4))
    part = model // N_TP
    half = rows // 2
    experts = w_q.shape[0]
    width = w_q.shape[2]
    heads = width // HEAD_DIM
    span = (PAST + 1) * half
    loads = []
    for i, (h, w) in enumerate(
        (
            (h_rest, rest),
            (h_o, w_o),
            (h_kv_all, kv_all),
            (h_probs, probs),
            (h_q_all, q_all),
            (h_q, w_q),
            (h_n2, n2),
            (h_dy, dy),
            (h_n1, n1),
            (h_kv, w_kv),
            (h_x0, x0),
            (h_wide, wide),
        )
    ):
        c = pltpu.make_async_copy(h, w, load.at[i])
        c.start()
        loads.append(c)
    greet([(me ^ d, tp) for d in range(1, N_CTX)] + [(me, tp ^ d) for d in range(1, N_TP)])
    a_sum = CtxSum(a_src, a_core, a_held, None, ctx_send, ctx_recv, 0)
    b_sum = CtxSum(b_src, b_core, b_held, None, ctx_send, ctx_recv, 1)
    heads_sum = CtxSum(heads_src, heads_core, heads_held, heads_out, ctx_send, ctx_recv, 2)
    ff = Scatter(ff_parts, ff_held, ff_relay, tp_send, tp_recv, 4)
    for d in (5, 6, 7, 1, 2, 3):
        ff.copy(d).start()

    lane = lax.broadcasted_iota(jnp.int32, (rows, 128), 1)
    seq = lax.broadcasted_iota(jnp.int32, (rows, 128), 0) // half
    hots = (hot0, hot1)

    loads[0].wait()
    pair_lane = lax.broadcasted_iota(jnp.int32, (rows, 256), 1)
    mine = pair_lane // 128 == lax.broadcasted_iota(jnp.int32, (rows, 256), 0) // half
    dz_o = dot(dx1[...], rest[:, 256:512])
    loads[1].wait()
    g = [jnp.zeros((rows, width), f32), jnp.zeros((rows, width), f32)]
    g_ao = jnp.zeros((256, width), f32)
    for e in range(experts):
        dz_e = jnp.where(mine & ((pair_lane % 128) // 16 == e), dz_o, 0.0)
        g_e = dot_nt(dx1[...], w_o[e]) + dot(dz_e.astype(bf16), a_o[...])
        o_e = jnp.where(hot0[:, e : e + 1] > 0, ob[0].astype(f32), 0.0)
        o_e = o_e + jnp.where(hot1[:, e : e + 1] > 0, ob[1].astype(f32), 0.0)
        o_e = o_e.astype(bf16)
        dz_e = (dz_e * gates[:, e : e + 1]).astype(bf16)
        g_ao = g_ao + dot_tn(dz_e, o_e)
        for k in range(2):
            g[k] = g[k] + jnp.where(hots[k][:, e : e + 1] > 0, g_e, 0.0)
    d_gates = jnp.zeros((rows, 128), f32)
    for k in range(2):
        d_gate = jnp.sum(g[k] * ob[k].astype(f32), axis=1, keepdims=True)
        d_gates = d_gates + jnp.where(hots[k][...] > 0, d_gate, 0.0)
        gate = jnp.sum(hots[k][...] * gates[...], axis=1, keepdims=True)
        d_out = (g[k] * gate).astype(bf16)
        for s in range(2):
            for h in range(heads):
                dob[s * heads + h, k * half : k * half + half, :] = d_out[
                    half * s : half * s + half, HEAD_DIM * h : HEAD_DIM * h + HEAD_DIM
                ]
    d_logits = gates[...] * (d_gates - jnp.sum(gates[...] * d_gates, axis=1, keepdims=True))
    d_logits = d_logits.astype(bf16)

    def attend_back(i, carry):
        s = i // heads
        h = lax.rem(i, heads)
        at = pl.ds(pl.multiple_of(h * HEAD_DIM, HEAD_DIM), HEAD_DIM)
        v_at = pl.ds(pl.multiple_of(width + h * HEAD_DIM, HEAD_DIM), HEAD_DIM)
        keys = kv_all[:, s, :, at].reshape(span, HEAD_DIM)
        values = kv_all[:, s, :, v_at].reshape(span, HEAD_DIM)
        seq_rows = pl.ds(pl.multiple_of(s * half, half), half)
        d_keys = jnp.zeros((span, HEAD_DIM), f32)
        d_values = jnp.zeros((span, HEAD_DIM), f32)
        for k in range(2):
            k_rows = slice(k * half, k * half + half)
            d_o = dob[i, k_rows, :]
            p = probs[i, k_rows, :]
            delta = jnp.sum(d_o.astype(f32) * ob[k, seq_rows, at].astype(f32), axis=1, keepdims=True)
            d_s = (p.astype(f32) * (dot_nt(d_o, values) - delta)).astype(bf16)
            d_q = dot(d_s, keys) * HEAD_DIM**-0.5
            turned = d_q * cosine[seq_rows, :] - pltpu.roll(d_q, HEAD_DIM // 2, 1) * sine[seq_rows, :]
            dq[k, seq_rows, at] = turned.astype(bf16)
            d_keys = d_keys + dot_tn(d_s, q_all[i, k_rows, :])
            d_values = d_values + dot_tn(p, d_o)
        d_keys = (d_keys * HEAD_DIM**-0.5).astype(bf16)
        dkv[:, s, :, at] = d_keys.reshape(PAST + 1, half, HEAD_DIM)
        dkv[:, s, :, v_at] = d_values.astype(bf16).reshape(PAST + 1, half, HEAD_DIM)
        return carry

    for i in (2, 3, 4):
        loads[i].wait()
    lax.fori_loop(0, 2 * heads, attend_back, 0)

    def to_core(back):
        return pltpu.make_async_remote_copy(
            src_ref=dkv.at[PAST - back],
            dst_ref=dkv_held.at[back // 2],
            send_sem=core_send.at[back // 2],
            recv_sem=core_recv.at[back // 2],
            device_id=(core, tp),
            device_id_type=MESH,
        )

    def to_owner(back):
        return pltpu.make_async_remote_copy(
            src_ref=dkv.at[PAST - back],
            dst_ref=dkv_held.at[3 + back // 2],
            send_sem=kv_send.at[back // 2],
            recv_sem=kv_recv.at[back // 2],
            device_id=(lax.rem(me + N_CTX - back, N_CTX), tp),
            device_id_type=MESH,
        )

    for back in (1, 3, 5, 7):
        to_core(back).start()
    for back in (1, 3, 5, 7):
        to_core(back).wait_recv()
        slot = PAST - (back - 1) - 2 * on_core
        dkv[slot] = (dkv[slot].astype(f32) + dkv_held[back // 2].astype(f32)).astype(bf16)
    for back in (2, 4, 6, 8):
        to_owner(back).start()

    ff.relay()
    loads[5].wait()
    loads[11].wait()
    dz_q = jnp.zeros((rows, 128), f32)
    g_bq = jnp.zeros((128, width), f32)
    chosen = []
    for e in range(experts):
        dq_e = jnp.where(hot0[:, e : e + 1] > 0, dq[0].astype(f32), 0.0)
        dq_e = dq_e + jnp.where(hot1[:, e : e + 1] > 0, dq[1].astype(f32), 0.0)
        dq_e = dq_e.astype(bf16)
        chosen.append(dq_e)
        keep = (lane // 64 == seq) & ((lane % 64) // 16 == e)
        dz_q = dz_q + jnp.where(keep, dot_nt(dq_e, b_q[...]), 0.0)
        z_e = jnp.where(keep, z_q[...].astype(f32), 0.0).astype(bf16)
        g_bq = g_bq + dot_tn(z_e, dq_e)
    dz_q = dz_q.astype(bf16)
    z_part[:, :128] = dz_q
    for j in range(N_TP):
        at = slice(part * j, part * j + part)
        total = dot_nt(dz_q, wide[at, :128]) + dot_nt(d_logits, router[at, :])
        for e in range(experts):
            total = total + dot_nt(chosen[e], w_q[e, at, :])
        dn[j] = total
    for i in (6, 7, 8):
        loads[i].wait()
    own_columns = lax.broadcasted_iota(jnp.int32, (model, part), 1)
    own_columns = (own_columns // 16) * 128 + tp * 16 + own_columns % 16
    pick = (lax.broadcasted_iota(jnp.int32, (model, part), 0) == own_columns).astype(bf16)

    def to_pairs(ref, at, values):
        values = values.astype(bf16).reshape(8, 2, 16, values.shape[1])
        for c in range(2):
            ref[c, :, :, at] = values[:, c]

    n2_own = dot(n2[...], pick).astype(bf16)
    dx1_cols = dot(dx1[...], pick).astype(bf16)
    dy_own = dot(dy[...], pick).astype(bf16)
    n1_own = dot(n1[...], pick).astype(bf16)
    lane_m = lax.broadcasted_iota(jnp.int32, (part, 128), 1)
    for s in range(2):
        at = slice(half * s, half * s + half)
        to_pairs(a_src, slice(128 * s, 128 * s + 128), dot_tn(n2_own[at], z_sum[at, :128]))
        low = jnp.where(
            lane_m < 64, dot_tn(dx1_cols[at], z_sum[at, 128:]), dot_tn(dy_own[at], z_sum[at, 128:])
        )
        to_pairs(a_src, slice(256 + 128 * s, 384 + 128 * s), low)
    a_sum.start()

    total = dkv[PAST].astype(f32)
    for back in (2, 4, 6, 8):
        to_owner(back).wait_recv()
        total = total + dkv_held[3 + back // 2].astype(f32)
    a_sum.chips()
    for h in range(heads):
        at = slice(HEAD_DIM * h, HEAD_DIM * h + HEAD_DIM)
        d_k = jnp.concatenate([total[0, :, at], total[1, :, at]], axis=0)
        turned = d_k * cosine[...] - pltpu.roll(d_k, HEAD_DIM // 2, 1) * sine[...]
        dkv_own[:, at] = turned.astype(bf16)
    dkv_own[:, width:] = jnp.concatenate([total[0, :, width:], total[1, :, width:]], axis=0).astype(bf16)
    loads[9].wait()
    loads[10].wait()
    dz_kv = dot_nt(dkv_own[...], b_kv[...])
    keep = (lane[:, :64] // 16) % 2 == seq[:, :64]
    dz_kv = jnp.where(keep, dz_kv, 0.0).astype(bf16)
    z_part[:, 128:] = jnp.pad(dz_kv.astype(f32), ((0, 0), (0, 64))).astype(bf16)

    scatter = Scatter(parts, held, relay, tp_send, tp_recv, 0)
    z_rows = rows // N_TP

    def z_region(ref, rank):
        return ref.at[pl.ds(pl.multiple_of(rank * z_rows, z_rows), z_rows), :]

    def z_scatter(d):
        return pltpu.make_async_remote_copy(
            src_ref=z_region(z_part, tp ^ d),
            dst_ref=z_held.at[d],
            send_sem=tp_send.at[1, d],
            recv_sem=tp_recv.at[1, d],
            device_id=(me, tp ^ d),
            device_id_type=MESH,
        )

    def z_spread(d, rank):
        return pltpu.make_async_remote_copy(
            src_ref=z_region(z_done, rank),
            dst_ref=z_region(z_done, rank),
            send_sem=tp_send.at[2, d],
            recv_sem=tp_recv.at[2, d],
            device_id=(me, tp ^ d),
            device_id_type=MESH,
        )

    def tail(d, rank):
        return pltpu.make_async_remote_copy(
            src_ref=tails.at[rank],
            dst_ref=tails.at[rank],
            send_sem=tp_send.at[3, d],
            recv_sem=tp_recv.at[3, d],
            device_id=(me, tp ^ d),
            device_id_type=MESH,
        )

    for d in range(1, N_TP):
        z_scatter(d).start()
    g_bkv = dot_tn(z_kv[...], dkv_own[...])
    blocks = [g_bq[32 * i : 32 * i + 32] for i in range(4)] + [g_bkv[:32, :width], g_bkv[32:64, width:]]
    blocks += [g_ao[128 * s + 32 * i : 128 * s + 32 * i + 32] for s in range(2) for i in range(2)]
    blocks += [jnp.zeros((32, width), f32)] * 6
    for i in range(N_CTX):
        heads_src[i % 2, i // 2] = blocks[i].astype(bf16)
    heads_sum.start()
    def finish_z():
        total = z_region(z_part, tp)[...].astype(f32)
        for d in range(1, N_TP):
            z_scatter(d).wait_recv()
            total = total + z_held[d].astype(f32)
        z_region(z_done, tp)[...] = total.astype(bf16)
        for d in range(1, N_TP):
            z_spread(d, tp).start()

    along = jnp.zeros((rows, 1), f32)
    for d in (5, 6, 7, 4, 1, 2, 3, 0):
        if d == FAR:
            finish_z()
        peer = tp ^ d
        at = pl.ds(pl.multiple_of(peer * part, part), part)
        total = dn[peer] + dot_nt(dz_kv, wide[at, 128:192]) + dot_nt(dkv_own[...], w_kv[at, :])
        scaled = total * gain[:, at]
        along = along + jnp.sum(scaled * x0[:, at].astype(f32), axis=1, keepdims=True)
        if d:
            parts[d] = total.astype(bf16)
            if d != FAR:
                scatter.copy(d).start()
        else:
            own[...] = total
    dots[...] = jnp.broadcast_to(along, dots.shape)
    tails[tp] = jnp.transpose(dots[...])[:8, :]
    for d in range(1, N_TP):
        tail(d, tp).start()
    heads_sum.chips()
    mixed[...] = ff.total(ff_own[...]).astype(bf16)
    scatter.relay()
    heads_sum.again()
    for d in range(1, N_TP):
        z_spread(d, tp ^ d).wait_recv()
    to_pairs(b_src, slice(0, part), dot_tn(n1_own, z_done[...]))
    b_sum.start()
    total = scatter.total(own[...])
    b_sum.chips()
    for d in range(1, N_TP):
        tail(d, tp ^ d).wait_recv()
    whole = tails[0]
    for d in range(1, N_TP):
        whole = whole + tails[d]
    dots[...] = jnp.transpose(jnp.broadcast_to(whole[:1], (128, rows)))
    own_at = pl.ds(pl.multiple_of(tp * part, part), part)
    own[...] = total * gain[:, own_at]
    step = 32

    def finish(i, carry):
        at = pl.ds(pl.multiple_of(i * step, step), step)
        x = x0[at, :].astype(f32)
        inverse = lax.rsqrt(jnp.mean(x * x, axis=1, keepdims=True) + eps)
        mean = dots[at, :1] * (1.0 / model)
        back = inverse * own[at, :] - x0[at, own_at].astype(f32) * inverse**3 * mean
        grad_tokens[at, :] = (dx1_own[at, :] + back).astype(bf16)
        return carry

    lax.fori_loop(0, rows // step, finish, 0)
    wide_a[...] = a_sum.total()
    heads_sum.other_core()
    wide_b[...] = b_sum.total()
    heads_sum.finish()
    for back in (1, 3, 5, 7):
        to_core(back).wait_send()
        to_owner(back + 1).wait_send()
    scatter.sent()
    ff.sent()
    for d in range(1, N_TP):
        z_scatter(d).wait_send()
        z_spread(d, tp).wait_send()
        tail(d, tp).wait_send()


def backward(vmem, hbm):
    dx1 = vmem[0]
    w_q = hbm[0]
    rows, model = dx1.shape
    part = model // N_TP
    width = w_q.shape[2]
    heads = width // HEAD_DIM
    half = rows // 2
    shape = jax.ShapeDtypeStruct
    reduced = [(2, 8, 16, 512), (2, 8, 16, part), (2, 8, 32, width)]
    return pl.pallas_call(
        backward_kernel,
        out_shape=(
            shape((rows, part), bf16),
            shape((rows, part), bf16),
            shape((16, 512), f32),
            shape((16, part), f32),
            shape(reduced[2], bf16),
        ),
        in_specs=[VMEM] * len(vmem) + [ANY] * len(hbm),
        out_specs=tuple([VMEM] * 5),
        scratch_shapes=[
            pltpu.VMEM(a.shape, bf16) for a in hbm
        ]
        + [
            pltpu.VMEM((2 * heads, rows, HEAD_DIM), bf16),
            pltpu.VMEM(hbm[9].shape, bf16),
            pltpu.VMEM((8,) + hbm[9].shape[1:], bf16),
            pltpu.VMEM((2, rows, width), bf16),
            pltpu.VMEM((rows, 2 * width), bf16),
            pltpu.VMEM((N_TP, rows, part), f32),
            pltpu.VMEM((N_TP, rows, part), bf16),
            pltpu.VMEM((rows, part), bf16),
            pltpu.VMEM((rows, part), f32),
            pltpu.VMEM((N_TP, rows, part), bf16),
            pltpu.VMEM((N_TP, rows, part), bf16),
            pltpu.VMEM((rows, part), bf16),
            pltpu.VMEM((rows, 256), bf16),
            pltpu.VMEM((N_TP, rows // N_TP, 256), bf16),
            pltpu.VMEM((rows, 256), bf16),
            pltpu.VMEM((rows, 128), f32),
            pltpu.VMEM((N_TP, 8, rows), f32),
        ]
        + [pltpu.VMEM(a, bf16) for a in reduced]
        + [pltpu.VMEM(a[1:], bf16) for a in reduced + reduced]
        + [
            pltpu.SemaphoreType.DMA((len(hbm),)),
            pltpu.SemaphoreType.DMA((5, N_TP)),
            pltpu.SemaphoreType.DMA((5, N_TP)),
            pltpu.SemaphoreType.DMA((4,)),
            pltpu.SemaphoreType.DMA((4,)),
            pltpu.SemaphoreType.DMA((5,)),
            pltpu.SemaphoreType.DMA((5,)),
            pltpu.SemaphoreType.DMA((3, 16)),
            pltpu.SemaphoreType.DMA((3, 16)),
        ],
        compiler_params=pltpu.CompilerParams(
            collective_id=3, has_side_effects=True, vmem_limit_bytes=60 << 20
        ),
        name="backward",
    )(*vmem, *hbm)


def shards(
    tokens,
    norm1_gain,
    router_attn,
    w_query,
    w_key_value,
    w_out,
    norm2_gain,
    router_ffn,
    w_gate_up,
    w_down,
    adapt_wide,
    adapt_heads,
    adapt_ffn,
    attention_routes,
    feedforward_routes,
    doc_lengths,
    adapter_index,
    cotangent,
):
    seqs, block, part = tokens.shape
    rows = seqs * block
    n_tp = lax.axis_size("tp")
    model = part * n_tp
    experts = w_query.shape[0]
    width = w_query.shape[2]
    heads = width // HEAD_DIM
    hidden = w_down.shape[1]
    rank = adapt_heads.shape[2]
    wide_slots = adapt_wide.shape[1]
    ctx_rank = lax.axis_index("ctx")


    def by_sequence(a):
        first = adapter_index[0] == 0
        return jnp.stack([jnp.where(first, a[0], a[1]), jnp.where(first, a[1], a[0])])

    wide_own = by_sequence(adapt_wide.astype(bf16))
    groups = [[6, 10, 7, 11, 8, 12, 9, 13], list(range(14, 22)), [0, 1, 2, 3], [4, 5]]
    order = [(q, s) for g in groups[:3] for q in range(seqs) for s in g]
    order += [(q, s) for s in groups[3] for q in range(seqs)]
    wide_cols = wide_own.reshape(seqs * wide_slots, rank, -1)[
        np.array([q * wide_slots + s for q, s in order])
    ].reshape(seqs * wide_slots * rank, -1).T
    heads_low = by_sequence(adapt_heads.astype(bf16))
    ffn_low = by_sequence(adapt_ffn.astype(bf16))
    route_a = attention_routes.reshape(rows, -1)
    route_f = feedforward_routes.reshape(rows, -1)

    positions = ctx_rank * block + jnp.arange(block, dtype=jnp.int32)
    doc_ids, offsets = doc_layout(doc_lengths, positions)
    half = HEAD_DIM // 2
    frequency = 10000.0 ** (-2.0 * jnp.arange(half, dtype=f32) / HEAD_DIM)
    angles = offsets.astype(f32).reshape(rows)[:, None] * frequency
    cosine, sine = jnp.cos(angles), jnp.sin(angles)
    cosine = jnp.concatenate([cosine, cosine], axis=1)
    sine = jnp.concatenate([-sine, sine], axis=1)

    b_q, b_kv, a_o = heads_low[:, :experts], heads_low[:, experts : experts + 2], heads_low[:, experts + 2 :]
    key_pos = (ctx_rank - PAST) * block + jnp.arange((PAST + 1) * block, dtype=jnp.int32)
    key_doc = doc_layout(doc_lengths, jnp.maximum(key_pos, 0))[0]
    key_doc = jnp.where(key_pos[None, :] >= 0, key_doc, -(1 << 20))
    blank = jnp.zeros((seqs, rank, width), bf16)
    b_kv_wide = jnp.concatenate(
        [
            jnp.concatenate([b_kv[:, 0], blank], axis=-1).reshape(seqs * rank, 2 * width),
            jnp.concatenate([blank, b_kv[:, 1]], axis=-1).reshape(seqs * rank, 2 * width),
        ],
        axis=0,
    )
    a_o_wide = jnp.pad(a_o.reshape(seqs, experts * rank, width), ((0, 0), (0, 64), (0, 0))).reshape(256, width)
    b_q = b_q.reshape(seqs * experts * rank, width)
    table = jnp.concatenate(
        [
            cosine,
            sine,
            widen_routes(route_a[:, :1], experts),
            widen_routes(route_a[:, 1:], experts),
            widen_routes(route_f, experts),
            jnp.broadcast_to(doc_ids.reshape(rows, 1).astype(f32), (rows, 128)),
        ],
        axis=1,
    )
    router_wide = jnp.pad(router_attn, ((0, 0), (0, 128 - experts)))
    (
        w_query, w_key_value, w_out, w_gate_up, w_down, wide, _, dy, rest,
        n1, kv_all, q_all, probs, x0, sum_out, ob, z_o_gated, z_q, z_kv, gates,
    ) = attention(
        [
            w_query,
            w_key_value.reshape(-1, 2 * width),
            w_out,
            gate_up_columns(w_gate_up[:, :, 0], w_gate_up[:, :, 1]),
            w_down,
        ],
        [tokens.reshape(rows, part), cotangent.reshape(rows, part), wide_cols[:, 512:], wide_cols[:, :512]],
        [
            norm1_gain[None],
            router_wide,
            table,
            jnp.broadcast_to(key_doc[:, None, :], (seqs, 8, key_doc.shape[1])).astype(f32),
            b_q,
            b_kv_wide,
            a_o_wide,
        ],
    )
    blank = jnp.zeros((seqs, experts, rank, hidden), bf16)
    b_gu = jnp.stack(
        [gate_up_columns(ffn_low[:, :experts], blank), gate_up_columns(blank, ffn_low[:, experts : 2 * experts])],
        axis=2,
    ).reshape(seqs, 2 * experts * rank, 2 * hidden)
    a_d = jnp.pad(ffn_low[:, 2 * experts :].reshape(seqs, experts * rank, hidden), ((0, 0), (64, 0), (0, 0)))
    rest = rest.reshape(model, 512)
    ff_parts, ff_own, dx1b, dx1_own, n2, z_sum, gu_sum, d_sum = feed_forward(
        [
            norm2_gain[None],
            jnp.pad(router_ffn, ((0, 0), (0, 128 - experts))),
            table,
            b_gu.reshape(256, 2 * hidden),
            a_d.reshape(256, hidden),
            z_o_gated,
        ],
        [x0, sum_out, rest, dy, w_gate_up, w_down],
    )
    mixed, grad_tokens, wide_a, wide_b, head_sum = backward(
        [
            dx1b, dx1_own, ob, gates, z_q, z_kv, z_sum, table, norm1_gain[None], router_wide, b_q, b_kv_wide, a_o_wide, ff_parts, ff_own,
        ],
        [w_query, w_key_value, w_out, wide, rest, x0, n1, n2, dy, kv_all, q_all, probs],
    )
    grad_wide = jnp.concatenate([wide_a, wide_b[:, : 704 - 512]], axis=1).T
    back_order = np.argsort(np.array([q * wide_slots + s for q, s in order]))
    grad_wide = grad_wide.reshape(seqs * wide_slots, rank, -1)[back_order]
    grad_wide = by_sequence(grad_wide.reshape(seqs, wide_slots, rank, -1))
    head_sum = jnp.swapaxes(head_sum, 0, 1).reshape(-1, rank, width).astype(f32)
    grad_heads = by_sequence(jnp.concatenate(
        [
            head_sum[: seqs * experts].reshape(seqs, experts, rank, width),
            jnp.swapaxes(head_sum[8:12].reshape(2, seqs, rank, width), 0, 1),
            head_sum[12:20].reshape(seqs, experts, rank, width),
        ],
        axis=1,
    ))
    gu_sum = jnp.swapaxes(gu_sum, 0, 1).reshape(seqs, experts, 2, rank, 768).astype(f32)
    grad_ffn = by_sequence(jnp.concatenate(
        [
            gu_sum[:, :, 0, :, :704],
            jnp.concatenate([gu_sum[:, :, 1, :, :640], gu_sum[:, :, 1, :, 704:]], axis=-1),
            jnp.swapaxes(d_sum, 0, 1).reshape(seqs, experts, rank, hidden),
        ],
        axis=1,
    ))
    mixed = mixed.reshape(seqs, block, part)
    grad_tokens = grad_tokens.reshape(seqs, block, part)
    return (mixed, grad_tokens, grad_wide, grad_heads, grad_ffn)


def solution(mesh):
    placed = (
        P(None, "ctx", "tp"),
        P(),
        P(),
        P(None, "ctx", "tp"),
        P("ctx", None, "tp"),
        P(None, "tp", "ctx"),
        P(),
        P(),
        P(None, "ctx", None, "tp"),
        P(None, "tp", "ctx"),
        P(None, None, None, ("ctx", "tp")),
        P(None, None, None, "tp"),
        P(None, None, None, "tp"),
        P(None, "ctx", None),
        P(None, "ctx", None),
        P(),
        P(),
        P(None, "ctx", "tp"),
    )
    return jax.shard_map(
        shards,
        mesh=mesh,
        in_specs=placed,
        out_specs=(
            P(None, "ctx", "tp"),
            P(None, "ctx", "tp"),
            P(None, None, None, ("ctx", "tp")),
            P(None, None, None, "tp"),
            P(None, None, None, "tp"),
        ),
        check_vma=False,
    )
```
